32 devices in a mesh: dp: 4 (over z), index: 8 (over y, x, core).
Axes of the slice: x: 2, y: 2, z: 4, core: 2. Of those that a mesh axis runs over, the one named last changes fastest.
Arguments:
- decoder_input: bfloat16 [8, 1024, 1024], P('dp', 'index'), may hold values from -6 to 6
- encoder_memory: bfloat16 [8, 1920, 1024], P('dp', 'index'), may hold values from -6 to 6
- question_vectors: bfloat16 [8, 768], P('dp', 'index'), may hold values from -12 to 12
- passage_vectors: bfloat16 [32768, 768], P('index'), may hold values from -0.21875 to 0.21875
- passage_ids: int32 [8, 10], P('dp'), may hold values from 0 to 32767
- valid_count: int32 [8], P('dp'), may hold values from 2 to 10, as said below
- output_grad: bfloat16 [8, 1024, 1024], P('dp', 'index'), may hold values from -6 to 6
- attention_weight: float32 [8, 1024, 1024], P(None, ('dp', 'index'))
- expand_weight: float32 [1024, 4096], P(('dp', 'index')), may hold values from -0.1875 to 0.1875
- contract_weight: float32 [4096, 1024], P(('dp', 'index')), may hold values from -0.09375 to 0.09375
- vector_params: float32 [17, 1024], P(None, ('dp', 'index'))
- attention_mean: float32 [8, 1024, 1024], P(None, ('dp', 'index')), may hold values from -16 to 16
- attention_square: float32 [8, 1024, 1024], P(None, ('dp', 'index')), may hold values from 0.36864 to 5.89824
- expand_mean: float32 [1024, 4096], P(('dp', 'index')), may hold values from -32 to 32
- expand_square: float32 [1024, 4096], P(('dp', 'index')), may hold values from 1.024 to 16.384
- contract_mean: float32 [4096, 1024], P(('dp', 'index')), may hold values from -32 to 32
- contract_square: float32 [4096, 1024], P(('dp', 'index')), may hold values from 1.024 to 16.384
- vector_mean: float32 [17, 1024], P(None, ('dp', 'index')), may hold values from -64 to 64
- vector_square: float32 [17, 1024], P(None, ('dp', 'index')), may hold values from 4.096 to 65.536
Outputs:
- layer_output: bfloat16 [8, 1024, 1024], P('dp', 'index')
- input_gradient: float32 [8, 1024, 1024], P('dp', 'index')
- memory_gradient: float32 [8, 1920, 1024], P('dp', 'index')
- question_gradient: float32 [8, 768], P('dp', 'index')
- updated_attention: float32 [8, 1024, 1024], P(None, ('dp', 'index'))
- mean_attention: float32 [8, 1024, 1024], P(None, ('dp', 'index'))
- square_attention: float32 [8, 1024, 1024], P(None, ('dp', 'index'))
- updated_expand: float32 [1024, 4096], P(('dp', 'index'))
- mean_expand: float32 [1024, 4096], P(('dp', 'index'))
- square_expand: float32 [1024, 4096], P(('dp', 'index'))
- updated_contract: float32 [4096, 1024], P(('dp', 'index'))
- mean_contract: float32 [4096, 1024], P(('dp', 'index'))
- square_contract: float32 [4096, 1024], P(('dp', 'index'))
- updated_vector: float32 [17, 1024], P(None, ('dp', 'index'))
- mean_vector: float32 [17, 1024], P(None, ('dp', 'index'))
- square_vector: float32 [17, 1024], P(None, ('dp', 'index'))
The draws below stay inside these ranges and needn't reach their ends.
Inputs may be any that keep to these rules, and one draw needn't show every extreme that they name: `valid_count`: some question has 10 usable candidates and some has 2.
All inputs are finite; a program needn't handle non-finite values.
Results may differ from the reference program's by a relative error of at most 0.023.
The reference program's roundings to bfloat16 on the way count: a program that leaves them out, or rounds other values in their place, can miss the bound.
Values may be sent and summed in bfloat16 or wider, within the bound.
No kernel may reach another device: no remote copies, remote signals or barrier semaphores. Data moves between devices by JAX's collectives and lax.ppermute only.
A program may use at most 384 MiB of HBM per device.

```python
import math
import jax
import jax.numpy as jnp
from jax import lax

D = 1024
HEADS = 16
HDIM = 64
FF = 4096
QD = 768
K_DOC = 10
MEM_P = 192
STEP = 10
LEN = 1024
SEQS = 8
MEM = 1920
NPASS = 32768


def draw_attention_weight(key, part):
    key = jax.random.fold_in(key, 11)
    base = jnp.clip(jax.random.normal(key, (8, D, D), jnp.float32), -5.0, 5.0) * D ** (-0.5)
    slot = jnp.arange(8)[:, None, None]
    factor = jnp.where(slot == 3, LEN ** 0.5 / 6.0, jnp.where(slot == 7, MEM ** 0.5 / 3.0, 1.0))
    return base * jnp.maximum(factor, 1.0)


def draw_vector_params(key, part):
    key = jax.random.fold_in(key, 12)
    base = jnp.clip(jax.random.normal(key, (17, D), jnp.float32), -4.0, 4.0)
    row_number = jnp.arange(17)[:, None]
    gain_row = (row_number == 11) | (row_number == 13) | (row_number == 15)
    return jnp.where(gain_row, 1.0 + 0.1 * base, 0.2 * base)


def draw_valid_count(key, part):
    key = jax.random.fold_in(key, 13)
    first_key, second_key = jax.random.split(key)
    counts = jax.random.randint(first_key, (SEQS,), 2, K_DOC + 1)
    spot = jax.random.randint(second_key, (), 0, SEQS)
    places = jnp.arange(SEQS)
    counts = jnp.where(places == spot, K_DOC, counts)
    return jnp.where(places == (spot + 1) % SEQS, 2, counts).astype(jnp.int32)


def place_ends(drawn, stream_key, least, top_value):
    longest = drawn.shape.index(max(drawn.shape))
    spots = []
    for shift in (0, 1):
        where = [jax.random.randint(jax.random.fold_in(stream_key, axis), (), 0, length) for axis, length in enumerate(drawn.shape)]
        where[longest] = (where[longest] + shift) % drawn.shape[longest]
        spots.append(tuple(where))
    return drawn.at[spots[0]].set(least).at[spots[1]].set(top_value)


def block_scale(rng, dims, pieces, least, high):
    factor_of = 1.0
    for axis_at, shards_of in pieces:
        draws = jax.random.uniform(jax.random.fold_in(jax.random.fold_in(rng, 6), axis_at), (shards_of,), jnp.float32, least / len(pieces), high / len(pieces))
        factor_of = factor_of * jnp.repeat(jnp.exp(draws), dims[axis_at] // shards_of).reshape((-1,) + (1,) * (len(dims) - 1 - axis_at))
    return factor_of


def centred(key, shape, deviation, limit, cuts=(), held_as=jnp.bfloat16):
    values = jax.random.normal(key, shape, jnp.float32) * deviation
    if len(cuts) > 0:
        values = block_scale(key, shape, cuts, -0.22, 0.18) * values
    return jnp.clip(values, min=-limit, max=limit).astype(held_as)


def setup_inputs(seed: int = 0) -> dict:
    streams_of = jax.random.split(jax.random.key(seed), 20)
    decoder_input = centred(streams_of[0], (SEQS, LEN, D), 1.0, 6.0, ((0, 4), (1, 8)))
    encoder_memory = centred(streams_of[1], (SEQS, MEM, D), 1.0, 6.0, ((0, 4), (1, 8)))
    question_vectors = centred(streams_of[2], (SEQS, QD), 2.0, 12.0, ((0, 4), (1, 8)))
    passage_vectors = centred(streams_of[3], (NPASS, QD), QD ** -0.5, 0.21875, ((0, 8),))
    passage_ids = place_ends(jax.random.randint(streams_of[4], (SEQS, K_DOC), 0, NPASS), jax.random.fold_in(streams_of[4], 1), 0, NPASS - 1).astype(jnp.int32)
    valid_count = draw_valid_count(jax.random.fold_in(streams_of[19], 71), 0)
    output_grad = centred(streams_of[6], (SEQS, LEN, D), 1.0, 6.0, ((0, 4), (1, 8)))
    attention_weight = draw_attention_weight(jax.random.fold_in(streams_of[19], 71), 0)
    expand_weight = centred(streams_of[8], (D, FF), D ** -0.5, 0.1875, ((0, 32),), jnp.float32)
    contract_weight = centred(streams_of[9], (FF, D), FF ** -0.5, 0.09375, ((0, 32),), jnp.float32)
    vector_params = draw_vector_params(jax.random.fold_in(streams_of[19], 71), 0)
    attention_mean = centred(streams_of[11], (8, D, D), (0.033 * (SEQS * LEN) ** 0.5), 16.0, ((1, 32),), jnp.float32)
    attention_square = jnp.clip(jnp.exp(math.log(5.89824) - 2.7725887 * jax.random.uniform(streams_of[12], (8, D, D), jnp.float32) ** block_scale(streams_of[12], (8, D, D), ((1, 32),), -0.2, 0.2)), 0.36864, 5.89824)
    expand_mean = centred(streams_of[13], (D, FF), (0.055 * (SEQS * LEN) ** 0.5), 32.0, ((0, 32),), jnp.float32)
    expand_square = jnp.clip(jnp.exp(math.log(16.384) - 2.7725887 * jax.random.uniform(streams_of[14], (D, FF), jnp.float32) ** block_scale(streams_of[14], (D, FF), ((0, 32),), -0.2, 0.2)), 1.024, 16.384)
    contract_mean = centred(streams_of[15], (FF, D), (0.055 * (SEQS * LEN) ** 0.5), 32.0, ((0, 32),), jnp.float32)
    contract_square = jnp.clip(jnp.exp(math.log(16.384) - 2.7725887 * jax.random.uniform(streams_of[16], (FF, D), jnp.float32) ** block_scale(streams_of[16], (FF, D), ((0, 32),), -0.2, 0.2)), 1.024, 16.384)
    vector_mean = centred(streams_of[17], (17, D), (0.11 * (SEQS * LEN) ** 0.5), 64.0, ((1, 32),), jnp.float32)
    vector_square = jnp.clip(jnp.exp(math.log(65.536) - 2.7725887 * jax.random.uniform(streams_of[18], (17, D), jnp.float32) ** block_scale(streams_of[18], (17, D), ((1, 32),), -0.2, 0.2)), 4.096, 65.536)
    return {"decoder_input": decoder_input, "encoder_memory": encoder_memory, "question_vectors": question_vectors, "passage_vectors": passage_vectors, "passage_ids": passage_ids, "valid_count": valid_count, "output_grad": output_grad, "attention_weight": attention_weight, "expand_weight": expand_weight, "contract_weight": contract_weight, "vector_params": vector_params, "attention_mean": attention_mean, "attention_square": attention_square, "expand_mean": expand_mean, "expand_square": expand_square, "contract_mean": contract_mean, "contract_square": contract_square, "vector_mean": vector_mean, "vector_square": vector_square}


@jax.custom_vjp
def low(v):
    return lax.optimization_barrier(v.astype(jnp.bfloat16)).astype(jnp.float32)

@jax.custom_vjp
def low_back(v):
    return v

def low_keep(v):
    return (low(v), None)

def low_pass(kept, grad):
    return (grad,)

def back_keep(v):
    return (v, None)

def back_low(kept, grad):
    return (low(grad),)
low.defvjp(low_keep, low_pass)
low_back.defvjp(back_keep, back_low)
highest = lax.Precision.HIGHEST
negative_fill = -1e+30
norm_eps = 1e-05
beta_first = 0.9
beta_second = 0.999
adam_eps = 1e-08
decay_matrix = 0.01
rate_attention = 0.1
rate_expand = 0.02
rate_contract = 0.01
rate_vector = 0.2

def project(left_side, weight):
    return jnp.dot(left_side, weight, precision=highest)

def layer_norm(hidden, norm_gain, norm_shift):
    center = hidden - lax.optimization_barrier(jnp.mean(hidden, axis=-1, keepdims=True))
    spread = lax.optimization_barrier(jnp.mean(center * center, axis=-1, keepdims=True))
    return center * lax.rsqrt(spread + norm_eps) * norm_gain + norm_shift

def split_heads(matrix):
    return matrix.reshape(matrix.shape[0], HEADS, HDIM)

def attention(queries, key_rows, values, score_bias, allowed):
    scores = jnp.einsum('qhd,khd->hqk', split_heads(queries), split_heads(key_rows), precision=highest) * 0.125 + score_bias
    scores = jnp.where(allowed, low_back(scores), negative_fill)
    maximum = lax.optimization_barrier(jnp.max(scores, axis=-1, keepdims=True))
    exponent = jnp.exp(scores - maximum)
    attend_prob = low(exponent / lax.optimization_barrier(jnp.sum(exponent, axis=-1, keepdims=True)))
    mixture = jnp.einsum('hqk,khd->qhd', attend_prob, split_heads(values), precision=highest)
    return low(low_back(mixture.reshape(queries.shape[0], D)))

def one_sequence(params_low, seq_items):
    attention_low, expand_low, contract_low, vector_low = params_low
    tokens, memory, question, passage_rows, counted = seq_items
    positions = jnp.arange(LEN)
    causal = (positions[None, :] <= positions[:, None])[None]
    self_query = low(low_back(project(tokens, attention_low[0])) + vector_low[0])
    self_key = low(low_back(project(tokens, attention_low[1])))
    self_value = low(low_back(project(tokens, attention_low[2])) + vector_low[1])
    self_mixed = attention(self_query, self_key, self_value, 0.0, causal)
    first_out = layer_norm(tokens + low_back(project(self_mixed, attention_low[3])) + vector_low[2], vector_low[11], vector_low[12])
    first_low = low(first_out)
    cross_query = low(low_back(project(first_low, attention_low[4])) + vector_low[3])
    cross_key = low(low_back(project(memory, attention_low[5])))
    cross_value = low(low_back(project(memory, attention_low[6])) + vector_low[4])
    passage_score = jnp.dot(passage_rows, question, precision=highest)
    usable = jnp.arange(K_DOC) < counted
    masked = jnp.where(usable, passage_score, negative_fill)
    maximum = jnp.max(masked)
    exponent = jnp.where(usable, jnp.exp(masked - maximum), 0.0)
    log_prior = masked - maximum - jnp.log(jnp.sum(exponent))
    member = jnp.arange(MEM) // MEM_P
    score_bias = jnp.repeat(log_prior, MEM_P)[None, None, :]
    allowed = (member < counted)[None, None, :]
    cross_mixed = attention(cross_query, cross_key, cross_value, score_bias, allowed)
    second_out = layer_norm(first_out + low_back(project(cross_mixed, attention_low[7])) + vector_low[5], vector_low[13], vector_low[14])
    second_low = low(second_out)
    inner_act = low_back(project(second_low, expand_low)) + vector_low[6:10].reshape(FF)
    activated = low(jax.nn.gelu(inner_act, approximate=False))
    return layer_norm(second_out + low_back(project(activated, contract_low)) + vector_low[10], vector_low[15], vector_low[16])

def adam_update(weight, moment_one, moment_two, gradient, step_rate, weight_decay):
    mean_new = beta_first * moment_one + (1.0 - beta_first) * gradient
    square_new = beta_second * moment_two + (1.0 - beta_second) * gradient * gradient
    mean_hat = mean_new / (1.0 - beta_first ** STEP)
    square_hat = square_new / (1.0 - beta_second ** STEP)
    updated = weight - step_rate * (mean_hat / (jnp.sqrt(square_hat) + adam_eps) + weight_decay * weight)
    return (updated, mean_new, square_new)

def reference(decoder_input, encoder_memory, question_vectors, passage_vectors, passage_ids, valid_count, output_grad, attention_weight, expand_weight, contract_weight, vector_params, attention_mean, attention_square, expand_mean, expand_square, contract_mean, contract_square, vector_mean, vector_square):
    passage_rows = passage_vectors[passage_ids].astype(jnp.float32)

    def forward(attention_full, expand_full, contract_full, vector_full, tokens, memory, question):
        params_low = (low(attention_full), low(expand_full), low(contract_full), low(vector_full))

        def per_sequence(seq_items):
            return one_sequence(params_low, seq_items)
        return lax.map(jax.checkpoint(per_sequence), (tokens, memory, question, passage_rows, valid_count))
    layer_value, pullback = jax.vjp(forward, attention_weight, expand_weight, contract_weight, vector_params, decoder_input.astype(jnp.float32), encoder_memory.astype(jnp.float32), question_vectors.astype(jnp.float32))
    gradients = pullback(output_grad.astype(jnp.float32))
    new_attention = adam_update(attention_weight, attention_mean, attention_square, gradients[0], rate_attention, decay_matrix)
    new_expand = adam_update(expand_weight, expand_mean, expand_square, gradients[1], rate_expand, decay_matrix)
    new_contract = adam_update(contract_weight, contract_mean, contract_square, gradients[2], rate_contract, decay_matrix)
    new_vector = adam_update(vector_params, vector_mean, vector_square, gradients[3], rate_vector, 0.0)
    return (layer_value.astype(jnp.bfloat16), gradients[4], gradients[5], gradients[6], new_attention[0], new_attention[1], new_attention[2], new_expand[0], new_expand[1], new_expand[2], new_contract[0], new_contract[1], new_contract[2], new_vector[0], new_vector[1], new_vector[2])
```

```python
from functools import partial

import jax
import jax.numpy as jnp
from jax import lax
from jax.experimental import pallas as pl
from jax.experimental.pallas import tpu as pltpu
from jax.sharding import PartitionSpec as P

HEADS = 16
MEM_P = 192
STEP = 10


negative_fill = -1e30
norm_eps = 1e-05
beta_first = 0.9
beta_second = 0.999
adam_eps = 1e-08
decay_matrix = 0.01
rate_attention = 0.1
rate_expand = 0.02
rate_contract = 0.01
rate_vector = 0.2


def layer_norm(hidden, norm_gain, norm_shift):
    center = hidden - jnp.mean(hidden, axis=-1, keepdims=True)
    spread = jnp.mean(center * center, axis=-1, keepdims=True)
    return center * lax.rsqrt(spread + norm_eps) * norm_gain + norm_shift


def split_heads(matrix):
    return matrix.reshape(matrix.shape[0], matrix.shape[1], HEADS, matrix.shape[2] // HEADS)


def merge_heads(matrix):
    return matrix.reshape(matrix.shape[0], matrix.shape[1], matrix.shape[2] * matrix.shape[3])


def project(left_side, weight):
    return jnp.einsum("srd,de->sre", left_side, weight, preferred_element_type=jnp.float32)


def project_back(gradient, weight):
    return jnp.einsum("sre,de->srd", gradient, weight, preferred_element_type=jnp.float32)


def weight_grad(left_side, gradient):
    return jnp.einsum("srd,sre->de", left_side, gradient, preferred_element_type=jnp.float32)


def row_total(values):
    return jnp.sum(values, axis=(0, 1))


def attend_forward(queries, key_rows, values, score_bias, allowed):
    scores = (
        jnp.einsum(
            "sqhd,skhd->shqk",
            split_heads(queries),
            split_heads(key_rows),
            preferred_element_type=jnp.float32,
        )
        * 0.125
        + score_bias
    )
    scores = jnp.where(allowed, scores, negative_fill)
    maximum = jnp.max(scores, axis=-1)
    exponent = jnp.exp(scores - maximum[..., None])
    partition = jnp.sum(exponent, axis=-1)
    attend_prob = exponent / partition[..., None]
    mixture = jnp.einsum(
        "shqk,skhd->sqhd",
        attend_prob.astype(jnp.bfloat16),
        split_heads(values),
        preferred_element_type=jnp.float32,
    )
    return (merge_heads(mixture).astype(jnp.bfloat16), attend_prob, maximum, partition)


def score_grads(grad_mixed, attend_prob, values):
    grad_prob = jnp.einsum(
        "sqhd,skhd->shqk",
        split_heads(grad_mixed),
        split_heads(values),
        preferred_element_type=jnp.float32,
    )
    row_inner = jnp.sum(attend_prob * grad_prob, axis=-1)
    return ((attend_prob * (grad_prob - row_inner[..., None])).astype(jnp.bfloat16), row_inner)


def to_queries(grad_score, key_rows):
    return (
        merge_heads(
            jnp.einsum(
                "shqk,skhd->sqhd",
                grad_score,
                split_heads(key_rows),
                preferred_element_type=jnp.float32,
            )
        )
        * 0.125
    )


def to_keys(grad_score, attend_prob, queries, grad_mixed):
    grad_key = (
        merge_heads(
            jnp.einsum(
                "shqk,sqhd->skhd",
                grad_score,
                split_heads(queries),
                preferred_element_type=jnp.float32,
            )
        )
        * 0.125
    )
    grad_value = merge_heads(
        jnp.einsum(
            "shqk,sqhd->skhd",
            attend_prob.astype(jnp.bfloat16),
            split_heads(grad_mixed),
            preferred_element_type=jnp.float32,
        )
    )
    return (grad_key, grad_value)


def adam_update(weight, moment_one, moment_two, gradient, step_rate, weight_decay):
    mean_new = beta_first * moment_one + (1.0 - beta_first) * gradient
    square_new = beta_second * moment_two + (1.0 - beta_second) * gradient * gradient
    mean_hat = mean_new / (1.0 - beta_first**STEP)
    square_hat = square_new / (1.0 - beta_second**STEP)
    updated = weight - step_rate * (
        mean_hat / (jnp.sqrt(square_hat) + adam_eps) + weight_decay * weight
    )
    return (updated, mean_new, square_new)


def general_body(
    decoder_input,
    encoder_memory,
    question_vectors,
    passage_vectors,
    passage_ids,
    valid_count,
    output_grad,
    attention_weight,
    expand_weight,
    contract_weight,
    vector_params,
    attention_mean,
    attention_square,
    expand_mean,
    expand_square,
    contract_mean,
    contract_square,
    vector_mean,
    vector_square,
):
    attention_low, expand_low, contract_low, vector_low = (
        lax.all_gather(attention_weight.astype(jnp.bfloat16), ("dp", "index"), axis=1, tiled=True),
        lax.all_gather(expand_weight.astype(jnp.bfloat16), ("dp", "index"), axis=0, tiled=True),
        lax.all_gather(contract_weight.astype(jnp.bfloat16), ("dp", "index"), axis=0, tiled=True),
        lax.all_gather(vector_params.astype(jnp.bfloat16), ("dp", "index"), axis=1, tiled=True),
    )
    vectors = vector_low.astype(jnp.float32)
    seqs_here, rows_here, model_width = decoder_input.shape
    shard_index = lax.axis_index("index")
    length = rows_here * lax.axis_size("index")
    ffn_width = expand_low.shape[1]
    self_query = (project(decoder_input, attention_low[0]) + vectors[0]).astype(jnp.bfloat16)
    self_key = project(decoder_input, attention_low[1]).astype(jnp.bfloat16)
    self_value = (project(decoder_input, attention_low[2]) + vectors[1]).astype(jnp.bfloat16)
    key_all, value_all = (
        lax.all_gather(self_key, "index", axis=1, tiled=True),
        lax.all_gather(self_value, "index", axis=1, tiled=True),
    )
    query_place = shard_index * rows_here + jnp.arange(rows_here)
    causal = (jnp.arange(length)[None, :] <= query_place[:, None])[None, None]
    self_mixed, self_prob, self_peak, self_total = attend_forward(
        self_query, key_all, value_all, 0.0, causal
    )
    first_in = (
        decoder_input.astype(jnp.float32) + project(self_mixed, attention_low[3]) + vectors[2]
    )
    first_out, first_back = jax.vjp(layer_norm, first_in, vectors[11], vectors[12])
    first_low = first_out.astype(jnp.bfloat16)
    cross_query = (project(first_low, attention_low[4]) + vectors[3]).astype(jnp.bfloat16)
    cross_key = project(encoder_memory, attention_low[5]).astype(jnp.bfloat16)
    cross_value = (project(encoder_memory, attention_low[6]) + vectors[4]).astype(jnp.bfloat16)
    memory_keys, memory_values = (
        lax.all_gather(cross_key, "index", axis=1, tiled=True),
        lax.all_gather(cross_value, "index", axis=1, tiled=True),
    )
    question_full = lax.all_gather(question_vectors, "index", axis=1, tiled=True)
    passages_here = passage_vectors.shape[0]
    local_ids = passage_ids - shard_index * passages_here
    owned_slot = (local_ids >= 0) & (local_ids < passages_here)
    picked = passage_vectors[jnp.clip(local_ids, 0, passages_here - 1)]
    local_scores = jnp.einsum(
        "sc,skc->sk", question_full, picked, preferred_element_type=jnp.float32
    )
    slots = passage_ids.shape[1]
    usable = jnp.arange(slots)[None, :] < valid_count[:, None]
    local_peak = jnp.max(jnp.where(owned_slot & usable, local_scores, negative_fill), axis=1)
    maximum = lax.pmax(local_peak, "index")
    local_exp = jnp.where(owned_slot & usable, jnp.exp(local_scores - maximum[:, None]), 0.0)
    exponent, scores = lax.psum((local_exp, jnp.where(owned_slot, local_scores, 0.0)), "index")
    masked = jnp.where(usable, scores, negative_fill)
    partition = jnp.sum(exponent, axis=1)
    passage_prob = exponent / partition[:, None]
    log_prior = masked - maximum[:, None] - jnp.log(partition)[:, None]
    memory_total = memory_keys.shape[1]
    bias_rows = jnp.repeat(log_prior, MEM_P, axis=1)
    key_bias = bias_rows[:, None, None, :]
    key_usable = ((jnp.arange(memory_total) // MEM_P)[None, :] < valid_count[:, None])[
        :, None, None, :
    ]
    cross_mixed, cross_prob, cross_peak, cross_total = attend_forward(
        cross_query, memory_keys, memory_values, key_bias, key_usable
    )
    second_in = first_out + project(cross_mixed, attention_low[7]) + vectors[5]
    second_out, second_back = jax.vjp(layer_norm, second_in, vectors[13], vectors[14])
    second_low = second_out.astype(jnp.bfloat16)
    inner_act = project(second_low, expand_low) + vectors[6:10].reshape(ffn_width)
    activated, gelu_back = jax.vjp(partial(jax.nn.gelu, approximate=False), inner_act)
    activ_low = activated.astype(jnp.bfloat16)
    third_in = second_out + project(activ_low, contract_low) + vectors[10]
    layer_output, third_back = jax.vjp(layer_norm, third_in, vectors[15], vectors[16])
    grad_third, gain_three, shift_three = third_back(output_grad.astype(jnp.float32))
    grad_ffn_low = grad_third.astype(jnp.bfloat16)
    grad_contract = weight_grad(activ_low, grad_ffn_low)
    (grad_inner,) = gelu_back(project_back(grad_ffn_low, contract_low))
    grad_inner_low = grad_inner.astype(jnp.bfloat16)
    grad_expand = weight_grad(second_low, grad_inner_low)
    grad_second = grad_third + project_back(grad_inner_low, expand_low)
    grad_second_in, gain_two, shift_two = second_back(grad_second)
    grad_cross_low = grad_second_in.astype(jnp.bfloat16)
    grad_cmix = project_back(grad_cross_low, attention_low[7]).astype(jnp.bfloat16)
    cross_score, cross_inner = score_grads(grad_cmix, cross_prob, memory_values)
    grad_cq = to_queries(cross_score, memory_keys)
    prior_part = (
        jnp.sum(cross_score, axis=(1, 2), dtype=jnp.float32)
        .reshape(seqs_here, slots, MEM_P)
        .sum(axis=-1)
    )
    prior_grad = jnp.where(usable, lax.psum(prior_part, "index"), 0.0)
    score_doc = jnp.where(
        usable, prior_grad - passage_prob * jnp.sum(prior_grad, axis=1, keepdims=True), 0.0
    )
    question_part = jnp.einsum(
        "sk,skc->sc",
        jnp.where(owned_slot, score_doc, 0.0),
        picked.astype(jnp.float32),
        precision=lax.Precision.HIGHEST,
    )
    question_gradient = lax.psum_scatter(question_part, "index", scatter_dimension=1, tiled=True)
    grad_cq_low = grad_cq.astype(jnp.bfloat16)
    grad_first = grad_second_in + project_back(grad_cq_low, attention_low[4])
    ck_part, cv_part = to_keys(cross_score, cross_prob, cross_query, grad_cmix)
    grad_ck, grad_cv = (
        lax.psum_scatter(
            ck_part.astype(jnp.bfloat16), "index", scatter_dimension=1, tiled=True
        ).astype(jnp.float32),
        lax.psum_scatter(
            cv_part.astype(jnp.bfloat16), "index", scatter_dimension=1, tiled=True
        ).astype(jnp.float32),
    )
    grad_ck_low = grad_ck.astype(jnp.bfloat16)
    grad_cv_low = grad_cv.astype(jnp.bfloat16)
    memory_gradient = project_back(grad_ck_low, attention_low[5]) + project_back(
        grad_cv_low, attention_low[6]
    )
    grad_first_in, gain_one, shift_one = first_back(grad_first)
    grad_self_low = grad_first_in.astype(jnp.bfloat16)
    grad_smix = project_back(grad_self_low, attention_low[3]).astype(jnp.bfloat16)
    self_score, row_inner = score_grads(grad_smix, self_prob, value_all)
    grad_sq = to_queries(self_score, key_all)
    key_part, value_part = to_keys(self_score, self_prob, self_query, grad_smix)
    grad_sk, grad_sv = (
        lax.psum_scatter(
            key_part.astype(jnp.bfloat16), "index", scatter_dimension=1, tiled=True
        ).astype(jnp.float32),
        lax.psum_scatter(
            value_part.astype(jnp.bfloat16), "index", scatter_dimension=1, tiled=True
        ).astype(jnp.float32),
    )
    grad_sq_low = grad_sq.astype(jnp.bfloat16)
    grad_sk_low = grad_sk.astype(jnp.bfloat16)
    grad_sv_low = grad_sv.astype(jnp.bfloat16)
    input_gradient = (
        grad_first_in
        + project_back(grad_sq_low, attention_low[0])
        + project_back(grad_sk_low, attention_low[1])
        + project_back(grad_sv_low, attention_low[2])
    )
    attention_grads = jnp.stack(
        [
            weight_grad(decoder_input, grad_sq_low),
            weight_grad(decoder_input, grad_sk_low),
            weight_grad(decoder_input, grad_sv_low),
            weight_grad(self_mixed, grad_self_low),
            weight_grad(first_low, grad_cq_low),
            weight_grad(encoder_memory, grad_ck_low),
            weight_grad(encoder_memory, grad_cv_low),
            weight_grad(cross_mixed, grad_cross_low),
        ]
    )
    vector_grads = jnp.concatenate(
        [
            jnp.stack(
                [
                    row_total(grad_sq),
                    row_total(grad_sv),
                    row_total(grad_first_in),
                    row_total(grad_cq),
                    row_total(grad_cv),
                    row_total(grad_second_in),
                ]
            ),
            row_total(grad_inner).reshape(ffn_width // model_width, model_width),
            jnp.stack(
                [
                    row_total(grad_third),
                    gain_one,
                    shift_one,
                    gain_two,
                    shift_two,
                    gain_three,
                    shift_three,
                ]
            ),
        ]
    )
    attention_sum, expand_sum, contract_sum, vector_sum = (
        lax.psum_scatter(attention_grads, ("dp", "index"), scatter_dimension=1, tiled=True),
        lax.psum_scatter(grad_expand, ("dp", "index"), scatter_dimension=0, tiled=True),
        lax.psum_scatter(grad_contract, ("dp", "index"), scatter_dimension=0, tiled=True),
        lax.psum_scatter(vector_grads, ("dp", "index"), scatter_dimension=1, tiled=True),
    )
    new_attention = adam_update(
        attention_weight,
        attention_mean,
        attention_square,
        attention_sum,
        rate_attention,
        decay_matrix,
    )
    new_expand = adam_update(
        expand_weight, expand_mean, expand_square, expand_sum, rate_expand, decay_matrix
    )
    new_contract = adam_update(
        contract_weight, contract_mean, contract_square, contract_sum, rate_contract, decay_matrix
    )
    new_vector = adam_update(
        vector_params, vector_mean, vector_square, vector_sum, rate_vector, 0.0
    )
    return (
        layer_output.astype(jnp.bfloat16),
        input_gradient,
        memory_gradient,
        question_gradient,
        new_attention[0],
        new_attention[1],
        new_attention[2],
        new_expand[0],
        new_expand[1],
        new_expand[2],
        new_contract[0],
        new_contract[1],
        new_contract[2],
        new_vector[0],
        new_vector[1],
        new_vector[2],
    )


NT = (((1,), (1,)), ((), ()))
NN = (((1,), (0,)), ((), ()))
TN = (((0,), (0,)), ((), ()))
CHIPS = 4
DP_ORDER = (0, 2, 1, 3)
VMEM_LIMIT = 56 << 20


def dot(left_side, right_side, dims):
    return lax.dot_general(left_side, right_side, dims, preferred_element_type=jnp.float32)


def norm_parts(hidden):
    center = hidden - jnp.mean(hidden, axis=-1, keepdims=True)
    inverse = lax.rsqrt(jnp.mean(center * center, axis=-1, keepdims=True) + norm_eps)
    return center * inverse, inverse


def norm_back(gradient, unit, inverse, gain):
    scaled = gradient * gain
    return inverse * (
        scaled
        - jnp.mean(scaled, axis=-1, keepdims=True)
        - unit * jnp.mean(scaled * unit, axis=-1, keepdims=True)
    )


def column_sum(values):
    return jnp.sum(values, axis=0, keepdims=True)


def join(parts, place=None):
    picked = [parts[j] if place is None else parts[j, place] for j in range(parts.shape[0])]
    return jnp.concatenate(
        [block.reshape(block.shape[0] * block.shape[1], block.shape[2]) for block in picked],
        axis=1,
    )


def spread(out_ref, value):
    count, seqs, rows, width = out_ref.shape
    for j in range(count):
        out_ref[j] = value[:, j * width : (j + 1) * width].reshape(seqs, rows, width)


def times(activation, weight):
    count, groups, rows, width = weight.shape
    depth = count * rows
    total = None
    for d in range(groups):
        part = dot(
            activation[:, d * depth : (d + 1) * depth], weight[:, d].reshape(depth, width), NN
        )
        total = part if total is None else total + part
    return total


def times_back(gradient, weight):
    count, groups, rows, width = weight.shape
    depth = count * rows
    return jnp.concatenate(
        [dot(gradient, weight[:, d].reshape(depth, width), NT) for d in range(groups)], axis=1
    )


def outer(out_ref, left_side, gradient):
    count, groups, rows, width = out_ref.shape
    depth = count * rows
    for d in range(groups):
        out_ref[:, d] = (
            dot(left_side[:, d * depth : (d + 1) * depth], gradient, TN)
            .astype(jnp.bfloat16)
            .reshape(count, rows, width)
        )


def whole(array):
    return pl.BlockSpec(array.shape, lambda *_, rank=len(array.shape): (0,) * rank)


def shape(dims, dtype):
    return jax.ShapeDtypeStruct(tuple(dims), dtype)


def params():
    return pltpu.CompilerParams(vmem_limit_bytes=VMEM_LIMIT)


def cost(flops, moved):
    return pl.CostEstimate(flops=int(flops) // 16, bytes_accessed=int(moved) // 16, transcendentals=0)


def in_head(dims, head_width, head):
    return lax.broadcasted_iota(jnp.int32, dims, 1) // head_width == head


def attend_forward_kernel(causal, head_width, q_ref, k_ref, v_ref, bias_ref, out_ref, stat_ref):
    count, _, tile, width = q_ref.shape
    keys = k_ref.shape[0] * k_ref.shape[2]
    key_rows, values = k_ref[...].reshape(keys, width), v_ref[...].reshape(keys, width)
    step = 2
    rows = step * tile
    for b in range(count // step):
        queries = q_ref[b * step : (b + 1) * step].reshape(rows, width)
        seen = (b + 1) * rows if causal else keys
        mixed = None
        for h in range(width // head_width):
            mask = in_head((rows, width), head_width, h)
            scores = dot(
                jnp.where(mask, queries * 0.125, 0).astype(jnp.bfloat16), key_rows[:seen], NT
            )
            if causal:
                corner = scores[:, seen - rows :]
                corner = jnp.where(
                    lax.broadcasted_iota(jnp.int32, corner.shape, 1)
                    <= lax.broadcasted_iota(jnp.int32, corner.shape, 0),
                    corner,
                    negative_fill,
                )
                if b == 0:
                    scores = corner
                else:
                    scores = jnp.concatenate([scores[:, : seen - rows], corner], axis=1)
            else:
                scores = scores + bias_ref[0]
            peak = jnp.max(scores, axis=1, keepdims=True)
            exponent = jnp.exp(scores - peak)
            total = jnp.sum(exponent, axis=1, keepdims=True)
            prob = (exponent * (1.0 / total)).astype(jnp.bfloat16)
            part = dot(prob, values[:seen], NN)
            mixed = part if mixed is None else jnp.where(mask, part, mixed)
            log_total = jnp.broadcast_to(peak + jnp.log(total), (rows, 128))
            stat_ref[0, h : h + 1, b * rows : (b + 1) * rows] = log_total.T[0:1]
        out_ref[b * step : (b + 1) * step] = mixed.astype(jnp.bfloat16).reshape(
            step, 1, tile, width
        )


def attend_backward_kernel(
    causal,
    head_width,
    q_ref,
    k_ref,
    v_ref,
    grad_ref,
    stat_ref,
    bias_ref,
    _,
    dq_ref,
    dkv_ref,
    prior_ref,
    dk_sum,
    dv_sum,
    prior_sum,
):
    count, _, tile, width = q_ref.shape
    keys = k_ref.shape[0] * k_ref.shape[2]
    key_rows, values = k_ref[...].reshape(keys, width), v_ref[...].reshape(keys, width)
    step = 2
    rows = step * tile
    dk_sum[...] = jnp.zeros_like(dk_sum)
    dv_sum[...] = jnp.zeros_like(dv_sum)
    if not causal:
        prior_sum[...] = jnp.zeros_like(prior_sum)
    for b in range(count // step):
        queries = q_ref[b * step : (b + 1) * step].reshape(rows, width)
        gradient = grad_ref[b * step : (b + 1) * step].reshape(rows, width)
        seen = (b + 1) * rows if causal else keys
        query_grad = None
        for h in range(width // head_width):
            mask = in_head((rows, width), head_width, h)
            one_query = jnp.where(mask, queries * 0.125, 0).astype(jnp.bfloat16)
            one_grad = jnp.where(mask, gradient, 0).astype(jnp.bfloat16)
            scores = dot(key_rows[:seen], one_query, NT)
            if causal:
                corner = scores[seen - rows :]
                corner = jnp.where(
                    lax.broadcasted_iota(jnp.int32, corner.shape, 0)
                    <= lax.broadcasted_iota(jnp.int32, corner.shape, 1),
                    corner,
                    negative_fill,
                )
                if b == 0:
                    scores = corner
                else:
                    scores = jnp.concatenate([scores[: seen - rows], corner], axis=0)
            else:
                scores = scores + bias_ref[0]
            prob = jnp.exp(scores - stat_ref[0, h : h + 1, b * rows : (b + 1) * rows])
            grad_prob = dot(values[:seen], one_grad, NT)
            inner = jnp.sum(prob * grad_prob, axis=0, keepdims=True)
            grad_score = prob * (grad_prob - inner)
            score_low = grad_score.astype(jnp.bfloat16)
            dv_sum[:seen] += dot(prob.astype(jnp.bfloat16), one_grad, NN)
            dk_sum[:seen] += dot(score_low, one_query, NN)
            if not causal:
                partial_sum = grad_score[:, :128]
                for piece in range(128, rows, 128):
                    partial_sum = partial_sum + grad_score[:, piece : piece + 128]
                prior_sum[...] += partial_sum
            part = dot(score_low, key_rows[:seen], TN)
            query_grad = part if query_grad is None else jnp.where(mask, part, query_grad)
        dq_ref[b * step : (b + 1) * step] = (
            (query_grad * 0.125).astype(jnp.bfloat16).reshape(step, 1, tile, width)
        )
    dkv_ref[:, 0] = dk_sum[...].astype(jnp.bfloat16).reshape(k_ref.shape)
    dkv_ref[:, 1] = dv_sum[...].astype(jnp.bfloat16).reshape(k_ref.shape)
    if causal:
        prior_ref[...] = jnp.zeros_like(prior_ref)
    else:
        prior_ref[0] = jnp.sum(prior_sum[...], axis=1, keepdims=True)


def pick(array, place):
    count, _, _, rows, width = array.shape
    return pl.BlockSpec((count, None, 1, rows, width), lambda s: (0, place, s, 0, 0))


def attend(causal, queries, query_at, keys, key_at, value_at, bias):
    count, _, seqs, tile, width = queries.shape
    key_rows = keys.shape[0] * keys.shape[3]
    head_width = width * count // HEADS
    length = count * tile
    heads = width // head_width
    return pl.pallas_call(
        partial(attend_forward_kernel, causal, head_width),
        grid=(seqs,),
        in_specs=[
            pick(queries, query_at),
            pick(keys, key_at),
            pick(keys, value_at),
            pl.BlockSpec(memory_space=pl.ANY)
            if causal
            else pl.BlockSpec((1, 1, key_rows), lambda s: (s, 0, 0)),
        ],
        out_specs=[
            pl.BlockSpec((count, 1, tile, width), lambda s: (0, s, 0, 0)),
            pl.BlockSpec((1, heads, length), lambda s: (s, 0, 0)),
        ],
        out_shape=[
            shape((count, seqs, tile, width), jnp.bfloat16),
            shape((seqs, heads, length), jnp.float32),
        ],
        compiler_params=params(),
        cost_estimate=cost(
            16 * seqs * length * key_rows * width, 4 * seqs * (length + key_rows) * width
        ),
        name="attend_self" if causal else "attend_memory",
    )(queries, keys, keys, bias)


def attend_back(
    causal, queries, query_at, keys, key_at, value_at, gradient, stat, bias, after
):
    count, _, seqs, tile, width = queries.shape
    key_tile = keys.shape[3]
    key_rows = count * key_tile
    head_width = width * count // HEADS
    length = count * tile
    heads = width // head_width
    return pl.pallas_call(
        partial(attend_backward_kernel, causal, head_width),
        grid=(seqs,),
        in_specs=[
            pick(queries, query_at),
            pick(keys, key_at),
            pick(keys, value_at),
            pl.BlockSpec((count, 1, tile, width), lambda s: (0, s, 0, 0)),
            pl.BlockSpec((1, heads, length), lambda s: (s, 0, 0)),
            pl.BlockSpec(memory_space=pl.ANY)
            if causal
            else pl.BlockSpec((1, key_rows, 1), lambda s: (s, 0, 0)),
            pl.BlockSpec(memory_space=pl.ANY),
        ],
        out_specs=[
            pl.BlockSpec((count, 1, tile, width), lambda s: (0, s, 0, 0)),
            pl.BlockSpec((count, 2, 1, key_tile, width), lambda s: (0, 0, s, 0, 0)),
            pl.BlockSpec((1, key_rows, 1), lambda s: (s, 0, 0)),
        ],
        out_shape=[
            shape((count, seqs, tile, width), jnp.bfloat16),
            shape((count, 2, seqs, key_tile, width), jnp.bfloat16),
            shape((seqs, key_rows, 1), jnp.float32),
        ],
        scratch_shapes=[
            pltpu.VMEM((key_rows, width), jnp.float32),
            pltpu.VMEM((key_rows, width), jnp.float32),
            pltpu.VMEM((key_rows, 128), jnp.float32),
        ],
        compiler_params=params(),
        cost_estimate=cost(
            40 * seqs * length * key_rows * width, 8 * seqs * (length + key_rows) * width
        ),
        name="attend_self_back" if causal else "attend_memory_back",
    )(queries, keys, keys, gradient, stat, bias, after)


def take_columns(scratch, slices, first):
    width = slices.shape[3]
    depth = scratch.shape[0]
    rows = depth // (slices.shape[0] * slices.shape[1])
    for m in range(scratch.shape[1] // width):
        start = (first + m) * rows
        scratch[:, m * width : (m + 1) * width] = slices[:, :, start : start + rows].reshape(
            depth, width
        )


def columns_kernel(first, row_ref, slice_ref, bias_ref, out_ref, weight):
    @pl.when(pl.program_id(0) == 0)
    def _():
        take_columns(weight, slice_ref, first)

    _, many, seqs, rows, width = out_ref.shape
    taken = row_ref[0, :, :rows].reshape(seqs * rows, weight.shape[0])
    result = dot(taken, weight[...], NN) + bias_ref[...]
    for m in range(many):
        out_ref[0, m] = (
            result[:, m * width : (m + 1) * width]
            .astype(jnp.bfloat16)
            .reshape(seqs, rows, width)
        )


def project_columns(name, gathered_rows, block_rows, row_block, rows, slices, first, many, bias):
    count, seqs, _, depth = gathered_rows.shape
    width = slices.shape[3]
    return pl.pallas_call(
        partial(columns_kernel, first),
        grid=(count,),
        in_specs=[
            pl.BlockSpec((1, seqs, block_rows, depth), lambda i: (i, 0, row_block, 0)),
            whole(slices),
            whole(bias),
        ],
        out_specs=pl.BlockSpec((1, many, seqs, rows, width), lambda i: (i, 0, 0, 0, 0)),
        out_shape=shape((count, many, seqs, rows, width), jnp.bfloat16),
        scratch_shapes=[pltpu.VMEM((depth, many * width), jnp.bfloat16)],
        compiler_params=params(),
        cost_estimate=cost(
            2 * many * count * seqs * rows * depth * width, 2 * count * seqs * rows * depth
        ),
        name=name,
    )(gathered_rows, slices, bias)


def columns_back_kernel(
    first, _, row_ref, *refs
):
    grad_refs, (slice_ref, mine_out, other_out, dw_ref, bias_ref, weight, total) = (
        refs[:-7],
        refs[-7:],
    )
    turn, step = pl.program_id(0), pl.program_id(1)

    @pl.when((turn == 0) & (step == 0))
    def _():
        take_columns(weight, slice_ref, first)
        total[...] = jnp.zeros_like(total)
        bias_ref[...] = jnp.zeros_like(bias_ref)

    depth = weight.shape[0]
    pieces = []
    for grad_ref in grad_refs:
        seqs, rows, width = grad_ref.shape[-3:]
        for m in range(grad_ref.shape[1] if len(grad_ref.shape) == 5 else 1):
            piece = grad_ref[0, m] if len(grad_ref.shape) == 5 else grad_ref[0]
            pieces.append(piece.reshape(seqs * rows, width))
    gradient = jnp.concatenate(pieces, axis=1)
    taken = row_ref[0, :, :rows].reshape(seqs * rows, depth)
    bias_ref[...] += column_sum(gradient.astype(jnp.float32))
    total[...] += dot(taken, gradient, TN)
    row_grad = dot(gradient, weight[...], NT).astype(jnp.bfloat16)

    @pl.when(turn == 0)
    def _():
        mine_out[0, 0] = row_grad

    @pl.when(turn == 1)
    def _():
        other_out[0, 0] = row_grad

    @pl.when((turn == 1) & (step == pl.num_programs(1) - 1))
    def _():
        groups, count, all_rows, _ = dw_ref.shape
        part = depth // (groups * count)
        for m in range(all_rows // part):
            dw_ref[:, :, m * part : (m + 1) * part] = (
                total[:, m * width : (m + 1) * width]
                .astype(jnp.bfloat16)
                .reshape(groups, count, part, width)
            )


def project_columns_back(
    name, order, gathered_rows, block_rows, row_block, rows, gradients, slices, first, many
):
    count, seqs, _, depth = gathered_rows.shape
    half = count // 2
    groups, _, _, width = slices.shape
    part = depth // (groups * count)

    def one_device(array):
        rest = (0,) * (len(array.shape) - 1)
        return pl.BlockSpec(
            (1,) + array.shape[1:], lambda p, k, order: (order[p * half + k],) + rest
        )

    dw_shape = shape((groups, count, many * part, width), jnp.bfloat16)
    return pl.pallas_call(
        partial(columns_back_kernel, first),
        grid_spec=pltpu.PrefetchScalarGridSpec(
            num_scalar_prefetch=1,
            grid=(2, half),
            in_specs=[
                pl.BlockSpec(
                    (1, seqs, block_rows, depth),
                    lambda p, k, order: (order[p * half + k], 0, row_block, 0),
                ),
                *[one_device(array) for array in gradients],
                whole(slices),
            ],
            out_specs=[
                pl.BlockSpec(
                    (1, 1, seqs * rows, depth),
                    lambda p, k, _: (jnp.where(p == 0, k, half - 1), 0, 0, 0),
                ),
                pl.BlockSpec(
                    (1, 1, seqs * rows, depth), lambda p, k, _: (jnp.where(p == 0, 0, k), 0, 0, 0)
                ),
                whole(dw_shape),
                pl.BlockSpec((1, many * width), lambda *_: (0, 0)),
            ],
            scratch_shapes=[
                pltpu.VMEM((depth, many * width), jnp.bfloat16),
                pltpu.VMEM((depth, many * width), jnp.float32),
            ],
        ),
        out_shape=[
            shape((half, 1, seqs * rows, depth), jnp.bfloat16),
            shape((half, 1, seqs * rows, depth), jnp.bfloat16),
            dw_shape,
            shape((1, many * width), jnp.float32),
        ],
        compiler_params=params(),
        cost_estimate=cost(
            4 * many * count * seqs * rows * depth * width, 4 * count * seqs * rows * depth
        ),
        name=name,
    )(order, gathered_rows, *gradients, slices)


def gathered(weights, width, place):
    count, groups, rows, _ = weights.shape
    return pl.BlockSpec((count, groups, rows, width), lambda *_: (0, 0, 0, place))


def first_kernel(
    mixed_ref, x_ref, out_w, query_w, vector_ref, _, mixed_out, in_out, low_out, query_out
):
    mixed = join(mixed_ref)
    mixed_out[...] = mixed
    first_in = x_ref[...].astype(jnp.float32) + times(mixed, out_w) + vector_ref[2:3]
    in_out[...] = first_in
    unit, _ = norm_parts(first_in)
    low = (unit * vector_ref[11:12] + vector_ref[12:13]).astype(jnp.bfloat16)
    low_out[...] = low
    spread(query_out, (times(low, query_w) + vector_ref[3:4]).astype(jnp.bfloat16))


def first_forward(mixed, x_rows, weights, vectors, after):
    rows, depth = x_rows.shape
    return pl.pallas_call(
        first_kernel,
        grid=(1,),
        in_specs=[
            whole(mixed),
            whole(x_rows),
            gathered(weights, depth, 0),
            gathered(weights, depth, 1),
            whole(vectors),
            pl.BlockSpec(memory_space=pl.ANY),
        ],
        out_specs=[whole(x_rows), whole(x_rows), whole(x_rows), whole(mixed)],
        out_shape=[
            shape((rows, depth), jnp.bfloat16),
            shape((rows, depth), jnp.float32),
            shape((rows, depth), jnp.bfloat16),
            shape(mixed.shape, jnp.bfloat16),
        ],
        compiler_params=params(),
        cost_estimate=cost(4 * rows * depth * depth, 4 * depth * depth),
        name="first_forward",
    )(mixed, x_rows, weights, weights, vectors, after)


def ffn_kernel(
    order,
    places,
    mixed_ref,
    first_ref,
    out_w,
    vector_ref,
    bias_ref,
    grad_ref,
    wide_ref,
    mine_ref,
    other_ref,
    mixed_out,
    layer_out,
    wide_grad,
    mine_grad,
    other_grad,
    dbias_ref,
    second_grad,
    cross_low,
    mixed_grad,
    stat_out,
    columns,
    contracts,
    active,
    slope,
    low,
    third_low,
    second_in,
    total,
    wide_sem,
    contract_sem,
):
    blocks, count, groups, rows, block = columns.shape
    part = block // CHIPS
    depth = vector_ref.shape[1]

    def wide_copies(t, array, outward):
        result = []
        for k in range(CHIPS):
            column = pl.multiple_of(order[t % 2 * CHIPS + k] * part, part)
            row = pl.multiple_of(places[t // 2] * rows, rows)
            there = array.at[:, :, pl.ds(row, rows), pl.ds(column, part)]
            here = columns.at[t, :, :, :, pl.ds(k * part, part)]
            ends = (here, there) if outward else (there, here)
            result.append(pltpu.make_async_copy(*ends, wide_sem.at[t, k]))
        return result

    def contract_copy(t, mine, other, outward):
        there = (mine, other)[t % 2].at[t // 2]
        here = contracts.at[t]
        ends = (here, there) if outward else (there, here)
        return pltpu.make_async_copy(*ends, contract_sem.at[t])

    for t in range(blocks):
        for copy in wide_copies(t, wide_ref, False):
            copy.start()
        contract_copy(t, mine_ref, other_ref, False).start()

    mixed = join(mixed_ref)
    mixed_out[...] = mixed
    unit, _ = norm_parts(first_ref[...])
    second_in[...] = (
        unit * vector_ref[11:12] + vector_ref[12:13] + times(mixed, out_w) + vector_ref[5:6]
    )
    unit, _ = norm_parts(second_in[...])
    second = unit * vector_ref[13:14] + vector_ref[14:15]
    low[...] = second.astype(jnp.bfloat16)
    total[...] = second + vector_ref[10:11]

    def shard(t, k):
        return places[t // 2] * count + order[t % 2 * CHIPS + k]

    for t in range(blocks):
        for copy in wide_copies(t, wide_ref, False):
            copy.wait()
        bias = jnp.concatenate([bias_ref[pl.ds(shard(t, k), 1)] for k in range(CHIPS)], axis=1)
        inner = times(low[...], columns.at[t]) + bias
        phi = 0.5 + 0.5 * lax.erf(inner * (0.5**0.5))
        out = (inner * phi).astype(jnp.bfloat16)
        active[t] = out
        slope[t] = phi + inner * jnp.exp(-0.5 * inner * inner) * 0.3989422804014327
        contract_copy(t, mine_ref, other_ref, False).wait()
        total[...] += dot(out, contracts[t].reshape(block, depth), NN)

    unit, inverse = norm_parts(total[...])
    gain = vector_ref[15:16]
    layer_out[...] = (unit * gain + vector_ref[16:17]).astype(jnp.bfloat16)
    gradient = grad_ref[...].astype(jnp.float32)
    grad_third = norm_back(gradient, unit, inverse, gain)
    stat_out[...] = jnp.zeros_like(stat_out)
    stat_out[0:1] = column_sum(grad_third)
    stat_out[1:2] = column_sum(gradient * unit)
    stat_out[2:3] = column_sum(gradient)
    total[...] = grad_third
    third_low[...] = grad_third.astype(jnp.bfloat16)
    turned = low[...].T

    for t in range(blocks):
        grad_inner = dot(third_low[...], contracts[t].reshape(block, depth), NT) * slope[t]
        inner_low = grad_inner.astype(jnp.bfloat16)
        sums = column_sum(grad_inner)
        for k in range(CHIPS):
            dbias_ref[pl.ds(shard(t, k), 1)] = sums[:, k * part : (k + 1) * part]
        contracts[t] = (
            dot(active[t], third_low[...], TN).astype(jnp.bfloat16).reshape(CHIPS, part, depth)
        )
        contract_copy(t, mine_grad, other_grad, True).start()
        total[...] += times_back(inner_low, columns.at[t])
        result = dot(turned, inner_low, NN).astype(jnp.bfloat16)
        for d in range(groups):
            columns[t, :, d] = result[d * count * rows : (d + 1) * count * rows].reshape(
                count, rows, block
            )
        for copy in wide_copies(t, wide_grad, True):
            copy.start()

    unit, inverse = norm_parts(second_in[...])
    grad_second = total[...]
    grad_in = norm_back(grad_second, unit, inverse, vector_ref[13:14])
    second_grad[...] = grad_in
    grad_low = grad_in.astype(jnp.bfloat16)
    cross_low[...] = grad_low
    spread(mixed_grad, times_back(grad_low, out_w).astype(jnp.bfloat16))
    stat_out[8:9] = column_sum(grad_in)
    stat_out[9:10] = column_sum(grad_second * unit)
    stat_out[10:11] = column_sum(grad_second)
    for t in range(blocks):
        contract_copy(t, mine_grad, other_grad, True).wait()
        for copy in wide_copies(t, wide_grad, True):
            copy.wait()


def ffn(orders, mixed, first_in, wide, contract, vectors, bias, output_grad):
    rows, depth = first_in.shape
    hidden = bias.size
    block = depth // 2
    count, groups, all_rows, _ = wide.shape
    part = depth // (count * groups)
    blocks = hidden // block
    full = whole(first_in)
    anywhere = pl.BlockSpec(memory_space=pl.ANY)
    heads_out = shape(mixed.shape, jnp.bfloat16)
    stats = shape((16, depth), jnp.float32)
    return pl.pallas_call(
        ffn_kernel,
        grid_spec=pltpu.PrefetchScalarGridSpec(
            num_scalar_prefetch=2,
            grid=(1,),
            in_specs=[
                whole(mixed),
                full,
                pl.BlockSpec((count, groups, part, depth), lambda *_: (0, 0, groups, 0)),
                whole(vectors),
                whole(bias),
                full,
                anywhere,
                anywhere,
                anywhere,
            ],
            out_specs=[
                full,
                full,
                anywhere,
                anywhere,
                anywhere,
                whole(bias),
                full,
                full,
                whole(heads_out),
                whole(stats),
            ],
            scratch_shapes=[
                pltpu.VMEM((blocks, count, groups, part, block), jnp.bfloat16),
                pltpu.VMEM((blocks,) + contract[0].shape[1:], jnp.bfloat16),
                pltpu.VMEM((blocks, rows, block), jnp.bfloat16),
                pltpu.VMEM((blocks, rows, block), jnp.float32),
                pltpu.VMEM((rows, depth), jnp.bfloat16),
                pltpu.VMEM((rows, depth), jnp.bfloat16),
                pltpu.VMEM((rows, depth), jnp.float32),
                pltpu.VMEM((rows, depth), jnp.float32),
                pltpu.SemaphoreType.DMA((blocks, CHIPS)),
                pltpu.SemaphoreType.DMA((blocks,)),
            ],
        ),
        out_shape=[
            shape((rows, depth), jnp.bfloat16),
            shape((rows, depth), jnp.bfloat16),
            shape((count, groups, all_rows - part, depth), jnp.bfloat16),
            shape(contract[0].shape, jnp.bfloat16),
            shape(contract[0].shape, jnp.bfloat16),
            shape(bias.shape, jnp.float32),
            shape((rows, depth), jnp.float32),
            shape((rows, depth), jnp.bfloat16),
            heads_out,
            stats,
        ],
        compiler_params=params(),
        cost_estimate=cost(12 * rows * depth * hidden, 16 * depth * hidden),
        name="ffn",
    )(*orders, mixed, first_in, wide, vectors, bias, output_grad, wide, *contract)


def first_back_kernel(
    dq_ref,
    second_grad,
    first_ref,
    out_w,
    query_w,
    vector_ref,
    _,
    query_low,
    grad_in_out,
    self_low,
    mixed_grad,
    stat_out,
):
    query_grad = join(dq_ref)
    query_low[...] = query_grad
    grad_first = second_grad[...] + times_back(query_grad, query_w)
    unit, inverse = norm_parts(first_ref[...])
    grad_in = norm_back(grad_first, unit, inverse, vector_ref[11:12])
    grad_in_out[...] = grad_in
    grad_low = grad_in.astype(jnp.bfloat16)
    self_low[...] = grad_low
    spread(mixed_grad, times_back(grad_low, out_w).astype(jnp.bfloat16))
    stat_out[...] = jnp.zeros_like(stat_out)
    stat_out[0:1] = column_sum(query_grad.astype(jnp.float32))
    stat_out[1:2] = column_sum(grad_in)
    stat_out[2:3] = column_sum(grad_first * unit)
    stat_out[3:4] = column_sum(grad_first)


def first_back(dq, second_grad, first_in, weights, vectors, after):
    rows, depth = first_in.shape
    full = whole(first_in)
    return pl.pallas_call(
        first_back_kernel,
        grid=(1,),
        in_specs=[
            whole(dq),
            full,
            full,
            gathered(weights, depth, 0),
            gathered(weights, depth, 1),
            whole(vectors),
            pl.BlockSpec(memory_space=pl.ANY),
        ],
        out_specs=[full, full, full, whole(dq), pl.BlockSpec((8, depth), lambda *_: (0, 0))],
        out_shape=[
            shape((rows, depth), jnp.bfloat16),
            shape((rows, depth), jnp.float32),
            shape((rows, depth), jnp.bfloat16),
            shape(dq.shape, jnp.bfloat16),
            shape((8, depth), jnp.float32),
        ],
        compiler_params=params(),
        cost_estimate=cost(4 * rows * depth * depth, 4 * depth * depth),
        name="first_back",
    )(dq, second_grad, first_in, weights, weights, vectors, after)


def weight_grads_kernel(
    order,
    mixed,
    self_low,
    first_low,
    query_low,
    cross,
    cross_low,
    mine_out,
    other_out,
    result,
):
    step = pl.program_id(0)
    pairs = ((mixed, self_low), (first_low, query_low), (cross, cross_low))
    half, groups, part, _ = mine_out.shape
    for m, (left_side, gradient) in enumerate(pairs):

        @pl.when(step == m)
        def _(left_side=left_side, gradient=gradient):
            result[...] = dot(left_side[...], gradient[...], TN).astype(jnp.bfloat16)

    for d in range(groups):
        for k in range(half):
            for p, out_ref in enumerate((mine_out, other_out)):
                row = pl.multiple_of((2 * half * d + order[p * half + k]) * part, part)
                out_ref[k, d] = result[pl.ds(row, part)]


def weight_grads(dims, order, mixed, self_low, first_low, query_low, cross, cross_low):
    count, groups, part, depth = dims
    half = pl.BlockSpec((count // 2, groups, part, depth), lambda m, _: (0, 0, m, 0))
    return pl.pallas_call(
        weight_grads_kernel,
        grid_spec=pltpu.PrefetchScalarGridSpec(
            num_scalar_prefetch=1,
            grid=(3,),
            in_specs=[whole(mixed)] * 6,
            out_specs=[half, half],
            scratch_shapes=[pltpu.VMEM((depth, depth), jnp.bfloat16)],
        ),
        out_shape=[shape((count // 2, groups, 3 * part, depth), jnp.bfloat16)] * 2,
        compiler_params=params(),
        cost_estimate=cost(6 * mixed.shape[0] * depth * depth, 6 * depth * depth),
        name="weight_grads",
    )(order, mixed, self_low, first_low, query_low, cross, cross_low)


def send_dp(piece):
    size = lax.axis_size("dp")
    return [
        lax.ppermute(piece, "dp", [(i, (i + shift) % size) for i in range(size)])
        for shift in range(1, size)
    ]


def place_dp(piece, arrived):
    size, me = lax.axis_size("dp"), lax.axis_index("dp")
    result = jnp.zeros((size,) + piece.shape, piece.dtype)
    result = lax.dynamic_update_index_in_dim(result, piece, me, 0)
    for shift, got in enumerate(arrived, 1):
        result = lax.dynamic_update_index_in_dim(result, got, lax.rem(me - shift + size, size), 0)
    return result


class HalvingDp:
    def __init__(self, pieces):
        me = lax.axis_index("dp")
        self.parts = [
            lax.dynamic_index_in_dim(pieces, me ^ flip, 0, keepdims=False) for flip in DP_ORDER
        ]

    def first(self):
        return jnp.stack(self.parts[2:]).astype(jnp.bfloat16)

    def second(self, sent):
        self.got = exchange_dp(sent, 1)
        return low_sum(self.parts[1], self.got[1])

    def finish(self, sent):
        last = exchange_dp(sent, 2)
        return sum(
            one.astype(jnp.float32) for one in (self.parts[0], self.got[0], last)
        )


def sum_dp(pieces):
    halves = HalvingDp(pieces)
    return halves.finish(halves.second(halves.first()))


def relative_order():
    size, me = lax.axis_size("index"), lax.axis_index("index")
    steps = jnp.arange(size // 2, dtype=jnp.int32) * 2
    return jnp.concatenate([me ^ steps, me ^ 1 ^ steps])


def exchange(piece, flip):
    size = lax.axis_size("index")
    return lax.ppermute(piece, "index", [(i, i ^ flip) for i in range(size)])


def exchange_dp(piece, flip):
    size = lax.axis_size("dp")
    return lax.ppermute(piece, "dp", [(i, i ^ flip) for i in range(size)])


def low_sum(*parts):
    return sum(part.astype(jnp.float32) for part in parts).astype(jnp.bfloat16)


class Halving:
    def __init__(self, mine, other):
        self.pair = (mine, exchange(other, 1))
        middle = mine.shape[2] // 2
        self.top, self.low = slice(0, middle), slice(middle, None)

    def total(self, k, rows, *more):
        result = sum(one[k, :, rows].astype(jnp.float32) for one in self.pair)
        return sum((one.astype(jnp.float32) for one in more), result)

    def first(self):
        return [
            jnp.stack([self.total(k, rows) for k in blocks]).astype(jnp.bfloat16)
            for blocks, rows in (((1, 3), self.top), ((2, 3), self.low))
        ]

    def send(self, sent):
        return [exchange(sent[0], 2), exchange(sent[1], 4)]

    def second(self, got):
        self.got = got
        return [
            self.total(2, self.top, self.got[0][1]).astype(jnp.bfloat16),
            self.total(1, self.low, self.got[1][1]).astype(jnp.bfloat16),
        ]

    def finish(self, sent):
        last = exchange(sent[0], 4), exchange(sent[1], 2)
        return jnp.concatenate(
            [
                self.total(0, self.top, self.got[0][0], last[0]),
                self.total(0, self.low, self.got[1][0], last[1]),
            ],
            axis=1,
        )


def small_sum(values):
    size = lax.axis_size("index")
    flat = jnp.pad(values.reshape(-1), (0, 1024 - values.size)).reshape(1, 8, 128)
    arrived = swap(jnp.broadcast_to(flat, (size, 8, 128)))
    return jnp.sum(arrived, axis=0).reshape(-1)[: values.size].reshape(values.shape)


def hold_kernel(*_):
    pass


def hold(values, *others):
    anywhere = pl.BlockSpec(memory_space=pl.ANY)
    return pl.pallas_call(
        hold_kernel,
        in_specs=[anywhere] * (len(values) + len(others)),
        out_specs=[anywhere] * len(values),
        out_shape=[shape(value.shape, value.dtype) for value in values],
        input_output_aliases={i: i for i in range(len(values))},
        name="hold",
    )(*values, *others)


def swap(pieces):
    return lax.all_to_all(pieces, "index", 0, 0, tiled=True)


def head_body(
    decoder_input,
    encoder_memory,
    question_vectors,
    passage_vectors,
    passage_ids,
    valid_count,
    output_grad,
    attention_weight,
    expand_weight,
    contract_weight,
    vector_params,
    attention_mean,
    attention_square,
    expand_mean,
    expand_square,
    contract_mean,
    contract_square,
    vector_mean,
    vector_square,
):
    low = jnp.bfloat16
    count, groups = lax.axis_size("index"), lax.axis_size("dp")
    place = lax.axis_index("index")
    seqs, rows_here, depth = decoder_input.shape
    memory_here = encoder_memory.shape[1]
    width = depth // count
    part = attention_weight.shape[1]
    hidden = expand_weight.shape[1]
    vector_rows, vector_width = vector_params.shape
    question_width = question_vectors.shape[1]
    rows = seqs * rows_here

    attention_low = attention_weight.astype(low)
    extras = jnp.concatenate(
        [vector_params.astype(low).reshape(-1), question_vectors.reshape(-1)]
    )
    extra_rows = -(-extras.shape[0] // (16 * width)) * 16
    extras = jnp.pad(extras, (0, extra_rows * width - extras.shape[0])).reshape(
        1, extra_rows, width
    )
    split = jnp.concatenate([attention_low[:3], attention_low[5:7]], axis=0)
    columns = split.reshape(5, part, count, width).transpose(2, 0, 1, 3)
    package = jnp.concatenate(
        [
            columns.reshape(count, 5 * part, width),
            jnp.broadcast_to(extras, (count, extra_rows, width)),
        ],
        axis=1,
    )
    order = relative_order()
    memory_block = -(-memory_here // rows_here) * rows_here
    rows_all = lax.all_gather(
        jnp.concatenate(
            [
                jnp.pad(encoder_memory, ((0, 0), (0, memory_block - memory_here), (0, 0))),
                decoder_input,
            ],
            axis=1,
        ),
        "index",
        axis=0,
        tiled=False,
    )
    input_rows = (rows_all, rows_here, memory_block // rows_here, rows_here)
    memory_rows = (rows_all, memory_block, 0, memory_here)
    square = attention_low[3:5].transpose(1, 0, 2).reshape(part, 2 * depth)
    received = swap(package)
    arrived = hold(send_dp(square), received)
    (received,) = hold([received], *arrived)
    square = lax.all_gather(place_dp(square, arrived), "index", axis=0, tiled=False)
    received_sent = send_dp(received)
    (contract,) = hold([contract_weight.astype(low)], received)
    contract = jnp.stack([contract] + [exchange(contract, 2 * k) for k in range(1, CHIPS)])
    slices = place_dp(received, hold(received_sent, contract))
    vectors = (
        slices[:, :, 5 * part :]
        .reshape(groups, count, extra_rows * width)[:, :, : vector_rows * vector_width]
        .reshape(groups, count, vector_rows, vector_width)
        .transpose(2, 0, 1, 3)
        .reshape(vector_rows, depth)
        .astype(jnp.float32)
    )
    question_full = (
        received[:, 5 * part :]
        .reshape(count, extra_rows * width)[:, vector_rows * vector_width :][
            :, : seqs * question_width
        ]
        .reshape(count, seqs, question_width)
        .transpose(1, 0, 2)
        .reshape(seqs, count * question_width)
    )
    expand_part = hidden // depth * part
    late = jnp.concatenate(
        [
            expand_weight.astype(low)
            .reshape(part, hidden // depth, depth)
            .transpose(1, 0, 2)
            .reshape(expand_part, depth),
            attention_low[7],
        ],
        axis=0,
    )
    (late,) = hold([late], slices)
    across = exchange_dp(jnp.concatenate([late, contract.reshape(-1, depth)], axis=0), 2)
    late_arrived = send_dp(late)
    late_arrived[1] = across

    passages_here = passage_vectors.shape[0]
    local_ids = passage_ids - place * passages_here
    owned_slot = (local_ids >= 0) & (local_ids < passages_here)
    picked = passage_vectors[jnp.clip(local_ids, 0, passages_here - 1)]
    local_scores = jnp.einsum(
        "sc,skc->sk", question_full, picked, preferred_element_type=jnp.float32
    )
    slots = passage_ids.shape[1]
    usable = jnp.arange(slots)[None, :] < valid_count[:, None]
    scores = small_sum(jnp.where(owned_slot, local_scores, 0.0))
    masked = jnp.where(usable, scores, negative_fill)
    maximum = jnp.max(masked, axis=1)
    exponent = jnp.where(usable, jnp.exp(masked - maximum[:, None]), 0.0)
    partition = jnp.sum(exponent, axis=1)
    passage_prob = exponent / partition[:, None]
    log_prior = jnp.where(
        usable, masked - maximum[:, None] - jnp.log(partition)[:, None], negative_fill
    )
    key_bias = jnp.repeat(log_prior, MEM_P, axis=1)

    vector_here = lax.dynamic_slice_in_dim(vectors[:5], place * width, width, axis=1)
    no_bias = jnp.zeros((1, width), jnp.float32)
    qkv_bias = jnp.concatenate([vector_here[0:1], no_bias, vector_here[1:2]], axis=1)
    kv_bias = jnp.concatenate([no_bias, vector_here[4:5]], axis=1)
    x_rows = decoder_input.reshape(rows, depth)
    qkv = project_columns("self_qkv", *input_rows, slices, 0, 3, qkv_bias)
    self_out, self_stat = attend(True, qkv, 0, qkv, 1, 2, key_bias[:, None, :])
    self_got = swap(self_out)
    memory_kv = project_columns("memory_kv", *memory_rows, slices, 3, 2, kv_bias)
    late_arrived = list(hold(late_arrived, self_got))
    across = late_arrived[1][late.shape[0] :]
    late_arrived[1] = late_arrived[1][: late.shape[0]]
    contract = jnp.stack([contract, across.reshape(contract.shape)])
    late = place_dp(late, late_arrived)
    late = lax.all_gather(late, "index", axis=0, tiled=False)
    (self_got,) = hold([self_got], contract)
    contract_far = exchange_dp(contract, 1)
    self_mixed, first_in, first_low, cross_query = first_forward(
        self_got, x_rows, square, vectors, memory_kv
    )
    cross_query = swap(cross_query)[:, None]
    cross_out, cross_stat = attend(
        False, cross_query, 0, memory_kv, 0, 1, key_bias[:, None, :]
    )
    contract = jnp.concatenate([contract, *hold([contract_far], cross_out)], axis=0)
    places = lax.axis_index("dp") ^ jnp.array(DP_ORDER, jnp.int32)
    (
        cross_mixed,
        layer_output,
        wide_grad,
        contract_mine,
        contract_other,
        inner_total,
        second_grad,
        cross_low,
        cross_mix_grad,
        stats,
    ) = ffn(
        (order, places),
        swap(cross_out),
        first_in,
        late,
        (contract, exchange(contract, 1)),
        vectors,
        vectors[6:10].reshape(groups * count, -1),
        output_grad.reshape(rows, depth),
    )
    third_stat, second_stat = stats[:8], stats[8:]

    expand_part_sum = lax.psum_scatter(wide_grad, "index", scatter_dimension=0, tiled=False)
    contract_pair = (contract_mine, exchange(contract_other, 1))
    contract_sent = low_sum(*(one[2:] for one in contract_pair))
    cross_mix_got, contract_sent = hold([swap(cross_mix_grad), contract_sent])
    contract_got = exchange_dp(contract_sent, 1)
    contract_next = low_sum(*(one[1] for one in contract_pair), contract_got[1])
    cross_dq, cross_dkv, prior_rows = attend_back(
        False,
        cross_query,
        0,
        memory_kv,
        0,
        1,
        cross_mix_got,
        cross_stat,
        key_bias[:, :, None],
        contract_sent,
    )
    memory_mine, memory_other, kv_grads, kv_total = project_columns_back(
        "memory_kv_back", order, *memory_rows, [cross_dkv], slices, 3, 2
    )
    cross_dq_got, contract_next = hold([swap(cross_dq), contract_next], memory_mine)
    contract_last = exchange_dp(contract_next, 2)
    query_low, first_grad, self_low, self_mix_grad, first_stat = first_back(
        cross_dq_got, second_grad, first_in, square, vectors, memory_mine
    )
    memory_sum = Halving(memory_mine, memory_other)
    memory_sent = memory_sum.first()
    square_mine, square_other = weight_grads(
        (count, groups, part, depth),
        order,
        self_mixed,
        self_low,
        first_low,
        query_low,
        cross_mixed,
        cross_low,
    )
    square_sum = Halving(square_mine, square_other)
    (self_mix_got,) = hold([swap(self_mix_grad)], *memory_sent)
    self_dq, self_dkv, _ = attend_back(
        True, qkv, 0, qkv, 1, 2, self_mix_got, self_stat, self_stat, square_mine
    )
    square_sent = square_sum.first()
    self_dq, expand_part_sum = hold([self_dq, expand_part_sum], *square_sent)
    dx_mine, dx_other, qkv_slice_grads, qkv_total = project_columns_back(
        "self_qkv_back", order, *input_rows, [self_dq, self_dkv], slices, 0, 3
    )
    own = jnp.concatenate(
        [qkv_total[:, :width], qkv_total[:, 2 * width :], kv_total[:, width:]], axis=0
    )
    own = lax.dynamic_update_slice(
        jnp.zeros((3, depth), jnp.float32), own, (jnp.int32(0), place * width)
    )
    vector_grads = jnp.concatenate(
        [
            own[:2],
            first_stat[1:2],
            first_stat[0:1],
            own[2:],
            second_stat[0:1],
            inner_total.reshape(hidden // depth, depth),
            third_stat[0:1],
            first_stat[2:4],
            second_stat[1:3],
            third_stat[1:3],
        ],
        axis=0,
    )
    vector_size = vector_rows * vector_width
    question_size = seqs * question_width
    vector_send = (
        vector_grads.reshape(vector_rows, groups, count, vector_width)
        .transpose(1, 2, 0, 3)
        .reshape(groups, count, vector_size)
    )
    vector_send = jnp.pad(
        vector_send, ((0, 0), (0, 0), (0, extra_rows * width - vector_size))
    ).reshape(groups, count, extra_rows, width)
    slice_sum = HalvingDp(
        jnp.concatenate([qkv_slice_grads, kv_grads, vector_send.astype(low)], axis=2)
    )
    (
        dx_mine,
        dx_other,
        slice_sent,
        expand_part_sum,
        contract_last,
        memory_top,
        memory_low,
        square_top,
        square_low,
    ) = hold(
        [
            dx_mine,
            dx_other,
            slice_sum.first(),
            expand_part_sum,
            contract_last,
            *memory_sum.send(memory_sent),
            *square_sum.send(square_sent),
        ]
    )
    square_last = square_sum.second([square_top, square_low])
    memory_last = memory_sum.second([memory_top, memory_low])
    expand_sum = HalvingDp(expand_part_sum)
    expand_sent = expand_sum.first()
    dx_sum = Halving(dx_mine, dx_other)
    dx_sent = dx_sum.first()
    dx_last = dx_sum.second(dx_sum.send(dx_sent))
    memory_last = hold(memory_last, *dx_sent)
    memory_gradient = memory_sum.finish(memory_last).reshape(encoder_memory.shape)
    contract_four = low_sum(*(one[0] for one in contract_pair), contract_got[0], contract_last)
    (contract_four,) = hold([contract_four], *dx_sent)
    contract_sum = sum(
        (exchange(contract_four[k], 2 * k).astype(jnp.float32) for k in range(1, CHIPS)),
        contract_four[0].astype(jnp.float32),
    )
    square_part = square_sum.finish(square_last).astype(low)
    input_gradient = first_grad + dx_sum.finish(dx_last).reshape(rows, depth)

    prior_part = prior_rows.reshape(seqs, slots, MEM_P).sum(axis=-1)
    prior_grad = jnp.where(usable, small_sum(prior_part), 0.0)
    score_doc = jnp.where(
        usable, prior_grad - passage_prob * jnp.sum(prior_grad, axis=1, keepdims=True), 0.0
    )
    question_part = jnp.einsum(
        "sk,skc->sc",
        jnp.where(owned_slot, score_doc, 0.0),
        picked.astype(jnp.float32),
        precision=lax.Precision.HIGHEST,
    )

    square_far = HalvingDp(square_part)
    (square_sent,) = hold([square_far.first()], *dx_sent)
    square_next = square_far.second(square_sent)
    (slice_next,) = hold([slice_sum.second(slice_sent)], *dx_last)
    slice_sum = slice_sum.finish(slice_next)
    question_send = (
        question_part.reshape(seqs, count, question_width)
        .transpose(1, 0, 2)
        .reshape(count, question_size)
    )
    question_send = jnp.pad(
        question_send,
        ((0, 0), (vector_size, extra_rows * width - vector_size - question_size)),
    ).reshape(count, extra_rows, width)
    slice_sum = jnp.concatenate(
        [slice_sum[:, : 5 * part], slice_sum[:, 5 * part :] + question_send], axis=1
    )
    (slice_send,) = hold(
        [slice_sum.astype(low)], contract_sum, memory_gradient, input_gradient
    )
    arrived = swap(slice_send).astype(jnp.float32)
    split_grads = (
        arrived[:, : 5 * part]
        .reshape(count, 5, part, width)
        .transpose(1, 2, 0, 3)
        .reshape(5, part, depth)
    )
    extra_sum = jnp.sum(arrived[:, 5 * part :].reshape(count, extra_rows * width), axis=0)
    vector_sum = extra_sum[:vector_size].reshape(vector_rows, vector_width)
    question_gradient = extra_sum[vector_size : vector_size + question_size].reshape(
        seqs, question_width
    )

    expand_sum = (
        expand_sum.finish(expand_sum.second(expand_sent))
        .reshape(hidden // depth, part, depth)
        .transpose(1, 0, 2)
        .reshape(part, hidden)
    )
    square_total = square_far.finish(square_next).reshape(3, part, depth)
    attention_sum = jnp.concatenate(
        [split_grads[:3], square_total[:2], split_grads[3:], square_total[2:]], axis=0
    )

    new_attention = adam_update(
        attention_weight,
        attention_mean,
        attention_square,
        attention_sum,
        rate_attention,
        decay_matrix,
    )
    new_expand = adam_update(
        expand_weight, expand_mean, expand_square, expand_sum, rate_expand, decay_matrix
    )
    new_contract = adam_update(
        contract_weight, contract_mean, contract_square, contract_sum, rate_contract, decay_matrix
    )
    new_vector = adam_update(
        vector_params, vector_mean, vector_square, vector_sum, rate_vector, 0.0
    )
    return (
        layer_output.reshape(decoder_input.shape),
        input_gradient.reshape(decoder_input.shape),
        memory_gradient,
        question_gradient,
        *new_attention,
        *new_expand,
        *new_contract,
        *new_vector,
    )


def body(sizes, *arrays):
    depth = arrays[0].shape[2]
    if sizes == (4, 8) and depth // 8 % 128 == 0:
        return head_body(*arrays)
    return general_body(*arrays)


def solution(mesh):
    return jax.shard_map(
        partial(body, (mesh.shape["dp"], mesh.shape["index"])),
        mesh=mesh,
        in_specs=(
            P("dp", "index", None),
            P("dp", "index", None),
            P("dp", "index"),
            P("index", None),
            P("dp", None),
            P("dp"),
            P("dp", "index", None),
            P(None, ("dp", "index"), None),
            P(("dp", "index"), None),
            P(("dp", "index"), None),
            P(None, ("dp", "index")),
            P(None, ("dp", "index"), None),
            P(None, ("dp", "index"), None),
            P(("dp", "index"), None),
            P(("dp", "index"), None),
            P(("dp", "index"), None),
            P(("dp", "index"), None),
            P(None, ("dp", "index")),
            P(None, ("dp", "index")),
        ),
        out_specs=(
            P("dp", "index", None),
            P("dp", "index", None),
            P("dp", "index", None),
            P("dp", "index"),
            P(None, ("dp", "index"), None),
            P(None, ("dp", "index"), None),
            P(None, ("dp", "index"), None),
            P(("dp", "index"), None),
            P(("dp", "index"), None),
            P(("dp", "index"), None),
            P(("dp", "index"), None),
            P(("dp", "index"), None),
            P(("dp", "index"), None),
            P(None, ("dp", "index")),
            P(None, ("dp", "index")),
            P(None, ("dp", "index")),
        ),
        check_vma=False,
    )
```

```python
from functools import partial

import jax
import jax.numpy as jnp
from jax import lax
from jax.experimental import pallas as pl
from jax.experimental.pallas import tpu as pltpu
from jax.sharding import PartitionSpec as P

HEADS = 16
MEM_P = 192
STEP = 10


negative_fill = -1e30
norm_eps = 1e-05
beta_first = 0.9
beta_second = 0.999
adam_eps = 1e-08
decay_matrix = 0.01
rate_attention = 0.1
rate_expand = 0.02
rate_contract = 0.01
rate_vector = 0.2


def layer_norm(hidden, norm_gain, norm_shift):
    center = hidden - jnp.mean(hidden, axis=-1, keepdims=True)
    spread = jnp.mean(center * center, axis=-1, keepdims=True)
    return center * lax.rsqrt(spread + norm_eps) * norm_gain + norm_shift


def split_heads(matrix):
    return matrix.reshape(matrix.shape[0], matrix.shape[1], HEADS, matrix.shape[2] // HEADS)


def merge_heads(matrix):
    return matrix.reshape(matrix.shape[0], matrix.shape[1], matrix.shape[2] * matrix.shape[3])


def project(left_side, weight):
    return jnp.einsum("srd,de->sre", left_side, weight, preferred_element_type=jnp.float32)


def project_back(gradient, weight):
    return jnp.einsum("sre,de->srd", gradient, weight, preferred_element_type=jnp.float32)


def weight_grad(left_side, gradient):
    return jnp.einsum("srd,sre->de", left_side, gradient, preferred_element_type=jnp.float32)


def row_total(values):
    return jnp.sum(values, axis=(0, 1))


def attend_forward(queries, key_rows, values, score_bias, allowed):
    scores = (
        jnp.einsum(
            "sqhd,skhd->shqk",
            split_heads(queries),
            split_heads(key_rows),
            preferred_element_type=jnp.float32,
        )
        * 0.125
        + score_bias
    )
    scores = jnp.where(allowed, scores, negative_fill)
    maximum = jnp.max(scores, axis=-1)
    exponent = jnp.exp(scores - maximum[..., None])
    partition = jnp.sum(exponent, axis=-1)
    attend_prob = exponent / partition[..., None]
    mixture = jnp.einsum(
        "shqk,skhd->sqhd",
        attend_prob.astype(jnp.bfloat16),
        split_heads(values),
        preferred_element_type=jnp.float32,
    )
    return (merge_heads(mixture).astype(jnp.bfloat16), attend_prob, maximum, partition)


def score_grads(grad_mixed, attend_prob, values):
    grad_prob = jnp.einsum(
        "sqhd,skhd->shqk",
        split_heads(grad_mixed),
        split_heads(values),
        preferred_element_type=jnp.float32,
    )
    row_inner = jnp.sum(attend_prob * grad_prob, axis=-1)
    return ((attend_prob * (grad_prob - row_inner[..., None])).astype(jnp.bfloat16), row_inner)


def to_queries(grad_score, key_rows):
    return (
        merge_heads(
            jnp.einsum(
                "shqk,skhd->sqhd",
                grad_score,
                split_heads(key_rows),
                preferred_element_type=jnp.float32,
            )
        )
        * 0.125
    )


def to_keys(grad_score, attend_prob, queries, grad_mixed):
    grad_key = (
        merge_heads(
            jnp.einsum(
                "shqk,sqhd->skhd",
                grad_score,
                split_heads(queries),
                preferred_element_type=jnp.float32,
            )
        )
        * 0.125
    )
    grad_value = merge_heads(
        jnp.einsum(
            "shqk,sqhd->skhd",
            attend_prob.astype(jnp.bfloat16),
            split_heads(grad_mixed),
            preferred_element_type=jnp.float32,
        )
    )
    return (grad_key, grad_value)


def adam_update(weight, moment_one, moment_two, gradient, step_rate, weight_decay):
    mean_new = beta_first * moment_one + (1.0 - beta_first) * gradient
    square_new = beta_second * moment_two + (1.0 - beta_second) * gradient * gradient
    mean_hat = mean_new / (1.0 - beta_first**STEP)
    square_hat = square_new / (1.0 - beta_second**STEP)
    updated = weight - step_rate * (
        mean_hat / (jnp.sqrt(square_hat) + adam_eps) + weight_decay * weight
    )
    return (updated, mean_new, square_new)


def general_body(
    decoder_input,
    encoder_memory,
    question_vectors,
    passage_vectors,
    passage_ids,
    valid_count,
    output_grad,
    attention_weight,
    expand_weight,
    contract_weight,
    vector_params,
    attention_mean,
    attention_square,
    expand_mean,
    expand_square,
    contract_mean,
    contract_square,
    vector_mean,
    vector_square,
):
    attention_low, expand_low, contract_low, vector_low = (
        lax.all_gather(attention_weight.astype(jnp.bfloat16), ("dp", "index"), axis=1, tiled=True),
        lax.all_gather(expand_weight.astype(jnp.bfloat16), ("dp", "index"), axis=0, tiled=True),
        lax.all_gather(contract_weight.astype(jnp.bfloat16), ("dp", "index"), axis=0, tiled=True),
        lax.all_gather(vector_params.astype(jnp.bfloat16), ("dp", "index"), axis=1, tiled=True),
    )
    vectors = vector_low.astype(jnp.float32)
    seqs_here, rows_here, model_width = decoder_input.shape
    shard_index = lax.axis_index("index")
    length = rows_here * lax.axis_size("index")
    ffn_width = expand_low.shape[1]
    self_query = (project(decoder_input, attention_low[0]) + vectors[0]).astype(jnp.bfloat16)
    self_key = project(decoder_input, attention_low[1]).astype(jnp.bfloat16)
    self_value = (project(decoder_input, attention_low[2]) + vectors[1]).astype(jnp.bfloat16)
    key_all, value_all = (
        lax.all_gather(self_key, "index", axis=1, tiled=True),
        lax.all_gather(self_value, "index", axis=1, tiled=True),
    )
    query_place = shard_index * rows_here + jnp.arange(rows_here)
    causal = (jnp.arange(length)[None, :] <= query_place[:, None])[None, None]
    self_mixed, self_prob, self_peak, self_total = attend_forward(
        self_query, key_all, value_all, 0.0, causal
    )
    first_in = (
        decoder_input.astype(jnp.float32) + project(self_mixed, attention_low[3]) + vectors[2]
    )
    first_out, first_back = jax.vjp(layer_norm, first_in, vectors[11], vectors[12])
    first_low = first_out.astype(jnp.bfloat16)
    cross_query = (project(first_low, attention_low[4]) + vectors[3]).astype(jnp.bfloat16)
    cross_key = project(encoder_memory, attention_low[5]).astype(jnp.bfloat16)
    cross_value = (project(encoder_memory, attention_low[6]) + vectors[4]).astype(jnp.bfloat16)
    memory_keys, memory_values = (
        lax.all_gather(cross_key, "index", axis=1, tiled=True),
        lax.all_gather(cross_value, "index", axis=1, tiled=True),
    )
    question_full = lax.all_gather(question_vectors, "index", axis=1, tiled=True)
    passages_here = passage_vectors.shape[0]
    local_ids = passage_ids - shard_index * passages_here
    owned_slot = (local_ids >= 0) & (local_ids < passages_here)
    picked = passage_vectors[jnp.clip(local_ids, 0, passages_here - 1)]
    local_scores = jnp.einsum(
        "sc,skc->sk", question_full, picked, preferred_element_type=jnp.float32
    )
    slots = passage_ids.shape[1]
    usable = jnp.arange(slots)[None, :] < valid_count[:, None]
    local_peak = jnp.max(jnp.where(owned_slot & usable, local_scores, negative_fill), axis=1)
    maximum = lax.pmax(local_peak, "index")
    local_exp = jnp.where(owned_slot & usable, jnp.exp(local_scores - maximum[:, None]), 0.0)
    exponent, scores = lax.psum((local_exp, jnp.where(owned_slot, local_scores, 0.0)), "index")
    masked = jnp.where(usable, scores, negative_fill)
    partition = jnp.sum(exponent, axis=1)
    passage_prob = exponent / partition[:, None]
    log_prior = masked - maximum[:, None] - jnp.log(partition)[:, None]
    memory_total = memory_keys.shape[1]
    bias_rows = jnp.repeat(log_prior, MEM_P, axis=1)
    key_bias = bias_rows[:, None, None, :]
    key_usable = ((jnp.arange(memory_total) // MEM_P)[None, :] < valid_count[:, None])[
        :, None, None, :
    ]
    cross_mixed, cross_prob, cross_peak, cross_total = attend_forward(
        cross_query, memory_keys, memory_values, key_bias, key_usable
    )
    second_in = first_out + project(cross_mixed, attention_low[7]) + vectors[5]
    second_out, second_back = jax.vjp(layer_norm, second_in, vectors[13], vectors[14])
    second_low = second_out.astype(jnp.bfloat16)
    inner_act = project(second_low, expand_low) + vectors[6:10].reshape(ffn_width)
    activated, gelu_back = jax.vjp(partial(jax.nn.gelu, approximate=False), inner_act)
    activ_low = activated.astype(jnp.bfloat16)
    third_in = second_out + project(activ_low, contract_low) + vectors[10]
    layer_output, third_back = jax.vjp(layer_norm, third_in, vectors[15], vectors[16])
    grad_third, gain_three, shift_three = third_back(output_grad.astype(jnp.float32))
    grad_ffn_low = grad_third.astype(jnp.bfloat16)
    grad_contract = weight_grad(activ_low, grad_ffn_low)
    (grad_inner,) = gelu_back(project_back(grad_ffn_low, contract_low))
    grad_inner_low = grad_inner.astype(jnp.bfloat16)
    grad_expand = weight_grad(second_low, grad_inner_low)
    grad_second = grad_third + project_back(grad_inner_low, expand_low)
    grad_second_in, gain_two, shift_two = second_back(grad_second)
    grad_cross_low = grad_second_in.astype(jnp.bfloat16)
    grad_cmix = project_back(grad_cross_low, attention_low[7]).astype(jnp.bfloat16)
    cross_score, cross_inner = score_grads(grad_cmix, cross_prob, memory_values)
    grad_cq = to_queries(cross_score, memory_keys)
    prior_part = (
        jnp.sum(cross_score, axis=(1, 2), dtype=jnp.float32)
        .reshape(seqs_here, slots, MEM_P)
        .sum(axis=-1)
    )
    prior_grad = jnp.where(usable, lax.psum(prior_part, "index"), 0.0)
    score_doc = jnp.where(
        usable, prior_grad - passage_prob * jnp.sum(prior_grad, axis=1, keepdims=True), 0.0
    )
    question_part = jnp.einsum(
        "sk,skc->sc",
        jnp.where(owned_slot, score_doc, 0.0),
        picked.astype(jnp.float32),
        precision=lax.Precision.HIGHEST,
    )
    question_gradient = lax.psum_scatter(question_part, "index", scatter_dimension=1, tiled=True)
    grad_cq_low = grad_cq.astype(jnp.bfloat16)
    grad_first = grad_second_in + project_back(grad_cq_low, attention_low[4])
    ck_part, cv_part = to_keys(cross_score, cross_prob, cross_query, grad_cmix)
    grad_ck, grad_cv = (
        lax.psum_scatter(
            ck_part.astype(jnp.bfloat16), "index", scatter_dimension=1, tiled=True
        ).astype(jnp.float32),
        lax.psum_scatter(
            cv_part.astype(jnp.bfloat16), "index", scatter_dimension=1, tiled=True
        ).astype(jnp.float32),
    )
    grad_ck_low = grad_ck.astype(jnp.bfloat16)
    grad_cv_low = grad_cv.astype(jnp.bfloat16)
    memory_gradient = project_back(grad_ck_low, attention_low[5]) + project_back(
        grad_cv_low, attention_low[6]
    )
    grad_first_in, gain_one, shift_one = first_back(grad_first)
    grad_self_low = grad_first_in.astype(jnp.bfloat16)
    grad_smix = project_back(grad_self_low, attention_low[3]).astype(jnp.bfloat16)
    self_score, row_inner = score_grads(grad_smix, self_prob, value_all)
    grad_sq = to_queries(self_score, key_all)
    key_part, value_part = to_keys(self_score, self_prob, self_query, grad_smix)
    grad_sk, grad_sv = (
        lax.psum_scatter(
            key_part.astype(jnp.bfloat16), "index", scatter_dimension=1, tiled=True
        ).astype(jnp.float32),
        lax.psum_scatter(
            value_part.astype(jnp.bfloat16), "index", scatter_dimension=1, tiled=True
        ).astype(jnp.float32),
    )
    grad_sq_low = grad_sq.astype(jnp.bfloat16)
    grad_sk_low = grad_sk.astype(jnp.bfloat16)
    grad_sv_low = grad_sv.astype(jnp.bfloat16)
    input_gradient = (
        grad_first_in
        + project_back(grad_sq_low, attention_low[0])
        + project_back(grad_sk_low, attention_low[1])
        + project_back(grad_sv_low, attention_low[2])
    )
    attention_grads = jnp.stack(
        [
            weight_grad(decoder_input, grad_sq_low),
            weight_grad(decoder_input, grad_sk_low),
            weight_grad(decoder_input, grad_sv_low),
            weight_grad(self_mixed, grad_self_low),
            weight_grad(first_low, grad_cq_low),
            weight_grad(encoder_memory, grad_ck_low),
            weight_grad(encoder_memory, grad_cv_low),
            weight_grad(cross_mixed, grad_cross_low),
        ]
    )
    vector_grads = jnp.concatenate(
        [
            jnp.stack(
                [
                    row_total(grad_sq),
                    row_total(grad_sv),
                    row_total(grad_first_in),
                    row_total(grad_cq),
                    row_total(grad_cv),
                    row_total(grad_second_in),
                ]
            ),
            row_total(grad_inner).reshape(ffn_width // model_width, model_width),
            jnp.stack(
                [
                    row_total(grad_third),
                    gain_one,
                    shift_one,
                    gain_two,
                    shift_two,
                    gain_three,
                    shift_three,
                ]
            ),
        ]
    )
    attention_sum, expand_sum, contract_sum, vector_sum = (
        lax.psum_scatter(attention_grads, ("dp", "index"), scatter_dimension=1, tiled=True),
        lax.psum_scatter(grad_expand, ("dp", "index"), scatter_dimension=0, tiled=True),
        lax.psum_scatter(grad_contract, ("dp", "index"), scatter_dimension=0, tiled=True),
        lax.psum_scatter(vector_grads, ("dp", "index"), scatter_dimension=1, tiled=True),
    )
    new_attention = adam_update(
        attention_weight,
        attention_mean,
        attention_square,
        attention_sum,
        rate_attention,
        decay_matrix,
    )
    new_expand = adam_update(
        expand_weight, expand_mean, expand_square, expand_sum, rate_expand, decay_matrix
    )
    new_contract = adam_update(
        contract_weight, contract_mean, contract_square, contract_sum, rate_contract, decay_matrix
    )
    new_vector = adam_update(
        vector_params, vector_mean, vector_square, vector_sum, rate_vector, 0.0
    )
    return (
        layer_output.astype(jnp.bfloat16),
        input_gradient,
        memory_gradient,
        question_gradient,
        new_attention[0],
        new_attention[1],
        new_attention[2],
        new_expand[0],
        new_expand[1],
        new_expand[2],
        new_contract[0],
        new_contract[1],
        new_contract[2],
        new_vector[0],
        new_vector[1],
        new_vector[2],
    )


NT = (((1,), (1,)), ((), ()))
NN = (((1,), (0,)), ((), ()))
TN = (((0,), (0,)), ((), ()))
CHIPS = 4
DP_ORDER = (0, 2, 1, 3)
VMEM_LIMIT = 56 << 20


def dot(left_side, right_side, dims):
    return lax.dot_general(left_side, right_side, dims, preferred_element_type=jnp.float32)


def norm_parts(hidden):
    center = hidden - jnp.mean(hidden, axis=-1, keepdims=True)
    inverse = lax.rsqrt(jnp.mean(center * center, axis=-1, keepdims=True) + norm_eps)
    return center * inverse, inverse


def norm_back(gradient, unit, inverse, gain):
    scaled = gradient * gain
    return inverse * (
        scaled
        - jnp.mean(scaled, axis=-1, keepdims=True)
        - unit * jnp.mean(scaled * unit, axis=-1, keepdims=True)
    )


def column_sum(values):
    return jnp.sum(values, axis=0, keepdims=True)


def join(parts, place=None):
    picked = [parts[j] if place is None else parts[j, place] for j in range(parts.shape[0])]
    return jnp.concatenate(
        [block.reshape(block.shape[0] * block.shape[1], block.shape[2]) for block in picked],
        axis=1,
    )


def spread(out_ref, value):
    count, seqs, rows, width = out_ref.shape
    for j in range(count):
        out_ref[j] = value[:, j * width : (j + 1) * width].reshape(seqs, rows, width)


def times(activation, weight):
    count, groups, rows, width = weight.shape
    depth = count * rows
    total = None
    for d in range(groups):
        part = dot(
            activation[:, d * depth : (d + 1) * depth], weight[:, d].reshape(depth, width), NN
        )
        total = part if total is None else total + part
    return total


def times_back(gradient, weight):
    count, groups, rows, width = weight.shape
    depth = count * rows
    return jnp.concatenate(
        [dot(gradient, weight[:, d].reshape(depth, width), NT) for d in range(groups)], axis=1
    )


def outer(out_ref, left_side, gradient):
    count, groups, rows, width = out_ref.shape
    depth = count * rows
    for d in range(groups):
        out_ref[:, d] = (
            dot(left_side[:, d * depth : (d + 1) * depth], gradient, TN)
            .astype(jnp.bfloat16)
            .reshape(count, rows, width)
        )


def whole(array):
    return pl.BlockSpec(array.shape, lambda *_, rank=len(array.shape): (0,) * rank)


def shape(dims, dtype):
    return jax.ShapeDtypeStruct(tuple(dims), dtype)


def params():
    return pltpu.CompilerParams(vmem_limit_bytes=VMEM_LIMIT)


def cost(flops, moved):
    return pl.CostEstimate(flops=int(flops) // 16, bytes_accessed=int(moved) // 16, transcendentals=0)


def in_head(dims, head_width, head):
    return lax.broadcasted_iota(jnp.int32, dims, 1) // head_width == head


def attend_forward_kernel(causal, head_width, q_ref, k_ref, v_ref, bias_ref, out_ref, stat_ref):
    count, _, tile, width = q_ref.shape
    keys = k_ref.shape[0] * k_ref.shape[2]
    key_rows, values = k_ref[...].reshape(keys, width), v_ref[...].reshape(keys, width)
    step = 2
    rows = step * tile
    for b in range(count // step):
        queries = q_ref[b * step : (b + 1) * step].reshape(rows, width)
        seen = (b + 1) * rows if causal else keys
        mixed = None
        for h in range(width // head_width):
            mask = in_head((rows, width), head_width, h)
            scores = dot(
                jnp.where(mask, queries * 0.125, 0).astype(jnp.bfloat16), key_rows[:seen], NT
            )
            if causal:
                corner = scores[:, seen - rows :]
                corner = jnp.where(
                    lax.broadcasted_iota(jnp.int32, corner.shape, 1)
                    <= lax.broadcasted_iota(jnp.int32, corner.shape, 0),
                    corner,
                    negative_fill,
                )
                if b == 0:
                    scores = corner
                else:
                    scores = jnp.concatenate([scores[:, : seen - rows], corner], axis=1)
            else:
                scores = scores + bias_ref[0]
            peak = jnp.max(scores, axis=1, keepdims=True)
            exponent = jnp.exp(scores - peak)
            total = jnp.sum(exponent, axis=1, keepdims=True)
            prob = (exponent * (1.0 / total)).astype(jnp.bfloat16)
            part = dot(prob, values[:seen], NN)
            mixed = part if mixed is None else jnp.where(mask, part, mixed)
            log_total = jnp.broadcast_to(peak + jnp.log(total), (rows, 128))
            stat_ref[0, h : h + 1, b * rows : (b + 1) * rows] = log_total.T[0:1]
        out_ref[b * step : (b + 1) * step] = mixed.astype(jnp.bfloat16).reshape(
            step, 1, tile, width
        )


def attend_backward_kernel(
    causal,
    head_width,
    q_ref,
    k_ref,
    v_ref,
    grad_ref,
    stat_ref,
    bias_ref,
    _,
    dq_ref,
    dkv_ref,
    prior_ref,
    dk_sum,
    dv_sum,
    prior_sum,
):
    count, _, tile, width = q_ref.shape
    keys = k_ref.shape[0] * k_ref.shape[2]
    key_rows, values = k_ref[...].reshape(keys, width), v_ref[...].reshape(keys, width)
    step = 2
    rows = step * tile
    if not causal:
        bias = jnp.broadcast_to(bias_ref[0], (128, keys)).T[:, :1]
    dk_sum[...] = jnp.zeros_like(dk_sum)
    dv_sum[...] = jnp.zeros_like(dv_sum)
    if not causal:
        prior_sum[...] = jnp.zeros_like(prior_sum)
    for b in range(count // step):
        queries = q_ref[b * step : (b + 1) * step].reshape(rows, width)
        gradient = grad_ref[b * step : (b + 1) * step].reshape(rows, width)
        seen = (b + 1) * rows if causal else keys
        query_grad = None
        for h in range(width // head_width):
            mask = in_head((rows, width), head_width, h)
            one_query = jnp.where(mask, queries * 0.125, 0).astype(jnp.bfloat16)
            one_grad = jnp.where(mask, gradient, 0).astype(jnp.bfloat16)
            scores = dot(key_rows[:seen], one_query, NT)
            if causal:
                corner = scores[seen - rows :]
                corner = jnp.where(
                    lax.broadcasted_iota(jnp.int32, corner.shape, 0)
                    <= lax.broadcasted_iota(jnp.int32, corner.shape, 1),
                    corner,
                    negative_fill,
                )
                if b == 0:
                    scores = corner
                else:
                    scores = jnp.concatenate([scores[: seen - rows], corner], axis=0)
            else:
                scores = scores + bias
            prob = jnp.exp(scores - stat_ref[0, h : h + 1, b * rows : (b + 1) * rows])
            grad_prob = dot(values[:seen], one_grad, NT)
            inner = jnp.sum(prob * grad_prob, axis=0, keepdims=True)
            grad_score = prob * (grad_prob - inner)
            score_low = grad_score.astype(jnp.bfloat16)
            dv_sum[:seen] += dot(prob.astype(jnp.bfloat16), one_grad, NN)
            dk_sum[:seen] += dot(score_low, one_query, NN)
            if not causal:
                partial_sum = grad_score[:, :128]
                for piece in range(128, rows, 128):
                    partial_sum = partial_sum + grad_score[:, piece : piece + 128]
                prior_sum[...] += partial_sum
            part = dot(score_low, key_rows[:seen], TN)
            query_grad = part if query_grad is None else jnp.where(mask, part, query_grad)
        dq_ref[b * step : (b + 1) * step] = (
            (query_grad * 0.125).astype(jnp.bfloat16).reshape(step, 1, tile, width)
        )
    dkv_ref[:, 0] = dk_sum[...].astype(jnp.bfloat16).reshape(k_ref.shape)
    dkv_ref[:, 1] = dv_sum[...].astype(jnp.bfloat16).reshape(k_ref.shape)
    if causal:
        prior_ref[...] = jnp.zeros_like(prior_ref)
    else:
        prior_ref[0] = column_sum(prior_sum[...].T)


def pick(array, place):
    count, _, _, rows, width = array.shape
    return pl.BlockSpec((count, None, 1, rows, width), lambda s: (0, place, s, 0, 0))


def attend(causal, queries, query_at, keys, key_at, value_at, bias):
    count, _, seqs, tile, width = queries.shape
    key_rows = keys.shape[0] * keys.shape[3]
    head_width = width * count // HEADS
    length = count * tile
    heads = width // head_width
    return pl.pallas_call(
        partial(attend_forward_kernel, causal, head_width),
        grid=(seqs,),
        in_specs=[
            pick(queries, query_at),
            pick(keys, key_at),
            pick(keys, value_at),
            pl.BlockSpec(memory_space=pl.ANY)
            if causal
            else pl.BlockSpec((1, 1, key_rows), lambda s: (s, 0, 0)),
        ],
        out_specs=[
            pl.BlockSpec((count, 1, tile, width), lambda s: (0, s, 0, 0)),
            pl.BlockSpec((1, heads, length), lambda s: (s, 0, 0)),
        ],
        out_shape=[
            shape((count, seqs, tile, width), jnp.bfloat16),
            shape((seqs, heads, length), jnp.float32),
        ],
        compiler_params=params(),
        cost_estimate=cost(
            16 * seqs * length * key_rows * width, 4 * seqs * (length + key_rows) * width
        ),
        name="attend_self" if causal else "attend_memory",
    )(queries, keys, keys, bias)


def attend_back(
    causal, queries, query_at, keys, key_at, value_at, gradient, stat, bias, after
):
    count, _, seqs, tile, width = queries.shape
    key_tile = keys.shape[3]
    key_rows = count * key_tile
    head_width = width * count // HEADS
    length = count * tile
    heads = width // head_width
    return pl.pallas_call(
        partial(attend_backward_kernel, causal, head_width),
        grid=(seqs,),
        in_specs=[
            pick(queries, query_at),
            pick(keys, key_at),
            pick(keys, value_at),
            pl.BlockSpec((count, 1, tile, width), lambda s: (0, s, 0, 0)),
            pl.BlockSpec((1, heads, length), lambda s: (s, 0, 0)),
            pl.BlockSpec(memory_space=pl.ANY)
            if causal
            else pl.BlockSpec((1, 1, key_rows), lambda s: (s, 0, 0)),
            pl.BlockSpec(memory_space=pl.ANY),
        ],
        out_specs=[
            pl.BlockSpec((count, 1, tile, width), lambda s: (0, s, 0, 0)),
            pl.BlockSpec((count, 2, 1, key_tile, width), lambda s: (0, 0, s, 0, 0)),
            pl.BlockSpec((1, 1, key_rows), lambda s: (s, 0, 0)),
        ],
        out_shape=[
            shape((count, seqs, tile, width), jnp.bfloat16),
            shape((count, 2, seqs, key_tile, width), jnp.bfloat16),
            shape((seqs, 1, key_rows), jnp.float32),
        ],
        scratch_shapes=[
            pltpu.VMEM((key_rows, width), jnp.float32),
            pltpu.VMEM((key_rows, width), jnp.float32),
            pltpu.VMEM((key_rows, 128), jnp.float32),
        ],
        compiler_params=params(),
        cost_estimate=cost(
            40 * seqs * length * key_rows * width, 8 * seqs * (length + key_rows) * width
        ),
        name="attend_self_back" if causal else "attend_memory_back",
    )(queries, keys, keys, gradient, stat, bias, after)


def take_columns(scratch, slices, first):
    width = slices.shape[3]
    depth = scratch.shape[0]
    rows = depth // (slices.shape[0] * slices.shape[1])
    for m in range(scratch.shape[1] // width):
        start = (first + m) * rows
        scratch[:, m * width : (m + 1) * width] = slices[:, :, start : start + rows].reshape(
            depth, width
        )


def columns_kernel(first, row_ref, slice_ref, bias_ref, out_ref, weight):
    @pl.when(pl.program_id(0) == 0)
    def _():
        take_columns(weight, slice_ref, first)

    _, many, seqs, rows, width = out_ref.shape
    taken = row_ref[0, :, :rows].reshape(seqs * rows, weight.shape[0])
    result = dot(taken, weight[...], NN) + bias_ref[...]
    for m in range(many):
        out_ref[0, m] = (
            result[:, m * width : (m + 1) * width]
            .astype(jnp.bfloat16)
            .reshape(seqs, rows, width)
        )


def project_columns(name, gathered_rows, block_rows, row_block, rows, slices, first, many, bias):
    count, seqs, _, depth = gathered_rows.shape
    width = slices.shape[3]
    return pl.pallas_call(
        partial(columns_kernel, first),
        grid=(count,),
        in_specs=[
            pl.BlockSpec((1, seqs, block_rows, depth), lambda i: (i, 0, row_block, 0)),
            whole(slices),
            whole(bias),
        ],
        out_specs=pl.BlockSpec((1, many, seqs, rows, width), lambda i: (i, 0, 0, 0, 0)),
        out_shape=shape((count, many, seqs, rows, width), jnp.bfloat16),
        scratch_shapes=[pltpu.VMEM((depth, many * width), jnp.bfloat16)],
        compiler_params=params(),
        cost_estimate=cost(
            2 * many * count * seqs * rows * depth * width, 2 * count * seqs * rows * depth
        ),
        name=name,
    )(gathered_rows, slices, bias)


def columns_back_kernel(
    first, _, row_ref, *refs
):
    grad_refs, (slice_ref, mine_out, other_out, dw_ref, bias_ref, weight, total) = (
        refs[:-7],
        refs[-7:],
    )
    turn, step = pl.program_id(0), pl.program_id(1)

    @pl.when((turn == 0) & (step == 0))
    def _():
        take_columns(weight, slice_ref, first)
        total[...] = jnp.zeros_like(total)
        bias_ref[...] = jnp.zeros_like(bias_ref)

    depth = weight.shape[0]
    pieces = []
    for grad_ref in grad_refs:
        seqs, rows, width = grad_ref.shape[-3:]
        for m in range(grad_ref.shape[1] if len(grad_ref.shape) == 5 else 1):
            piece = grad_ref[0, m] if len(grad_ref.shape) == 5 else grad_ref[0]
            pieces.append(piece.reshape(seqs * rows, width))
    gradient = jnp.concatenate(pieces, axis=1)
    taken = row_ref[0, :, :rows].reshape(seqs * rows, depth)
    bias_ref[...] += column_sum(gradient.astype(jnp.float32))
    total[...] += dot(taken, gradient, TN)
    row_grad = dot(gradient, weight[...], NT).astype(jnp.bfloat16)

    @pl.when(turn == 0)
    def _():
        mine_out[0, 0] = row_grad

    @pl.when(turn == 1)
    def _():
        other_out[0, 0] = row_grad

    @pl.when((turn == 1) & (step == pl.num_programs(1) - 1))
    def _():
        groups, count, all_rows, _ = dw_ref.shape
        part = depth // (groups * count)
        for m in range(all_rows // part):
            dw_ref[:, :, m * part : (m + 1) * part] = (
                total[:, m * width : (m + 1) * width]
                .astype(jnp.bfloat16)
                .reshape(groups, count, part, width)
            )


def project_columns_back(
    name, order, gathered_rows, block_rows, row_block, rows, gradients, slices, first, many
):
    count, seqs, _, depth = gathered_rows.shape
    half = count // 2
    groups, _, _, width = slices.shape
    part = depth // (groups * count)

    def one_device(array):
        rest = (0,) * (len(array.shape) - 1)
        return pl.BlockSpec(
            (1,) + array.shape[1:], lambda p, k, order: (order[p * half + k],) + rest
        )

    dw_shape = shape((groups, count, many * part, width), jnp.bfloat16)
    return pl.pallas_call(
        partial(columns_back_kernel, first),
        grid_spec=pltpu.PrefetchScalarGridSpec(
            num_scalar_prefetch=1,
            grid=(2, half),
            in_specs=[
                pl.BlockSpec(
                    (1, seqs, block_rows, depth),
                    lambda p, k, order: (order[p * half + k], 0, row_block, 0),
                ),
                *[one_device(array) for array in gradients],
                whole(slices),
            ],
            out_specs=[
                pl.BlockSpec(
                    (1, 1, seqs * rows, depth),
                    lambda p, k, _: (jnp.where(p == 0, k, half - 1), 0, 0, 0),
                ),
                pl.BlockSpec(
                    (1, 1, seqs * rows, depth), lambda p, k, _: (jnp.where(p == 0, 0, k), 0, 0, 0)
                ),
                whole(dw_shape),
                pl.BlockSpec((1, many * width), lambda *_: (0, 0)),
            ],
            scratch_shapes=[
                pltpu.VMEM((depth, many * width), jnp.bfloat16),
                pltpu.VMEM((depth, many * width), jnp.float32),
            ],
        ),
        out_shape=[
            shape((half, 1, seqs * rows, depth), jnp.bfloat16),
            shape((half, 1, seqs * rows, depth), jnp.bfloat16),
            dw_shape,
            shape((1, many * width), jnp.float32),
        ],
        compiler_params=params(),
        cost_estimate=cost(
            4 * many * count * seqs * rows * depth * width, 4 * count * seqs * rows * depth
        ),
        name=name,
    )(order, gathered_rows, *gradients, slices)


def gathered(weights, width, place):
    count, groups, rows, _ = weights.shape
    return pl.BlockSpec((count, groups, rows, width), lambda *_: (0, 0, 0, place))


def first_kernel(
    mixed_ref, x_ref, out_w, query_w, vector_ref, _, mixed_out, in_out, low_out, query_out
):
    mixed = join(mixed_ref)
    mixed_out[...] = mixed
    first_in = x_ref[...].astype(jnp.float32) + times(mixed, out_w) + vector_ref[2:3]
    in_out[...] = first_in
    unit, _ = norm_parts(first_in)
    low = (unit * vector_ref[11:12] + vector_ref[12:13]).astype(jnp.bfloat16)
    low_out[...] = low
    spread(query_out, (times(low, query_w) + vector_ref[3:4]).astype(jnp.bfloat16))


def first_forward(mixed, x_rows, weights, vectors, after):
    rows, depth = x_rows.shape
    return pl.pallas_call(
        first_kernel,
        grid=(1,),
        in_specs=[
            whole(mixed),
            whole(x_rows),
            gathered(weights, depth, 0),
            gathered(weights, depth, 1),
            whole(vectors),
            pl.BlockSpec(memory_space=pl.ANY),
        ],
        out_specs=[whole(x_rows), whole(x_rows), whole(x_rows), whole(mixed)],
        out_shape=[
            shape((rows, depth), jnp.bfloat16),
            shape((rows, depth), jnp.float32),
            shape((rows, depth), jnp.bfloat16),
            shape(mixed.shape, jnp.bfloat16),
        ],
        compiler_params=params(),
        cost_estimate=cost(4 * rows * depth * depth, 4 * depth * depth),
        name="first_forward",
    )(mixed, x_rows, weights, weights, vectors, after)


def ffn_kernel(
    order,
    places,
    mixed_ref,
    first_ref,
    out_w,
    vector_ref,
    bias_ref,
    grad_ref,
    wide_ref,
    *refs,
):
    contract_refs, refs = refs[:8], refs[8:]
    mixed_out, layer_out, wide_grad = refs[:3]
    contract_grads, refs = refs[3:11], refs[11:]
    dbias_ref, second_grad, cross_low, mixed_grad, stat_out, columns, contracts = refs[:7]
    active, slope, low, third_low, second_in, total, wide_sem, contract_sem = refs[7:]
    blocks, count, groups, rows, block = columns.shape
    part = block // CHIPS
    depth = vector_ref.shape[1]

    def wide_copies(t, array, outward):
        result = []
        for k in range(CHIPS):
            column = pl.multiple_of(order[t % 2 * CHIPS + k] * part, part)
            row = pl.multiple_of(places[t // 2] * rows, rows)
            there = array.at[:, :, pl.ds(row, rows), pl.ds(column, part)]
            here = columns.at[t, :, :, :, pl.ds(k * part, part)]
            ends = (here, there) if outward else (there, here)
            result.append(pltpu.make_async_copy(*ends, wide_sem.at[t, k]))
        return result

    def contract_copies(t, pieces, outward):
        near, far = divmod(DP_ORDER[t // 2], 2)
        first = pieces[t % 2 * 4 + far].at[near]
        last = pieces[t % 2 * 4 + 2 + near].at[far]
        result = []
        for half, there in enumerate((first, last)):
            here = contracts.at[t, pl.ds(half * CHIPS // 2, CHIPS // 2)]
            ends = (here, there) if outward else (there, here)
            result.append(pltpu.make_async_copy(*ends, contract_sem.at[t, half]))
        return result

    for t in range(blocks):
        for copy in wide_copies(t, wide_ref, False):
            copy.start()
        for copy in contract_copies(t, contract_refs, False):
            copy.start()

    mixed = join(mixed_ref)
    mixed_out[...] = mixed
    unit, _ = norm_parts(first_ref[...])
    second_in[...] = (
        unit * vector_ref[11:12] + vector_ref[12:13] + times(mixed, out_w) + vector_ref[5:6]
    )
    unit, _ = norm_parts(second_in[...])
    second = unit * vector_ref[13:14] + vector_ref[14:15]
    low[...] = second.astype(jnp.bfloat16)
    total[...] = second + vector_ref[10:11]

    def shard(t, k):
        return places[t // 2] * count + order[t % 2 * CHIPS + k]

    for t in range(blocks):
        for copy in wide_copies(t, wide_ref, False):
            copy.wait()
        bias = jnp.concatenate([bias_ref[pl.ds(shard(t, k), 1)] for k in range(CHIPS)], axis=1)
        inner = times(low[...], columns.at[t]) + bias
        phi = 0.5 + 0.5 * lax.erf(inner * (0.5**0.5))
        out = (inner * phi).astype(jnp.bfloat16)
        active[t] = out
        slope[t] = phi + inner * jnp.exp(-0.5 * inner * inner) * 0.3989422804014327
        for copy in contract_copies(t, contract_refs, False):
            copy.wait()
        total[...] += dot(out, contracts[t].reshape(block, depth), NN)

    unit, inverse = norm_parts(total[...])
    gain = vector_ref[15:16]
    layer_out[...] = (unit * gain + vector_ref[16:17]).astype(jnp.bfloat16)
    gradient = grad_ref[...].astype(jnp.float32)
    grad_third = norm_back(gradient, unit, inverse, gain)
    stat_out[...] = jnp.zeros_like(stat_out)
    stat_out[0:1] = column_sum(grad_third)
    stat_out[1:2] = column_sum(gradient * unit)
    stat_out[2:3] = column_sum(gradient)
    total[...] = grad_third
    third_low[...] = grad_third.astype(jnp.bfloat16)
    turned = low[...].T

    for t in range(blocks):
        grad_inner = dot(third_low[...], contracts[t].reshape(block, depth), NT) * slope[t]
        inner_low = grad_inner.astype(jnp.bfloat16)
        sums = column_sum(grad_inner)
        for k in range(CHIPS):
            dbias_ref[pl.ds(shard(t, k), 1)] = sums[:, k * part : (k + 1) * part]
        contracts[t] = (
            dot(active[t], third_low[...], TN).astype(jnp.bfloat16).reshape(CHIPS, part, depth)
        )
        for copy in contract_copies(t, contract_grads, True):
            copy.start()
        total[...] += times_back(inner_low, columns.at[t])
        result = dot(turned, inner_low, NN).astype(jnp.bfloat16)
        for d in range(groups):
            columns[t, :, d] = result[d * count * rows : (d + 1) * count * rows].reshape(
                count, rows, block
            )
        for copy in wide_copies(t, wide_grad, True):
            copy.start()

    unit, inverse = norm_parts(second_in[...])
    grad_second = total[...]
    grad_in = norm_back(grad_second, unit, inverse, vector_ref[13:14])
    second_grad[...] = grad_in
    grad_low = grad_in.astype(jnp.bfloat16)
    cross_low[...] = grad_low
    spread(mixed_grad, times_back(grad_low, out_w).astype(jnp.bfloat16))
    stat_out[8:9] = column_sum(grad_in)
    stat_out[9:10] = column_sum(grad_second * unit)
    stat_out[10:11] = column_sum(grad_second)
    for t in range(blocks):
        for copy in contract_copies(t, contract_grads, True) + wide_copies(t, wide_grad, True):
            copy.wait()


def ffn(orders, mixed, first_in, wide, contract, vectors, bias, output_grad):
    rows, depth = first_in.shape
    hidden = bias.size
    block = depth // 2
    count, groups, all_rows, _ = wide.shape
    part = depth // (count * groups)
    blocks = hidden // block
    full = whole(first_in)
    anywhere = pl.BlockSpec(memory_space=pl.ANY)
    heads_out = shape(mixed.shape, jnp.bfloat16)
    stats = shape((16, depth), jnp.float32)
    return pl.pallas_call(
        ffn_kernel,
        grid_spec=pltpu.PrefetchScalarGridSpec(
            num_scalar_prefetch=2,
            grid=(1,),
            in_specs=[
                whole(mixed),
                full,
                pl.BlockSpec((count, groups, part, depth), lambda *_: (0, 0, groups, 0)),
                whole(vectors),
                whole(bias),
                full,
                *[anywhere] * 9,
            ],
            out_specs=[
                full,
                full,
                *[anywhere] * 9,
                whole(bias),
                full,
                full,
                whole(heads_out),
                whole(stats),
            ],
            scratch_shapes=[
                pltpu.VMEM((blocks, count, groups, part, block), jnp.bfloat16),
                pltpu.VMEM((blocks, CHIPS) + contract[0].shape[2:], jnp.bfloat16),
                pltpu.VMEM((blocks, rows, block), jnp.bfloat16),
                pltpu.VMEM((blocks, rows, block), jnp.float32),
                pltpu.VMEM((rows, depth), jnp.bfloat16),
                pltpu.VMEM((rows, depth), jnp.bfloat16),
                pltpu.VMEM((rows, depth), jnp.float32),
                pltpu.VMEM((rows, depth), jnp.float32),
                pltpu.SemaphoreType.DMA((blocks, CHIPS)),
                pltpu.SemaphoreType.DMA((blocks, 2)),
            ],
        ),
        out_shape=[
            shape((rows, depth), jnp.bfloat16),
            shape((rows, depth), jnp.bfloat16),
            shape((count, groups, all_rows - part, depth), jnp.bfloat16),
            *[shape(piece.shape, jnp.bfloat16) for piece in contract],
            shape(bias.shape, jnp.float32),
            shape((rows, depth), jnp.float32),
            shape((rows, depth), jnp.bfloat16),
            heads_out,
            stats,
        ],
        compiler_params=params(),
        cost_estimate=cost(12 * rows * depth * hidden, 16 * depth * hidden),
        name="ffn",
    )(*orders, mixed, first_in, wide, vectors, bias, output_grad, wide, *contract)


def first_back_kernel(
    dq_ref,
    second_grad,
    first_ref,
    out_w,
    query_w,
    vector_ref,
    _,
    query_low,
    grad_in_out,
    self_low,
    mixed_grad,
    stat_out,
):
    query_grad = join(dq_ref)
    query_low[...] = query_grad
    grad_first = second_grad[...] + times_back(query_grad, query_w)
    unit, inverse = norm_parts(first_ref[...])
    grad_in = norm_back(grad_first, unit, inverse, vector_ref[11:12])
    grad_in_out[...] = grad_in
    grad_low = grad_in.astype(jnp.bfloat16)
    self_low[...] = grad_low
    spread(mixed_grad, times_back(grad_low, out_w).astype(jnp.bfloat16))
    stat_out[...] = jnp.zeros_like(stat_out)
    stat_out[0:1] = column_sum(query_grad.astype(jnp.float32))
    stat_out[1:2] = column_sum(grad_in)
    stat_out[2:3] = column_sum(grad_first * unit)
    stat_out[3:4] = column_sum(grad_first)


def first_back(dq, second_grad, first_in, weights, vectors, after):
    rows, depth = first_in.shape
    full = whole(first_in)
    return pl.pallas_call(
        first_back_kernel,
        grid=(1,),
        in_specs=[
            whole(dq),
            full,
            full,
            gathered(weights, depth, 0),
            gathered(weights, depth, 1),
            whole(vectors),
            pl.BlockSpec(memory_space=pl.ANY),
        ],
        out_specs=[full, full, full, whole(dq), pl.BlockSpec((8, depth), lambda *_: (0, 0))],
        out_shape=[
            shape((rows, depth), jnp.bfloat16),
            shape((rows, depth), jnp.float32),
            shape((rows, depth), jnp.bfloat16),
            shape(dq.shape, jnp.bfloat16),
            shape((8, depth), jnp.float32),
        ],
        compiler_params=params(),
        cost_estimate=cost(4 * rows * depth * depth, 4 * depth * depth),
        name="first_back",
    )(dq, second_grad, first_in, weights, weights, vectors, after)


def weight_grads_kernel(
    order,
    mixed,
    self_low,
    first_low,
    query_low,
    cross,
    cross_low,
    mine_out,
    other_out,
    result,
):
    step = pl.program_id(0)
    pairs = ((mixed, self_low), (first_low, query_low), (cross, cross_low))
    half, groups, part, _ = mine_out.shape
    for m, (left_side, gradient) in enumerate(pairs):

        @pl.when(step == m)
        def _(left_side=left_side, gradient=gradient):
            result[...] = dot(left_side[...], gradient[...], TN).astype(jnp.bfloat16)

    for d in range(groups):
        for k in range(half):
            for p, out_ref in enumerate((mine_out, other_out)):
                row = pl.multiple_of((2 * half * d + order[p * half + k]) * part, part)
                out_ref[k, d] = result[pl.ds(row, part)]


def weight_grads(dims, order, mixed, self_low, first_low, query_low, cross, cross_low):
    count, groups, part, depth = dims
    half = pl.BlockSpec((count // 2, groups, part, depth), lambda m, _: (0, 0, m, 0))
    return pl.pallas_call(
        weight_grads_kernel,
        grid_spec=pltpu.PrefetchScalarGridSpec(
            num_scalar_prefetch=1,
            grid=(3,),
            in_specs=[whole(mixed)] * 6,
            out_specs=[half, half],
            scratch_shapes=[pltpu.VMEM((depth, depth), jnp.bfloat16)],
        ),
        out_shape=[shape((count // 2, groups, 3 * part, depth), jnp.bfloat16)] * 2,
        compiler_params=params(),
        cost_estimate=cost(6 * mixed.shape[0] * depth * depth, 6 * depth * depth),
        name="weight_grads",
    )(order, mixed, self_low, first_low, query_low, cross, cross_low)


def send_dp(piece):
    size = lax.axis_size("dp")
    return [
        lax.ppermute(piece, "dp", [(i, (i + shift) % size) for i in range(size)])
        for shift in range(1, size)
    ]


def place_dp(piece, arrived):
    size, me = lax.axis_size("dp"), lax.axis_index("dp")
    result = jnp.zeros((size,) + piece.shape, piece.dtype)
    result = lax.dynamic_update_index_in_dim(result, piece, me, 0)
    for shift, got in enumerate(arrived, 1):
        result = lax.dynamic_update_index_in_dim(result, got, lax.rem(me - shift + size, size), 0)
    return result


class HalvingDp:
    def __init__(self, pieces):
        me = lax.axis_index("dp")
        self.parts = [
            lax.dynamic_index_in_dim(pieces, me ^ flip, 0, keepdims=False) for flip in DP_ORDER
        ]

    def first(self):
        return jnp.stack(self.parts[2:]).astype(jnp.bfloat16)

    def second(self, got):
        self.got = got
        return (
            self.parts[1].astype(jnp.float32) + self.got[1].astype(jnp.float32)
        ).astype(jnp.bfloat16)

    def finish(self, last):
        return sum(one.astype(jnp.float32) for one in (self.parts[0], self.got[0], last))


def relative_order():
    size, me = lax.axis_size("index"), lax.axis_index("index")
    steps = jnp.arange(size // 2, dtype=jnp.int32) * 2
    return jnp.concatenate([me ^ steps, me ^ 1 ^ steps])


def exchange(piece, flip):
    size = lax.axis_size("index")
    return lax.ppermute(piece, "index", [(i, i ^ flip) for i in range(size)])


def exchange_dp(piece, flip):
    size = lax.axis_size("dp")
    return lax.ppermute(piece, "dp", [(i, i ^ flip) for i in range(size)])


def add_kernel(*refs):
    total = sum(ref[...].astype(jnp.float32) for ref in refs[:-1])
    refs[-1][...] = total.astype(jnp.bfloat16)


def add(*terms):
    flat, specs = [], []
    first = terms[0]
    dims = first[0].shape[1:] if isinstance(first, tuple) else first.shape
    rows = 1
    for size in dims[:-1]:
        rows *= size
    block = min(rows, 256)
    for term in terms:
        array, entry = term if isinstance(term, tuple) else (term, 0)
        flat.append(array.reshape(-1, dims[-1]))
        start = entry * rows // block
        specs.append(pl.BlockSpec((block, dims[-1]), lambda i, start=start: (start + i, 0)))
    return pl.pallas_call(
        add_kernel,
        grid=(rows // block,),
        in_specs=specs,
        out_specs=pl.BlockSpec((block, dims[-1]), lambda i: (i, 0)),
        out_shape=shape((rows, dims[-1]), jnp.bfloat16),
        compiler_params=params(),
        cost_estimate=cost(0, 0),
        name="add",
    )(*flat).reshape(dims)


def halves_kernel(*refs):
    count = (len(refs) - 2) // 2
    for half in range(2):
        total = sum(ref[...].astype(jnp.float32) for ref in refs[half * count : (half + 1) * count])
        refs[2 * count + half][...] = total.astype(jnp.bfloat16)


class Halving:
    def __init__(self, *parts):
        self.parts = [part.reshape(CHIPS, -1, part.shape[-1]) for part in parts]
        self.middle = self.parts[0].shape[1] // 2

    def total(self, k, half, *more):
        rows = slice(half * self.middle, (half + 1) * self.middle)
        return sum(one.astype(jnp.float32) for one in [p[k, rows] for p in self.parts] + [*more])

    def first(self):
        depth = self.parts[0].shape[2]
        block = (1, self.middle, depth)
        top = pl.BlockSpec(block, lambda e: (2 * e + 1, 0, 0))
        low = pl.BlockSpec(block, lambda e: (2 + e, 1, 0))
        out = pl.BlockSpec(block, lambda e: (e, 0, 0))
        count = len(self.parts)
        return pl.pallas_call(
            halves_kernel,
            grid=(2,),
            in_specs=[top] * count + [low] * count,
            out_specs=[out, out],
            out_shape=[shape((2, self.middle, depth), jnp.bfloat16)] * 2,
            compiler_params=params(),
            cost_estimate=cost(0, 0),
            name="halves",
        )(*self.parts, *self.parts)

    def second(self, top, low):
        self.got = top, low
        return [
            self.total(2, 0, top[1]).astype(jnp.bfloat16),
            self.total(1, 1, low[1]).astype(jnp.bfloat16),
        ]

    def finish(self, top, low):
        return jnp.concatenate(
            [self.total(0, 0, self.got[0][0], top), self.total(0, 1, self.got[1][0], low)], axis=0
        )


def seconds_kernel(*refs):
    top_out, low_out = refs[-2:]
    start = 0
    ins = refs[:-2]
    while ins:
        (top, top_got, low, low_got), ins = (ins[0:2], ins[2], ins[3:5], ins[5]), ins[6:]
        rows = top_got.shape[1]
        for parts, got, out_ref in ((top, top_got, top_out), (low, low_got, low_out)):
            total = sum(ref[0].astype(jnp.float32) for ref in (*parts, got))
            out_ref[start : start + rows] = total.astype(jnp.bfloat16)
        start += rows


def seconds(*sums):
    arrays, specs = [], []
    for one, top, low in sums:
        one.got = top, low
        block = (1, one.middle, top.shape[2])
        for k, half, got in ((2, 0, top), (1, 1, low)):
            arrays += [*one.parts, got]
            specs += [pl.BlockSpec(block, lambda i, k=k, half=half: (k, half, 0))] * 2
            specs += [pl.BlockSpec(block, lambda i: (1, 0, 0))]
    out = shape((sum(one[0].middle for one in sums), arrays[0].shape[2]), jnp.bfloat16)
    return pl.pallas_call(
        seconds_kernel,
        grid=(1,),
        in_specs=specs,
        out_specs=[whole(out)] * 2,
        out_shape=[out] * 2,
        compiler_params=params(),
        cost_estimate=cost(0, 0),
        name="seconds",
    )(*arrays)


def send_first(top, low):
    return [exchange(top, 2), exchange(low, 4)]


def send_last(top, low):
    return [exchange(top, 4), exchange(low, 2)]


def merge(first, second):
    return [jnp.concatenate(pair, axis=-2) for pair in zip(first, second)]


def split_rows(arrays, rows):
    return [a[..., :rows, :] for a in arrays], [a[..., rows:, :] for a in arrays]


def small_send(values):
    size = lax.axis_size("index")
    flat = jnp.pad(values.reshape(-1), (0, 1024 - values.size)).reshape(1, 8, 128)
    return swap(jnp.broadcast_to(flat, (size, 8, 128)))


def small_take(arrived, dims):
    size = 1
    for dim in dims:
        size *= dim
    return jnp.sum(arrived, axis=0).reshape(-1)[:size].reshape(dims)


def hold_kernel(*_):
    pass


def hold(values, *others):
    anywhere = pl.BlockSpec(memory_space=pl.ANY)
    return pl.pallas_call(
        hold_kernel,
        in_specs=[anywhere] * (len(values) + len(others)),
        out_specs=[anywhere] * len(values),
        out_shape=[shape(value.shape, value.dtype) for value in values],
        input_output_aliases={i: i for i in range(len(values))},
        name="hold",
    )(*values, *others)


def swap(pieces):
    return lax.all_to_all(pieces, "index", 0, 0, tiled=True)


def head_body(
    decoder_input,
    encoder_memory,
    question_vectors,
    passage_vectors,
    passage_ids,
    valid_count,
    output_grad,
    attention_weight,
    expand_weight,
    contract_weight,
    vector_params,
    attention_mean,
    attention_square,
    expand_mean,
    expand_square,
    contract_mean,
    contract_square,
    vector_mean,
    vector_square,
):
    low = jnp.bfloat16
    count, groups = lax.axis_size("index"), lax.axis_size("dp")
    place = lax.axis_index("index")
    seqs, rows_here, depth = decoder_input.shape
    memory_here = encoder_memory.shape[1]
    width = depth // count
    part = attention_weight.shape[1]
    hidden = expand_weight.shape[1]
    vector_rows, vector_width = vector_params.shape
    question_width = question_vectors.shape[1]
    rows = seqs * rows_here

    attention_low = attention_weight.astype(low)
    extras = jnp.concatenate(
        [vector_params.astype(low).reshape(-1), question_vectors.reshape(-1)]
    )
    extra_rows = -(-extras.shape[0] // (16 * width)) * 16
    extras = jnp.pad(extras, (0, extra_rows * width - extras.shape[0])).reshape(
        1, extra_rows, width
    )
    split = jnp.concatenate([attention_low[:3], attention_low[5:7]], axis=0)
    columns = split.reshape(5, part, count, width).transpose(2, 0, 1, 3)
    package = jnp.concatenate(
        [
            columns.reshape(count, 5 * part, width),
            jnp.broadcast_to(extras, (count, extra_rows, width)),
        ],
        axis=1,
    )
    order = relative_order()
    memory_block = -(-memory_here // rows_here) * rows_here
    rows_all = lax.all_gather(
        jnp.concatenate(
            [
                jnp.pad(encoder_memory, ((0, 0), (0, memory_block - memory_here), (0, 0))),
                decoder_input,
            ],
            axis=1,
        ),
        "index",
        axis=0,
        tiled=False,
    )
    input_rows = (rows_all, rows_here, memory_block // rows_here, rows_here)
    memory_rows = (rows_all, memory_block, 0, memory_here)
    square = attention_low[3:5].transpose(1, 0, 2).reshape(part, 2 * depth)
    received = swap(package)
    square_arrived = hold(send_dp(square), received)
    (received,) = hold([received], *square_arrived)
    received_sent = send_dp(received)
    (contract,) = hold([contract_weight.astype(low)], received)
    contract = [contract] + [exchange(contract, 2 * k) for k in range(1, CHIPS)]
    slices_arrived = hold(received_sent, *contract[1:])
    square_arrived = hold(square_arrived, *slices_arrived)
    square = lax.all_gather(place_dp(square, square_arrived), "index", axis=0, tiled=False)
    slices = place_dp(received, slices_arrived)
    vectors = (
        slices[:, :, 5 * part :]
        .reshape(groups, count, extra_rows * width)[:, :, : vector_rows * vector_width]
        .reshape(groups, count, vector_rows, vector_width)
        .transpose(2, 0, 1, 3)
        .reshape(vector_rows, depth)
        .astype(jnp.float32)
    )
    question_full = (
        received[:, 5 * part :]
        .reshape(count, extra_rows * width)[:, vector_rows * vector_width :][
            :, : seqs * question_width
        ]
        .reshape(count, seqs, question_width)
        .transpose(1, 0, 2)
        .reshape(seqs, count * question_width)
    )
    expand_part = hidden // depth * part
    late = jnp.concatenate(
        [
            expand_weight.astype(low)
            .reshape(part, hidden // depth, depth)
            .transpose(1, 0, 2)
            .reshape(expand_part, depth),
            attention_low[7],
        ],
        axis=0,
    )
    (late,) = hold([late], *slices_arrived)
    late_sent = send_dp(late)

    (passage_ids,) = hold([passage_ids], *slices_arrived)
    passages_here = passage_vectors.shape[0]
    local_ids = passage_ids - place * passages_here
    owned_slot = (local_ids >= 0) & (local_ids < passages_here)
    picked = passage_vectors[jnp.clip(local_ids, 0, passages_here - 1)]
    local_scores = jnp.einsum(
        "sc,skc->sk", question_full, picked, preferred_element_type=jnp.float32
    )
    slots = passage_ids.shape[1]
    usable = jnp.arange(slots)[None, :] < valid_count[:, None]
    scores = small_take(small_send(jnp.where(owned_slot, local_scores, 0.0)), local_scores.shape)
    masked = jnp.where(usable, scores, negative_fill)
    maximum = jnp.max(masked, axis=1)
    exponent = jnp.where(usable, jnp.exp(masked - maximum[:, None]), 0.0)
    partition = jnp.sum(exponent, axis=1)
    passage_prob = exponent / partition[:, None]
    log_prior = jnp.where(
        usable, masked - maximum[:, None] - jnp.log(partition)[:, None], negative_fill
    )
    key_bias = jnp.repeat(log_prior, MEM_P, axis=1)

    vector_here = lax.dynamic_slice_in_dim(vectors[:5], place * width, width, axis=1)
    no_bias = jnp.zeros((1, width), jnp.float32)
    qkv_bias = jnp.concatenate([vector_here[0:1], no_bias, vector_here[1:2]], axis=1)
    kv_bias = jnp.concatenate([no_bias, vector_here[4:5]], axis=1)
    x_rows = decoder_input.reshape(rows, depth)
    qkv = project_columns("self_qkv", *input_rows, slices, 0, 3, qkv_bias)
    self_out, self_stat = attend(True, qkv, 0, qkv, 1, 2, key_bias[:, None, :])
    self_out, *late_arrived = hold([self_out, *late_sent])
    self_got = swap(self_out)
    late = lax.all_gather(place_dp(late, late_arrived), "index", axis=0, tiled=False)
    ahead, across = hold([jnp.stack(contract[:2]), jnp.stack(contract[2:])], *late_arrived)
    self_got, ahead_far, across_far, slices = hold(
        [self_got, exchange_dp(ahead, 2), exchange_dp(across, 1), slices]
    )
    memory_kv = project_columns("memory_kv", *memory_rows, slices, 3, 2, kv_bias)
    ahead = jnp.stack([ahead, ahead_far])
    across = jnp.stack([across, across_far])
    contract_sent = [exchange_dp(ahead, 1), exchange_dp(across, 2)]
    self_mixed, first_in, first_low, cross_query = first_forward(
        self_got, x_rows, square, vectors, memory_kv
    )
    cross_query = swap(cross_query)[:, None]
    cross_out, cross_stat = attend(
        False, cross_query, 0, memory_kv, 0, 1, key_bias[:, None, :]
    )
    ahead_far, across_far = hold(contract_sent, cross_out)
    contract = [ahead, ahead_far, across, across_far]
    contract += [exchange(piece, 1) for piece in contract]
    places = lax.axis_index("dp") ^ jnp.array(DP_ORDER, jnp.int32)
    (
        cross_mixed,
        layer_output,
        wide_grad,
        *contract_grads,
        inner_total,
        second_grad,
        cross_low,
        cross_mix_grad,
        stats,
    ) = ffn(
        (order, places),
        swap(cross_out),
        first_in,
        late,
        contract,
        vectors,
        vectors[6:10].reshape(groups * count, -1),
        output_grad.reshape(rows, depth),
    )
    third_stat, second_stat = stats[:8], stats[8:]

    expand_part_sum = lax.psum_scatter(wide_grad, "index", scatter_dimension=0, tiled=False)
    ahead, ahead_far, across, across_far = contract_grads[:4]
    cores = [exchange(piece, 1) for piece in contract_grads[4:]]
    cross_mix_got, *contract_sent = hold(
        [swap(cross_mix_grad), add(ahead_far, cores[1]), add(across_far, cores[3])]
    )
    contract_got = [exchange_dp(contract_sent[0], 1), exchange_dp(contract_sent[1], 2)]
    cross_dq, cross_dkv, prior_rows = attend_back(
        False,
        cross_query,
        0,
        memory_kv,
        0,
        1,
        cross_mix_got,
        cross_stat,
        key_bias[:, None, :],
        contract_sent[0],
    )
    memory_mine, memory_other, kv_grads, kv_total = project_columns_back(
        "memory_kv_back", order, *memory_rows, [cross_dkv], slices, 3, 2
    )
    cross_dq, *contract_got = hold([cross_dq, *contract_got], memory_mine)
    contract_next = [
        add((ahead, 1), (cores[0], 1), (contract_got[0], 1)),
        add((across, 1), (cores[2], 1), (contract_got[1], 1)),
    ]
    cross_dq_got, *contract_next = hold([swap(cross_dq), *contract_next])
    contract_last = [exchange_dp(contract_next[0], 2), exchange_dp(contract_next[1], 1)]
    query_low, first_grad, self_low, self_mix_grad, first_stat = first_back(
        cross_dq_got, second_grad, first_in, square, vectors, memory_mine
    )
    kv_far = HalvingDp(kv_grads)
    memory_sum = Halving(memory_mine, exchange(memory_other, 1))
    memory_sent = memory_sum.first()
    square_mine, square_other = weight_grads(
        (count, groups, part, depth),
        order,
        self_mixed,
        self_low,
        first_low,
        query_low,
        cross_mixed,
        cross_low,
    )
    square_sum = Halving(square_mine, exchange(square_other, 1))
    square_sent = square_sum.first()
    self_mix_got, *contract_last = hold(
        [swap(self_mix_grad), *contract_last], *memory_sent, *square_sent
    )
    memory_got = send_first(*memory_sent)
    square_got = send_first(*square_sent)
    self_dq, self_dkv, _ = attend_back(
        True, qkv, 0, qkv, 1, 2, self_mix_got, self_stat, self_stat, square_mine
    )
    expand_sum = HalvingDp(expand_part_sum)
    self_dq, expand_sent = hold([self_dq, expand_sum.first()])
    expand_got = exchange_dp(expand_sent, 1)
    dx_mine, dx_other, qkv_slice_grads, qkv_total = project_columns_back(
        "self_qkv_back", order, *input_rows, [self_dq, self_dkv], slices, 0, 3
    )
    dx_mine, dx_other, expand_got, *got = hold(
        [dx_mine, dx_other, expand_got, *memory_got, *square_got]
    )
    dx_got = exchange(dx_other, 1)
    square_rows = square_sum.middle
    last = seconds((square_sum, *got[2:]), (memory_sum, *got[:2]))
    qkv_slice_grads, qkv_total, kv_total, prior_rows, expand_got, *contract_last = hold(
        [qkv_slice_grads, qkv_total, kv_total, prior_rows, expand_got, *contract_last], *last
    )
    last = send_last(*last)
    expand_last = exchange_dp(expand_sum.second(expand_got), 2)
    own = jnp.concatenate(
        [qkv_total[:, :width], qkv_total[:, 2 * width :], kv_total[:, width:]], axis=0
    )
    own = lax.dynamic_update_slice(
        jnp.zeros((3, depth), jnp.float32), own, (jnp.int32(0), place * width)
    )
    vector_grads = jnp.concatenate(
        [
            own[:2],
            first_stat[1:2],
            first_stat[0:1],
            own[2:],
            second_stat[0:1],
            inner_total.reshape(hidden // depth, depth),
            third_stat[0:1],
            first_stat[2:4],
            second_stat[1:3],
            third_stat[1:3],
        ],
        axis=0,
    )
    vector_size = vector_rows * vector_width
    question_size = seqs * question_width
    vector_send = (
        vector_grads.reshape(vector_rows, groups, count, vector_width)
        .transpose(1, 2, 0, 3)
        .reshape(groups, count, vector_size)
    )
    vector_send = jnp.pad(
        vector_send, ((0, 0), (0, 0), (0, extra_rows * width - vector_size))
    ).reshape(groups, count, extra_rows, width)
    slice_sum = HalvingDp(
        jnp.concatenate([qkv_slice_grads, kv_grads, vector_send.astype(low)], axis=2)
    )
    slice_got = exchange_dp(slice_sum.first(), 1)
    prior_arrived = small_send(prior_rows.reshape(seqs, slots, MEM_P).sum(axis=-1))
    dx_got, expand_last, prior_arrived, *last = hold(
        [dx_got, expand_last, prior_arrived, *last]
    )
    square_last, memory_last = split_rows(last, square_rows)
    square_far = HalvingDp(square_sum.finish(*square_last).reshape(groups, 3 * part, depth))
    square_sent = square_far.first()
    dx_sum = Halving(dx_mine, dx_got)
    contract_sum = Halving(
        jnp.concatenate(
            [
                add((one, 0), (core, 0), (got, 0), last)
                for one, core, got, last in zip(
                    (ahead, across), (cores[0], cores[2]), contract_got, contract_last
                )
            ],
            axis=0,
        )
    )
    got = send_first(*merge(dx_sum.first(), contract_sum.first()))
    square_got = exchange_dp(square_sent, 1)
    memory_gradient = memory_sum.finish(*memory_last).reshape(encoder_memory.shape)
    square_got, slice_got, *got = hold([square_got, slice_got, *got], memory_gradient)
    dx_got, contract_got = split_rows(got, dx_sum.middle)
    last = send_last(*merge(dx_sum.second(*dx_got), contract_sum.second(*contract_got)))
    square_last = exchange_dp(square_far.second(square_got), 2)
    slice_last = exchange_dp(slice_sum.second(slice_got), 2)
    slice_last, *last = hold([slice_last, *last])
    dx_last, contract_last = split_rows(last, dx_sum.middle)
    input_gradient = first_grad + dx_sum.finish(*dx_last)
    contract_sum = contract_sum.finish(*contract_last)
    slice_sum = slice_sum.finish(slice_last)

    prior_grad = jnp.where(usable, small_take(prior_arrived, (seqs, slots)), 0.0)
    score_doc = jnp.where(
        usable, prior_grad - passage_prob * jnp.sum(prior_grad, axis=1, keepdims=True), 0.0
    )
    question_part = jnp.einsum(
        "sk,skc->sc",
        jnp.where(owned_slot, score_doc, 0.0),
        picked.astype(jnp.float32),
        precision=lax.Precision.HIGHEST,
    )

    question_send = (
        question_part.reshape(seqs, count, question_width)
        .transpose(1, 0, 2)
        .reshape(count, question_size)
    )
    question_send = jnp.pad(
        question_send,
        ((0, 0), (vector_size, extra_rows * width - vector_size - question_size)),
    ).reshape(count, extra_rows, width)
    slice_sum = jnp.concatenate(
        [slice_sum[:, : 5 * part], slice_sum[:, 5 * part :] + question_send], axis=1
    )
    arrived = swap(slice_sum.astype(low)).astype(jnp.float32)
    split_grads = (
        arrived[:, : 5 * part]
        .reshape(count, 5, part, width)
        .transpose(1, 2, 0, 3)
        .reshape(5, part, depth)
    )
    extra_sum = jnp.sum(arrived[:, 5 * part :].reshape(count, extra_rows * width), axis=0)
    vector_sum = extra_sum[:vector_size].reshape(vector_rows, vector_width)
    question_gradient = extra_sum[vector_size : vector_size + question_size].reshape(
        seqs, question_width
    )

    expand_sum = (
        expand_sum.finish(expand_last)
        .reshape(hidden // depth, part, depth)
        .transpose(1, 0, 2)
        .reshape(part, hidden)
    )
    square_total = square_far.finish(square_last).reshape(3, part, depth)
    attention_sum = jnp.concatenate(
        [split_grads[:3], square_total[:2], split_grads[3:], square_total[2:]], axis=0
    )

    new_attention = adam_update(
        attention_weight,
        attention_mean,
        attention_square,
        attention_sum,
        rate_attention,
        decay_matrix,
    )
    new_expand = adam_update(
        expand_weight, expand_mean, expand_square, expand_sum, rate_expand, decay_matrix
    )
    new_contract = adam_update(
        contract_weight, contract_mean, contract_square, contract_sum, rate_contract, decay_matrix
    )
    new_vector = adam_update(
        vector_params, vector_mean, vector_square, vector_sum, rate_vector, 0.0
    )
    return (
        layer_output.reshape(decoder_input.shape),
        input_gradient.reshape(decoder_input.shape),
        memory_gradient,
        question_gradient,
        *new_attention,
        *new_expand,
        *new_contract,
        *new_vector,
    )


def body(sizes, *arrays):
    depth = arrays[0].shape[2]
    if sizes == (4, 8) and depth // 8 % 128 == 0:
        return head_body(*arrays)
    return general_body(*arrays)


def solution(mesh):
    return jax.shard_map(
        partial(body, (mesh.shape["dp"], mesh.shape["index"])),
        mesh=mesh,
        in_specs=(
            P("dp", "index", None),
            P("dp", "index", None),
            P("dp", "index"),
            P("index", None),
            P("dp", None),
            P("dp"),
            P("dp", "index", None),
            P(None, ("dp", "index"), None),
            P(("dp", "index"), None),
            P(("dp", "index"), None),
            P(None, ("dp", "index")),
            P(None, ("dp", "index"), None),
            P(None, ("dp", "index"), None),
            P(("dp", "index"), None),
            P(("dp", "index"), None),
            P(("dp", "index"), None),
            P(("dp", "index"), None),
            P(None, ("dp", "index")),
            P(None, ("dp", "index")),
        ),
        out_specs=(
            P("dp", "index", None),
            P("dp", "index", None),
            P("dp", "index", None),
            P("dp", "index"),
            P(None, ("dp", "index"), None),
            P(None, ("dp", "index"), None),
            P(None, ("dp", "index"), None),
            P(("dp", "index"), None),
            P(("dp", "index"), None),
            P(("dp", "index"), None),
            P(("dp", "index"), None),
            P(("dp", "index"), None),
            P(("dp", "index"), None),
            P(None, ("dp", "index")),
            P(None, ("dp", "index")),
            P(None, ("dp", "index")),
        ),
        check_vma=False,
    )
```

```python
from functools import partial

import jax
import jax.numpy as jnp
from jax import lax
from jax.experimental import pallas as pl
from jax.experimental.pallas import tpu as pltpu
from jax.sharding import PartitionSpec as P

HEADS = 16
MEM_P = 192
STEP = 10


negative_fill = -1e30
norm_eps = 1e-05
beta_first = 0.9
beta_second = 0.999
adam_eps = 1e-08
decay_matrix = 0.01
rate_attention = 0.1
rate_expand = 0.02
rate_contract = 0.01
rate_vector = 0.2


def layer_norm(hidden, norm_gain, norm_shift):
    center = hidden - jnp.mean(hidden, axis=-1, keepdims=True)
    spread = jnp.mean(center * center, axis=-1, keepdims=True)
    return center * lax.rsqrt(spread + norm_eps) * norm_gain + norm_shift


def split_heads(matrix):
    return matrix.reshape(matrix.shape[0], matrix.shape[1], HEADS, matrix.shape[2] // HEADS)


def merge_heads(matrix):
    return matrix.reshape(matrix.shape[0], matrix.shape[1], matrix.shape[2] * matrix.shape[3])


def project(left_side, weight):
    return jnp.einsum("srd,de->sre", left_side, weight, preferred_element_type=jnp.float32)


def project_back(gradient, weight):
    return jnp.einsum("sre,de->srd", gradient, weight, preferred_element_type=jnp.float32)


def weight_grad(left_side, gradient):
    return jnp.einsum("srd,sre->de", left_side, gradient, preferred_element_type=jnp.float32)


def row_total(values):
    return jnp.sum(values, axis=(0, 1))


def attend_forward(queries, key_rows, values, score_bias, allowed):
    scores = (
        jnp.einsum(
            "sqhd,skhd->shqk",
            split_heads(queries),
            split_heads(key_rows),
            preferred_element_type=jnp.float32,
        )
        * 0.125
        + score_bias
    )
    scores = jnp.where(allowed, scores, negative_fill)
    maximum = jnp.max(scores, axis=-1)
    exponent = jnp.exp(scores - maximum[..., None])
    partition = jnp.sum(exponent, axis=-1)
    attend_prob = exponent / partition[..., None]
    mixture = jnp.einsum(
        "shqk,skhd->sqhd",
        attend_prob.astype(jnp.bfloat16),
        split_heads(values),
        preferred_element_type=jnp.float32,
    )
    return (merge_heads(mixture).astype(jnp.bfloat16), attend_prob, maximum, partition)


def score_grads(grad_mixed, attend_prob, values):
    grad_prob = jnp.einsum(
        "sqhd,skhd->shqk",
        split_heads(grad_mixed),
        split_heads(values),
        preferred_element_type=jnp.float32,
    )
    row_inner = jnp.sum(attend_prob * grad_prob, axis=-1)
    return ((attend_prob * (grad_prob - row_inner[..., None])).astype(jnp.bfloat16), row_inner)


def to_queries(grad_score, key_rows):
    return (
        merge_heads(
            jnp.einsum(
                "shqk,skhd->sqhd",
                grad_score,
                split_heads(key_rows),
                preferred_element_type=jnp.float32,
            )
        )
        * 0.125
    )


def to_keys(grad_score, attend_prob, queries, grad_mixed):
    grad_key = (
        merge_heads(
            jnp.einsum(
                "shqk,sqhd->skhd",
                grad_score,
                split_heads(queries),
                preferred_element_type=jnp.float32,
            )
        )
        * 0.125
    )
    grad_value = merge_heads(
        jnp.einsum(
            "shqk,sqhd->skhd",
            attend_prob.astype(jnp.bfloat16),
            split_heads(grad_mixed),
            preferred_element_type=jnp.float32,
        )
    )
    return (grad_key, grad_value)


def adam_update(weight, moment_one, moment_two, gradient, step_rate, weight_decay):
    mean_new = beta_first * moment_one + (1.0 - beta_first) * gradient
    square_new = beta_second * moment_two + (1.0 - beta_second) * gradient * gradient
    mean_hat = mean_new / (1.0 - beta_first**STEP)
    square_hat = square_new / (1.0 - beta_second**STEP)
    updated = weight - step_rate * (
        mean_hat / (jnp.sqrt(square_hat) + adam_eps) + weight_decay * weight
    )
    return (updated, mean_new, square_new)


def general_body(
    decoder_input,
    encoder_memory,
    question_vectors,
    passage_vectors,
    passage_ids,
    valid_count,
    output_grad,
    attention_weight,
    expand_weight,
    contract_weight,
    vector_params,
    attention_mean,
    attention_square,
    expand_mean,
    expand_square,
    contract_mean,
    contract_square,
    vector_mean,
    vector_square,
):
    attention_low, expand_low, contract_low, vector_low = (
        lax.all_gather(attention_weight.astype(jnp.bfloat16), ("dp", "index"), axis=1, tiled=True),
        lax.all_gather(expand_weight.astype(jnp.bfloat16), ("dp", "index"), axis=0, tiled=True),
        lax.all_gather(contract_weight.astype(jnp.bfloat16), ("dp", "index"), axis=0, tiled=True),
        lax.all_gather(vector_params.astype(jnp.bfloat16), ("dp", "index"), axis=1, tiled=True),
    )
    vectors = vector_low.astype(jnp.float32)
    seqs_here, rows_here, model_width = decoder_input.shape
    shard_index = lax.axis_index("index")
    length = rows_here * lax.axis_size("index")
    ffn_width = expand_low.shape[1]
    self_query = (project(decoder_input, attention_low[0]) + vectors[0]).astype(jnp.bfloat16)
    self_key = project(decoder_input, attention_low[1]).astype(jnp.bfloat16)
    self_value = (project(decoder_input, attention_low[2]) + vectors[1]).astype(jnp.bfloat16)
    key_all, value_all = (
        lax.all_gather(self_key, "index", axis=1, tiled=True),
        lax.all_gather(self_value, "index", axis=1, tiled=True),
    )
    query_place = shard_index * rows_here + jnp.arange(rows_here)
    causal = (jnp.arange(length)[None, :] <= query_place[:, None])[None, None]
    self_mixed, self_prob, self_peak, self_total = attend_forward(
        self_query, key_all, value_all, 0.0, causal
    )
    first_in = (
        decoder_input.astype(jnp.float32) + project(self_mixed, attention_low[3]) + vectors[2]
    )
    first_out, first_back = jax.vjp(layer_norm, first_in, vectors[11], vectors[12])
    first_low = first_out.astype(jnp.bfloat16)
    cross_query = (project(first_low, attention_low[4]) + vectors[3]).astype(jnp.bfloat16)
    cross_key = project(encoder_memory, attention_low[5]).astype(jnp.bfloat16)
    cross_value = (project(encoder_memory, attention_low[6]) + vectors[4]).astype(jnp.bfloat16)
    memory_keys, memory_values = (
        lax.all_gather(cross_key, "index", axis=1, tiled=True),
        lax.all_gather(cross_value, "index", axis=1, tiled=True),
    )
    question_full = lax.all_gather(question_vectors, "index", axis=1, tiled=True)
    passages_here = passage_vectors.shape[0]
    local_ids = passage_ids - shard_index * passages_here
    owned_slot = (local_ids >= 0) & (local_ids < passages_here)
    picked = passage_vectors[jnp.clip(local_ids, 0, passages_here - 1)]
    local_scores = jnp.einsum(
        "sc,skc->sk", question_full, picked, preferred_element_type=jnp.float32
    )
    slots = passage_ids.shape[1]
    usable = jnp.arange(slots)[None, :] < valid_count[:, None]
    local_peak = jnp.max(jnp.where(owned_slot & usable, local_scores, negative_fill), axis=1)
    maximum = lax.pmax(local_peak, "index")
    local_exp = jnp.where(owned_slot & usable, jnp.exp(local_scores - maximum[:, None]), 0.0)
    exponent, scores = lax.psum((local_exp, jnp.where(owned_slot, local_scores, 0.0)), "index")
    masked = jnp.where(usable, scores, negative_fill)
    partition = jnp.sum(exponent, axis=1)
    passage_prob = exponent / partition[:, None]
    log_prior = masked - maximum[:, None] - jnp.log(partition)[:, None]
    memory_total = memory_keys.shape[1]
    bias_rows = jnp.repeat(log_prior, MEM_P, axis=1)
    key_bias = bias_rows[:, None, None, :]
    key_usable = ((jnp.arange(memory_total) // MEM_P)[None, :] < valid_count[:, None])[
        :, None, None, :
    ]
    cross_mixed, cross_prob, cross_peak, cross_total = attend_forward(
        cross_query, memory_keys, memory_values, key_bias, key_usable
    )
    second_in = first_out + project(cross_mixed, attention_low[7]) + vectors[5]
    second_out, second_back = jax.vjp(layer_norm, second_in, vectors[13], vectors[14])
    second_low = second_out.astype(jnp.bfloat16)
    inner_act = project(second_low, expand_low) + vectors[6:10].reshape(ffn_width)
    activated, gelu_back = jax.vjp(partial(jax.nn.gelu, approximate=False), inner_act)
    activ_low = activated.astype(jnp.bfloat16)
    third_in = second_out + project(activ_low, contract_low) + vectors[10]
    layer_output, third_back = jax.vjp(layer_norm, third_in, vectors[15], vectors[16])
    grad_third, gain_three, shift_three = third_back(output_grad.astype(jnp.float32))
    grad_ffn_low = grad_third.astype(jnp.bfloat16)
    grad_contract = weight_grad(activ_low, grad_ffn_low)
    (grad_inner,) = gelu_back(project_back(grad_ffn_low, contract_low))
    grad_inner_low = grad_inner.astype(jnp.bfloat16)
    grad_expand = weight_grad(second_low, grad_inner_low)
    grad_second = grad_third + project_back(grad_inner_low, expand_low)
    grad_second_in, gain_two, shift_two = second_back(grad_second)
    grad_cross_low = grad_second_in.astype(jnp.bfloat16)
    grad_cmix = project_back(grad_cross_low, attention_low[7]).astype(jnp.bfloat16)
    cross_score, cross_inner = score_grads(grad_cmix, cross_prob, memory_values)
    grad_cq = to_queries(cross_score, memory_keys)
    prior_part = (
        jnp.sum(cross_score, axis=(1, 2), dtype=jnp.float32)
        .reshape(seqs_here, slots, MEM_P)
        .sum(axis=-1)
    )
    prior_grad = jnp.where(usable, lax.psum(prior_part, "index"), 0.0)
    score_doc = jnp.where(
        usable, prior_grad - passage_prob * jnp.sum(prior_grad, axis=1, keepdims=True), 0.0
    )
    question_part = jnp.einsum(
        "sk,skc->sc",
        jnp.where(owned_slot, score_doc, 0.0),
        picked.astype(jnp.float32),
        precision=lax.Precision.HIGHEST,
    )
    question_gradient = lax.psum_scatter(question_part, "index", scatter_dimension=1, tiled=True)
    grad_cq_low = grad_cq.astype(jnp.bfloat16)
    grad_first = grad_second_in + project_back(grad_cq_low, attention_low[4])
    ck_part, cv_part = to_keys(cross_score, cross_prob, cross_query, grad_cmix)
    grad_ck, grad_cv = (
        lax.psum_scatter(
            ck_part.astype(jnp.bfloat16), "index", scatter_dimension=1, tiled=True
        ).astype(jnp.float32),
        lax.psum_scatter(
            cv_part.astype(jnp.bfloat16), "index", scatter_dimension=1, tiled=True
        ).astype(jnp.float32),
    )
    grad_ck_low = grad_ck.astype(jnp.bfloat16)
    grad_cv_low = grad_cv.astype(jnp.bfloat16)
    memory_gradient = project_back(grad_ck_low, attention_low[5]) + project_back(
        grad_cv_low, attention_low[6]
    )
    grad_first_in, gain_one, shift_one = first_back(grad_first)
    grad_self_low = grad_first_in.astype(jnp.bfloat16)
    grad_smix = project_back(grad_self_low, attention_low[3]).astype(jnp.bfloat16)
    self_score, row_inner = score_grads(grad_smix, self_prob, value_all)
    grad_sq = to_queries(self_score, key_all)
    key_part, value_part = to_keys(self_score, self_prob, self_query, grad_smix)
    grad_sk, grad_sv = (
        lax.psum_scatter(
            key_part.astype(jnp.bfloat16), "index", scatter_dimension=1, tiled=True
        ).astype(jnp.float32),
        lax.psum_scatter(
            value_part.astype(jnp.bfloat16), "index", scatter_dimension=1, tiled=True
        ).astype(jnp.float32),
    )
    grad_sq_low = grad_sq.astype(jnp.bfloat16)
    grad_sk_low = grad_sk.astype(jnp.bfloat16)
    grad_sv_low = grad_sv.astype(jnp.bfloat16)
    input_gradient = (
        grad_first_in
        + project_back(grad_sq_low, attention_low[0])
        + project_back(grad_sk_low, attention_low[1])
        + project_back(grad_sv_low, attention_low[2])
    )
    attention_grads = jnp.stack(
        [
            weight_grad(decoder_input, grad_sq_low),
            weight_grad(decoder_input, grad_sk_low),
            weight_grad(decoder_input, grad_sv_low),
            weight_grad(self_mixed, grad_self_low),
            weight_grad(first_low, grad_cq_low),
            weight_grad(encoder_memory, grad_ck_low),
            weight_grad(encoder_memory, grad_cv_low),
            weight_grad(cross_mixed, grad_cross_low),
        ]
    )
    vector_grads = jnp.concatenate(
        [
            jnp.stack(
                [
                    row_total(grad_sq),
                    row_total(grad_sv),
                    row_total(grad_first_in),
                    row_total(grad_cq),
                    row_total(grad_cv),
                    row_total(grad_second_in),
                ]
            ),
            row_total(grad_inner).reshape(ffn_width // model_width, model_width),
            jnp.stack(
                [
                    row_total(grad_third),
                    gain_one,
                    shift_one,
                    gain_two,
                    shift_two,
                    gain_three,
                    shift_three,
                ]
            ),
        ]
    )
    attention_sum, expand_sum, contract_sum, vector_sum = (
        lax.psum_scatter(attention_grads, ("dp", "index"), scatter_dimension=1, tiled=True),
        lax.psum_scatter(grad_expand, ("dp", "index"), scatter_dimension=0, tiled=True),
        lax.psum_scatter(grad_contract, ("dp", "index"), scatter_dimension=0, tiled=True),
        lax.psum_scatter(vector_grads, ("dp", "index"), scatter_dimension=1, tiled=True),
    )
    new_attention = adam_update(
        attention_weight,
        attention_mean,
        attention_square,
        attention_sum,
        rate_attention,
        decay_matrix,
    )
    new_expand = adam_update(
        expand_weight, expand_mean, expand_square, expand_sum, rate_expand, decay_matrix
    )
    new_contract = adam_update(
        contract_weight, contract_mean, contract_square, contract_sum, rate_contract, decay_matrix
    )
    new_vector = adam_update(
        vector_params, vector_mean, vector_square, vector_sum, rate_vector, 0.0
    )
    return (
        layer_output.astype(jnp.bfloat16),
        input_gradient,
        memory_gradient,
        question_gradient,
        new_attention[0],
        new_attention[1],
        new_attention[2],
        new_expand[0],
        new_expand[1],
        new_expand[2],
        new_contract[0],
        new_contract[1],
        new_contract[2],
        new_vector[0],
        new_vector[1],
        new_vector[2],
    )


NT = (((1,), (1,)), ((), ()))
NN = (((1,), (0,)), ((), ()))
TN = (((0,), (0,)), ((), ()))
CHIPS = 4
DP_ORDER = (0, 2, 1, 3)
VMEM_LIMIT = 56 << 20


def dot(left_side, right_side, dims):
    return lax.dot_general(left_side, right_side, dims, preferred_element_type=jnp.float32)


def norm_parts(hidden):
    center = hidden - jnp.mean(hidden, axis=-1, keepdims=True)
    inverse = lax.rsqrt(jnp.mean(center * center, axis=-1, keepdims=True) + norm_eps)
    return center * inverse, inverse


def norm_back(gradient, unit, inverse, gain):
    scaled = gradient * gain
    return inverse * (
        scaled
        - jnp.mean(scaled, axis=-1, keepdims=True)
        - unit * jnp.mean(scaled * unit, axis=-1, keepdims=True)
    )


def column_sum(values):
    return jnp.sum(values, axis=0, keepdims=True)


def join(parts, place=None):
    picked = [parts[j] if place is None else parts[j, place] for j in range(parts.shape[0])]
    return jnp.concatenate(
        [block.reshape(block.shape[0] * block.shape[1], block.shape[2]) for block in picked],
        axis=1,
    )


def spread(out_ref, value):
    count, seqs, rows, width = out_ref.shape
    for j in range(count):
        out_ref[j] = value[:, j * width : (j + 1) * width].reshape(seqs, rows, width)


def times(activation, weight):
    count, groups, rows, width = weight.shape
    depth = count * rows
    total = None
    for d in range(groups):
        part = dot(
            activation[:, d * depth : (d + 1) * depth], weight[:, d].reshape(depth, width), NN
        )
        total = part if total is None else total + part
    return total


def times_back(gradient, weight):
    count, groups, rows, width = weight.shape
    depth = count * rows
    return jnp.concatenate(
        [dot(gradient, weight[:, d].reshape(depth, width), NT) for d in range(groups)], axis=1
    )


def outer(out_ref, left_side, gradient):
    count, groups, rows, width = out_ref.shape
    depth = count * rows
    for d in range(groups):
        out_ref[:, d] = (
            dot(left_side[:, d * depth : (d + 1) * depth], gradient, TN)
            .astype(jnp.bfloat16)
            .reshape(count, rows, width)
        )


def whole(array):
    return pl.BlockSpec(array.shape, lambda *_, rank=len(array.shape): (0,) * rank)


def shape(dims, dtype):
    return jax.ShapeDtypeStruct(tuple(dims), dtype)


def params():
    return pltpu.CompilerParams(vmem_limit_bytes=VMEM_LIMIT)


def cost(flops, moved):
    return pl.CostEstimate(flops=int(flops) // 16, bytes_accessed=int(moved) // 16, transcendentals=0)


def in_head(dims, head_width, head):
    return lax.broadcasted_iota(jnp.int32, dims, 1) // head_width == head


def attend_forward_kernel(causal, head_width, q_ref, k_ref, v_ref, bias_ref, out_ref, stat_ref):
    count, _, tile, width = q_ref.shape
    keys = k_ref.shape[0] * k_ref.shape[2]
    key_rows, values = k_ref[...].reshape(keys, width), v_ref[...].reshape(keys, width)
    step = 2
    rows = step * tile
    for b in range(count // step):
        queries = q_ref[b * step : (b + 1) * step].reshape(rows, width)
        seen = (b + 1) * rows if causal else keys
        mixed = None
        for h in range(width // head_width):
            mask = in_head((rows, width), head_width, h)
            scores = dot(
                jnp.where(mask, queries * 0.125, 0).astype(jnp.bfloat16), key_rows[:seen], NT
            )
            if causal:
                corner = scores[:, seen - rows :]
                corner = jnp.where(
                    lax.broadcasted_iota(jnp.int32, corner.shape, 1)
                    <= lax.broadcasted_iota(jnp.int32, corner.shape, 0),
                    corner,
                    negative_fill,
                )
                if b == 0:
                    scores = corner
                else:
                    scores = jnp.concatenate([scores[:, : seen - rows], corner], axis=1)
            else:
                scores = scores + bias_ref[0]
            peak = jnp.max(scores, axis=1, keepdims=True)
            exponent = jnp.exp(scores - peak)
            total = jnp.sum(exponent, axis=1, keepdims=True)
            prob = (exponent * (1.0 / total)).astype(jnp.bfloat16)
            part = dot(prob, values[:seen], NN)
            mixed = part if mixed is None else jnp.where(mask, part, mixed)
            log_total = jnp.broadcast_to(peak + jnp.log(total), (rows, 128))
            stat_ref[0, h : h + 1, b * rows : (b + 1) * rows] = log_total.T[0:1]
        out_ref[b * step : (b + 1) * step] = mixed.astype(jnp.bfloat16).reshape(
            step, 1, tile, width
        )


def attend_backward_kernel(
    causal,
    head_width,
    q_ref,
    k_ref,
    v_ref,
    grad_ref,
    stat_ref,
    bias_ref,
    _,
    dq_ref,
    dkv_ref,
    prior_ref,
    dk_sum,
    dv_sum,
    prior_sum,
):
    count, _, tile, width = q_ref.shape
    keys = k_ref.shape[0] * k_ref.shape[2]
    key_rows, values = k_ref[...].reshape(keys, width), v_ref[...].reshape(keys, width)
    step = 2
    rows = step * tile
    if not causal:
        bias = jnp.broadcast_to(bias_ref[0], (128, keys)).T[:, :1]
    dk_sum[...] = jnp.zeros_like(dk_sum)
    dv_sum[...] = jnp.zeros_like(dv_sum)
    if not causal:
        prior_sum[...] = jnp.zeros_like(prior_sum)
    for b in range(count // step):
        queries = q_ref[b * step : (b + 1) * step].reshape(rows, width)
        gradient = grad_ref[b * step : (b + 1) * step].reshape(rows, width)
        seen = (b + 1) * rows if causal else keys
        query_grad = None
        for h in range(width // head_width):
            mask = in_head((rows, width), head_width, h)
            one_query = jnp.where(mask, queries * 0.125, 0).astype(jnp.bfloat16)
            one_grad = jnp.where(mask, gradient, 0).astype(jnp.bfloat16)
            scores = dot(key_rows[:seen], one_query, NT)
            if causal:
                corner = scores[seen - rows :]
                corner = jnp.where(
                    lax.broadcasted_iota(jnp.int32, corner.shape, 0)
                    <= lax.broadcasted_iota(jnp.int32, corner.shape, 1),
                    corner,
                    negative_fill,
                )
                if b == 0:
                    scores = corner
                else:
                    scores = jnp.concatenate([scores[: seen - rows], corner], axis=0)
            else:
                scores = scores + bias
            prob = jnp.exp(scores - stat_ref[0, h : h + 1, b * rows : (b + 1) * rows])
            grad_prob = dot(values[:seen], one_grad, NT)
            inner = jnp.sum(prob * grad_prob, axis=0, keepdims=True)
            grad_score = prob * (grad_prob - inner)
            score_low = grad_score.astype(jnp.bfloat16)
            dv_sum[:seen] += dot(prob.astype(jnp.bfloat16), one_grad, NN)
            dk_sum[:seen] += dot(score_low, one_query, NN)
            if not causal:
                partial_sum = grad_score[:, :128]
                for piece in range(128, rows, 128):
                    partial_sum = partial_sum + grad_score[:, piece : piece + 128]
                prior_sum[...] += partial_sum
            part = dot(score_low, key_rows[:seen], TN)
            query_grad = part if query_grad is None else jnp.where(mask, part, query_grad)
        dq_ref[b * step : (b + 1) * step] = (
            (query_grad * 0.125).astype(jnp.bfloat16).reshape(step, 1, tile, width)
        )
    dkv_ref[:, 0] = dk_sum[...].astype(jnp.bfloat16).reshape(k_ref.shape)
    dkv_ref[:, 1] = dv_sum[...].astype(jnp.bfloat16).reshape(k_ref.shape)
    if causal:
        prior_ref[...] = jnp.zeros_like(prior_ref)
    else:
        prior_ref[0] = column_sum(prior_sum[...].T)


def pick(array, place):
    count, _, _, rows, width = array.shape
    return pl.BlockSpec((count, None, 1, rows, width), lambda s: (0, place, s, 0, 0))


def attend(causal, queries, query_at, keys, key_at, value_at, bias):
    count, _, seqs, tile, width = queries.shape
    key_rows = keys.shape[0] * keys.shape[3]
    head_width = width * count // HEADS
    length = count * tile
    heads = width // head_width
    return pl.pallas_call(
        partial(attend_forward_kernel, causal, head_width),
        grid=(seqs,),
        in_specs=[
            pick(queries, query_at),
            pick(keys, key_at),
            pick(keys, value_at),
            pl.BlockSpec(memory_space=pl.ANY)
            if causal
            else pl.BlockSpec((1, 1, key_rows), lambda s: (s, 0, 0)),
        ],
        out_specs=[
            pl.BlockSpec((count, 1, tile, width), lambda s: (0, s, 0, 0)),
            pl.BlockSpec((1, heads, length), lambda s: (s, 0, 0)),
        ],
        out_shape=[
            shape((count, seqs, tile, width), jnp.bfloat16),
            shape((seqs, heads, length), jnp.float32),
        ],
        compiler_params=params(),
        cost_estimate=cost(
            16 * seqs * length * key_rows * width, 4 * seqs * (length + key_rows) * width
        ),
        name="attend_self" if causal else "attend_memory",
    )(queries, keys, keys, bias)


def attend_back(
    causal, queries, query_at, keys, key_at, value_at, gradient, stat, bias, after
):
    count, _, seqs, tile, width = queries.shape
    key_tile = keys.shape[3]
    key_rows = count * key_tile
    head_width = width * count // HEADS
    length = count * tile
    heads = width // head_width
    return pl.pallas_call(
        partial(attend_backward_kernel, causal, head_width),
        grid=(seqs,),
        in_specs=[
            pick(queries, query_at),
            pick(keys, key_at),
            pick(keys, value_at),
            pl.BlockSpec((count, 1, tile, width), lambda s: (0, s, 0, 0)),
            pl.BlockSpec((1, heads, length), lambda s: (s, 0, 0)),
            pl.BlockSpec(memory_space=pl.ANY)
            if causal
            else pl.BlockSpec((1, 1, key_rows), lambda s: (s, 0, 0)),
            pl.BlockSpec(memory_space=pl.ANY),
        ],
        out_specs=[
            pl.BlockSpec((count, 1, tile, width), lambda s: (0, s, 0, 0)),
            pl.BlockSpec((count, 2, 1, key_tile, width), lambda s: (0, 0, s, 0, 0)),
            pl.BlockSpec((1, 1, key_rows), lambda s: (s, 0, 0)),
        ],
        out_shape=[
            shape((count, seqs, tile, width), jnp.bfloat16),
            shape((count, 2, seqs, key_tile, width), jnp.bfloat16),
            shape((seqs, 1, key_rows), jnp.float32),
        ],
        scratch_shapes=[
            pltpu.VMEM((key_rows, width), jnp.float32),
            pltpu.VMEM((key_rows, width), jnp.float32),
            pltpu.VMEM((key_rows, 128), jnp.float32),
        ],
        compiler_params=params(),
        cost_estimate=cost(
            40 * seqs * length * key_rows * width, 8 * seqs * (length + key_rows) * width
        ),
        name="attend_self_back" if causal else "attend_memory_back",
    )(queries, keys, keys, gradient, stat, bias, after)


def take_columns(scratch, slices, first):
    width = slices.shape[3]
    depth = scratch.shape[0]
    rows = depth // (slices.shape[0] * slices.shape[1])
    for m in range(scratch.shape[1] // width):
        start = (first + m) * rows
        scratch[:, m * width : (m + 1) * width] = slices[:, :, start : start + rows].reshape(
            depth, width
        )


def columns_kernel(first, row_ref, slice_ref, bias_ref, out_ref, weight):
    @pl.when(pl.program_id(0) == 0)
    def _():
        take_columns(weight, slice_ref, first)

    _, many, seqs, rows, width = out_ref.shape
    taken = row_ref[0, :, :rows].reshape(seqs * rows, weight.shape[0])
    result = dot(taken, weight[...], NN) + bias_ref[...]
    for m in range(many):
        out_ref[0, m] = (
            result[:, m * width : (m + 1) * width]
            .astype(jnp.bfloat16)
            .reshape(seqs, rows, width)
        )


def project_columns(name, gathered_rows, block_rows, row_block, rows, slices, first, many, bias):
    count, seqs, _, depth = gathered_rows.shape
    width = slices.shape[3]
    return pl.pallas_call(
        partial(columns_kernel, first),
        grid=(count,),
        in_specs=[
            pl.BlockSpec((1, seqs, block_rows, depth), lambda i: (i, 0, row_block, 0)),
            whole(slices),
            whole(bias),
        ],
        out_specs=pl.BlockSpec((1, many, seqs, rows, width), lambda i: (i, 0, 0, 0, 0)),
        out_shape=shape((count, many, seqs, rows, width), jnp.bfloat16),
        scratch_shapes=[pltpu.VMEM((depth, many * width), jnp.bfloat16)],
        compiler_params=params(),
        cost_estimate=cost(
            2 * many * count * seqs * rows * depth * width, 2 * count * seqs * rows * depth
        ),
        name=name,
    )(gathered_rows, slices, bias)


def columns_back_kernel(
    first, _, row_ref, *refs
):
    grad_refs, (slice_ref, mine_out, other_out, dw_ref, bias_ref, weight, total) = (
        refs[:-7],
        refs[-7:],
    )
    turn, step = pl.program_id(0), pl.program_id(1)

    @pl.when((turn == 0) & (step == 0))
    def _():
        take_columns(weight, slice_ref, first)
        total[...] = jnp.zeros_like(total)
        bias_ref[...] = jnp.zeros_like(bias_ref)

    depth = weight.shape[0]
    pieces = []
    for grad_ref in grad_refs:
        seqs, rows, width = grad_ref.shape[-3:]
        for m in range(grad_ref.shape[1] if len(grad_ref.shape) == 5 else 1):
            piece = grad_ref[0, m] if len(grad_ref.shape) == 5 else grad_ref[0]
            pieces.append(piece.reshape(seqs * rows, width))
    gradient = jnp.concatenate(pieces, axis=1)
    taken = row_ref[0, :, :rows].reshape(seqs * rows, depth)
    bias_ref[...] += column_sum(gradient.astype(jnp.float32))
    total[...] += dot(taken, gradient, TN)
    row_grad = dot(gradient, weight[...], NT).astype(jnp.bfloat16)

    @pl.when(turn == 0)
    def _():
        mine_out[0, 0] = row_grad

    @pl.when(turn == 1)
    def _():
        other_out[0, 0] = row_grad

    @pl.when((turn == 1) & (step == pl.num_programs(1) - 1))
    def _():
        groups, count, all_rows, _ = dw_ref.shape
        part = depth // (groups * count)
        for m in range(all_rows // part):
            dw_ref[:, :, m * part : (m + 1) * part] = (
                total[:, m * width : (m + 1) * width]
                .astype(jnp.bfloat16)
                .reshape(groups, count, part, width)
            )


def project_columns_back(
    name, order, gathered_rows, block_rows, row_block, rows, gradients, slices, first, many
):
    count, seqs, _, depth = gathered_rows.shape
    half = count // 2
    groups, _, _, width = slices.shape
    part = depth // (groups * count)

    def one_device(array):
        rest = (0,) * (len(array.shape) - 1)
        return pl.BlockSpec(
            (1,) + array.shape[1:], lambda p, k, order: (order[p * half + k],) + rest
        )

    dw_shape = shape((groups, count, many * part, width), jnp.bfloat16)
    return pl.pallas_call(
        partial(columns_back_kernel, first),
        grid_spec=pltpu.PrefetchScalarGridSpec(
            num_scalar_prefetch=1,
            grid=(2, half),
            in_specs=[
                pl.BlockSpec(
                    (1, seqs, block_rows, depth),
                    lambda p, k, order: (order[p * half + k], 0, row_block, 0),
                ),
                *[one_device(array) for array in gradients],
                whole(slices),
            ],
            out_specs=[
                pl.BlockSpec(
                    (1, 1, seqs * rows, depth),
                    lambda p, k, _: (jnp.where(p == 0, k, half - 1), 0, 0, 0),
                ),
                pl.BlockSpec(
                    (1, 1, seqs * rows, depth), lambda p, k, _: (jnp.where(p == 0, 0, k), 0, 0, 0)
                ),
                whole(dw_shape),
                pl.BlockSpec((1, many * width), lambda *_: (0, 0)),
            ],
            scratch_shapes=[
                pltpu.VMEM((depth, many * width), jnp.bfloat16),
                pltpu.VMEM((depth, many * width), jnp.float32),
            ],
        ),
        out_shape=[
            shape((half, 1, seqs * rows, depth), jnp.bfloat16),
            shape((half, 1, seqs * rows, depth), jnp.bfloat16),
            dw_shape,
            shape((1, many * width), jnp.float32),
        ],
        compiler_params=params(),
        cost_estimate=cost(
            4 * many * count * seqs * rows * depth * width, 4 * count * seqs * rows * depth
        ),
        name=name,
    )(order, gathered_rows, *gradients, slices)


def gathered(weights, width, place):
    count, groups, rows, _ = weights.shape
    return pl.BlockSpec((count, groups, rows, width), lambda *_: (0, 0, 0, place))


def first_kernel(
    mixed_ref, x_ref, out_w, query_w, vector_ref, _, mixed_out, in_out, low_out, query_out
):
    mixed = join(mixed_ref)
    mixed_out[...] = mixed
    first_in = x_ref[...].astype(jnp.float32) + times(mixed, out_w) + vector_ref[2:3]
    in_out[...] = first_in
    unit, _ = norm_parts(first_in)
    low = (unit * vector_ref[11:12] + vector_ref[12:13]).astype(jnp.bfloat16)
    low_out[...] = low
    spread(query_out, (times(low, query_w) + vector_ref[3:4]).astype(jnp.bfloat16))


def first_forward(mixed, x_rows, weights, vectors, after):
    rows, depth = x_rows.shape
    return pl.pallas_call(
        first_kernel,
        grid=(1,),
        in_specs=[
            whole(mixed),
            whole(x_rows),
            gathered(weights, depth, 0),
            gathered(weights, depth, 1),
            whole(vectors),
            pl.BlockSpec(memory_space=pl.ANY),
        ],
        out_specs=[whole(x_rows), whole(x_rows), whole(x_rows), whole(mixed)],
        out_shape=[
            shape((rows, depth), jnp.bfloat16),
            shape((rows, depth), jnp.float32),
            shape((rows, depth), jnp.bfloat16),
            shape(mixed.shape, jnp.bfloat16),
        ],
        compiler_params=params(),
        cost_estimate=cost(4 * rows * depth * depth, 4 * depth * depth),
        name="first_forward",
    )(mixed, x_rows, weights, weights, vectors, after)


def ffn_kernel(
    order,
    places,
    mixed_ref,
    first_ref,
    out_w,
    vector_ref,
    bias_ref,
    grad_ref,
    wide_ref,
    *refs,
):
    contract_refs, refs = refs[:8], refs[8:]
    mixed_out, layer_out, wide_grad = refs[:3]
    contract_grads, refs = refs[3:11], refs[11:]
    dbias_ref, second_grad, cross_low, mixed_grad, stat_out, columns, contracts = refs[:7]
    active, slope, low, third_low, second_in, total, wide_sem, contract_sem = refs[7:]
    blocks, count, groups, rows, block = columns.shape
    part = block // CHIPS
    depth = vector_ref.shape[1]

    def wide_copies(t, array, outward):
        result = []
        for k in range(CHIPS):
            column = pl.multiple_of(order[t % 2 * CHIPS + k] * part, part)
            row = pl.multiple_of(places[t // 2] * rows, rows)
            there = array.at[:, :, pl.ds(row, rows), pl.ds(column, part)]
            here = columns.at[t, :, :, :, pl.ds(k * part, part)]
            ends = (here, there) if outward else (there, here)
            result.append(pltpu.make_async_copy(*ends, wide_sem.at[t, k]))
        return result

    def contract_copies(t, pieces, outward):
        near, far = divmod(DP_ORDER[t // 2], 2)
        first = pieces[t % 2 * 4 + far].at[near]
        last = pieces[t % 2 * 4 + 2 + near].at[far]
        result = []
        for half, there in enumerate((first, last)):
            here = contracts.at[t, pl.ds(half * CHIPS // 2, CHIPS // 2)]
            ends = (here, there) if outward else (there, here)
            result.append(pltpu.make_async_copy(*ends, contract_sem.at[t, half]))
        return result

    for t in range(blocks):
        for copy in wide_copies(t, wide_ref, False):
            copy.start()
        for copy in contract_copies(t, contract_refs, False):
            copy.start()

    mixed = join(mixed_ref)
    mixed_out[...] = mixed
    unit, _ = norm_parts(first_ref[...])
    second_in[...] = (
        unit * vector_ref[11:12] + vector_ref[12:13] + times(mixed, out_w) + vector_ref[5:6]
    )
    unit, _ = norm_parts(second_in[...])
    second = unit * vector_ref[13:14] + vector_ref[14:15]
    low[...] = second.astype(jnp.bfloat16)
    total[...] = second + vector_ref[10:11]

    def shard(t, k):
        return places[t // 2] * count + order[t % 2 * CHIPS + k]

    for t in range(blocks):
        for copy in wide_copies(t, wide_ref, False):
            copy.wait()
        bias = jnp.concatenate([bias_ref[pl.ds(shard(t, k), 1)] for k in range(CHIPS)], axis=1)
        inner = times(low[...], columns.at[t]) + bias
        phi = 0.5 + 0.5 * lax.erf(inner * (0.5**0.5))
        out = (inner * phi).astype(jnp.bfloat16)
        active[t] = out
        slope[t] = phi + inner * jnp.exp(-0.5 * inner * inner) * 0.3989422804014327
        for copy in contract_copies(t, contract_refs, False):
            copy.wait()
        total[...] += dot(out, contracts[t].reshape(block, depth), NN)

    unit, inverse = norm_parts(total[...])
    gain = vector_ref[15:16]
    layer_out[...] = (unit * gain + vector_ref[16:17]).astype(jnp.bfloat16)
    gradient = grad_ref[...].astype(jnp.float32)
    grad_third = norm_back(gradient, unit, inverse, gain)
    stat_out[...] = jnp.zeros_like(stat_out)
    stat_out[0:1] = column_sum(grad_third)
    stat_out[1:2] = column_sum(gradient * unit)
    stat_out[2:3] = column_sum(gradient)
    total[...] = grad_third
    third_low[...] = grad_third.astype(jnp.bfloat16)
    turned = low[...].T

    for t in range(blocks):
        grad_inner = dot(third_low[...], contracts[t].reshape(block, depth), NT) * slope[t]
        inner_low = grad_inner.astype(jnp.bfloat16)
        sums = column_sum(grad_inner)
        for k in range(CHIPS):
            dbias_ref[pl.ds(shard(t, k), 1)] = sums[:, k * part : (k + 1) * part]
        contracts[t] = (
            dot(active[t], third_low[...], TN).astype(jnp.bfloat16).reshape(CHIPS, part, depth)
        )
        for copy in contract_copies(t, contract_grads, True):
            copy.start()
        total[...] += times_back(inner_low, columns.at[t])
        result = dot(turned, inner_low, NN).astype(jnp.bfloat16)
        for d in range(groups):
            columns[t, :, d] = result[d * count * rows : (d + 1) * count * rows].reshape(
                count, rows, block
            )
        for copy in wide_copies(t, wide_grad, True):
            copy.start()

    unit, inverse = norm_parts(second_in[...])
    grad_second = total[...]
    grad_in = norm_back(grad_second, unit, inverse, vector_ref[13:14])
    second_grad[...] = grad_in
    grad_low = grad_in.astype(jnp.bfloat16)
    cross_low[...] = grad_low
    spread(mixed_grad, times_back(grad_low, out_w).astype(jnp.bfloat16))
    stat_out[8:9] = column_sum(grad_in)
    stat_out[9:10] = column_sum(grad_second * unit)
    stat_out[10:11] = column_sum(grad_second)
    for t in range(blocks):
        for copy in contract_copies(t, contract_grads, True) + wide_copies(t, wide_grad, True):
            copy.wait()


def ffn(orders, mixed, first_in, wide, contract, vectors, bias, output_grad):
    rows, depth = first_in.shape
    hidden = bias.size
    block = depth // 2
    count, groups, all_rows, _ = wide.shape
    part = depth // (count * groups)
    blocks = hidden // block
    full = whole(first_in)
    anywhere = pl.BlockSpec(memory_space=pl.ANY)
    heads_out = shape(mixed.shape, jnp.bfloat16)
    stats = shape((16, depth), jnp.float32)
    return pl.pallas_call(
        ffn_kernel,
        grid_spec=pltpu.PrefetchScalarGridSpec(
            num_scalar_prefetch=2,
            grid=(1,),
            in_specs=[
                whole(mixed),
                full,
                pl.BlockSpec((count, groups, part, depth), lambda *_: (0, 0, groups, 0)),
                whole(vectors),
                whole(bias),
                full,
                *[anywhere] * 9,
            ],
            out_specs=[
                full,
                full,
                *[anywhere] * 9,
                whole(bias),
                full,
                full,
                whole(heads_out),
                whole(stats),
            ],
            scratch_shapes=[
                pltpu.VMEM((blocks, count, groups, part, block), jnp.bfloat16),
                pltpu.VMEM((blocks, CHIPS) + contract[0].shape[2:], jnp.bfloat16),
                pltpu.VMEM((blocks, rows, block), jnp.bfloat16),
                pltpu.VMEM((blocks, rows, block), jnp.float32),
                pltpu.VMEM((rows, depth), jnp.bfloat16),
                pltpu.VMEM((rows, depth), jnp.bfloat16),
                pltpu.VMEM((rows, depth), jnp.float32),
                pltpu.VMEM((rows, depth), jnp.float32),
                pltpu.SemaphoreType.DMA((blocks, CHIPS)),
                pltpu.SemaphoreType.DMA((blocks, 2)),
            ],
        ),
        out_shape=[
            shape((rows, depth), jnp.bfloat16),
            shape((rows, depth), jnp.bfloat16),
            shape((count, groups, all_rows - part, depth), jnp.bfloat16),
            *[shape(piece.shape, jnp.bfloat16) for piece in contract],
            shape(bias.shape, jnp.float32),
            shape((rows, depth), jnp.float32),
            shape((rows, depth), jnp.bfloat16),
            heads_out,
            stats,
        ],
        compiler_params=params(),
        cost_estimate=cost(12 * rows * depth * hidden, 16 * depth * hidden),
        name="ffn",
    )(*orders, mixed, first_in, wide, vectors, bias, output_grad, wide, *contract)


def first_back_kernel(
    dq_ref,
    second_grad,
    first_ref,
    out_w,
    query_w,
    vector_ref,
    _,
    query_low,
    grad_in_out,
    self_low,
    mixed_grad,
    stat_out,
):
    query_grad = join(dq_ref)
    query_low[...] = query_grad
    grad_first = second_grad[...] + times_back(query_grad, query_w)
    unit, inverse = norm_parts(first_ref[...])
    grad_in = norm_back(grad_first, unit, inverse, vector_ref[11:12])
    grad_in_out[...] = grad_in
    grad_low = grad_in.astype(jnp.bfloat16)
    self_low[...] = grad_low
    spread(mixed_grad, times_back(grad_low, out_w).astype(jnp.bfloat16))
    stat_out[...] = jnp.zeros_like(stat_out)
    stat_out[0:1] = column_sum(query_grad.astype(jnp.float32))
    stat_out[1:2] = column_sum(grad_in)
    stat_out[2:3] = column_sum(grad_first * unit)
    stat_out[3:4] = column_sum(grad_first)


def first_back(dq, second_grad, first_in, weights, vectors, after):
    rows, depth = first_in.shape
    full = whole(first_in)
    return pl.pallas_call(
        first_back_kernel,
        grid=(1,),
        in_specs=[
            whole(dq),
            full,
            full,
            gathered(weights, depth, 0),
            gathered(weights, depth, 1),
            whole(vectors),
            pl.BlockSpec(memory_space=pl.ANY),
        ],
        out_specs=[full, full, full, whole(dq), pl.BlockSpec((8, depth), lambda *_: (0, 0))],
        out_shape=[
            shape((rows, depth), jnp.bfloat16),
            shape((rows, depth), jnp.float32),
            shape((rows, depth), jnp.bfloat16),
            shape(dq.shape, jnp.bfloat16),
            shape((8, depth), jnp.float32),
        ],
        compiler_params=params(),
        cost_estimate=cost(4 * rows * depth * depth, 4 * depth * depth),
        name="first_back",
    )(dq, second_grad, first_in, weights, weights, vectors, after)


def weight_grads_kernel(
    order,
    mixed,
    self_low,
    first_low,
    query_low,
    cross,
    cross_low,
    mine_out,
    other_out,
    result,
):
    step = pl.program_id(0)
    pairs = ((mixed, self_low), (first_low, query_low), (cross, cross_low))
    half, groups, part, _ = mine_out.shape
    for m, (left_side, gradient) in enumerate(pairs):

        @pl.when(step == m)
        def _(left_side=left_side, gradient=gradient):
            result[...] = dot(left_side[...], gradient[...], TN).astype(jnp.bfloat16)

    for d in range(groups):
        for k in range(half):
            for p, out_ref in enumerate((mine_out, other_out)):
                row = pl.multiple_of((2 * half * d + order[p * half + k]) * part, part)
                out_ref[k, d] = result[pl.ds(row, part)]


def weight_grads(dims, order, mixed, self_low, first_low, query_low, cross, cross_low):
    count, groups, part, depth = dims
    half = pl.BlockSpec((count // 2, groups, part, depth), lambda m, _: (0, 0, m, 0))
    return pl.pallas_call(
        weight_grads_kernel,
        grid_spec=pltpu.PrefetchScalarGridSpec(
            num_scalar_prefetch=1,
            grid=(3,),
            in_specs=[whole(mixed)] * 6,
            out_specs=[half, half],
            scratch_shapes=[pltpu.VMEM((depth, depth), jnp.bfloat16)],
        ),
        out_shape=[shape((count // 2, groups, 3 * part, depth), jnp.bfloat16)] * 2,
        compiler_params=params(),
        cost_estimate=cost(6 * mixed.shape[0] * depth * depth, 6 * depth * depth),
        name="weight_grads",
    )(order, mixed, self_low, first_low, query_low, cross, cross_low)


def send_dp(piece):
    size = lax.axis_size("dp")
    return [
        lax.ppermute(piece, "dp", [(i, (i + shift) % size) for i in range(size)])
        for shift in range(1, size)
    ]


def place_dp(piece, arrived):
    size, me = lax.axis_size("dp"), lax.axis_index("dp")
    result = jnp.zeros((size,) + piece.shape, piece.dtype)
    result = lax.dynamic_update_index_in_dim(result, piece, me, 0)
    for shift, got in enumerate(arrived, 1):
        result = lax.dynamic_update_index_in_dim(result, got, lax.rem(me - shift + size, size), 0)
    return result


def to_chips(block):
    return [exchange(block, 2 * k) for k in range(1, CHIPS)]


def gather_index(mine):
    size, me = lax.axis_size("index"), lax.axis_index("index")
    block = mine[0]
    other = exchange(jnp.stack(mine), 1)
    result = jnp.zeros((size,) + block.shape, block.dtype)
    for k in range(CHIPS):
        result = lax.dynamic_update_index_in_dim(result, mine[k], me ^ (2 * k), 0)
        result = lax.dynamic_update_index_in_dim(result, other[k], me ^ (2 * k) ^ 1, 0)
    return result


class HalvingDp:
    def __init__(self, pieces):
        me = lax.axis_index("dp")
        self.parts = [
            lax.dynamic_index_in_dim(pieces, me ^ flip, 0, keepdims=False) for flip in DP_ORDER
        ]

    def first(self):
        return jnp.stack(self.parts[2:]).astype(jnp.bfloat16)

    def second(self, got):
        self.got = got
        return (
            self.parts[1].astype(jnp.float32) + self.got[1].astype(jnp.float32)
        ).astype(jnp.bfloat16)

    def finish(self, last):
        return sum(one.astype(jnp.float32) for one in (self.parts[0], self.got[0], last))


def relative_order():
    size, me = lax.axis_size("index"), lax.axis_index("index")
    steps = jnp.arange(size // 2, dtype=jnp.int32) * 2
    return jnp.concatenate([me ^ steps, me ^ 1 ^ steps])


def exchange(piece, flip):
    size = lax.axis_size("index")
    return lax.ppermute(piece, "index", [(i, i ^ flip) for i in range(size)])


def exchange_dp(piece, flip):
    size = lax.axis_size("dp")
    return lax.ppermute(piece, "dp", [(i, i ^ flip) for i in range(size)])


def add_kernel(*refs):
    total = sum(ref[...].astype(jnp.float32) for ref in refs[:-1])
    refs[-1][...] = total.astype(jnp.bfloat16)


def add(*terms):
    flat, specs = [], []
    first = terms[0]
    dims = first[0].shape[1:] if isinstance(first, tuple) else first.shape
    rows = 1
    for size in dims[:-1]:
        rows *= size
    block = min(rows, 256)
    for term in terms:
        array, entry = term if isinstance(term, tuple) else (term, 0)
        flat.append(array.reshape(-1, dims[-1]))
        start = entry * rows // block
        specs.append(pl.BlockSpec((block, dims[-1]), lambda i, start=start: (start + i, 0)))
    return pl.pallas_call(
        add_kernel,
        grid=(rows // block,),
        in_specs=specs,
        out_specs=pl.BlockSpec((block, dims[-1]), lambda i: (i, 0)),
        out_shape=shape((rows, dims[-1]), jnp.bfloat16),
        compiler_params=params(),
        cost_estimate=cost(0, 0),
        name="add",
    )(*flat).reshape(dims)


def combine_kernel(plan, *refs):
    ins, outs = list(refs[: -len(plan)]), refs[-len(plan) :]
    for out_ref, entries in zip(outs, plan):
        for e, segments in enumerate(entries):
            start = 0
            for count, rows in segments:
                terms, ins = ins[:count], ins[count:]
                total = sum(ref[0].astype(jnp.float32) for ref in terms)
                out_ref[e, start : start + rows] = total.astype(jnp.bfloat16)
                start += rows


def combine(*outputs):
    arrays, specs, plan, shapes = [], [], [], []
    for entries in outputs:
        plan.append([])
        for segments in entries:
            plan[-1].append([])
            for terms in segments:
                plan[-1][-1].append((len(terms), terms[0][2]))
                for array, e, rows, place in terms:
                    arrays.append(array)
                    specs.append(
                        pl.BlockSpec(
                            (1, rows, array.shape[2]), lambda i, e=e, place=place: (e, place, 0)
                        )
                    )
        rows = sum(rows for _, rows in plan[-1][0])
        shapes.append(shape((len(entries), rows, arrays[0].shape[2]), jnp.bfloat16))
    return pl.pallas_call(
        partial(combine_kernel, plan),
        grid=(1,),
        in_specs=specs,
        out_specs=[whole(out) for out in shapes],
        out_shape=shapes,
        compiler_params=params(),
        cost_estimate=cost(0, 0),
        name="combine",
    )(*arrays)


class Halving:
    def __init__(self, chips):
        self.chips = chips
        self.middle = chips[0][0][0].shape[1] // 2

    def terms(self, k, half, *more):
        middle = self.middle
        return [(array, e, middle, half) for array, e in self.chips[k]] + [
            (array, e, middle, 0) for array, e in more
        ]

    def total(self, k, half, *more):
        rows = slice(half * self.middle, (half + 1) * self.middle)
        parts = [array[e, rows] for array, e in self.chips[k]] + [*more]
        return sum(one.astype(jnp.float32) for one in parts)

    def finish(self, top, low):
        return jnp.concatenate(
            [self.total(0, 0, self.got[0][0], top), self.total(0, 1, self.got[1][0], low)], axis=0
        )


def both_cores(mine, other):
    parts = [part.reshape(CHIPS, -1, part.shape[-1]) for part in (mine, other)]
    return Halving([[(part, k) for part in parts] for k in range(CHIPS)])


def firsts(*sums):
    return combine(
        [[one.terms(k, 0) for one in sums] for k in (1, 3)],
        [[one.terms(k, 1) for one in sums] for k in (2, 3)],
    )


def seconds(*sums):
    for one, top, low in sums:
        one.got = top, low
    top, low = combine(
        [[one.terms(2, 0, (top, 1)) for one, top, _ in sums]],
        [[one.terms(1, 1, (low, 1)) for one, _, low in sums]],
    )
    return top[0], low[0]


def send_first(top, low):
    return [exchange(top, 2), exchange(low, 4)]


def send_last(top, low):
    return [exchange(top, 4), exchange(low, 2)]


def split_rows(arrays, rows):
    return [a[..., :rows, :] for a in arrays], [a[..., rows:, :] for a in arrays]


def small_send(values):
    size = lax.axis_size("index")
    flat = jnp.pad(values.reshape(-1), (0, 1024 - values.size)).reshape(1, 8, 128)
    return swap(jnp.broadcast_to(flat, (size, 8, 128)))


def small_take(arrived, dims):
    size = 1
    for dim in dims:
        size *= dim
    return jnp.sum(arrived, axis=0).reshape(-1)[:size].reshape(dims)


def hold_kernel(*_):
    pass


def hold(values, *others):
    anywhere = pl.BlockSpec(memory_space=pl.ANY)
    return pl.pallas_call(
        hold_kernel,
        in_specs=[anywhere] * (len(values) + len(others)),
        out_specs=[anywhere] * len(values),
        out_shape=[shape(value.shape, value.dtype) for value in values],
        input_output_aliases={i: i for i in range(len(values))},
        name="hold",
    )(*values, *others)


def swap(pieces):
    return lax.all_to_all(pieces, "index", 0, 0, tiled=True)


def head_body(
    decoder_input,
    encoder_memory,
    question_vectors,
    passage_vectors,
    passage_ids,
    valid_count,
    output_grad,
    attention_weight,
    expand_weight,
    contract_weight,
    vector_params,
    attention_mean,
    attention_square,
    expand_mean,
    expand_square,
    contract_mean,
    contract_square,
    vector_mean,
    vector_square,
):
    low = jnp.bfloat16
    count, groups = lax.axis_size("index"), lax.axis_size("dp")
    place = lax.axis_index("index")
    seqs, rows_here, depth = decoder_input.shape
    memory_here = encoder_memory.shape[1]
    width = depth // count
    part = attention_weight.shape[1]
    hidden = expand_weight.shape[1]
    vector_rows, vector_width = vector_params.shape
    question_width = question_vectors.shape[1]
    rows = seqs * rows_here

    attention_low = attention_weight.astype(low)
    extras = jnp.concatenate(
        [vector_params.astype(low).reshape(-1), question_vectors.reshape(-1)]
    )
    extra_rows = -(-extras.shape[0] // (16 * width)) * 16
    extras = jnp.pad(extras, (0, extra_rows * width - extras.shape[0])).reshape(
        1, extra_rows, width
    )
    split = jnp.concatenate([attention_low[:3], attention_low[5:7]], axis=0)
    columns = split.reshape(5, part, count, width).transpose(2, 0, 1, 3)
    package = jnp.concatenate(
        [
            columns.reshape(count, 5 * part, width),
            jnp.broadcast_to(extras, (count, extra_rows, width)),
        ],
        axis=1,
    )
    order = relative_order()
    memory_block = -(-memory_here // rows_here) * rows_here
    rows_all = lax.all_gather(
        jnp.concatenate(
            [
                jnp.pad(encoder_memory, ((0, 0), (0, memory_block - memory_here), (0, 0))),
                decoder_input,
            ],
            axis=1,
        ),
        "index",
        axis=0,
        tiled=False,
    )
    input_rows = (rows_all, rows_here, memory_block // rows_here, rows_here)
    memory_rows = (rows_all, memory_block, 0, memory_here)
    square = attention_low[3:5].transpose(1, 0, 2).reshape(part, 2 * depth)
    received = swap(package)
    square_arrived = hold(send_dp(square), received)
    (received,) = hold([received], *square_arrived)
    received_sent = send_dp(received)
    square = place_dp(square, square_arrived)
    *slices_arrived, x, y, xy = hold([*received_sent, *to_chips(square)])
    slices = place_dp(received, slices_arrived)
    square = [square, x, y, xy]
    (contract,) = hold([contract_weight.astype(low)], x)
    contract_sent = to_chips(contract)
    vectors = (
        slices[:, :, 5 * part :]
        .reshape(groups, count, extra_rows * width)[:, :, : vector_rows * vector_width]
        .reshape(groups, count, vector_rows, vector_width)
        .transpose(2, 0, 1, 3)
        .reshape(vector_rows, depth)
        .astype(jnp.float32)
    )
    question_full = (
        received[:, 5 * part :]
        .reshape(count, extra_rows * width)[:, vector_rows * vector_width :][
            :, : seqs * question_width
        ]
        .reshape(count, seqs, question_width)
        .transpose(1, 0, 2)
        .reshape(seqs, count * question_width)
    )
    expand_part = hidden // depth * part
    late = jnp.concatenate(
        [
            expand_weight.astype(low)
            .reshape(part, hidden // depth, depth)
            .transpose(1, 0, 2)
            .reshape(expand_part, depth),
            attention_low[7],
        ],
        axis=0,
    )
    (late,) = hold([late], *slices_arrived)
    late_sent = send_dp(late)

    (passage_ids,) = hold([passage_ids], *slices_arrived)
    passages_here = passage_vectors.shape[0]
    local_ids = passage_ids - place * passages_here
    owned_slot = (local_ids >= 0) & (local_ids < passages_here)
    picked = passage_vectors[jnp.clip(local_ids, 0, passages_here - 1)]
    local_scores = jnp.einsum(
        "sc,skc->sk", question_full, picked, preferred_element_type=jnp.float32
    )
    slots = passage_ids.shape[1]
    usable = jnp.arange(slots)[None, :] < valid_count[:, None]
    scores = small_take(small_send(jnp.where(owned_slot, local_scores, 0.0)), local_scores.shape)
    masked = jnp.where(usable, scores, negative_fill)
    maximum = jnp.max(masked, axis=1)
    exponent = jnp.where(usable, jnp.exp(masked - maximum[:, None]), 0.0)
    partition = jnp.sum(exponent, axis=1)
    passage_prob = exponent / partition[:, None]
    log_prior = jnp.where(
        usable, masked - maximum[:, None] - jnp.log(partition)[:, None], negative_fill
    )
    key_bias = jnp.repeat(log_prior, MEM_P, axis=1)

    vector_here = lax.dynamic_slice_in_dim(vectors[:5], place * width, width, axis=1)
    no_bias = jnp.zeros((1, width), jnp.float32)
    qkv_bias = jnp.concatenate([vector_here[0:1], no_bias, vector_here[1:2]], axis=1)
    kv_bias = jnp.concatenate([no_bias, vector_here[4:5]], axis=1)
    x_rows = decoder_input.reshape(rows, depth)
    (slices,) = hold([slices], key_bias)
    qkv = project_columns("self_qkv", *input_rows, slices, 0, 3, qkv_bias)
    qkv, *late_arrived = hold([qkv, *late_sent])
    late = lax.all_gather(place_dp(late, late_arrived), "index", axis=0, tiled=False)
    self_out, self_stat = attend(True, qkv, 0, qkv, 1, 2, key_bias[:, None, :])
    self_out, *contract_sent = hold([self_out, *contract_sent])
    contract = [contract, *contract_sent]
    self_got = swap(self_out)
    square = gather_index(hold(square, self_out))
    ahead, across = hold([jnp.stack(contract[:2]), jnp.stack(contract[2:])], self_out)
    self_got, ahead_far, across_far, square = hold(
        [self_got, exchange_dp(ahead, 2), exchange_dp(across, 1), square]
    )
    ahead = jnp.stack([ahead, ahead_far])
    across = jnp.stack([across, across_far])
    contract_sent = [exchange_dp(ahead, 1), exchange_dp(across, 2)]
    self_mixed, first_in, first_low, cross_query = first_forward(
        self_got, x_rows, square, vectors, ahead_far
    )
    (slices,) = hold([slices], first_low)
    memory_kv = project_columns("memory_kv", *memory_rows, slices, 3, 2, kv_bias)
    cross_query = swap(cross_query)[:, None]
    cross_out, cross_stat = attend(
        False, cross_query, 0, memory_kv, 0, 1, key_bias[:, None, :]
    )
    ahead_far, across_far = hold(contract_sent, cross_out)
    contract = [ahead, ahead_far, across, across_far]
    contract += [exchange(piece, 1) for piece in contract]
    places = lax.axis_index("dp") ^ jnp.array(DP_ORDER, jnp.int32)
    (
        cross_mixed,
        layer_output,
        wide_grad,
        *contract_grads,
        inner_total,
        second_grad,
        cross_low,
        cross_mix_grad,
        stats,
    ) = ffn(
        (order, places),
        swap(cross_out),
        first_in,
        late,
        contract,
        vectors,
        vectors[6:10].reshape(groups * count, -1),
        output_grad.reshape(rows, depth),
    )
    third_stat, second_stat = stats[:8], stats[8:]

    expand_part_sum = lax.psum_scatter(wide_grad, "index", scatter_dimension=0, tiled=False)
    ahead, ahead_far, across, across_far = contract_grads[:4]
    cores = [exchange(piece, 1) for piece in contract_grads[4:]]
    cross_mix_got, *contract_sent = hold(
        [swap(cross_mix_grad), add(ahead_far, cores[1]), add(across_far, cores[3])]
    )
    contract_got = [exchange_dp(contract_sent[0], 1), exchange_dp(contract_sent[1], 2)]
    cross_dq, cross_dkv, prior_rows = attend_back(
        False,
        cross_query,
        0,
        memory_kv,
        0,
        1,
        cross_mix_got,
        cross_stat,
        key_bias[:, None, :],
        contract_sent[0],
    )
    memory_mine, memory_other, kv_grads, kv_total = project_columns_back(
        "memory_kv_back", order, *memory_rows, [cross_dkv], slices, 3, 2
    )
    cross_dq, *contract_got = hold([cross_dq, *contract_got], memory_mine)
    contract_next = [
        add((ahead, 1), (cores[0], 1), (contract_got[0], 1)),
        add((across, 1), (cores[2], 1), (contract_got[1], 1)),
    ]
    cross_dq_got, *contract_next = hold([swap(cross_dq), *contract_next])
    contract_last = [exchange_dp(contract_next[0], 2), exchange_dp(contract_next[1], 1)]
    query_low, first_grad, self_low, self_mix_grad, first_stat = first_back(
        cross_dq_got, second_grad, first_in, square, vectors, memory_mine
    )
    memory_sum = both_cores(memory_mine, exchange(memory_other, 1))
    memory_sent = firsts(memory_sum)
    square_mine, square_other = weight_grads(
        (count, groups, part, depth),
        order,
        self_mixed,
        self_low,
        first_low,
        query_low,
        cross_mixed,
        cross_low,
    )
    square_sum = both_cores(square_mine, exchange(square_other, 1))
    square_sent = firsts(square_sum)
    self_mix_got, *contract_last = hold(
        [swap(self_mix_grad), *contract_last], *memory_sent, *square_sent
    )
    memory_got = send_first(*memory_sent)
    square_got = send_first(*square_sent)
    self_dq, self_dkv, _ = attend_back(
        True, qkv, 0, qkv, 1, 2, self_mix_got, self_stat, self_stat, square_mine
    )
    expand_sum = HalvingDp(expand_part_sum)
    self_dq, expand_sent = hold([self_dq, expand_sum.first()])
    expand_got = exchange_dp(expand_sent, 1)
    dx_mine, dx_other, qkv_slice_grads, qkv_total = project_columns_back(
        "self_qkv_back", order, *input_rows, [self_dq, self_dkv], slices, 0, 3
    )
    dx_mine, dx_other, *got = hold([dx_mine, dx_other, *memory_got, *square_got])
    own = jnp.concatenate(
        [qkv_total[:, :width], qkv_total[:, 2 * width :], kv_total[:, width:]], axis=0
    )
    own = lax.dynamic_update_slice(
        jnp.zeros((3, depth), jnp.float32), own, (jnp.int32(0), place * width)
    )
    vector_grads = jnp.concatenate(
        [
            own[:2],
            first_stat[1:2],
            first_stat[0:1],
            own[2:],
            second_stat[0:1],
            inner_total.reshape(hidden // depth, depth),
            third_stat[0:1],
            first_stat[2:4],
            second_stat[1:3],
            third_stat[1:3],
        ],
        axis=0,
    )
    vector_size = vector_rows * vector_width
    question_size = seqs * question_width
    vector_send = (
        vector_grads.reshape(vector_rows, groups, count, vector_width)
        .transpose(1, 2, 0, 3)
        .reshape(groups, count, vector_size)
    )
    vector_send = jnp.pad(
        vector_send, ((0, 0), (0, 0), (0, extra_rows * width - vector_size))
    ).reshape(groups, count, extra_rows, width)
    slice_sum = HalvingDp(
        jnp.concatenate([qkv_slice_grads, kv_grads, vector_send.astype(low)], axis=2)
    )
    slice_sent = slice_sum.first()
    slice_got = exchange_dp(slice_sent, 1)
    dx_other, *got = hold([dx_other, *got], slice_sent)
    dx_got = exchange(dx_other, 1)
    square_rows = square_sum.middle
    last = seconds((square_sum, *got[2:]), (memory_sum, *got[:2]))
    prior_rows, expand_got, *contract_last = hold(
        [prior_rows, expand_got, *contract_last], *last
    )
    last = send_last(*last)
    expand_last = exchange_dp(expand_sum.second(expand_got), 2)
    prior_arrived = small_send(prior_rows.reshape(seqs, slots, MEM_P).sum(axis=-1))
    dx_got, expand_last, prior_arrived, slice_got, *last = hold(
        [dx_got, expand_last, prior_arrived, slice_got, *last]
    )
    slice_last = exchange_dp(slice_sum.second(slice_got), 2)
    dx_sum = both_cores(dx_mine, dx_got)
    contract_sum = Halving(
        [
            [(one.reshape((-1,) + one.shape[-2:]), k % 2) for one in parts]
            for k, parts in enumerate(
                [(ahead, cores[0], contract_got[0], contract_last[0])] * 2
                + [(across, cores[2], contract_got[1], contract_last[1])] * 2
            )
        ]
    )
    dx_sent = firsts(dx_sum, contract_sum)
    got = send_first(*dx_sent)
    last = hold(last, *dx_sent)
    square_last, memory_last = split_rows(last, square_rows)
    square_far = HalvingDp(square_sum.finish(*square_last).reshape(groups, 3 * part, depth))
    square_got = exchange_dp(square_far.first(), 1)
    memory_gradient = memory_sum.finish(*memory_last).reshape(encoder_memory.shape)
    square_got, slice_last, *got = hold([square_got, slice_last, *got], memory_gradient)
    dx_got, contract_got = split_rows(got, dx_sum.middle)
    last = send_last(*seconds((dx_sum, *dx_got), (contract_sum, *contract_got)))
    square_last = exchange_dp(square_far.second(square_got), 2)
    dx_last, contract_last = split_rows(last, dx_sum.middle)
    input_gradient = first_grad + dx_sum.finish(*dx_last)
    contract_sum = contract_sum.finish(*contract_last)
    slice_sum = slice_sum.finish(slice_last)

    prior_grad = jnp.where(usable, small_take(prior_arrived, (seqs, slots)), 0.0)
    score_doc = jnp.where(
        usable, prior_grad - passage_prob * jnp.sum(prior_grad, axis=1, keepdims=True), 0.0
    )
    question_part = jnp.einsum(
        "sk,skc->sc",
        jnp.where(owned_slot, score_doc, 0.0),
        picked.astype(jnp.float32),
        precision=lax.Precision.HIGHEST,
    )

    question_send = (
        question_part.reshape(seqs, count, question_width)
        .transpose(1, 0, 2)
        .reshape(count, question_size)
    )
    question_send = jnp.pad(
        question_send,
        ((0, 0), (vector_size, extra_rows * width - vector_size - question_size)),
    ).reshape(count, extra_rows, width)
    slice_sum = jnp.concatenate(
        [slice_sum[:, : 5 * part], slice_sum[:, 5 * part :] + question_send], axis=1
    )
    arrived = swap(slice_sum.astype(low)).astype(jnp.float32)
    split_grads = (
        arrived[:, : 5 * part]
        .reshape(count, 5, part, width)
        .transpose(1, 2, 0, 3)
        .reshape(5, part, depth)
    )
    extra_sum = jnp.sum(arrived[:, 5 * part :].reshape(count, extra_rows * width), axis=0)
    vector_sum = extra_sum[:vector_size].reshape(vector_rows, vector_width)
    question_gradient = extra_sum[vector_size : vector_size + question_size].reshape(
        seqs, question_width
    )

    expand_sum = (
        expand_sum.finish(expand_last)
        .reshape(hidden // depth, part, depth)
        .transpose(1, 0, 2)
        .reshape(part, hidden)
    )
    square_total = square_far.finish(square_last).reshape(3, part, depth)
    attention_sum = jnp.concatenate(
        [split_grads[:3], square_total[:2], split_grads[3:], square_total[2:]], axis=0
    )

    new_attention = adam_update(
        attention_weight,
        attention_mean,
        attention_square,
        attention_sum,
        rate_attention,
        decay_matrix,
    )
    new_expand = adam_update(
        expand_weight, expand_mean, expand_square, expand_sum, rate_expand, decay_matrix
    )
    new_contract = adam_update(
        contract_weight, contract_mean, contract_square, contract_sum, rate_contract, decay_matrix
    )
    new_vector = adam_update(
        vector_params, vector_mean, vector_square, vector_sum, rate_vector, 0.0
    )
    return (
        layer_output.reshape(decoder_input.shape),
        input_gradient.reshape(decoder_input.shape),
        memory_gradient,
        question_gradient,
        *new_attention,
        *new_expand,
        *new_contract,
        *new_vector,
    )


def body(sizes, *arrays):
    depth = arrays[0].shape[2]
    if sizes == (4, 8) and depth // 8 % 128 == 0:
        return head_body(*arrays)
    return general_body(*arrays)


def solution(mesh):
    return jax.shard_map(
        partial(body, (mesh.shape["dp"], mesh.shape["index"])),
        mesh=mesh,
        in_specs=(
            P("dp", "index", None),
            P("dp", "index", None),
            P("dp", "index"),
            P("index", None),
            P("dp", None),
            P("dp"),
            P("dp", "index", None),
            P(None, ("dp", "index"), None),
            P(("dp", "index"), None),
            P(("dp", "index"), None),
            P(None, ("dp", "index")),
            P(None, ("dp", "index"), None),
            P(None, ("dp", "index"), None),
            P(("dp", "index"), None),
            P(("dp", "index"), None),
            P(("dp", "index"), None),
            P(("dp", "index"), None),
            P(None, ("dp", "index")),
            P(None, ("dp", "index")),
        ),
        out_specs=(
            P("dp", "index", None),
            P("dp", "index", None),
            P("dp", "index", None),
            P("dp", "index"),
            P(None, ("dp", "index"), None),
            P(None, ("dp", "index"), None),
            P(None, ("dp", "index"), None),
            P(("dp", "index"), None),
            P(("dp", "index"), None),
            P(("dp", "index"), None),
            P(("dp", "index"), None),
            P(("dp", "index"), None),
            P(("dp", "index"), None),
            P(None, ("dp", "index")),
            P(None, ("dp", "index")),
            P(None, ("dp", "index")),
        ),
        check_vma=False,
    )
```

```python
from functools import partial

import jax
import jax.numpy as jnp
from jax import lax
from jax.experimental import pallas as pl
from jax.experimental.pallas import tpu as pltpu
from jax.sharding import PartitionSpec as P

HEADS = 16
MEM_P = 192
STEP = 10


negative_fill = -1e30
norm_eps = 1e-05
beta_first = 0.9
beta_second = 0.999
adam_eps = 1e-08
decay_matrix = 0.01
rate_attention = 0.1
rate_expand = 0.02
rate_contract = 0.01
rate_vector = 0.2


def layer_norm(hidden, norm_gain, norm_shift):
    center = hidden - jnp.mean(hidden, axis=-1, keepdims=True)
    spread = jnp.mean(center * center, axis=-1, keepdims=True)
    return center * lax.rsqrt(spread + norm_eps) * norm_gain + norm_shift


def split_heads(matrix):
    return matrix.reshape(matrix.shape[0], matrix.shape[1], HEADS, matrix.shape[2] // HEADS)


def merge_heads(matrix):
    return matrix.reshape(matrix.shape[0], matrix.shape[1], matrix.shape[2] * matrix.shape[3])


def project(left_side, weight):
    return jnp.einsum("srd,de->sre", left_side, weight, preferred_element_type=jnp.float32)


def project_back(gradient, weight):
    return jnp.einsum("sre,de->srd", gradient, weight, preferred_element_type=jnp.float32)


def weight_grad(left_side, gradient):
    return jnp.einsum("srd,sre->de", left_side, gradient, preferred_element_type=jnp.float32)


def row_total(values):
    return jnp.sum(values, axis=(0, 1))


def attend_forward(queries, key_rows, values, score_bias, allowed):
    scores = (
        jnp.einsum(
            "sqhd,skhd->shqk",
            split_heads(queries),
            split_heads(key_rows),
            preferred_element_type=jnp.float32,
        )
        * 0.125
        + score_bias
    )
    scores = jnp.where(allowed, scores, negative_fill)
    maximum = jnp.max(scores, axis=-1)
    exponent = jnp.exp(scores - maximum[..., None])
    partition = jnp.sum(exponent, axis=-1)
    attend_prob = exponent / partition[..., None]
    mixture = jnp.einsum(
        "shqk,skhd->sqhd",
        attend_prob.astype(jnp.bfloat16),
        split_heads(values),
        preferred_element_type=jnp.float32,
    )
    return (merge_heads(mixture).astype(jnp.bfloat16), attend_prob, maximum, partition)


def score_grads(grad_mixed, attend_prob, values):
    grad_prob = jnp.einsum(
        "sqhd,skhd->shqk",
        split_heads(grad_mixed),
        split_heads(values),
        preferred_element_type=jnp.float32,
    )
    row_inner = jnp.sum(attend_prob * grad_prob, axis=-1)
    return ((attend_prob * (grad_prob - row_inner[..., None])).astype(jnp.bfloat16), row_inner)


def to_queries(grad_score, key_rows):
    return (
        merge_heads(
            jnp.einsum(
                "shqk,skhd->sqhd",
                grad_score,
                split_heads(key_rows),
                preferred_element_type=jnp.float32,
            )
        )
        * 0.125
    )


def to_keys(grad_score, attend_prob, queries, grad_mixed):
    grad_key = (
        merge_heads(
            jnp.einsum(
                "shqk,sqhd->skhd",
                grad_score,
                split_heads(queries),
                preferred_element_type=jnp.float32,
            )
        )
        * 0.125
    )
    grad_value = merge_heads(
        jnp.einsum(
            "shqk,sqhd->skhd",
            attend_prob.astype(jnp.bfloat16),
            split_heads(grad_mixed),
            preferred_element_type=jnp.float32,
        )
    )
    return (grad_key, grad_value)


def adam_update(weight, moment_one, moment_two, gradient, step_rate, weight_decay):
    mean_new = beta_first * moment_one + (1.0 - beta_first) * gradient
    square_new = beta_second * moment_two + (1.0 - beta_second) * gradient * gradient
    mean_hat = mean_new / (1.0 - beta_first**STEP)
    square_hat = square_new / (1.0 - beta_second**STEP)
    updated = weight - step_rate * (
        mean_hat / (jnp.sqrt(square_hat) + adam_eps) + weight_decay * weight
    )
    return (updated, mean_new, square_new)


def general_body(
    decoder_input,
    encoder_memory,
    question_vectors,
    passage_vectors,
    passage_ids,
    valid_count,
    output_grad,
    attention_weight,
    expand_weight,
    contract_weight,
    vector_params,
    attention_mean,
    attention_square,
    expand_mean,
    expand_square,
    contract_mean,
    contract_square,
    vector_mean,
    vector_square,
):
    attention_low, expand_low, contract_low, vector_low = (
        lax.all_gather(attention_weight.astype(jnp.bfloat16), ("dp", "index"), axis=1, tiled=True),
        lax.all_gather(expand_weight.astype(jnp.bfloat16), ("dp", "index"), axis=0, tiled=True),
        lax.all_gather(contract_weight.astype(jnp.bfloat16), ("dp", "index"), axis=0, tiled=True),
        lax.all_gather(vector_params.astype(jnp.bfloat16), ("dp", "index"), axis=1, tiled=True),
    )
    vectors = vector_low.astype(jnp.float32)
    seqs_here, rows_here, model_width = decoder_input.shape
    shard_index = lax.axis_index("index")
    length = rows_here * lax.axis_size("index")
    ffn_width = expand_low.shape[1]
    self_query = (project(decoder_input, attention_low[0]) + vectors[0]).astype(jnp.bfloat16)
    self_key = project(decoder_input, attention_low[1]).astype(jnp.bfloat16)
    self_value = (project(decoder_input, attention_low[2]) + vectors[1]).astype(jnp.bfloat16)
    key_all, value_all = (
        lax.all_gather(self_key, "index", axis=1, tiled=True),
        lax.all_gather(self_value, "index", axis=1, tiled=True),
    )
    query_place = shard_index * rows_here + jnp.arange(rows_here)
    causal = (jnp.arange(length)[None, :] <= query_place[:, None])[None, None]
    self_mixed, self_prob, self_peak, self_total = attend_forward(
        self_query, key_all, value_all, 0.0, causal
    )
    first_in = (
        decoder_input.astype(jnp.float32) + project(self_mixed, attention_low[3]) + vectors[2]
    )
    first_out, first_back = jax.vjp(layer_norm, first_in, vectors[11], vectors[12])
    first_low = first_out.astype(jnp.bfloat16)
    cross_query = (project(first_low, attention_low[4]) + vectors[3]).astype(jnp.bfloat16)
    cross_key = project(encoder_memory, attention_low[5]).astype(jnp.bfloat16)
    cross_value = (project(encoder_memory, attention_low[6]) + vectors[4]).astype(jnp.bfloat16)
    memory_keys, memory_values = (
        lax.all_gather(cross_key, "index", axis=1, tiled=True),
        lax.all_gather(cross_value, "index", axis=1, tiled=True),
    )
    question_full = lax.all_gather(question_vectors, "index", axis=1, tiled=True)
    passages_here = passage_vectors.shape[0]
    local_ids = passage_ids - shard_index * passages_here
    owned_slot = (local_ids >= 0) & (local_ids < passages_here)
    picked = passage_vectors[jnp.clip(local_ids, 0, passages_here - 1)]
    local_scores = jnp.einsum(
        "sc,skc->sk", question_full, picked, preferred_element_type=jnp.float32
    )
    slots = passage_ids.shape[1]
    usable = jnp.arange(slots)[None, :] < valid_count[:, None]
    local_peak = jnp.max(jnp.where(owned_slot & usable, local_scores, negative_fill), axis=1)
    maximum = lax.pmax(local_peak, "index")
    local_exp = jnp.where(owned_slot & usable, jnp.exp(local_scores - maximum[:, None]), 0.0)
    exponent, scores = lax.psum((local_exp, jnp.where(owned_slot, local_scores, 0.0)), "index")
    masked = jnp.where(usable, scores, negative_fill)
    partition = jnp.sum(exponent, axis=1)
    passage_prob = exponent / partition[:, None]
    log_prior = masked - maximum[:, None] - jnp.log(partition)[:, None]
    memory_total = memory_keys.shape[1]
    bias_rows = jnp.repeat(log_prior, MEM_P, axis=1)
    key_bias = bias_rows[:, None, None, :]
    key_usable = ((jnp.arange(memory_total) // MEM_P)[None, :] < valid_count[:, None])[
        :, None, None, :
    ]
    cross_mixed, cross_prob, cross_peak, cross_total = attend_forward(
        cross_query, memory_keys, memory_values, key_bias, key_usable
    )
    second_in = first_out + project(cross_mixed, attention_low[7]) + vectors[5]
    second_out, second_back = jax.vjp(layer_norm, second_in, vectors[13], vectors[14])
    second_low = second_out.astype(jnp.bfloat16)
    inner_act = project(second_low, expand_low) + vectors[6:10].reshape(ffn_width)
    activated, gelu_back = jax.vjp(partial(jax.nn.gelu, approximate=False), inner_act)
    activ_low = activated.astype(jnp.bfloat16)
    third_in = second_out + project(activ_low, contract_low) + vectors[10]
    layer_output, third_back = jax.vjp(layer_norm, third_in, vectors[15], vectors[16])
    grad_third, gain_three, shift_three = third_back(output_grad.astype(jnp.float32))
    grad_ffn_low = grad_third.astype(jnp.bfloat16)
    grad_contract = weight_grad(activ_low, grad_ffn_low)
    (grad_inner,) = gelu_back(project_back(grad_ffn_low, contract_low))
    grad_inner_low = grad_inner.astype(jnp.bfloat16)
    grad_expand = weight_grad(second_low, grad_inner_low)
    grad_second = grad_third + project_back(grad_inner_low, expand_low)
    grad_second_in, gain_two, shift_two = second_back(grad_second)
    grad_cross_low = grad_second_in.astype(jnp.bfloat16)
    grad_cmix = project_back(grad_cross_low, attention_low[7]).astype(jnp.bfloat16)
    cross_score, cross_inner = score_grads(grad_cmix, cross_prob, memory_values)
    grad_cq = to_queries(cross_score, memory_keys)
    prior_part = (
        jnp.sum(cross_score, axis=(1, 2), dtype=jnp.float32)
        .reshape(seqs_here, slots, MEM_P)
        .sum(axis=-1)
    )
    prior_grad = jnp.where(usable, lax.psum(prior_part, "index"), 0.0)
    score_doc = jnp.where(
        usable, prior_grad - passage_prob * jnp.sum(prior_grad, axis=1, keepdims=True), 0.0
    )
    question_part = jnp.einsum(
        "sk,skc->sc",
        jnp.where(owned_slot, score_doc, 0.0),
        picked.astype(jnp.float32),
        precision=lax.Precision.HIGHEST,
    )
    question_gradient = lax.psum_scatter(question_part, "index", scatter_dimension=1, tiled=True)
    grad_cq_low = grad_cq.astype(jnp.bfloat16)
    grad_first = grad_second_in + project_back(grad_cq_low, attention_low[4])
    ck_part, cv_part = to_keys(cross_score, cross_prob, cross_query, grad_cmix)
    grad_ck, grad_cv = (
        lax.psum_scatter(
            ck_part.astype(jnp.bfloat16), "index", scatter_dimension=1, tiled=True
        ).astype(jnp.float32),
        lax.psum_scatter(
            cv_part.astype(jnp.bfloat16), "index", scatter_dimension=1, tiled=True
        ).astype(jnp.float32),
    )
    grad_ck_low = grad_ck.astype(jnp.bfloat16)
    grad_cv_low = grad_cv.astype(jnp.bfloat16)
    memory_gradient = project_back(grad_ck_low, attention_low[5]) + project_back(
        grad_cv_low, attention_low[6]
    )
    grad_first_in, gain_one, shift_one = first_back(grad_first)
    grad_self_low = grad_first_in.astype(jnp.bfloat16)
    grad_smix = project_back(grad_self_low, attention_low[3]).astype(jnp.bfloat16)
    self_score, row_inner = score_grads(grad_smix, self_prob, value_all)
    grad_sq = to_queries(self_score, key_all)
    key_part, value_part = to_keys(self_score, self_prob, self_query, grad_smix)
    grad_sk, grad_sv = (
        lax.psum_scatter(
            key_part.astype(jnp.bfloat16), "index", scatter_dimension=1, tiled=True
        ).astype(jnp.float32),
        lax.psum_scatter(
            value_part.astype(jnp.bfloat16), "index", scatter_dimension=1, tiled=True
        ).astype(jnp.float32),
    )
    grad_sq_low = grad_sq.astype(jnp.bfloat16)
    grad_sk_low = grad_sk.astype(jnp.bfloat16)
    grad_sv_low = grad_sv.astype(jnp.bfloat16)
    input_gradient = (
        grad_first_in
        + project_back(grad_sq_low, attention_low[0])
        + project_back(grad_sk_low, attention_low[1])
        + project_back(grad_sv_low, attention_low[2])
    )
    attention_grads = jnp.stack(
        [
            weight_grad(decoder_input, grad_sq_low),
            weight_grad(decoder_input, grad_sk_low),
            weight_grad(decoder_input, grad_sv_low),
            weight_grad(self_mixed, grad_self_low),
            weight_grad(first_low, grad_cq_low),
            weight_grad(encoder_memory, grad_ck_low),
            weight_grad(encoder_memory, grad_cv_low),
            weight_grad(cross_mixed, grad_cross_low),
        ]
    )
    vector_grads = jnp.concatenate(
        [
            jnp.stack(
                [
                    row_total(grad_sq),
                    row_total(grad_sv),
                    row_total(grad_first_in),
                    row_total(grad_cq),
                    row_total(grad_cv),
                    row_total(grad_second_in),
                ]
            ),
            row_total(grad_inner).reshape(ffn_width // model_width, model_width),
            jnp.stack(
                [
                    row_total(grad_third),
                    gain_one,
                    shift_one,
                    gain_two,
                    shift_two,
                    gain_three,
                    shift_three,
                ]
            ),
        ]
    )
    attention_sum, expand_sum, contract_sum, vector_sum = (
        lax.psum_scatter(attention_grads, ("dp", "index"), scatter_dimension=1, tiled=True),
        lax.psum_scatter(grad_expand, ("dp", "index"), scatter_dimension=0, tiled=True),
        lax.psum_scatter(grad_contract, ("dp", "index"), scatter_dimension=0, tiled=True),
        lax.psum_scatter(vector_grads, ("dp", "index"), scatter_dimension=1, tiled=True),
    )
    new_attention = adam_update(
        attention_weight,
        attention_mean,
        attention_square,
        attention_sum,
        rate_attention,
        decay_matrix,
    )
    new_expand = adam_update(
        expand_weight, expand_mean, expand_square, expand_sum, rate_expand, decay_matrix
    )
    new_contract = adam_update(
        contract_weight, contract_mean, contract_square, contract_sum, rate_contract, decay_matrix
    )
    new_vector = adam_update(
        vector_params, vector_mean, vector_square, vector_sum, rate_vector, 0.0
    )
    return (
        layer_output.astype(jnp.bfloat16),
        input_gradient,
        memory_gradient,
        question_gradient,
        new_attention[0],
        new_attention[1],
        new_attention[2],
        new_expand[0],
        new_expand[1],
        new_expand[2],
        new_contract[0],
        new_contract[1],
        new_contract[2],
        new_vector[0],
        new_vector[1],
        new_vector[2],
    )


NT = (((1,), (1,)), ((), ()))
NN = (((1,), (0,)), ((), ()))
TN = (((0,), (0,)), ((), ()))
CHIPS = 4
DP_ORDER = (0, 2, 1, 3)
VMEM_LIMIT = 56 << 20


def dot(left_side, right_side, dims):
    return lax.dot_general(left_side, right_side, dims, preferred_element_type=jnp.float32)


def norm_parts(hidden):
    center = hidden - jnp.mean(hidden, axis=-1, keepdims=True)
    inverse = lax.rsqrt(jnp.mean(center * center, axis=-1, keepdims=True) + norm_eps)
    return center * inverse, inverse


def norm_back(gradient, unit, inverse, gain):
    scaled = gradient * gain
    return inverse * (
        scaled
        - jnp.mean(scaled, axis=-1, keepdims=True)
        - unit * jnp.mean(scaled * unit, axis=-1, keepdims=True)
    )


def column_sum(values):
    return jnp.sum(values, axis=0, keepdims=True)


def join(parts, place=None):
    picked = [parts[j] if place is None else parts[j, place] for j in range(parts.shape[0])]
    return jnp.concatenate(
        [block.reshape(block.shape[0] * block.shape[1], block.shape[2]) for block in picked],
        axis=1,
    )


def spread(out_ref, value):
    count, seqs, rows, width = out_ref.shape
    for j in range(count):
        out_ref[j] = value[:, j * width : (j + 1) * width].reshape(seqs, rows, width)


def times(activation, weight):
    count, groups, rows, width = weight.shape
    depth = count * rows
    total = None
    for d in range(groups):
        part = dot(
            activation[:, d * depth : (d + 1) * depth], weight[:, d].reshape(depth, width), NN
        )
        total = part if total is None else total + part
    return total


def times_back(gradient, weight):
    count, groups, rows, width = weight.shape
    depth = count * rows
    return jnp.concatenate(
        [dot(gradient, weight[:, d].reshape(depth, width), NT) for d in range(groups)], axis=1
    )


def outer(out_ref, left_side, gradient):
    count, groups, rows, width = out_ref.shape
    depth = count * rows
    for d in range(groups):
        out_ref[:, d] = (
            dot(left_side[:, d * depth : (d + 1) * depth], gradient, TN)
            .astype(jnp.bfloat16)
            .reshape(count, rows, width)
        )


def whole(array):
    return pl.BlockSpec(array.shape, lambda *_, rank=len(array.shape): (0,) * rank)


def shape(dims, dtype):
    return jax.ShapeDtypeStruct(tuple(dims), dtype)


def params():
    return pltpu.CompilerParams(vmem_limit_bytes=VMEM_LIMIT)


def cost(flops, moved):
    return pl.CostEstimate(flops=int(flops) // 16, bytes_accessed=int(moved) // 16, transcendentals=0)


def in_head(dims, head_width, head):
    return lax.broadcasted_iota(jnp.int32, dims, 1) // head_width == head


def attend_forward_kernel(causal, head_width, q_ref, k_ref, v_ref, bias_ref, out_ref, stat_ref):
    count, _, tile, width = q_ref.shape
    keys = k_ref.shape[0] * k_ref.shape[2]
    key_rows, values = k_ref[...].reshape(keys, width), v_ref[...].reshape(keys, width)
    step = 2
    rows = step * tile
    for b in range(count // step):
        queries = q_ref[b * step : (b + 1) * step].reshape(rows, width)
        seen = (b + 1) * rows if causal else keys
        mixed = None
        for h in range(width // head_width):
            mask = in_head((rows, width), head_width, h)
            scores = dot(
                jnp.where(mask, queries * 0.125, 0).astype(jnp.bfloat16), key_rows[:seen], NT
            )
            if causal:
                corner = scores[:, seen - rows :]
                corner = jnp.where(
                    lax.broadcasted_iota(jnp.int32, corner.shape, 1)
                    <= lax.broadcasted_iota(jnp.int32, corner.shape, 0),
                    corner,
                    negative_fill,
                )
                if b == 0:
                    scores = corner
                else:
                    scores = jnp.concatenate([scores[:, : seen - rows], corner], axis=1)
            else:
                scores = scores + bias_ref[0]
            peak = jnp.max(scores, axis=1, keepdims=True)
            exponent = jnp.exp(scores - peak)
            total = jnp.sum(exponent, axis=1, keepdims=True)
            prob = (exponent * (1.0 / total)).astype(jnp.bfloat16)
            part = dot(prob, values[:seen], NN)
            mixed = part if mixed is None else jnp.where(mask, part, mixed)
            log_total = jnp.broadcast_to(peak + jnp.log(total), (rows, 128))
            stat_ref[0, h : h + 1, b * rows : (b + 1) * rows] = log_total.T[0:1]
        out_ref[b * step : (b + 1) * step] = mixed.astype(jnp.bfloat16).reshape(
            step, 1, tile, width
        )


def attend_backward_kernel(
    causal,
    head_width,
    q_ref,
    k_ref,
    v_ref,
    grad_ref,
    stat_ref,
    bias_ref,
    _,
    dq_ref,
    dkv_ref,
    prior_ref,
    dk_sum,
    dv_sum,
    prior_sum,
):
    count, _, tile, width = q_ref.shape
    keys = k_ref.shape[0] * k_ref.shape[2]
    key_rows, values = k_ref[...].reshape(keys, width), v_ref[...].reshape(keys, width)
    step = 2
    rows = step * tile
    if not causal:
        bias = jnp.broadcast_to(bias_ref[0], (128, keys)).T[:, :1]
    dk_sum[...] = jnp.zeros_like(dk_sum)
    dv_sum[...] = jnp.zeros_like(dv_sum)
    if not causal:
        prior_sum[...] = jnp.zeros_like(prior_sum)
    for b in range(count // step):
        queries = q_ref[b * step : (b + 1) * step].reshape(rows, width)
        gradient = grad_ref[b * step : (b + 1) * step].reshape(rows, width)
        seen = (b + 1) * rows if causal else keys
        query_grad = None
        for h in range(width // head_width):
            mask = in_head((rows, width), head_width, h)
            one_query = jnp.where(mask, queries * 0.125, 0).astype(jnp.bfloat16)
            one_grad = jnp.where(mask, gradient, 0).astype(jnp.bfloat16)
            scores = dot(key_rows[:seen], one_query, NT)
            if causal:
                corner = scores[seen - rows :]
                corner = jnp.where(
                    lax.broadcasted_iota(jnp.int32, corner.shape, 0)
                    <= lax.broadcasted_iota(jnp.int32, corner.shape, 1),
                    corner,
                    negative_fill,
                )
                if b == 0:
                    scores = corner
                else:
                    scores = jnp.concatenate([scores[: seen - rows], corner], axis=0)
            else:
                scores = scores + bias
            prob = jnp.exp(scores - stat_ref[0, h : h + 1, b * rows : (b + 1) * rows])
            grad_prob = dot(values[:seen], one_grad, NT)
            inner = jnp.sum(prob * grad_prob, axis=0, keepdims=True)
            grad_score = prob * (grad_prob - inner)
            score_low = grad_score.astype(jnp.bfloat16)
            dv_sum[:seen] += dot(prob.astype(jnp.bfloat16), one_grad, NN)
            dk_sum[:seen] += dot(score_low, one_query, NN)
            if not causal:
                partial_sum = grad_score[:, :128]
                for piece in range(128, rows, 128):
                    partial_sum = partial_sum + grad_score[:, piece : piece + 128]
                prior_sum[...] += partial_sum
            part = dot(score_low, key_rows[:seen], TN)
            query_grad = part if query_grad is None else jnp.where(mask, part, query_grad)
        dq_ref[b * step : (b + 1) * step] = (
            (query_grad * 0.125).astype(jnp.bfloat16).reshape(step, 1, tile, width)
        )
    dkv_ref[:, 0] = dk_sum[...].astype(jnp.bfloat16).reshape(k_ref.shape)
    dkv_ref[:, 1] = dv_sum[...].astype(jnp.bfloat16).reshape(k_ref.shape)
    if causal:
        prior_ref[...] = jnp.zeros_like(prior_ref)
    else:
        prior_ref[0] = column_sum(prior_sum[...].T)


def pick(array, place):
    count, _, _, rows, width = array.shape
    return pl.BlockSpec((count, None, 1, rows, width), lambda s: (0, place, s, 0, 0))


def attend(causal, queries, query_at, keys, key_at, value_at, bias):
    count, _, seqs, tile, width = queries.shape
    key_rows = keys.shape[0] * keys.shape[3]
    head_width = width * count // HEADS
    length = count * tile
    heads = width // head_width
    return pl.pallas_call(
        partial(attend_forward_kernel, causal, head_width),
        grid=(seqs,),
        in_specs=[
            pick(queries, query_at),
            pick(keys, key_at),
            pick(keys, value_at),
            pl.BlockSpec(memory_space=pl.ANY)
            if causal
            else pl.BlockSpec((1, 1, key_rows), lambda s: (s, 0, 0)),
        ],
        out_specs=[
            pl.BlockSpec((count, 1, tile, width), lambda s: (0, s, 0, 0)),
            pl.BlockSpec((1, heads, length), lambda s: (s, 0, 0)),
        ],
        out_shape=[
            shape((count, seqs, tile, width), jnp.bfloat16),
            shape((seqs, heads, length), jnp.float32),
        ],
        compiler_params=params(),
        cost_estimate=cost(
            16 * seqs * length * key_rows * width, 4 * seqs * (length + key_rows) * width
        ),
        name="attend_self" if causal else "attend_memory",
    )(queries, keys, keys, bias)


def attend_back(
    causal, queries, query_at, keys, key_at, value_at, gradient, stat, bias, after
):
    count, _, seqs, tile, width = queries.shape
    key_tile = keys.shape[3]
    key_rows = count * key_tile
    head_width = width * count // HEADS
    length = count * tile
    heads = width // head_width
    return pl.pallas_call(
        partial(attend_backward_kernel, causal, head_width),
        grid=(seqs,),
        in_specs=[
            pick(queries, query_at),
            pick(keys, key_at),
            pick(keys, value_at),
            pl.BlockSpec((count, 1, tile, width), lambda s: (0, s, 0, 0)),
            pl.BlockSpec((1, heads, length), lambda s: (s, 0, 0)),
            pl.BlockSpec(memory_space=pl.ANY)
            if causal
            else pl.BlockSpec((1, 1, key_rows), lambda s: (s, 0, 0)),
            pl.BlockSpec(memory_space=pl.ANY),
        ],
        out_specs=[
            pl.BlockSpec((count, 1, tile, width), lambda s: (0, s, 0, 0)),
            pl.BlockSpec((count, 2, 1, key_tile, width), lambda s: (0, 0, s, 0, 0)),
            pl.BlockSpec((1, 1, key_rows), lambda s: (s, 0, 0)),
        ],
        out_shape=[
            shape((count, seqs, tile, width), jnp.bfloat16),
            shape((count, 2, seqs, key_tile, width), jnp.bfloat16),
            shape((seqs, 1, key_rows), jnp.float32),
        ],
        scratch_shapes=[
            pltpu.VMEM((key_rows, width), jnp.float32),
            pltpu.VMEM((key_rows, width), jnp.float32),
            pltpu.VMEM((key_rows, 128), jnp.float32),
        ],
        compiler_params=params(),
        cost_estimate=cost(
            40 * seqs * length * key_rows * width, 8 * seqs * (length + key_rows) * width
        ),
        name="attend_self_back" if causal else "attend_memory_back",
    )(queries, keys, keys, gradient, stat, bias, after)


def take_columns(scratch, slices, first):
    width = slices.shape[3]
    depth = scratch.shape[0]
    rows = depth // (slices.shape[0] * slices.shape[1])
    for m in range(scratch.shape[1] // width):
        start = (first + m) * rows
        scratch[:, m * width : (m + 1) * width] = slices[:, :, start : start + rows].reshape(
            depth, width
        )


def columns_kernel(first, row_ref, slice_ref, bias_ref, out_ref, weight):
    @pl.when(pl.program_id(0) == 0)
    def _():
        take_columns(weight, slice_ref, first)

    _, many, seqs, rows, width = out_ref.shape
    taken = row_ref[0, :, :rows].reshape(seqs * rows, weight.shape[0])
    result = dot(taken, weight[...], NN) + bias_ref[...]
    for m in range(many):
        out_ref[0, m] = (
            result[:, m * width : (m + 1) * width]
            .astype(jnp.bfloat16)
            .reshape(seqs, rows, width)
        )


def project_columns(name, gathered_rows, block_rows, row_block, rows, slices, first, many, bias):
    count, seqs, _, depth = gathered_rows.shape
    width = slices.shape[3]
    return pl.pallas_call(
        partial(columns_kernel, first),
        grid=(count,),
        in_specs=[
            pl.BlockSpec((1, seqs, block_rows, depth), lambda i: (i, 0, row_block, 0)),
            whole(slices),
            whole(bias),
        ],
        out_specs=pl.BlockSpec((1, many, seqs, rows, width), lambda i: (i, 0, 0, 0, 0)),
        out_shape=shape((count, many, seqs, rows, width), jnp.bfloat16),
        scratch_shapes=[pltpu.VMEM((depth, many * width), jnp.bfloat16)],
        compiler_params=params(),
        cost_estimate=cost(
            2 * many * count * seqs * rows * depth * width, 2 * count * seqs * rows * depth
        ),
        name=name,
    )(gathered_rows, slices, bias)


def columns_back_kernel(
    first, _, row_ref, *refs
):
    grad_refs, (slice_ref, mine_out, other_out, dw_ref, bias_ref, weight, total) = (
        refs[:-7],
        refs[-7:],
    )
    turn, step = pl.program_id(0), pl.program_id(1)

    @pl.when((turn == 0) & (step == 0))
    def _():
        take_columns(weight, slice_ref, first)
        total[...] = jnp.zeros_like(total)
        bias_ref[...] = jnp.zeros_like(bias_ref)

    depth = weight.shape[0]
    pieces = []
    for grad_ref in grad_refs:
        seqs, rows, width = grad_ref.shape[-3:]
        for m in range(grad_ref.shape[1] if len(grad_ref.shape) == 5 else 1):
            piece = grad_ref[0, m] if len(grad_ref.shape) == 5 else grad_ref[0]
            pieces.append(piece.reshape(seqs * rows, width))
    gradient = jnp.concatenate(pieces, axis=1)
    taken = row_ref[0, :, :rows].reshape(seqs * rows, depth)
    bias_ref[...] += column_sum(gradient.astype(jnp.float32))
    total[...] += dot(taken, gradient, TN)
    row_grad = dot(gradient, weight[...], NT).astype(jnp.bfloat16)

    @pl.when(turn == 0)
    def _():
        mine_out[0, 0] = row_grad

    @pl.when(turn == 1)
    def _():
        other_out[0, 0] = row_grad

    @pl.when((turn == 1) & (step == pl.num_programs(1) - 1))
    def _():
        groups, count, all_rows, _ = dw_ref.shape
        part = depth // (groups * count)
        for m in range(all_rows // part):
            dw_ref[:, :, m * part : (m + 1) * part] = (
                total[:, m * width : (m + 1) * width]
                .astype(jnp.bfloat16)
                .reshape(groups, count, part, width)
            )


def project_columns_back(
    name, order, gathered_rows, block_rows, row_block, rows, gradients, slices, first, many
):
    count, seqs, _, depth = gathered_rows.shape
    half = count // 2
    groups, _, _, width = slices.shape
    part = depth // (groups * count)

    def one_device(array):
        rest = (0,) * (len(array.shape) - 1)
        return pl.BlockSpec(
            (1,) + array.shape[1:], lambda p, k, order: (order[p * half + k],) + rest
        )

    dw_shape = shape((groups, count, many * part, width), jnp.bfloat16)
    return pl.pallas_call(
        partial(columns_back_kernel, first),
        grid_spec=pltpu.PrefetchScalarGridSpec(
            num_scalar_prefetch=1,
            grid=(2, half),
            in_specs=[
                pl.BlockSpec(
                    (1, seqs, block_rows, depth),
                    lambda p, k, order: (order[p * half + k], 0, row_block, 0),
                ),
                *[one_device(array) for array in gradients],
                whole(slices),
            ],
            out_specs=[
                pl.BlockSpec(
                    (1, 1, seqs * rows, depth),
                    lambda p, k, _: (jnp.where(p == 0, k, half - 1), 0, 0, 0),
                ),
                pl.BlockSpec(
                    (1, 1, seqs * rows, depth), lambda p, k, _: (jnp.where(p == 0, 0, k), 0, 0, 0)
                ),
                whole(dw_shape),
                pl.BlockSpec((1, many * width), lambda *_: (0, 0)),
            ],
            scratch_shapes=[
                pltpu.VMEM((depth, many * width), jnp.bfloat16),
                pltpu.VMEM((depth, many * width), jnp.float32),
            ],
        ),
        out_shape=[
            shape((half, 1, seqs * rows, depth), jnp.bfloat16),
            shape((half, 1, seqs * rows, depth), jnp.bfloat16),
            dw_shape,
            shape((1, many * width), jnp.float32),
        ],
        compiler_params=params(),
        cost_estimate=cost(
            4 * many * count * seqs * rows * depth * width, 4 * count * seqs * rows * depth
        ),
        name=name,
    )(order, gathered_rows, *gradients, slices)


def gathered(weights, width, place):
    count, groups, rows, _ = weights.shape
    return pl.BlockSpec((count, groups, rows, width), lambda *_: (0, 0, 0, place))


def first_kernel(
    mixed_ref, x_ref, out_w, query_w, vector_ref, _, mixed_out, in_out, low_out, query_out
):
    mixed = join(mixed_ref)
    mixed_out[...] = mixed
    first_in = x_ref[...].astype(jnp.float32) + times(mixed, out_w) + vector_ref[2:3]
    in_out[...] = first_in
    unit, _ = norm_parts(first_in)
    low = (unit * vector_ref[11:12] + vector_ref[12:13]).astype(jnp.bfloat16)
    low_out[...] = low
    spread(query_out, (times(low, query_w) + vector_ref[3:4]).astype(jnp.bfloat16))


def first_forward(mixed, x_rows, weights, vectors, after):
    rows, depth = x_rows.shape
    return pl.pallas_call(
        first_kernel,
        grid=(1,),
        in_specs=[
            whole(mixed),
            whole(x_rows),
            gathered(weights, depth, 0),
            gathered(weights, depth, 1),
            whole(vectors),
            pl.BlockSpec(memory_space=pl.ANY),
        ],
        out_specs=[whole(x_rows), whole(x_rows), whole(x_rows), whole(mixed)],
        out_shape=[
            shape((rows, depth), jnp.bfloat16),
            shape((rows, depth), jnp.float32),
            shape((rows, depth), jnp.bfloat16),
            shape(mixed.shape, jnp.bfloat16),
        ],
        compiler_params=params(),
        cost_estimate=cost(4 * rows * depth * depth, 4 * depth * depth),
        name="first_forward",
    )(mixed, x_rows, weights, weights, vectors, after)


def ffn_kernel(
    order,
    places,
    mixed_ref,
    first_ref,
    out_w,
    vector_ref,
    bias_ref,
    grad_ref,
    wide_ref,
    *refs,
):
    contract_refs, refs = refs[:8], refs[8:]
    mixed_out, layer_out, wide_grad = refs[:3]
    contract_grads, refs = refs[3:11], refs[11:]
    dbias_ref, second_grad, cross_low, mixed_grad, stat_out, columns, contracts = refs[:7]
    active, slope, low, third_low, second_in, total, wide_sem, contract_sem = refs[7:]
    blocks, count, groups, rows, block = columns.shape
    part = block // CHIPS
    depth = vector_ref.shape[1]

    def wide_copies(t, array, outward):
        result = []
        for k in range(CHIPS):
            column = pl.multiple_of(order[t % 2 * CHIPS + k] * part, part)
            row = pl.multiple_of(places[t // 2] * rows, rows)
            there = array.at[:, :, pl.ds(row, rows), pl.ds(column, part)]
            here = columns.at[t, :, :, :, pl.ds(k * part, part)]
            ends = (here, there) if outward else (there, here)
            result.append(pltpu.make_async_copy(*ends, wide_sem.at[t, k]))
        return result

    def contract_copies(t, pieces, outward):
        near, far = divmod(DP_ORDER[t // 2], 2)
        first = pieces[t % 2 * 4 + far].at[near]
        last = pieces[t % 2 * 4 + 2 + near].at[far]
        result = []
        for half, there in enumerate((first, last)):
            here = contracts.at[t, pl.ds(half * CHIPS // 2, CHIPS // 2)]
            ends = (here, there) if outward else (there, here)
            result.append(pltpu.make_async_copy(*ends, contract_sem.at[t, half]))
        return result

    for t in range(blocks):
        for copy in wide_copies(t, wide_ref, False):
            copy.start()
        for copy in contract_copies(t, contract_refs, False):
            copy.start()

    mixed = join(mixed_ref)
    mixed_out[...] = mixed
    unit, _ = norm_parts(first_ref[...])
    second_in[...] = (
        unit * vector_ref[11:12] + vector_ref[12:13] + times(mixed, out_w) + vector_ref[5:6]
    )
    unit, _ = norm_parts(second_in[...])
    second = unit * vector_ref[13:14] + vector_ref[14:15]
    low[...] = second.astype(jnp.bfloat16)
    total[...] = second + vector_ref[10:11]

    def shard(t, k):
        return places[t // 2] * count + order[t % 2 * CHIPS + k]

    for t in range(blocks):
        for copy in wide_copies(t, wide_ref, False):
            copy.wait()
        bias = jnp.concatenate([bias_ref[pl.ds(shard(t, k), 1)] for k in range(CHIPS)], axis=1)
        inner = times(low[...], columns.at[t]) + bias
        phi = 0.5 + 0.5 * lax.erf(inner * (0.5**0.5))
        out = (inner * phi).astype(jnp.bfloat16)
        active[t] = out
        slope[t] = phi + inner * jnp.exp(-0.5 * inner * inner) * 0.3989422804014327
        for copy in contract_copies(t, contract_refs, False):
            copy.wait()
        total[...] += dot(out, contracts[t].reshape(block, depth), NN)

    unit, inverse = norm_parts(total[...])
    gain = vector_ref[15:16]
    layer_out[...] = (unit * gain + vector_ref[16:17]).astype(jnp.bfloat16)
    gradient = grad_ref[...].astype(jnp.float32)
    grad_third = norm_back(gradient, unit, inverse, gain)
    stat_out[...] = jnp.zeros_like(stat_out)
    stat_out[0:1] = column_sum(grad_third)
    stat_out[1:2] = column_sum(gradient * unit)
    stat_out[2:3] = column_sum(gradient)
    total[...] = grad_third
    third_low[...] = grad_third.astype(jnp.bfloat16)
    turned = low[...].T

    for t in range(blocks):
        grad_inner = dot(third_low[...], contracts[t].reshape(block, depth), NT) * slope[t]
        inner_low = grad_inner.astype(jnp.bfloat16)
        sums = column_sum(grad_inner)
        for k in range(CHIPS):
            dbias_ref[pl.ds(shard(t, k), 1)] = sums[:, k * part : (k + 1) * part]
        contracts[t] = (
            dot(active[t], third_low[...], TN).astype(jnp.bfloat16).reshape(CHIPS, part, depth)
        )
        for copy in contract_copies(t, contract_grads, True):
            copy.start()
        total[...] += times_back(inner_low, columns.at[t])
        result = dot(turned, inner_low, NN).astype(jnp.bfloat16)
        for d in range(groups):
            columns[t, :, d] = result[d * count * rows : (d + 1) * count * rows].reshape(
                count, rows, block
            )
        for copy in wide_copies(t, wide_grad, True):
            copy.start()

    unit, inverse = norm_parts(second_in[...])
    grad_second = total[...]
    grad_in = norm_back(grad_second, unit, inverse, vector_ref[13:14])
    second_grad[...] = grad_in
    grad_low = grad_in.astype(jnp.bfloat16)
    cross_low[...] = grad_low
    spread(mixed_grad, times_back(grad_low, out_w).astype(jnp.bfloat16))
    stat_out[8:9] = column_sum(grad_in)
    stat_out[9:10] = column_sum(grad_second * unit)
    stat_out[10:11] = column_sum(grad_second)
    for t in range(blocks):
        for copy in contract_copies(t, contract_grads, True) + wide_copies(t, wide_grad, True):
            copy.wait()


def ffn(orders, mixed, first_in, wide, contract, vectors, bias, output_grad):
    rows, depth = first_in.shape
    hidden = bias.size
    block = depth // 2
    count, groups, all_rows, _ = wide.shape
    part = depth // (count * groups)
    blocks = hidden // block
    full = whole(first_in)
    anywhere = pl.BlockSpec(memory_space=pl.ANY)
    heads_out = shape(mixed.shape, jnp.bfloat16)
    stats = shape((16, depth), jnp.float32)
    return pl.pallas_call(
        ffn_kernel,
        grid_spec=pltpu.PrefetchScalarGridSpec(
            num_scalar_prefetch=2,
            grid=(1,),
            in_specs=[
                whole(mixed),
                full,
                pl.BlockSpec((count, groups, part, depth), lambda *_: (0, 0, groups, 0)),
                whole(vectors),
                whole(bias),
                full,
                *[anywhere] * 9,
            ],
            out_specs=[
                full,
                full,
                *[anywhere] * 9,
                whole(bias),
                full,
                full,
                whole(heads_out),
                whole(stats),
            ],
            scratch_shapes=[
                pltpu.VMEM((blocks, count, groups, part, block), jnp.bfloat16),
                pltpu.VMEM((blocks, CHIPS) + contract[0].shape[2:], jnp.bfloat16),
                pltpu.VMEM((blocks, rows, block), jnp.bfloat16),
                pltpu.VMEM((blocks, rows, block), jnp.float32),
                pltpu.VMEM((rows, depth), jnp.bfloat16),
                pltpu.VMEM((rows, depth), jnp.bfloat16),
                pltpu.VMEM((rows, depth), jnp.float32),
                pltpu.VMEM((rows, depth), jnp.float32),
                pltpu.SemaphoreType.DMA((blocks, CHIPS)),
                pltpu.SemaphoreType.DMA((blocks, 2)),
            ],
        ),
        out_shape=[
            shape((rows, depth), jnp.bfloat16),
            shape((rows, depth), jnp.bfloat16),
            shape((count, groups, all_rows - part, depth), jnp.bfloat16),
            *[shape(piece.shape, jnp.bfloat16) for piece in contract],
            shape(bias.shape, jnp.float32),
            shape((rows, depth), jnp.float32),
            shape((rows, depth), jnp.bfloat16),
            heads_out,
            stats,
        ],
        compiler_params=params(),
        cost_estimate=cost(12 * rows * depth * hidden, 16 * depth * hidden),
        name="ffn",
    )(*orders, mixed, first_in, wide, vectors, bias, output_grad, wide, *contract)


def first_back_kernel(
    dq_ref,
    second_grad,
    first_ref,
    out_w,
    query_w,
    vector_ref,
    _,
    query_low,
    grad_in_out,
    self_low,
    mixed_grad,
    stat_out,
):
    query_grad = join(dq_ref)
    query_low[...] = query_grad
    grad_first = second_grad[...] + times_back(query_grad, query_w)
    unit, inverse = norm_parts(first_ref[...])
    grad_in = norm_back(grad_first, unit, inverse, vector_ref[11:12])
    grad_in_out[...] = grad_in
    grad_low = grad_in.astype(jnp.bfloat16)
    self_low[...] = grad_low
    spread(mixed_grad, times_back(grad_low, out_w).astype(jnp.bfloat16))
    stat_out[...] = jnp.zeros_like(stat_out)
    stat_out[0:1] = column_sum(query_grad.astype(jnp.float32))
    stat_out[1:2] = column_sum(grad_in)
    stat_out[2:3] = column_sum(grad_first * unit)
    stat_out[3:4] = column_sum(grad_first)


def first_back(dq, second_grad, first_in, weights, vectors, after):
    rows, depth = first_in.shape
    full = whole(first_in)
    return pl.pallas_call(
        first_back_kernel,
        grid=(1,),
        in_specs=[
            whole(dq),
            full,
            full,
            gathered(weights, depth, 0),
            gathered(weights, depth, 1),
            whole(vectors),
            pl.BlockSpec(memory_space=pl.ANY),
        ],
        out_specs=[full, full, full, whole(dq), pl.BlockSpec((8, depth), lambda *_: (0, 0))],
        out_shape=[
            shape((rows, depth), jnp.bfloat16),
            shape((rows, depth), jnp.float32),
            shape((rows, depth), jnp.bfloat16),
            shape(dq.shape, jnp.bfloat16),
            shape((8, depth), jnp.float32),
        ],
        compiler_params=params(),
        cost_estimate=cost(4 * rows * depth * depth, 4 * depth * depth),
        name="first_back",
    )(dq, second_grad, first_in, weights, weights, vectors, after)


def weight_grads_kernel(
    order,
    mixed,
    self_low,
    first_low,
    query_low,
    cross,
    cross_low,
    mine_out,
    other_out,
    result,
):
    step = pl.program_id(0)
    pairs = ((mixed, self_low), (first_low, query_low), (cross, cross_low))
    half, groups, part, _ = mine_out.shape
    for m, (left_side, gradient) in enumerate(pairs):

        @pl.when(step == m)
        def _(left_side=left_side, gradient=gradient):
            result[...] = dot(left_side[...], gradient[...], TN).astype(jnp.bfloat16)

    for d in range(groups):
        for k in range(half):
            for p, out_ref in enumerate((mine_out, other_out)):
                row = pl.multiple_of((2 * half * d + order[p * half + k]) * part, part)
                out_ref[k, d] = result[pl.ds(row, part)]


def weight_grads(dims, order, mixed, self_low, first_low, query_low, cross, cross_low):
    count, groups, part, depth = dims
    half = pl.BlockSpec((count // 2, groups, part, depth), lambda m, _: (0, 0, m, 0))
    return pl.pallas_call(
        weight_grads_kernel,
        grid_spec=pltpu.PrefetchScalarGridSpec(
            num_scalar_prefetch=1,
            grid=(3,),
            in_specs=[whole(mixed)] * 6,
            out_specs=[half, half],
            scratch_shapes=[pltpu.VMEM((depth, depth), jnp.bfloat16)],
        ),
        out_shape=[shape((count // 2, groups, 3 * part, depth), jnp.bfloat16)] * 2,
        compiler_params=params(),
        cost_estimate=cost(6 * mixed.shape[0] * depth * depth, 6 * depth * depth),
        name="weight_grads",
    )(order, mixed, self_low, first_low, query_low, cross, cross_low)


def send_dp(piece):
    size = lax.axis_size("dp")
    return [
        lax.ppermute(piece, "dp", [(i, (i + shift) % size) for i in range(size)])
        for shift in range(1, size)
    ]


def place_dp(piece, arrived):
    size, me = lax.axis_size("dp"), lax.axis_index("dp")
    result = jnp.zeros((size,) + piece.shape, piece.dtype)
    result = lax.dynamic_update_index_in_dim(result, piece, me, 0)
    for shift, got in enumerate(arrived, 1):
        result = lax.dynamic_update_index_in_dim(result, got, lax.rem(me - shift + size, size), 0)
    return result


def to_chips(block):
    return [exchange(block, 2 * k) for k in range(1, CHIPS)]


def sends_dp(pieces):
    size, me = lax.axis_size("dp"), lax.axis_index("dp")
    own, *others = [
        lax.dynamic_index_in_dim(pieces, lax.rem(me + shift, size), 0, keepdims=False)
        for shift in range(size)
    ]
    return own, [
        lax.ppermute(piece, "dp", [(i, (i + shift) % size) for i in range(size)])
        for shift, piece in enumerate(others, 1)
    ]


def gather_index(mine):
    size, me = lax.axis_size("index"), lax.axis_index("index")
    block = mine[0]
    other = exchange(jnp.stack(mine), 1)
    result = jnp.zeros((size,) + block.shape, block.dtype)
    for k in range(CHIPS):
        result = lax.dynamic_update_index_in_dim(result, mine[k], me ^ (2 * k), 0)
        result = lax.dynamic_update_index_in_dim(result, other[k], me ^ (2 * k) ^ 1, 0)
    return result


class HalvingDp:
    def __init__(self, pieces):
        me = lax.axis_index("dp")
        self.parts = [
            lax.dynamic_index_in_dim(pieces, me ^ flip, 0, keepdims=False) for flip in DP_ORDER
        ]

    def first(self):
        return jnp.stack(self.parts[2:]).astype(jnp.bfloat16)

    def second(self, got):
        self.got = got
        return (
            self.parts[1].astype(jnp.float32) + self.got[1].astype(jnp.float32)
        ).astype(jnp.bfloat16)

    def finish(self, last):
        return sum(one.astype(jnp.float32) for one in (self.parts[0], self.got[0], last))


def relative_order():
    size, me = lax.axis_size("index"), lax.axis_index("index")
    steps = jnp.arange(size // 2, dtype=jnp.int32) * 2
    return jnp.concatenate([me ^ steps, me ^ 1 ^ steps])


def exchange(piece, flip):
    size = lax.axis_size("index")
    return lax.ppermute(piece, "index", [(i, i ^ flip) for i in range(size)])


def exchange_dp(piece, flip):
    size = lax.axis_size("dp")
    return lax.ppermute(piece, "dp", [(i, i ^ flip) for i in range(size)])


def add_kernel(*refs):
    total = sum(ref[...].astype(jnp.float32) for ref in refs[:-1])
    refs[-1][...] = total.astype(jnp.bfloat16)


def add(*terms):
    flat, specs = [], []
    first = terms[0]
    dims = first[0].shape[1:] if isinstance(first, tuple) else first.shape
    rows = 1
    for size in dims[:-1]:
        rows *= size
    block = min(rows, 256)
    for term in terms:
        array, entry = term if isinstance(term, tuple) else (term, 0)
        flat.append(array.reshape(-1, dims[-1]))
        start = entry * rows // block
        specs.append(pl.BlockSpec((block, dims[-1]), lambda i, start=start: (start + i, 0)))
    return pl.pallas_call(
        add_kernel,
        grid=(rows // block,),
        in_specs=specs,
        out_specs=pl.BlockSpec((block, dims[-1]), lambda i: (i, 0)),
        out_shape=shape((rows, dims[-1]), jnp.bfloat16),
        compiler_params=params(),
        cost_estimate=cost(0, 0),
        name="add",
    )(*flat).reshape(dims)


def combine_kernel(plan, *refs):
    ins, outs = list(refs[: -len(plan)]), refs[-len(plan) :]
    for out_ref, entries in zip(outs, plan):
        for e, segments in enumerate(entries):
            start = 0
            for count, rows in segments:
                terms, ins = ins[:count], ins[count:]
                total = sum(ref[0].astype(jnp.float32) for ref in terms)
                out_ref[e, start : start + rows] = total.astype(jnp.bfloat16)
                start += rows


def combine(*outputs):
    arrays, specs, plan, shapes = [], [], [], []
    for entries in outputs:
        plan.append([])
        for segments in entries:
            plan[-1].append([])
            for terms in segments:
                plan[-1][-1].append((len(terms), terms[0][2]))
                for array, e, rows, place in terms:
                    arrays.append(array)
                    specs.append(
                        pl.BlockSpec(
                            (1, rows, array.shape[2]), lambda i, e=e, place=place: (e, place, 0)
                        )
                    )
        rows = sum(rows for _, rows in plan[-1][0])
        shapes.append(shape((len(entries), rows, arrays[0].shape[2]), jnp.bfloat16))
    return pl.pallas_call(
        partial(combine_kernel, plan),
        grid=(1,),
        in_specs=specs,
        out_specs=[whole(out) for out in shapes],
        out_shape=shapes,
        compiler_params=params(),
        cost_estimate=cost(0, 0),
        name="combine",
    )(*arrays)


class Halving:
    def __init__(self, chips):
        self.chips = chips
        self.middle = chips[0][0][0].shape[1] // 2

    def terms(self, k, half, *more):
        middle = self.middle
        return [(array, e, middle, half) for array, e in self.chips[k]] + [
            (array, e, middle, start // middle) for array, e, start in more
        ]

    def total(self, k, half, *more):
        rows = slice(half * self.middle, (half + 1) * self.middle)
        parts = [array[e, rows] for array, e in self.chips[k]] + [*more]
        return sum(one.astype(jnp.float32) for one in parts)

    def finish(self, top, low):
        return jnp.concatenate(
            [self.total(0, 0, self.got[0][0], top), self.total(0, 1, self.got[1][0], low)], axis=0
        )


def both_cores(mine, other):
    parts = [part.reshape(CHIPS, -1, part.shape[-1]) for part in (mine, other)]
    return Halving([[(part, k) for part in parts] for k in range(CHIPS)])


def firsts(*sums):
    return combine(
        [[one.terms(k, 0) for one in sums] for k in (1, 3)],
        [[one.terms(k, 1) for one in sums] for k in (2, 3)],
    )


def seconds(*sums):
    for one, top, low, start in sums:
        rows = slice(start, start + one.middle)
        one.got = top[:, rows], low[:, rows]
    top, low = combine(
        [[one.terms(2, 0, (top, 1, start)) for one, top, _, start in sums]],
        [[one.terms(1, 1, (low, 1, start)) for one, _, low, start in sums]],
    )
    return top[0], low[0]


def send_first(top, low):
    return [exchange(top, 2), exchange(low, 4)]


def send_last(top, low):
    return [exchange(top, 4), exchange(low, 2)]


def split_rows(arrays, rows):
    return [a[..., :rows, :] for a in arrays], [a[..., rows:, :] for a in arrays]


def small_send(values):
    size = lax.axis_size("index")
    flat = jnp.pad(values.reshape(-1), (0, 1024 - values.size)).reshape(1, 8, 128)
    return swap(jnp.broadcast_to(flat, (size, 8, 128)))


def small_take(arrived, dims):
    size = 1
    for dim in dims:
        size *= dim
    return jnp.sum(arrived, axis=0).reshape(-1)[:size].reshape(dims)


def hold_kernel(*_):
    pass


def hold(values, *others):
    anywhere = pl.BlockSpec(memory_space=pl.ANY)
    return pl.pallas_call(
        hold_kernel,
        in_specs=[anywhere] * (len(values) + len(others)),
        out_specs=[anywhere] * len(values),
        out_shape=[shape(value.shape, value.dtype) for value in values],
        input_output_aliases={i: i for i in range(len(values))},
        name="hold",
    )(*values, *others)


def swap(pieces):
    return lax.all_to_all(pieces, "index", 0, 0, tiled=True)


def head_body(
    decoder_input,
    encoder_memory,
    question_vectors,
    passage_vectors,
    passage_ids,
    valid_count,
    output_grad,
    attention_weight,
    expand_weight,
    contract_weight,
    vector_params,
    attention_mean,
    attention_square,
    expand_mean,
    expand_square,
    contract_mean,
    contract_square,
    vector_mean,
    vector_square,
):
    low = jnp.bfloat16
    count, groups = lax.axis_size("index"), lax.axis_size("dp")
    place = lax.axis_index("index")
    seqs, rows_here, depth = decoder_input.shape
    memory_here = encoder_memory.shape[1]
    width = depth // count
    part = attention_weight.shape[1]
    hidden = expand_weight.shape[1]
    vector_rows, vector_width = vector_params.shape
    question_width = question_vectors.shape[1]
    rows = seqs * rows_here

    attention_low = attention_weight.astype(low)
    extras = jnp.concatenate(
        [vector_params.astype(low).reshape(-1), question_vectors.reshape(-1)]
    )
    extra_rows = -(-extras.shape[0] // (16 * width)) * 16
    extras = jnp.pad(extras, (0, extra_rows * width - extras.shape[0])).reshape(
        1, extra_rows, width
    )
    split = jnp.concatenate([attention_low[:3], attention_low[5:7]], axis=0)
    columns = split.reshape(5, part, count, width).transpose(2, 0, 1, 3)
    package = jnp.concatenate(
        [
            columns.reshape(count, 5 * part, width),
            jnp.broadcast_to(extras, (count, extra_rows, width)),
        ],
        axis=1,
    )
    order = relative_order()
    memory_block = -(-memory_here // rows_here) * rows_here
    rows_all = lax.all_gather(
        jnp.concatenate(
            [
                jnp.pad(encoder_memory, ((0, 0), (0, memory_block - memory_here), (0, 0))),
                decoder_input,
            ],
            axis=1,
        ),
        "index",
        axis=0,
        tiled=False,
    )
    input_rows = (rows_all, rows_here, memory_block // rows_here, rows_here)
    memory_rows = (rows_all, memory_block, 0, memory_here)
    square = attention_low[3:5].transpose(1, 0, 2).reshape(part, 2 * depth)
    received = swap(package)
    square_arrived = hold(send_dp(square), received)
    (received,) = hold([received], *square_arrived)
    received_sent = send_dp(received)
    square = place_dp(square, square_arrived)
    *slices_arrived, x, y, xy = hold([*received_sent, *to_chips(square)])
    slices = place_dp(received, slices_arrived)
    square = [square, x, y, xy]
    (contract,) = hold([contract_weight.astype(low)], x)
    contract_sent = to_chips(contract)
    vectors = (
        slices[:, :, 5 * part :]
        .reshape(groups, count, extra_rows * width)[:, :, : vector_rows * vector_width]
        .reshape(groups, count, vector_rows, vector_width)
        .transpose(2, 0, 1, 3)
        .reshape(vector_rows, depth)
        .astype(jnp.float32)
    )
    question_full = (
        received[:, 5 * part :]
        .reshape(count, extra_rows * width)[:, vector_rows * vector_width :][
            :, : seqs * question_width
        ]
        .reshape(count, seqs, question_width)
        .transpose(1, 0, 2)
        .reshape(seqs, count * question_width)
    )
    expand_part = hidden // depth * part
    late = jnp.concatenate(
        [
            expand_weight.astype(low)
            .reshape(part, hidden // depth, depth)
            .transpose(1, 0, 2)
            .reshape(expand_part, depth),
            attention_low[7],
        ],
        axis=0,
    )
    (late,) = hold([late], *slices_arrived)
    late_sent = send_dp(late)

    (passage_ids,) = hold([passage_ids], *slices_arrived)
    passages_here = passage_vectors.shape[0]
    local_ids = passage_ids - place * passages_here
    owned_slot = (local_ids >= 0) & (local_ids < passages_here)
    picked = passage_vectors[jnp.clip(local_ids, 0, passages_here - 1)]
    local_scores = jnp.einsum(
        "sc,skc->sk", question_full, picked, preferred_element_type=jnp.float32
    )
    slots = passage_ids.shape[1]
    usable = jnp.arange(slots)[None, :] < valid_count[:, None]
    scores = small_take(small_send(jnp.where(owned_slot, local_scores, 0.0)), local_scores.shape)
    masked = jnp.where(usable, scores, negative_fill)
    maximum = jnp.max(masked, axis=1)
    exponent = jnp.where(usable, jnp.exp(masked - maximum[:, None]), 0.0)
    partition = jnp.sum(exponent, axis=1)
    passage_prob = exponent / partition[:, None]
    log_prior = jnp.where(
        usable, masked - maximum[:, None] - jnp.log(partition)[:, None], negative_fill
    )
    key_bias = jnp.repeat(log_prior, MEM_P, axis=1)

    vector_here = lax.dynamic_slice_in_dim(vectors[:5], place * width, width, axis=1)
    no_bias = jnp.zeros((1, width), jnp.float32)
    qkv_bias = jnp.concatenate([vector_here[0:1], no_bias, vector_here[1:2]], axis=1)
    kv_bias = jnp.concatenate([no_bias, vector_here[4:5]], axis=1)
    x_rows = decoder_input.reshape(rows, depth)
    slices, *contract_sent = hold([slices, *contract_sent], key_bias)
    contract = [contract, *contract_sent]
    ahead, across = jnp.stack(contract[:2]), jnp.stack(contract[2:])
    qkv = project_columns("self_qkv", *input_rows, slices, 0, 3, qkv_bias)
    qkv, *late_arrived = hold([qkv, *late_sent])
    late = lax.all_gather(place_dp(late, late_arrived), "index", axis=0, tiled=False)
    self_out, self_stat = attend(True, qkv, 0, qkv, 1, 2, key_bias[:, None, :])
    self_out, ahead_far, across_far = hold(
        [self_out, exchange_dp(ahead, 2), exchange_dp(across, 1)]
    )
    self_got = swap(self_out)
    square = gather_index(hold(square, self_out))
    self_got, square = hold([self_got, square])
    ahead = jnp.stack([ahead, ahead_far])
    across = jnp.stack([across, across_far])
    contract_sent = [exchange_dp(ahead, 1), exchange_dp(across, 2)]
    self_mixed, first_in, first_low, cross_query = first_forward(
        self_got, x_rows, square, vectors, ahead_far
    )
    (slices,) = hold([slices], first_low)
    memory_kv = project_columns("memory_kv", *memory_rows, slices, 3, 2, kv_bias)
    cross_query = swap(cross_query)[:, None]
    cross_out, cross_stat = attend(
        False, cross_query, 0, memory_kv, 0, 1, key_bias[:, None, :]
    )
    ahead_far, across_far = hold(contract_sent, cross_out)
    contract = [ahead, ahead_far, across, across_far]
    contract += [exchange(piece, 1) for piece in contract]
    places = lax.axis_index("dp") ^ jnp.array(DP_ORDER, jnp.int32)
    (
        cross_mixed,
        layer_output,
        wide_grad,
        *contract_grads,
        inner_total,
        second_grad,
        cross_low,
        cross_mix_grad,
        stats,
    ) = ffn(
        (order, places),
        swap(cross_out),
        first_in,
        late,
        contract,
        vectors,
        vectors[6:10].reshape(groups * count, -1),
        output_grad.reshape(rows, depth),
    )
    third_stat, second_stat = stats[:8], stats[8:]

    expand_part_sum = lax.psum_scatter(wide_grad, "index", scatter_dimension=0, tiled=False)
    ahead, ahead_far, across, across_far = contract_grads[:4]
    cores = [exchange(piece, 1) for piece in contract_grads[4:]]
    cross_mix_got, *contract_sent = hold(
        [swap(cross_mix_grad), add(ahead_far, cores[1]), add(across_far, cores[3])]
    )
    contract_got = [exchange_dp(contract_sent[0], 1), exchange_dp(contract_sent[1], 2)]
    cross_dq, cross_dkv, prior_rows = attend_back(
        False,
        cross_query,
        0,
        memory_kv,
        0,
        1,
        cross_mix_got,
        cross_stat,
        key_bias[:, None, :],
        contract_sent[0],
    )
    memory_mine, memory_other, kv_grads, kv_total = project_columns_back(
        "memory_kv_back", order, *memory_rows, [cross_dkv], slices, 3, 2
    )
    cross_dq, *contract_got = hold([cross_dq, *contract_got], memory_mine)
    contract_next = [
        add((ahead, 1), (cores[0], 1), (contract_got[0], 1)),
        add((across, 1), (cores[2], 1), (contract_got[1], 1)),
    ]
    cross_dq_got, *contract_next = hold([swap(cross_dq), *contract_next])
    contract_last = [exchange_dp(contract_next[0], 2), exchange_dp(contract_next[1], 1)]
    query_low, first_grad, self_low, self_mix_grad, first_stat = first_back(
        cross_dq_got, second_grad, first_in, square, vectors, memory_mine
    )
    kv_sum = HalvingDp(kv_grads)
    kv_got = exchange_dp(kv_sum.first(), 1)
    memory_sum = both_cores(memory_mine, exchange(memory_other, 1))
    memory_sent = firsts(memory_sum)
    square_mine, square_other = weight_grads(
        (count, groups, part, depth),
        order,
        self_mixed,
        self_low,
        first_low,
        query_low,
        cross_mixed,
        cross_low,
    )
    square_sum = both_cores(square_mine, exchange(square_other, 1))
    square_sent = firsts(square_sum)
    self_mix_got, kv_got = hold(
        [swap(self_mix_grad), kv_got], *memory_sent, *square_sent
    )
    kv_last = exchange_dp(kv_sum.second(kv_got), 2)
    memory_got = send_first(*memory_sent)
    square_got = send_first(*square_sent)
    self_dq, self_dkv, _ = attend_back(
        True, qkv, 0, qkv, 1, 2, self_mix_got, self_stat, self_stat, square_mine
    )
    expand_sum = HalvingDp(expand_part_sum)
    self_dq, expand_sent, kv_last, *contract_last = hold(
        [self_dq, expand_sum.first(), kv_last, *contract_last]
    )
    dx_mine, dx_other, qkv_slice_grads, qkv_total = project_columns_back(
        "self_qkv_back", order, *input_rows, [self_dq, self_dkv], slices, 0, 3
    )
    dx_mine, dx_other, *got = hold([dx_mine, dx_other, *memory_got, *square_got])
    own = jnp.concatenate(
        [qkv_total[:, :width], qkv_total[:, 2 * width :], kv_total[:, width:]], axis=0
    )
    own = lax.dynamic_update_slice(
        jnp.zeros((3, depth), jnp.float32), own, (jnp.int32(0), place * width)
    )
    vector_grads = jnp.concatenate(
        [
            own[:2],
            first_stat[1:2],
            first_stat[0:1],
            own[2:],
            second_stat[0:1],
            inner_total.reshape(hidden // depth, depth),
            third_stat[0:1],
            first_stat[2:4],
            second_stat[1:3],
            third_stat[1:3],
        ],
        axis=0,
    )
    vector_size = vector_rows * vector_width
    question_size = seqs * question_width
    vector_send = (
        vector_grads.reshape(vector_rows, groups, count, vector_width)
        .transpose(1, 2, 0, 3)
        .reshape(groups, count, vector_size)
    )
    vector_send = jnp.pad(
        vector_send, ((0, 0), (0, 0), (0, extra_rows * width - vector_size))
    ).reshape(groups, count, extra_rows, width)
    slice_grads = jnp.concatenate([qkv_slice_grads, vector_send.astype(low)], axis=2)
    slice_own, slice_sent = sends_dp(slice_grads)
    dx_other, *got = hold([dx_other, *got], slice_grads)
    dx_got = exchange(dx_other, 1)
    square_rows = square_sum.middle
    last = seconds((square_sum, *got[2:], 0), (memory_sum, *got[:2], 0))
    prior_rows, *contract_last = hold([prior_rows, *contract_last], *last)
    last = send_last(*last)
    prior_arrived = small_send(prior_rows.reshape(seqs, slots, MEM_P).sum(axis=-1))
    dx_got, *last = hold([dx_got, *last])
    dx_sum = both_cores(dx_mine, dx_got)
    contract_sum = Halving(
        [
            [(one.reshape((-1,) + one.shape[-2:]), k % 2) for one in parts]
            for k, parts in enumerate(
                [(ahead, cores[0], contract_got[0], contract_last[0])] * 2
                + [(across, cores[2], contract_got[1], contract_last[1])] * 2
            )
        ]
    )
    dx_sent = firsts(dx_sum, contract_sum)
    got = send_first(*dx_sent)
    square_last, memory_last = split_rows(hold(last, *dx_sent), square_rows)
    square_far = HalvingDp(square_sum.finish(*square_last).reshape(groups, 3 * part, depth))
    square_got = exchange_dp(square_far.first(), 1)
    expand_got = exchange_dp(hold([expand_sent], *dx_sent)[0], 1)
    slice_sum = sum(
        (one.astype(jnp.float32) for one in hold(slice_sent, *dx_sent)),
        slice_own.astype(jnp.float32),
    )
    (prior_arrived,) = hold([prior_arrived], *dx_sent)
    prior_grad = jnp.where(usable, small_take(prior_arrived, (seqs, slots)), 0.0)
    score_doc = jnp.where(
        usable, prior_grad - passage_prob * jnp.sum(prior_grad, axis=1, keepdims=True), 0.0
    )
    question_part = jnp.einsum(
        "sk,skc->sc",
        jnp.where(owned_slot, score_doc, 0.0),
        picked.astype(jnp.float32),
        precision=lax.Precision.HIGHEST,
    )

    question_send = (
        question_part.reshape(seqs, count, question_width)
        .transpose(1, 0, 2)
        .reshape(count, question_size)
    )
    question_send = jnp.pad(
        question_send,
        ((0, 0), (vector_size, extra_rows * width - vector_size - question_size)),
    ).reshape(count, extra_rows, width)
    slice_sum = jnp.concatenate(
        [
            slice_sum[:, : 3 * part],
            kv_sum.finish(kv_last),
            slice_sum[:, 3 * part :] + question_send,
        ],
        axis=1,
    )
    arrived, square_got, expand_got, *got = hold(
        [swap(slice_sum.astype(low)), square_got, expand_got, *got]
    )
    expand_last = exchange_dp(expand_sum.second(expand_got), 2)
    start = dx_sum.middle
    last = send_last(*seconds((dx_sum, *got, 0), (contract_sum, *got, start)))
    square_last = exchange_dp(square_far.second(square_got), 2)
    dx_last, contract_last = split_rows(last, start)
    input_gradient = first_grad + dx_sum.finish(*dx_last)
    contract_sum = contract_sum.finish(*contract_last)
    memory_last = hold(memory_last, *got)
    memory_gradient = memory_sum.finish(*memory_last).reshape(encoder_memory.shape)
    arrived = arrived.astype(jnp.float32)
    split_grads = (
        arrived[:, : 5 * part]
        .reshape(count, 5, part, width)
        .transpose(1, 2, 0, 3)
        .reshape(5, part, depth)
    )
    extra_sum = jnp.sum(arrived[:, 5 * part :].reshape(count, extra_rows * width), axis=0)
    vector_sum = extra_sum[:vector_size].reshape(vector_rows, vector_width)
    question_gradient = extra_sum[vector_size : vector_size + question_size].reshape(
        seqs, question_width
    )

    expand_sum = (
        expand_sum.finish(expand_last)
        .reshape(hidden // depth, part, depth)
        .transpose(1, 0, 2)
        .reshape(part, hidden)
    )
    square_total = square_far.finish(square_last).reshape(3, part, depth)
    attention_sum = jnp.concatenate(
        [split_grads[:3], square_total[:2], split_grads[3:], square_total[2:]], axis=0
    )

    new_attention = adam_update(
        attention_weight,
        attention_mean,
        attention_square,
        attention_sum,
        rate_attention,
        decay_matrix,
    )
    new_expand = adam_update(
        expand_weight, expand_mean, expand_square, expand_sum, rate_expand, decay_matrix
    )
    new_contract = adam_update(
        contract_weight, contract_mean, contract_square, contract_sum, rate_contract, decay_matrix
    )
    new_vector = adam_update(
        vector_params, vector_mean, vector_square, vector_sum, rate_vector, 0.0
    )
    return (
        layer_output.reshape(decoder_input.shape),
        input_gradient.reshape(decoder_input.shape),
        memory_gradient,
        question_gradient,
        *new_attention,
        *new_expand,
        *new_contract,
        *new_vector,
    )


def body(sizes, *arrays):
    depth = arrays[0].shape[2]
    if sizes == (4, 8) and depth // 8 % 128 == 0:
        return head_body(*arrays)
    return general_body(*arrays)


def solution(mesh):
    return jax.shard_map(
        partial(body, (mesh.shape["dp"], mesh.shape["index"])),
        mesh=mesh,
        in_specs=(
            P("dp", "index", None),
            P("dp", "index", None),
            P("dp", "index"),
            P("index", None),
            P("dp", None),
            P("dp"),
            P("dp", "index", None),
            P(None, ("dp", "index"), None),
            P(("dp", "index"), None),
            P(("dp", "index"), None),
            P(None, ("dp", "index")),
            P(None, ("dp", "index"), None),
            P(None, ("dp", "index"), None),
            P(("dp", "index"), None),
            P(("dp", "index"), None),
            P(("dp", "index"), None),
            P(("dp", "index"), None),
            P(None, ("dp", "index")),
            P(None, ("dp", "index")),
        ),
        out_specs=(
            P("dp", "index", None),
            P("dp", "index", None),
            P("dp", "index", None),
            P("dp", "index"),
            P(None, ("dp", "index"), None),
            P(None, ("dp", "index"), None),
            P(None, ("dp", "index"), None),
            P(("dp", "index"), None),
            P(("dp", "index"), None),
            P(("dp", "index"), None),
            P(("dp", "index"), None),
            P(("dp", "index"), None),
            P(("dp", "index"), None),
            P(None, ("dp", "index")),
            P(None, ("dp", "index")),
            P(None, ("dp", "index")),
        ),
        check_vma=False,
    )
```

```python
from functools import partial

import jax
import jax.numpy as jnp
from jax import lax
from jax.experimental import pallas as pl
from jax.experimental.pallas import tpu as pltpu
from jax.sharding import PartitionSpec as P

HEADS = 16
MEM_P = 192
STEP = 10


negative_fill = -1e30
norm_eps = 1e-05
beta_first = 0.9
beta_second = 0.999
adam_eps = 1e-08
decay_matrix = 0.01
rate_attention = 0.1
rate_expand = 0.02
rate_contract = 0.01
rate_vector = 0.2


def layer_norm(hidden, norm_gain, norm_shift):
    center = hidden - jnp.mean(hidden, axis=-1, keepdims=True)
    spread = jnp.mean(center * center, axis=-1, keepdims=True)
    return center * lax.rsqrt(spread + norm_eps) * norm_gain + norm_shift


def split_heads(matrix):
    return matrix.reshape(matrix.shape[0], matrix.shape[1], HEADS, matrix.shape[2] // HEADS)


def merge_heads(matrix):
    return matrix.reshape(matrix.shape[0], matrix.shape[1], matrix.shape[2] * matrix.shape[3])


def project(left_side, weight):
    return jnp.einsum("srd,de->sre", left_side, weight, preferred_element_type=jnp.float32)


def project_back(gradient, weight):
    return jnp.einsum("sre,de->srd", gradient, weight, preferred_element_type=jnp.float32)


def weight_grad(left_side, gradient):
    return jnp.einsum("srd,sre->de", left_side, gradient, preferred_element_type=jnp.float32)


def row_total(values):
    return jnp.sum(values, axis=(0, 1))


def attend_forward(queries, key_rows, values, score_bias, allowed):
    scores = (
        jnp.einsum(
            "sqhd,skhd->shqk",
            split_heads(queries),
            split_heads(key_rows),
            preferred_element_type=jnp.float32,
        )
        * 0.125
        + score_bias
    )
    scores = jnp.where(allowed, scores, negative_fill)
    maximum = jnp.max(scores, axis=-1)
    exponent = jnp.exp(scores - maximum[..., None])
    partition = jnp.sum(exponent, axis=-1)
    attend_prob = exponent / partition[..., None]
    mixture = jnp.einsum(
        "shqk,skhd->sqhd",
        attend_prob.astype(jnp.bfloat16),
        split_heads(values),
        preferred_element_type=jnp.float32,
    )
    return (merge_heads(mixture).astype(jnp.bfloat16), attend_prob, maximum, partition)


def score_grads(grad_mixed, attend_prob, values):
    grad_prob = jnp.einsum(
        "sqhd,skhd->shqk",
        split_heads(grad_mixed),
        split_heads(values),
        preferred_element_type=jnp.float32,
    )
    row_inner = jnp.sum(attend_prob * grad_prob, axis=-1)
    return ((attend_prob * (grad_prob - row_inner[..., None])).astype(jnp.bfloat16), row_inner)


def to_queries(grad_score, key_rows):
    return (
        merge_heads(
            jnp.einsum(
                "shqk,skhd->sqhd",
                grad_score,
                split_heads(key_rows),
                preferred_element_type=jnp.float32,
            )
        )
        * 0.125
    )


def to_keys(grad_score, attend_prob, queries, grad_mixed):
    grad_key = (
        merge_heads(
            jnp.einsum(
                "shqk,sqhd->skhd",
                grad_score,
                split_heads(queries),
                preferred_element_type=jnp.float32,
            )
        )
        * 0.125
    )
    grad_value = merge_heads(
        jnp.einsum(
            "shqk,sqhd->skhd",
            attend_prob.astype(jnp.bfloat16),
            split_heads(grad_mixed),
            preferred_element_type=jnp.float32,
        )
    )
    return (grad_key, grad_value)


def adam_update(weight, moment_one, moment_two, gradient, step_rate, weight_decay):
    mean_new = beta_first * moment_one + (1.0 - beta_first) * gradient
    square_new = beta_second * moment_two + (1.0 - beta_second) * gradient * gradient
    mean_hat = mean_new / (1.0 - beta_first**STEP)
    square_hat = square_new / (1.0 - beta_second**STEP)
    updated = weight - step_rate * (
        mean_hat / (jnp.sqrt(square_hat) + adam_eps) + weight_decay * weight
    )
    return (updated, mean_new, square_new)


def general_body(
    decoder_input,
    encoder_memory,
    question_vectors,
    passage_vectors,
    passage_ids,
    valid_count,
    output_grad,
    attention_weight,
    expand_weight,
    contract_weight,
    vector_params,
    attention_mean,
    attention_square,
    expand_mean,
    expand_square,
    contract_mean,
    contract_square,
    vector_mean,
    vector_square,
):
    attention_low, expand_low, contract_low, vector_low = (
        lax.all_gather(attention_weight.astype(jnp.bfloat16), ("dp", "index"), axis=1, tiled=True),
        lax.all_gather(expand_weight.astype(jnp.bfloat16), ("dp", "index"), axis=0, tiled=True),
        lax.all_gather(contract_weight.astype(jnp.bfloat16), ("dp", "index"), axis=0, tiled=True),
        lax.all_gather(vector_params.astype(jnp.bfloat16), ("dp", "index"), axis=1, tiled=True),
    )
    vectors = vector_low.astype(jnp.float32)
    seqs_here, rows_here, model_width = decoder_input.shape
    shard_index = lax.axis_index("index")
    length = rows_here * lax.axis_size("index")
    ffn_width = expand_low.shape[1]
    self_query = (project(decoder_input, attention_low[0]) + vectors[0]).astype(jnp.bfloat16)
    self_key = project(decoder_input, attention_low[1]).astype(jnp.bfloat16)
    self_value = (project(decoder_input, attention_low[2]) + vectors[1]).astype(jnp.bfloat16)
    key_all, value_all = (
        lax.all_gather(self_key, "index", axis=1, tiled=True),
        lax.all_gather(self_value, "index", axis=1, tiled=True),
    )
    query_place = shard_index * rows_here + jnp.arange(rows_here)
    causal = (jnp.arange(length)[None, :] <= query_place[:, None])[None, None]
    self_mixed, self_prob, self_peak, self_total = attend_forward(
        self_query, key_all, value_all, 0.0, causal
    )
    first_in = (
        decoder_input.astype(jnp.float32) + project(self_mixed, attention_low[3]) + vectors[2]
    )
    first_out, first_back = jax.vjp(layer_norm, first_in, vectors[11], vectors[12])
    first_low = first_out.astype(jnp.bfloat16)
    cross_query = (project(first_low, attention_low[4]) + vectors[3]).astype(jnp.bfloat16)
    cross_key = project(encoder_memory, attention_low[5]).astype(jnp.bfloat16)
    cross_value = (project(encoder_memory, attention_low[6]) + vectors[4]).astype(jnp.bfloat16)
    memory_keys, memory_values = (
        lax.all_gather(cross_key, "index", axis=1, tiled=True),
        lax.all_gather(cross_value, "index", axis=1, tiled=True),
    )
    question_full = lax.all_gather(question_vectors, "index", axis=1, tiled=True)
    passages_here = passage_vectors.shape[0]
    local_ids = passage_ids - shard_index * passages_here
    owned_slot = (local_ids >= 0) & (local_ids < passages_here)
    picked = passage_vectors[jnp.clip(local_ids, 0, passages_here - 1)]
    local_scores = jnp.einsum(
        "sc,skc->sk", question_full, picked, preferred_element_type=jnp.float32
    )
    slots = passage_ids.shape[1]
    usable = jnp.arange(slots)[None, :] < valid_count[:, None]
    local_peak = jnp.max(jnp.where(owned_slot & usable, local_scores, negative_fill), axis=1)
    maximum = lax.pmax(local_peak, "index")
    local_exp = jnp.where(owned_slot & usable, jnp.exp(local_scores - maximum[:, None]), 0.0)
    exponent, scores = lax.psum((local_exp, jnp.where(owned_slot, local_scores, 0.0)), "index")
    masked = jnp.where(usable, scores, negative_fill)
    partition = jnp.sum(exponent, axis=1)
    passage_prob = exponent / partition[:, None]
    log_prior = masked - maximum[:, None] - jnp.log(partition)[:, None]
    memory_total = memory_keys.shape[1]
    bias_rows = jnp.repeat(log_prior, MEM_P, axis=1)
    key_bias = bias_rows[:, None, None, :]
    key_usable = ((jnp.arange(memory_total) // MEM_P)[None, :] < valid_count[:, None])[
        :, None, None, :
    ]
    cross_mixed, cross_prob, cross_peak, cross_total = attend_forward(
        cross_query, memory_keys, memory_values, key_bias, key_usable
    )
    second_in = first_out + project(cross_mixed, attention_low[7]) + vectors[5]
    second_out, second_back = jax.vjp(layer_norm, second_in, vectors[13], vectors[14])
    second_low = second_out.astype(jnp.bfloat16)
    inner_act = project(second_low, expand_low) + vectors[6:10].reshape(ffn_width)
    activated, gelu_back = jax.vjp(partial(jax.nn.gelu, approximate=False), inner_act)
    activ_low = activated.astype(jnp.bfloat16)
    third_in = second_out + project(activ_low, contract_low) + vectors[10]
    layer_output, third_back = jax.vjp(layer_norm, third_in, vectors[15], vectors[16])
    grad_third, gain_three, shift_three = third_back(output_grad.astype(jnp.float32))
    grad_ffn_low = grad_third.astype(jnp.bfloat16)
    grad_contract = weight_grad(activ_low, grad_ffn_low)
    (grad_inner,) = gelu_back(project_back(grad_ffn_low, contract_low))
    grad_inner_low = grad_inner.astype(jnp.bfloat16)
    grad_expand = weight_grad(second_low, grad_inner_low)
    grad_second = grad_third + project_back(grad_inner_low, expand_low)
    grad_second_in, gain_two, shift_two = second_back(grad_second)
    grad_cross_low = grad_second_in.astype(jnp.bfloat16)
    grad_cmix = project_back(grad_cross_low, attention_low[7]).astype(jnp.bfloat16)
    cross_score, cross_inner = score_grads(grad_cmix, cross_prob, memory_values)
    grad_cq = to_queries(cross_score, memory_keys)
    prior_part = (
        jnp.sum(cross_score, axis=(1, 2), dtype=jnp.float32)
        .reshape(seqs_here, slots, MEM_P)
        .sum(axis=-1)
    )
    prior_grad = jnp.where(usable, lax.psum(prior_part, "index"), 0.0)
    score_doc = jnp.where(
        usable, prior_grad - passage_prob * jnp.sum(prior_grad, axis=1, keepdims=True), 0.0
    )
    question_part = jnp.einsum(
        "sk,skc->sc",
        jnp.where(owned_slot, score_doc, 0.0),
        picked.astype(jnp.float32),
        precision=lax.Precision.HIGHEST,
    )
    question_gradient = lax.psum_scatter(question_part, "index", scatter_dimension=1, tiled=True)
    grad_cq_low = grad_cq.astype(jnp.bfloat16)
    grad_first = grad_second_in + project_back(grad_cq_low, attention_low[4])
    ck_part, cv_part = to_keys(cross_score, cross_prob, cross_query, grad_cmix)
    grad_ck, grad_cv = (
        lax.psum_scatter(
            ck_part.astype(jnp.bfloat16), "index", scatter_dimension=1, tiled=True
        ).astype(jnp.float32),
        lax.psum_scatter(
            cv_part.astype(jnp.bfloat16), "index", scatter_dimension=1, tiled=True
        ).astype(jnp.float32),
    )
    grad_ck_low = grad_ck.astype(jnp.bfloat16)
    grad_cv_low = grad_cv.astype(jnp.bfloat16)
    memory_gradient = project_back(grad_ck_low, attention_low[5]) + project_back(
        grad_cv_low, attention_low[6]
    )
    grad_first_in, gain_one, shift_one = first_back(grad_first)
    grad_self_low = grad_first_in.astype(jnp.bfloat16)
    grad_smix = project_back(grad_self_low, attention_low[3]).astype(jnp.bfloat16)
    self_score, row_inner = score_grads(grad_smix, self_prob, value_all)
    grad_sq = to_queries(self_score, key_all)
    key_part, value_part = to_keys(self_score, self_prob, self_query, grad_smix)
    grad_sk, grad_sv = (
        lax.psum_scatter(
            key_part.astype(jnp.bfloat16), "index", scatter_dimension=1, tiled=True
        ).astype(jnp.float32),
        lax.psum_scatter(
            value_part.astype(jnp.bfloat16), "index", scatter_dimension=1, tiled=True
        ).astype(jnp.float32),
    )
    grad_sq_low = grad_sq.astype(jnp.bfloat16)
    grad_sk_low = grad_sk.astype(jnp.bfloat16)
    grad_sv_low = grad_sv.astype(jnp.bfloat16)
    input_gradient = (
        grad_first_in
        + project_back(grad_sq_low, attention_low[0])
        + project_back(grad_sk_low, attention_low[1])
        + project_back(grad_sv_low, attention_low[2])
    )
    attention_grads = jnp.stack(
        [
            weight_grad(decoder_input, grad_sq_low),
            weight_grad(decoder_input, grad_sk_low),
            weight_grad(decoder_input, grad_sv_low),
            weight_grad(self_mixed, grad_self_low),
            weight_grad(first_low, grad_cq_low),
            weight_grad(encoder_memory, grad_ck_low),
            weight_grad(encoder_memory, grad_cv_low),
            weight_grad(cross_mixed, grad_cross_low),
        ]
    )
    vector_grads = jnp.concatenate(
        [
            jnp.stack(
                [
                    row_total(grad_sq),
                    row_total(grad_sv),
                    row_total(grad_first_in),
                    row_total(grad_cq),
                    row_total(grad_cv),
                    row_total(grad_second_in),
                ]
            ),
            row_total(grad_inner).reshape(ffn_width // model_width, model_width),
            jnp.stack(
                [
                    row_total(grad_third),
                    gain_one,
                    shift_one,
                    gain_two,
                    shift_two,
                    gain_three,
                    shift_three,
                ]
            ),
        ]
    )
    attention_sum, expand_sum, contract_sum, vector_sum = (
        lax.psum_scatter(attention_grads, ("dp", "index"), scatter_dimension=1, tiled=True),
        lax.psum_scatter(grad_expand, ("dp", "index"), scatter_dimension=0, tiled=True),
        lax.psum_scatter(grad_contract, ("dp", "index"), scatter_dimension=0, tiled=True),
        lax.psum_scatter(vector_grads, ("dp", "index"), scatter_dimension=1, tiled=True),
    )
    new_attention = adam_update(
        attention_weight,
        attention_mean,
        attention_square,
        attention_sum,
        rate_attention,
        decay_matrix,
    )
    new_expand = adam_update(
        expand_weight, expand_mean, expand_square, expand_sum, rate_expand, decay_matrix
    )
    new_contract = adam_update(
        contract_weight, contract_mean, contract_square, contract_sum, rate_contract, decay_matrix
    )
    new_vector = adam_update(
        vector_params, vector_mean, vector_square, vector_sum, rate_vector, 0.0
    )
    return (
        layer_output.astype(jnp.bfloat16),
        input_gradient,
        memory_gradient,
        question_gradient,
        new_attention[0],
        new_attention[1],
        new_attention[2],
        new_expand[0],
        new_expand[1],
        new_expand[2],
        new_contract[0],
        new_contract[1],
        new_contract[2],
        new_vector[0],
        new_vector[1],
        new_vector[2],
    )


NT = (((1,), (1,)), ((), ()))
NN = (((1,), (0,)), ((), ()))
TN = (((0,), (0,)), ((), ()))
CHIPS = 4
DP_ORDER = (0, 2, 1, 3)
VMEM_LIMIT = 56 << 20


def dot(left_side, right_side, dims):
    return lax.dot_general(left_side, right_side, dims, preferred_element_type=jnp.float32)


def norm_parts(hidden):
    center = hidden - jnp.mean(hidden, axis=-1, keepdims=True)
    inverse = lax.rsqrt(jnp.mean(center * center, axis=-1, keepdims=True) + norm_eps)
    return center * inverse, inverse


def norm_back(gradient, unit, inverse, gain):
    scaled = gradient * gain
    return inverse * (
        scaled
        - jnp.mean(scaled, axis=-1, keepdims=True)
        - unit * jnp.mean(scaled * unit, axis=-1, keepdims=True)
    )


def column_sum(values):
    return jnp.sum(values, axis=0, keepdims=True)


def join(parts, place=None):
    picked = [parts[j] if place is None else parts[j, place] for j in range(parts.shape[0])]
    return jnp.concatenate(
        [block.reshape(block.shape[0] * block.shape[1], block.shape[2]) for block in picked],
        axis=1,
    )


def spread(out_ref, value):
    count, seqs, rows, width = out_ref.shape
    for j in range(count):
        out_ref[j] = value[:, j * width : (j + 1) * width].reshape(seqs, rows, width)


def times(activation, weight):
    count, groups, rows, width = weight.shape
    depth = count * rows
    total = None
    for d in range(groups):
        part = dot(
            activation[:, d * depth : (d + 1) * depth], weight[:, d].reshape(depth, width), NN
        )
        total = part if total is None else total + part
    return total


def times_back(gradient, weight):
    count, groups, rows, width = weight.shape
    depth = count * rows
    return jnp.concatenate(
        [dot(gradient, weight[:, d].reshape(depth, width), NT) for d in range(groups)], axis=1
    )


def outer(out_ref, left_side, gradient):
    count, groups, rows, width = out_ref.shape
    depth = count * rows
    for d in range(groups):
        out_ref[:, d] = (
            dot(left_side[:, d * depth : (d + 1) * depth], gradient, TN)
            .astype(jnp.bfloat16)
            .reshape(count, rows, width)
        )


def whole(array):
    return pl.BlockSpec(array.shape, lambda *_, rank=len(array.shape): (0,) * rank)


def shape(dims, dtype):
    return jax.ShapeDtypeStruct(tuple(dims), dtype)


def params():
    return pltpu.CompilerParams(vmem_limit_bytes=VMEM_LIMIT)


def cost(flops, moved):
    return pl.CostEstimate(flops=int(flops) // 16, bytes_accessed=int(moved) // 16, transcendentals=0)


def in_head(dims, head_width, head):
    return lax.broadcasted_iota(jnp.int32, dims, 1) // head_width == head


def attend_forward_kernel(causal, head_width, q_ref, k_ref, v_ref, bias_ref, out_ref, stat_ref):
    count, _, tile, width = q_ref.shape
    keys = k_ref.shape[0] * k_ref.shape[2]
    key_rows, values = k_ref[...].reshape(keys, width), v_ref[...].reshape(keys, width)
    step = 4
    rows = step * tile
    for b in range(count // step):
        queries = q_ref[b * step : (b + 1) * step].reshape(rows, width)
        seen = (b + 1) * rows if causal else keys
        mixed = None
        for h in range(width // head_width):
            mask = in_head((rows, width), head_width, h)
            scores = dot(
                jnp.where(mask, queries * 0.125, 0).astype(jnp.bfloat16), key_rows[:seen], NT
            )
            if causal:
                corner = scores[:, seen - rows :]
                corner = jnp.where(
                    lax.broadcasted_iota(jnp.int32, corner.shape, 1)
                    <= lax.broadcasted_iota(jnp.int32, corner.shape, 0),
                    corner,
                    negative_fill,
                )
                if b == 0:
                    scores = corner
                else:
                    scores = jnp.concatenate([scores[:, : seen - rows], corner], axis=1)
            else:
                scores = scores + bias_ref[0]
            peak = jnp.max(scores, axis=1, keepdims=True)
            exponent = jnp.exp(scores - peak)
            total = jnp.sum(exponent, axis=1, keepdims=True)
            part = dot(exponent.astype(jnp.bfloat16), values[:seen], NN) * (1.0 / total)
            mixed = part if mixed is None else jnp.where(mask, part, mixed)
            log_total = jnp.broadcast_to(peak + jnp.log(total), (rows, 128))
            stat_ref[0, h : h + 1, b * rows : (b + 1) * rows] = log_total.T[0:1]
        out_ref[b * step : (b + 1) * step] = mixed.astype(jnp.bfloat16).reshape(
            step, 1, tile, width
        )


def attend_backward_kernel(
    causal,
    head_width,
    q_ref,
    k_ref,
    v_ref,
    grad_ref,
    stat_ref,
    bias_ref,
    _,
    dq_ref,
    dkv_ref,
    prior_ref,
    dk_sum,
    dv_sum,
    prior_sum,
):
    count, _, tile, width = q_ref.shape
    keys = k_ref.shape[0] * k_ref.shape[2]
    key_rows, values = k_ref[...].reshape(keys, width), v_ref[...].reshape(keys, width)
    step = 2
    rows = step * tile
    if not causal:
        bias = jnp.broadcast_to(bias_ref[0], (128, keys)).T[:, :1]
    dk_sum[...] = jnp.zeros_like(dk_sum)
    dv_sum[...] = jnp.zeros_like(dv_sum)
    if not causal:
        prior_sum[...] = jnp.zeros_like(prior_sum)
    for b in range(count // step):
        queries = q_ref[b * step : (b + 1) * step].reshape(rows, width)
        gradient = grad_ref[b * step : (b + 1) * step].reshape(rows, width)
        seen = (b + 1) * rows if causal else keys
        query_grad = None
        for h in range(width // head_width):
            mask = in_head((rows, width), head_width, h)
            one_query = jnp.where(mask, queries * 0.125, 0).astype(jnp.bfloat16)
            one_grad = jnp.where(mask, gradient, 0).astype(jnp.bfloat16)
            scores = dot(key_rows[:seen], one_query, NT)
            if causal:
                corner = scores[seen - rows :]
                corner = jnp.where(
                    lax.broadcasted_iota(jnp.int32, corner.shape, 0)
                    <= lax.broadcasted_iota(jnp.int32, corner.shape, 1),
                    corner,
                    negative_fill,
                )
                if b == 0:
                    scores = corner
                else:
                    scores = jnp.concatenate([scores[: seen - rows], corner], axis=0)
            else:
                scores = scores + bias
            prob = jnp.exp(scores - stat_ref[0, h : h + 1, b * rows : (b + 1) * rows])
            grad_prob = dot(values[:seen], one_grad, NT)
            inner = jnp.sum(prob * grad_prob, axis=0, keepdims=True)
            grad_score = prob * (grad_prob - inner)
            score_low = grad_score.astype(jnp.bfloat16)
            dv_sum[:seen] += dot(prob.astype(jnp.bfloat16), one_grad, NN)
            dk_sum[:seen] += dot(score_low, one_query, NN)
            if not causal:
                partial_sum = grad_score[:, :128]
                for piece in range(128, rows, 128):
                    partial_sum = partial_sum + grad_score[:, piece : piece + 128]
                prior_sum[...] += partial_sum
            part = dot(score_low, key_rows[:seen], TN)
            query_grad = part if query_grad is None else jnp.where(mask, part, query_grad)
        dq_ref[b * step : (b + 1) * step] = (
            (query_grad * 0.125).astype(jnp.bfloat16).reshape(step, 1, tile, width)
        )
    dkv_ref[:, 0] = dk_sum[...].astype(jnp.bfloat16).reshape(k_ref.shape)
    dkv_ref[:, 1] = dv_sum[...].astype(jnp.bfloat16).reshape(k_ref.shape)
    if causal:
        prior_ref[...] = jnp.zeros_like(prior_ref)
    else:
        prior_ref[0] = column_sum(prior_sum[...].T)


def pick(array, place):
    count, _, _, rows, width = array.shape
    return pl.BlockSpec((count, None, 1, rows, width), lambda s: (0, place, s, 0, 0))


def attend(causal, queries, query_at, keys, key_at, value_at, bias):
    count, _, seqs, tile, width = queries.shape
    key_rows = keys.shape[0] * keys.shape[3]
    head_width = width * count // HEADS
    length = count * tile
    heads = width // head_width
    return pl.pallas_call(
        partial(attend_forward_kernel, causal, head_width),
        grid=(seqs,),
        in_specs=[
            pick(queries, query_at),
            pick(keys, key_at),
            pick(keys, value_at),
            pl.BlockSpec(memory_space=pl.ANY)
            if causal
            else pl.BlockSpec((1, 1, key_rows), lambda s: (s, 0, 0)),
        ],
        out_specs=[
            pl.BlockSpec((count, 1, tile, width), lambda s: (0, s, 0, 0)),
            pl.BlockSpec((1, heads, length), lambda s: (s, 0, 0)),
        ],
        out_shape=[
            shape((count, seqs, tile, width), jnp.bfloat16),
            shape((seqs, heads, length), jnp.float32),
        ],
        compiler_params=params(),
        cost_estimate=cost(
            16 * seqs * length * key_rows * width, 4 * seqs * (length + key_rows) * width
        ),
        name="attend_self" if causal else "attend_memory",
    )(queries, keys, keys, bias)


def attend_back(
    causal, queries, query_at, keys, key_at, value_at, gradient, stat, bias, after
):
    count, _, seqs, tile, width = queries.shape
    key_tile = keys.shape[3]
    key_rows = count * key_tile
    head_width = width * count // HEADS
    length = count * tile
    heads = width // head_width
    return pl.pallas_call(
        partial(attend_backward_kernel, causal, head_width),
        grid=(seqs,),
        in_specs=[
            pick(queries, query_at),
            pick(keys, key_at),
            pick(keys, value_at),
            pl.BlockSpec((count, 1, tile, width), lambda s: (0, s, 0, 0)),
            pl.BlockSpec((1, heads, length), lambda s: (s, 0, 0)),
            pl.BlockSpec(memory_space=pl.ANY)
            if causal
            else pl.BlockSpec((1, 1, key_rows), lambda s: (s, 0, 0)),
            pl.BlockSpec(memory_space=pl.ANY),
        ],
        out_specs=[
            pl.BlockSpec((count, 1, tile, width), lambda s: (0, s, 0, 0)),
            pl.BlockSpec((count, 2, 1, key_tile, width), lambda s: (0, 0, s, 0, 0)),
            pl.BlockSpec((1, 1, key_rows), lambda s: (s, 0, 0)),
        ],
        out_shape=[
            shape((count, seqs, tile, width), jnp.bfloat16),
            shape((count, 2, seqs, key_tile, width), jnp.bfloat16),
            shape((seqs, 1, key_rows), jnp.float32),
        ],
        scratch_shapes=[
            pltpu.VMEM((key_rows, width), jnp.float32),
            pltpu.VMEM((key_rows, width), jnp.float32),
            pltpu.VMEM((key_rows, 128), jnp.float32),
        ],
        compiler_params=params(),
        cost_estimate=cost(
            40 * seqs * length * key_rows * width, 8 * seqs * (length + key_rows) * width
        ),
        name="attend_self_back" if causal else "attend_memory_back",
    )(queries, keys, keys, gradient, stat, bias, after)


def take_columns(scratch, slices, first):
    width = slices.shape[3]
    depth = scratch.shape[0]
    rows = depth // (slices.shape[0] * slices.shape[1])
    for m in range(scratch.shape[1] // width):
        start = (first + m) * rows
        scratch[:, m * width : (m + 1) * width] = slices[:, :, start : start + rows].reshape(
            depth, width
        )


def columns_kernel(first, start, seqs, rows, row_ref, slice_ref, bias_ref, out_ref, weight, taken, sem):
    def copy(i):
        return pltpu.make_async_copy(
            row_ref.at[i, :, pl.ds(start, rows)], taken.at[i], sem.at[i]
        )

    count, many = out_ref.shape[:2]
    width = out_ref.shape[4]
    for i in range(count):
        copy(i).start()
    take_columns(weight, slice_ref, first)
    for i in range(count):
        copy(i).wait()
        result = dot(taken[i].reshape(seqs * rows, weight.shape[0]), weight[...], NN) + bias_ref[...]
        for m in range(many):
            out_ref[i, m] = (
                result[:, m * width : (m + 1) * width]
                .astype(jnp.bfloat16)
                .reshape(seqs, rows, width)
            )


def project_columns(name, gathered_rows, start, rows, slices, first, many, bias):
    count, seqs, _, depth = gathered_rows.shape
    width = slices.shape[3]
    out = shape((count, many, seqs, rows, width), jnp.bfloat16)
    return pl.pallas_call(
        partial(columns_kernel, first, start, seqs, rows),
        grid=(1,),
        in_specs=[pl.BlockSpec(memory_space=pl.ANY), whole(slices), whole(bias)],
        out_specs=whole(out),
        out_shape=out,
        scratch_shapes=[
            pltpu.VMEM((depth, many * width), jnp.bfloat16),
            pltpu.VMEM((count, seqs, rows, depth), jnp.bfloat16),
            pltpu.SemaphoreType.DMA((count,)),
        ],
        compiler_params=params(),
        cost_estimate=cost(
            2 * many * count * seqs * rows * depth * width, 2 * count * seqs * rows * depth
        ),
        name=name,
    )(gathered_rows, slices, bias)


def columns_back_kernel(first, start, order, row_ref, *refs):
    grad_refs, (slice_ref, mine_out, other_out, dw_ref, bias_ref) = refs[:-12], refs[-12:-7]
    weight, taken, gradients, moved, total, in_sem, out_sem = refs[-7:]
    count, seqs, rows, depth = taken.shape
    half = count // 2

    def bring(r):
        return pltpu.make_async_copy(
            row_ref.at[order[r], :, pl.ds(start, rows)], taken.at[r], in_sem.at[r]
        )

    def send(r):
        there = (mine_out, other_out)[r // half].at[r % half, 0]
        return pltpu.make_async_copy(moved.at[r], there, out_sem.at[r])

    for r in range(count):
        bring(r).start()
    take_columns(weight, slice_ref, first)
    size = seqs * rows
    for r in range(count):
        i = order[r]
        pieces = []
        for grad_ref in grad_refs:
            width = grad_ref.shape[-1]
            for m in range(grad_ref.shape[1] if len(grad_ref.shape) == 5 else 1):
                piece = grad_ref[i, m] if len(grad_ref.shape) == 5 else grad_ref[i]
                pieces.append(piece.reshape(size, width))
        gradient = jnp.concatenate(pieces, axis=1)
        gradients[r * size : (r + 1) * size] = gradient
        moved[r] = dot(gradient, weight[...], NT).astype(jnp.bfloat16)
        send(r).start()
    whole_gradient = gradients[...]
    bias_ref[...] = column_sum(whole_gradient.astype(jnp.float32))
    for r in range(count):
        bring(r).wait()
    total[...] = dot(whole_gradient, taken[...].reshape(count * size, depth), TN)
    groups, shards, all_rows, _ = dw_ref.shape
    part = depth // (groups * shards)
    for m in range(all_rows // part):
        dw_ref[:, :, m * part : (m + 1) * part] = (
            total[m * width : (m + 1) * width]
            .T.astype(jnp.bfloat16)
            .reshape(groups, shards, part, width)
        )
    for r in range(count):
        send(r).wait()


def project_columns_back(name, order, gathered_rows, start, rows, gradients, slices, first, many):
    count, seqs, _, depth = gathered_rows.shape
    half = count // 2
    groups, shards, _, width = slices.shape
    part = depth // (groups * shards)
    anywhere = pl.BlockSpec(memory_space=pl.ANY)
    halves = shape((half, 1, seqs * rows, depth), jnp.bfloat16)
    dw_shape = shape((groups, shards, many * part, width), jnp.bfloat16)
    bias = shape((1, many * width), jnp.float32)
    return pl.pallas_call(
        partial(columns_back_kernel, first, start),
        grid_spec=pltpu.PrefetchScalarGridSpec(
            num_scalar_prefetch=1,
            grid=(1,),
            in_specs=[anywhere, *[whole(array) for array in gradients], whole(slices)],
            out_specs=[anywhere, anywhere, whole(dw_shape), whole(bias)],
            scratch_shapes=[
                pltpu.VMEM((depth, many * width), jnp.bfloat16),
                pltpu.VMEM((count, seqs, rows, depth), jnp.bfloat16),
                pltpu.VMEM((count * seqs * rows, many * width), jnp.bfloat16),
                pltpu.VMEM((count, seqs * rows, depth), jnp.bfloat16),
                pltpu.VMEM((many * width, depth), jnp.float32),
                pltpu.SemaphoreType.DMA((count,)),
                pltpu.SemaphoreType.DMA((count,)),
            ],
        ),
        out_shape=[halves, halves, dw_shape, bias],
        compiler_params=params(),
        cost_estimate=cost(
            4 * many * count * seqs * rows * depth * width, 4 * count * seqs * rows * depth
        ),
        name=name,
    )(order, gathered_rows, *gradients, slices)


def gathered(weights, width, place):
    count, groups, rows, _ = weights.shape
    return pl.BlockSpec((count, groups, rows, width), lambda *_: (0, 0, 0, place))


def first_kernel(
    mixed_ref, x_ref, out_w, query_w, vector_ref, _, mixed_out, in_out, low_out, query_out
):
    mixed = join(mixed_ref)
    mixed_out[...] = mixed
    first_in = x_ref[...].astype(jnp.float32) + times(mixed, out_w) + vector_ref[2:3]
    in_out[...] = first_in
    unit, _ = norm_parts(first_in)
    low = (unit * vector_ref[11:12] + vector_ref[12:13]).astype(jnp.bfloat16)
    low_out[...] = low
    spread(query_out, (times(low, query_w) + vector_ref[3:4]).astype(jnp.bfloat16))


def first_forward(mixed, x_rows, weights, vectors, after):
    rows, depth = x_rows.shape
    return pl.pallas_call(
        first_kernel,
        grid=(1,),
        in_specs=[
            whole(mixed),
            whole(x_rows),
            gathered(weights, depth, 0),
            gathered(weights, depth, 1),
            whole(vectors),
            pl.BlockSpec(memory_space=pl.ANY),
        ],
        out_specs=[whole(x_rows), whole(x_rows), whole(x_rows), whole(mixed)],
        out_shape=[
            shape((rows, depth), jnp.bfloat16),
            shape((rows, depth), jnp.float32),
            shape((rows, depth), jnp.bfloat16),
            shape(mixed.shape, jnp.bfloat16),
        ],
        compiler_params=params(),
        cost_estimate=cost(4 * rows * depth * depth, 4 * depth * depth),
        name="first_forward",
    )(mixed, x_rows, weights, weights, vectors, after)


def ffn_kernel(
    order,
    places,
    mixed_ref,
    first_ref,
    out_w,
    vector_ref,
    bias_ref,
    grad_ref,
    wide_ref,
    *refs,
):
    contract_refs, refs = refs[:8], refs[8:]
    mixed_out, layer_out, wide_grad = refs[:3]
    contract_grads, refs = refs[3:11], refs[11:]
    dbias_ref, second_grad, cross_low, mixed_grad, stat_out, columns, contracts = refs[:7]
    active, slope, low, third_low, second_in, total, wide_sem, contract_sem = refs[7:]
    blocks, count, groups, rows, block = columns.shape
    part = block // CHIPS
    depth = vector_ref.shape[1]

    def wide_copies(t, array, outward):
        result = []
        for k in range(CHIPS):
            column = pl.multiple_of(order[t % 2 * CHIPS + k] * part, part)
            row = pl.multiple_of(places[t // 2] * rows, rows)
            there = array.at[:, :, pl.ds(row, rows), pl.ds(column, part)]
            here = columns.at[t, :, :, :, pl.ds(k * part, part)]
            ends = (here, there) if outward else (there, here)
            result.append(pltpu.make_async_copy(*ends, wide_sem.at[t, k]))
        return result

    def contract_copies(t, pieces, outward):
        near, far = divmod(DP_ORDER[t // 2], 2)
        first = pieces[t % 2 * 4 + far].at[near]
        last = pieces[t % 2 * 4 + 2 + near].at[far]
        result = []
        for half, there in enumerate((first, last)):
            here = contracts.at[t, pl.ds(half * CHIPS // 2, CHIPS // 2)]
            ends = (here, there) if outward else (there, here)
            result.append(pltpu.make_async_copy(*ends, contract_sem.at[t, half]))
        return result

    for t in range(blocks):
        for copy in wide_copies(t, wide_ref, False):
            copy.start()
        for copy in contract_copies(t, contract_refs, False):
            copy.start()

    mixed = join(mixed_ref)
    mixed_out[...] = mixed
    unit, _ = norm_parts(first_ref[...])
    second_in[...] = (
        unit * vector_ref[11:12] + vector_ref[12:13] + times(mixed, out_w) + vector_ref[5:6]
    )
    unit, _ = norm_parts(second_in[...])
    second = unit * vector_ref[13:14] + vector_ref[14:15]
    low[...] = second.astype(jnp.bfloat16)
    total[...] = second + vector_ref[10:11]

    def shard(t, k):
        return places[t // 2] * count + order[t % 2 * CHIPS + k]

    for t in range(blocks):
        for copy in wide_copies(t, wide_ref, False):
            copy.wait()
        bias = jnp.concatenate([bias_ref[pl.ds(shard(t, k), 1)] for k in range(CHIPS)], axis=1)
        inner = times(low[...], columns.at[t]) + bias
        phi = 0.5 + 0.5 * lax.erf(inner * (0.5**0.5))
        out = (inner * phi).astype(jnp.bfloat16)
        active[t] = out
        slope[t] = phi + inner * jnp.exp(-0.5 * inner * inner) * 0.3989422804014327
        for copy in contract_copies(t, contract_refs, False):
            copy.wait()
        total[...] += dot(out, contracts[t].reshape(block, depth), NN)

    unit, inverse = norm_parts(total[...])
    gain = vector_ref[15:16]
    layer_out[...] = (unit * gain + vector_ref[16:17]).astype(jnp.bfloat16)
    gradient = grad_ref[...].astype(jnp.float32)
    grad_third = norm_back(gradient, unit, inverse, gain)
    stat_out[...] = jnp.zeros_like(stat_out)
    stat_out[0:1] = column_sum(grad_third)
    stat_out[1:2] = column_sum(gradient * unit)
    stat_out[2:3] = column_sum(gradient)
    total[...] = grad_third
    third_low[...] = grad_third.astype(jnp.bfloat16)
    turned = low[...].T

    for t in range(blocks):
        grad_inner = dot(third_low[...], contracts[t].reshape(block, depth), NT) * slope[t]
        inner_low = grad_inner.astype(jnp.bfloat16)
        sums = column_sum(grad_inner)
        for k in range(CHIPS):
            dbias_ref[pl.ds(shard(t, k), 1)] = sums[:, k * part : (k + 1) * part]
        contracts[t] = (
            dot(active[t], third_low[...], TN).astype(jnp.bfloat16).reshape(CHIPS, part, depth)
        )
        for copy in contract_copies(t, contract_grads, True):
            copy.start()
        total[...] += times_back(inner_low, columns.at[t])
        result = dot(turned, inner_low, NN).astype(jnp.bfloat16)
        for d in range(groups):
            columns[t, :, d] = result[d * count * rows : (d + 1) * count * rows].reshape(
                count, rows, block
            )
        for copy in wide_copies(t, wide_grad, True):
            copy.start()

    unit, inverse = norm_parts(second_in[...])
    grad_second = total[...]
    grad_in = norm_back(grad_second, unit, inverse, vector_ref[13:14])
    second_grad[...] = grad_in
    grad_low = grad_in.astype(jnp.bfloat16)
    cross_low[...] = grad_low
    spread(mixed_grad, times_back(grad_low, out_w).astype(jnp.bfloat16))
    stat_out[8:9] = column_sum(grad_in)
    stat_out[9:10] = column_sum(grad_second * unit)
    stat_out[10:11] = column_sum(grad_second)
    for t in range(blocks):
        for copy in contract_copies(t, contract_grads, True) + wide_copies(t, wide_grad, True):
            copy.wait()


def ffn(orders, mixed, first_in, wide, contract, vectors, bias, output_grad):
    rows, depth = first_in.shape
    hidden = bias.size
    block = depth // 2
    count, groups, all_rows, _ = wide.shape
    part = depth // (count * groups)
    blocks = hidden // block
    full = whole(first_in)
    anywhere = pl.BlockSpec(memory_space=pl.ANY)
    heads_out = shape(mixed.shape, jnp.bfloat16)
    stats = shape((16, depth), jnp.float32)
    return pl.pallas_call(
        ffn_kernel,
        grid_spec=pltpu.PrefetchScalarGridSpec(
            num_scalar_prefetch=2,
            grid=(1,),
            in_specs=[
                whole(mixed),
                full,
                pl.BlockSpec((count, groups, part, depth), lambda *_: (0, 0, groups, 0)),
                whole(vectors),
                whole(bias),
                full,
                *[anywhere] * 9,
            ],
            out_specs=[
                full,
                full,
                *[anywhere] * 9,
                whole(bias),
                full,
                full,
                whole(heads_out),
                whole(stats),
            ],
            scratch_shapes=[
                pltpu.VMEM((blocks, count, groups, part, block), jnp.bfloat16),
                pltpu.VMEM((blocks, CHIPS) + contract[0].shape[2:], jnp.bfloat16),
                pltpu.VMEM((blocks, rows, block), jnp.bfloat16),
                pltpu.VMEM((blocks, rows, block), jnp.float32),
                pltpu.VMEM((rows, depth), jnp.bfloat16),
                pltpu.VMEM((rows, depth), jnp.bfloat16),
                pltpu.VMEM((rows, depth), jnp.float32),
                pltpu.VMEM((rows, depth), jnp.float32),
                pltpu.SemaphoreType.DMA((blocks, CHIPS)),
                pltpu.SemaphoreType.DMA((blocks, 2)),
            ],
        ),
        out_shape=[
            shape((rows, depth), jnp.bfloat16),
            shape((rows, depth), jnp.bfloat16),
            shape((count, groups, all_rows - part, depth), jnp.bfloat16),
            *[shape(piece.shape, jnp.bfloat16) for piece in contract],
            shape(bias.shape, jnp.float32),
            shape((rows, depth), jnp.float32),
            shape((rows, depth), jnp.bfloat16),
            heads_out,
            stats,
        ],
        compiler_params=params(),
        cost_estimate=cost(12 * rows * depth * hidden, 16 * depth * hidden),
        name="ffn",
    )(*orders, mixed, first_in, wide, vectors, bias, output_grad, wide, *contract)


def first_back_kernel(
    dq_ref,
    second_grad,
    first_ref,
    out_w,
    query_w,
    vector_ref,
    _,
    query_low,
    grad_in_out,
    self_low,
    mixed_grad,
    stat_out,
):
    query_grad = join(dq_ref)
    query_low[...] = query_grad
    grad_first = second_grad[...] + times_back(query_grad, query_w)
    unit, inverse = norm_parts(first_ref[...])
    grad_in = norm_back(grad_first, unit, inverse, vector_ref[11:12])
    grad_in_out[...] = grad_in
    grad_low = grad_in.astype(jnp.bfloat16)
    self_low[...] = grad_low
    spread(mixed_grad, times_back(grad_low, out_w).astype(jnp.bfloat16))
    stat_out[...] = jnp.zeros_like(stat_out)
    stat_out[0:1] = column_sum(query_grad.astype(jnp.float32))
    stat_out[1:2] = column_sum(grad_in)
    stat_out[2:3] = column_sum(grad_first * unit)
    stat_out[3:4] = column_sum(grad_first)


def first_back(dq, second_grad, first_in, weights, vectors, after):
    rows, depth = first_in.shape
    full = whole(first_in)
    return pl.pallas_call(
        first_back_kernel,
        grid=(1,),
        in_specs=[
            whole(dq),
            full,
            full,
            gathered(weights, depth, 0),
            gathered(weights, depth, 1),
            whole(vectors),
            pl.BlockSpec(memory_space=pl.ANY),
        ],
        out_specs=[full, full, full, whole(dq), pl.BlockSpec((8, depth), lambda *_: (0, 0))],
        out_shape=[
            shape((rows, depth), jnp.bfloat16),
            shape((rows, depth), jnp.float32),
            shape((rows, depth), jnp.bfloat16),
            shape(dq.shape, jnp.bfloat16),
            shape((8, depth), jnp.float32),
        ],
        compiler_params=params(),
        cost_estimate=cost(4 * rows * depth * depth, 4 * depth * depth),
        name="first_back",
    )(dq, second_grad, first_in, weights, weights, vectors, after)


def weight_grads_kernel(
    order,
    mixed,
    self_low,
    first_low,
    query_low,
    cross,
    cross_low,
    mine_out,
    other_out,
    result,
):
    step = pl.program_id(0)
    pairs = ((mixed, self_low), (first_low, query_low), (cross, cross_low))
    half, groups, part, _ = mine_out.shape
    for m, (left_side, gradient) in enumerate(pairs):

        @pl.when(step == m)
        def _(left_side=left_side, gradient=gradient):
            result[...] = dot(left_side[...], gradient[...], TN).astype(jnp.bfloat16)

    for d in range(groups):
        for k in range(half):
            for p, out_ref in enumerate((mine_out, other_out)):
                row = pl.multiple_of((2 * half * d + order[p * half + k]) * part, part)
                out_ref[k, d] = result[pl.ds(row, part)]


def weight_grads(dims, order, mixed, self_low, first_low, query_low, cross, cross_low):
    count, groups, part, depth = dims
    half = pl.BlockSpec((count // 2, groups, part, depth), lambda m, _: (0, 0, m, 0))
    return pl.pallas_call(
        weight_grads_kernel,
        grid_spec=pltpu.PrefetchScalarGridSpec(
            num_scalar_prefetch=1,
            grid=(3,),
            in_specs=[whole(mixed)] * 6,
            out_specs=[half, half],
            scratch_shapes=[pltpu.VMEM((depth, depth), jnp.bfloat16)],
        ),
        out_shape=[shape((count // 2, groups, 3 * part, depth), jnp.bfloat16)] * 2,
        compiler_params=params(),
        cost_estimate=cost(6 * mixed.shape[0] * depth * depth, 6 * depth * depth),
        name="weight_grads",
    )(order, mixed, self_low, first_low, query_low, cross, cross_low)


def send_dp(piece):
    size = lax.axis_size("dp")
    return [
        lax.ppermute(piece, "dp", [(i, (i + shift) % size) for i in range(size)])
        for shift in range(1, size)
    ]


def place_dp(piece, arrived):
    size, me = lax.axis_size("dp"), lax.axis_index("dp")
    result = jnp.zeros((size,) + piece.shape, piece.dtype)
    result = lax.dynamic_update_index_in_dim(result, piece, me, 0)
    for shift, got in enumerate(arrived, 1):
        result = lax.dynamic_update_index_in_dim(result, got, lax.rem(me - shift + size, size), 0)
    return result


class HalvingDp:
    def __init__(self, pieces):
        me = lax.axis_index("dp")
        self.parts = [
            lax.dynamic_index_in_dim(pieces, me ^ flip, 0, keepdims=False) for flip in DP_ORDER
        ]

    def first(self):
        return jnp.stack(self.parts[2:]).astype(jnp.bfloat16)

    def second(self, got):
        self.got = got
        return (
            self.parts[1].astype(jnp.float32) + self.got[1].astype(jnp.float32)
        ).astype(jnp.bfloat16)

    def finish(self, last):
        return sum(one.astype(jnp.float32) for one in (self.parts[0], self.got[0], last))


def relative_order():
    size, me = lax.axis_size("index"), lax.axis_index("index")
    steps = jnp.arange(size // 2, dtype=jnp.int32) * 2
    return jnp.concatenate([me ^ steps, me ^ 1 ^ steps])


def exchange(piece, flip):
    size = lax.axis_size("index")
    return lax.ppermute(piece, "index", [(i, i ^ flip) for i in range(size)])


def exchange_dp(piece, flip):
    size = lax.axis_size("dp")
    return lax.ppermute(piece, "dp", [(i, i ^ flip) for i in range(size)])


def add_kernel(*refs):
    total = sum(ref[...].astype(jnp.float32) for ref in refs[:-1])
    refs[-1][...] = total.astype(jnp.bfloat16)


def add(*terms):
    flat, specs = [], []
    first = terms[0]
    dims = first[0].shape[1:] if isinstance(first, tuple) else first.shape
    rows = 1
    for size in dims[:-1]:
        rows *= size
    block = min(rows, 256)
    for term in terms:
        array, entry = term if isinstance(term, tuple) else (term, 0)
        flat.append(array.reshape(-1, dims[-1]))
        start = entry * rows // block
        specs.append(pl.BlockSpec((block, dims[-1]), lambda i, start=start: (start + i, 0)))
    return pl.pallas_call(
        add_kernel,
        grid=(rows // block,),
        in_specs=specs,
        out_specs=pl.BlockSpec((block, dims[-1]), lambda i: (i, 0)),
        out_shape=shape((rows, dims[-1]), jnp.bfloat16),
        compiler_params=params(),
        cost_estimate=cost(0, 0),
        name="add",
    )(*flat).reshape(dims)


def combine_kernel(plan, *refs):
    ins, outs = list(refs[: -len(plan)]), refs[-len(plan) :]
    for out_ref, entries in zip(outs, plan):
        for e, segments in enumerate(entries):
            start = 0
            for offsets, rows in segments:
                terms, ins = ins[: len(offsets)], ins[len(offsets) :]
                total = sum(
                    ref[0, offset : offset + rows].astype(jnp.float32)
                    for ref, offset in zip(terms, offsets)
                )
                out_ref[e, start : start + rows] = total.astype(jnp.bfloat16)
                start += rows


def combine(*outputs):
    arrays, specs, plan, shapes = [], [], [], []
    for entries in outputs:
        plan.append([])
        for segments in entries:
            plan[-1].append([])
            for terms in segments:
                offsets = []
                for array, e, rows, start in terms:
                    block, place, offset = rows, start // rows, 0
                    if start % rows or array.shape[1] % rows:
                        block, place, offset = array.shape[1], 0, start
                    offsets.append(offset)
                    arrays.append(array)
                    specs.append(
                        pl.BlockSpec(
                            (1, block, array.shape[2]), lambda i, e=e, place=place: (e, place, 0)
                        )
                    )
                plan[-1][-1].append((offsets, terms[0][2]))
        rows = sum(rows for _, rows in plan[-1][0])
        shapes.append(shape((len(entries), rows, arrays[0].shape[2]), jnp.bfloat16))
    return pl.pallas_call(
        partial(combine_kernel, plan),
        grid=(1,),
        in_specs=specs,
        out_specs=[whole(out) for out in shapes],
        out_shape=shapes,
        compiler_params=params(),
        cost_estimate=cost(0, 0),
        name="combine",
    )(*arrays)


class Halving:
    def __init__(self, chips):
        self.chips = chips
        self.middle = chips[0][0][0].shape[1] // 2

    def terms(self, k, half, *more):
        middle = self.middle
        return [(array, e, middle, half * middle) for array, e in self.chips[k]] + [
            (array, e, middle, start) for array, e, start in more
        ]

    def total(self, k, half, *more):
        rows = slice(half * self.middle, (half + 1) * self.middle)
        parts = [array[e, rows] for array, e in self.chips[k]] + [*more]
        return sum(one.astype(jnp.float32) for one in parts)

    def finish(self, top, low):
        return jnp.concatenate(
            [self.total(0, 0, self.got[0][0], top), self.total(0, 1, self.got[1][0], low)], axis=0
        )


def both_cores(mine, other):
    parts = [part.reshape(CHIPS, -1, part.shape[-1]) for part in (mine, other)]
    return Halving([[(part, k) for part in parts] for k in range(CHIPS)])


def firsts(*sums):
    return combine(
        [[one.terms(k, 0) for one in sums] for k in (1, 3)],
        [[one.terms(k, 1) for one in sums] for k in (2, 3)],
    )


def seconds(*sums):
    for one, top, low, start in sums:
        rows = slice(start, start + one.middle)
        one.got = top[:, rows], low[:, rows]
    top, low = combine(
        [[one.terms(2, 0, (top, 1, start)) for one, top, _, start in sums]],
        [[one.terms(1, 1, (low, 1, start)) for one, _, low, start in sums]],
    )
    return top[0], low[0]


def send_first(top, low):
    return [exchange(top, 2), exchange(low, 4)]


def send_last(top, low):
    return [exchange(top, 4), exchange(low, 2)]


def split_rows(arrays, rows):
    return [a[..., :rows, :] for a in arrays], [a[..., rows:, :] for a in arrays]


def small_send(values):
    size = lax.axis_size("index")
    flat = jnp.pad(values.reshape(-1), (0, 1024 - values.size)).reshape(1, 8, 128)
    return swap(jnp.broadcast_to(flat, (size, 8, 128)))


def small_take(arrived, dims):
    size = 1
    for dim in dims:
        size *= dim
    return jnp.sum(arrived, axis=0).reshape(-1)[:size].reshape(dims)


def hold_kernel(*_):
    pass


def hold(values, *others):
    anywhere = pl.BlockSpec(memory_space=pl.ANY)
    return pl.pallas_call(
        hold_kernel,
        in_specs=[anywhere] * (len(values) + len(others)),
        out_specs=[anywhere] * len(values),
        out_shape=[shape(value.shape, value.dtype) for value in values],
        input_output_aliases={i: i for i in range(len(values))},
        name="hold",
    )(*values, *others)


def swap(pieces):
    return lax.all_to_all(pieces, "index", 0, 0, tiled=True)


def head_body(
    decoder_input,
    encoder_memory,
    question_vectors,
    passage_vectors,
    passage_ids,
    valid_count,
    output_grad,
    attention_weight,
    expand_weight,
    contract_weight,
    vector_params,
    attention_mean,
    attention_square,
    expand_mean,
    expand_square,
    contract_mean,
    contract_square,
    vector_mean,
    vector_square,
):
    low = jnp.bfloat16
    count, groups = lax.axis_size("index"), lax.axis_size("dp")
    place = lax.axis_index("index")
    seqs, rows_here, depth = decoder_input.shape
    memory_here = encoder_memory.shape[1]
    width = depth // count
    part = attention_weight.shape[1]
    hidden = expand_weight.shape[1]
    vector_rows, vector_width = vector_params.shape
    question_width = question_vectors.shape[1]
    rows = seqs * rows_here

    attention_low = attention_weight.astype(low)
    extras = jnp.concatenate(
        [vector_params.astype(low).reshape(-1), question_vectors.reshape(-1)]
    )
    extra_rows = -(-extras.shape[0] // (16 * width)) * 16
    extras = jnp.pad(extras, (0, extra_rows * width - extras.shape[0])).reshape(
        1, extra_rows, width
    )
    split = jnp.concatenate([attention_low[:3], attention_low[5:7]], axis=0)
    columns = split.reshape(5, part, count, width).transpose(2, 0, 1, 3)
    package = jnp.concatenate(
        [
            columns.reshape(count, 5 * part, width),
            jnp.broadcast_to(extras, (count, extra_rows, width)),
        ],
        axis=1,
    )
    order = relative_order()
    memory_block = -(-memory_here // rows_here) * rows_here
    rows_all = lax.all_gather(
        jnp.concatenate(
            [
                jnp.pad(encoder_memory, ((0, 0), (0, memory_block - memory_here), (0, 0))),
                decoder_input,
            ],
            axis=1,
        ),
        "index",
        axis=0,
        tiled=False,
    )
    input_rows = (rows_all, memory_block, rows_here)
    memory_rows = (rows_all, 0, memory_here)
    square = attention_low[3:5].transpose(1, 0, 2).reshape(part, 2 * depth)
    received = swap(package)
    square_arrived = hold(send_dp(square), received)
    (received,) = hold([received], *square_arrived)
    received_sent = send_dp(received)
    (contract,) = hold([contract_weight.astype(low)], received)
    contract = [contract] + [exchange(contract, 2 * k) for k in range(1, CHIPS)]
    slices_arrived = hold(received_sent, *contract[1:])
    square_arrived = hold(square_arrived, *slices_arrived)
    square = lax.all_gather(place_dp(square, square_arrived), "index", axis=0, tiled=False)
    slices = place_dp(received, slices_arrived)
    vectors = (
        slices[:, :, 5 * part :]
        .reshape(groups, count, extra_rows * width)[:, :, : vector_rows * vector_width]
        .reshape(groups, count, vector_rows, vector_width)
        .transpose(2, 0, 1, 3)
        .reshape(vector_rows, depth)
        .astype(jnp.float32)
    )
    question_full = (
        received[:, 5 * part :]
        .reshape(count, extra_rows * width)[:, vector_rows * vector_width :][
            :, : seqs * question_width
        ]
        .reshape(count, seqs, question_width)
        .transpose(1, 0, 2)
        .reshape(seqs, count * question_width)
    )
    expand_part = hidden // depth * part
    late = jnp.concatenate(
        [
            expand_weight.astype(low)
            .reshape(part, hidden // depth, depth)
            .transpose(1, 0, 2)
            .reshape(expand_part, depth),
            attention_low[7],
        ],
        axis=0,
    )
    (late,) = hold([late], *slices_arrived)
    late_sent = send_dp(late)

    (passage_ids,) = hold([passage_ids], *slices_arrived)
    passages_here = passage_vectors.shape[0]
    local_ids = passage_ids - place * passages_here
    owned_slot = (local_ids >= 0) & (local_ids < passages_here)
    picked = passage_vectors[jnp.clip(local_ids, 0, passages_here - 1)]
    local_scores = jnp.einsum(
        "sc,skc->sk", question_full, picked, preferred_element_type=jnp.float32
    )
    slots = passage_ids.shape[1]
    usable = jnp.arange(slots)[None, :] < valid_count[:, None]
    scores = small_take(small_send(jnp.where(owned_slot, local_scores, 0.0)), local_scores.shape)
    masked = jnp.where(usable, scores, negative_fill)
    maximum = jnp.max(masked, axis=1)
    exponent = jnp.where(usable, jnp.exp(masked - maximum[:, None]), 0.0)
    partition = jnp.sum(exponent, axis=1)
    passage_prob = exponent / partition[:, None]
    log_prior = jnp.where(
        usable, masked - maximum[:, None] - jnp.log(partition)[:, None], negative_fill
    )
    key_bias = jnp.repeat(log_prior, MEM_P, axis=1)

    vector_here = lax.dynamic_slice_in_dim(vectors[:5], place * width, width, axis=1)
    no_bias = jnp.zeros((1, width), jnp.float32)
    qkv_bias = jnp.concatenate([vector_here[0:1], no_bias, vector_here[1:2]], axis=1)
    kv_bias = jnp.concatenate([no_bias, vector_here[4:5]], axis=1)
    x_rows = decoder_input.reshape(rows, depth)
    qkv = project_columns("self_qkv", *input_rows, slices, 0, 3, qkv_bias)
    self_out, self_stat = attend(True, qkv, 0, qkv, 1, 2, key_bias[:, None, :])
    self_out, *late_arrived = hold([self_out, *late_sent])
    self_got = swap(self_out)
    late = lax.all_gather(place_dp(late, late_arrived), "index", axis=0, tiled=False)
    ahead, across = hold([jnp.stack(contract[:2]), jnp.stack(contract[2:])], *late_arrived)
    self_got, ahead_far, across_far = hold(
        [self_got, exchange_dp(ahead, 2), exchange_dp(across, 1)]
    )
    ahead = jnp.stack([ahead, ahead_far])
    across = jnp.stack([across, across_far])
    contract_sent = [exchange_dp(ahead, 1), exchange_dp(across, 2)]
    self_mixed, first_in, first_low, cross_query = first_forward(
        self_got, x_rows, square, vectors, ahead_far
    )
    (slices,) = hold([slices], first_low)
    memory_kv = project_columns("memory_kv", *memory_rows, slices, 3, 2, kv_bias)
    cross_query = swap(cross_query)[:, None]
    cross_out, cross_stat = attend(
        False, cross_query, 0, memory_kv, 0, 1, key_bias[:, None, :]
    )
    ahead_far, across_far = hold(contract_sent, cross_out)
    contract = [ahead, ahead_far, across, across_far]
    contract += [exchange(piece, 1) for piece in contract]
    places = lax.axis_index("dp") ^ jnp.array(DP_ORDER, jnp.int32)
    (
        cross_mixed,
        layer_output,
        wide_grad,
        *contract_grads,
        inner_total,
        second_grad,
        cross_low,
        cross_mix_grad,
        stats,
    ) = ffn(
        (order, places),
        swap(cross_out),
        first_in,
        late,
        contract,
        vectors,
        vectors[6:10].reshape(groups * count, -1),
        output_grad.reshape(rows, depth),
    )
    third_stat, second_stat = stats[:8], stats[8:]

    expand_part_sum = lax.psum_scatter(wide_grad, "index", scatter_dimension=0, tiled=False)
    ahead, ahead_far, across, across_far = contract_grads[:4]
    cores = [exchange(piece, 1) for piece in contract_grads[4:]]
    cross_mix_got, *contract_sent = hold(
        [swap(cross_mix_grad), add(ahead_far, cores[1]), add(across_far, cores[3])]
    )
    contract_got = [exchange_dp(contract_sent[0], 1), exchange_dp(contract_sent[1], 2)]
    cross_dq, cross_dkv, prior_rows = attend_back(
        False,
        cross_query,
        0,
        memory_kv,
        0,
        1,
        cross_mix_got,
        cross_stat,
        key_bias[:, None, :],
        contract_sent[0],
    )
    memory_mine, memory_other, kv_grads, kv_total = project_columns_back(
        "memory_kv_back", order, *memory_rows, [cross_dkv], slices, 3, 2
    )
    cross_dq, *contract_got = hold([cross_dq, *contract_got], memory_mine)
    contract_next = [
        add((ahead, 1), (cores[0], 1), (contract_got[0], 1)),
        add((across, 1), (cores[2], 1), (contract_got[1], 1)),
    ]
    cross_dq_got, *contract_next = hold([swap(cross_dq), *contract_next])
    contract_last = [exchange_dp(contract_next[0], 2), exchange_dp(contract_next[1], 1)]
    query_low, first_grad, self_low, self_mix_grad, first_stat = first_back(
        cross_dq_got, second_grad, first_in, square, vectors, memory_mine
    )
    memory_sum = both_cores(memory_mine, exchange(memory_other, 1))
    memory_sent = firsts(memory_sum)
    square_mine, square_other = weight_grads(
        (count, groups, part, depth),
        order,
        self_mixed,
        self_low,
        first_low,
        query_low,
        cross_mixed,
        cross_low,
    )
    square_sum = both_cores(square_mine, exchange(square_other, 1))
    square_sent = firsts(square_sum)
    self_mix_got, *contract_last = hold(
        [swap(self_mix_grad), *contract_last], *memory_sent, *square_sent
    )
    memory_got = send_first(*memory_sent)
    square_got = send_first(*square_sent)
    self_dq, self_dkv, _ = attend_back(
        True, qkv, 0, qkv, 1, 2, self_mix_got, self_stat, self_stat, square_mine
    )
    expand_sum = HalvingDp(expand_part_sum)
    self_dq, expand_sent = hold([self_dq, expand_sum.first()])
    expand_got = exchange_dp(expand_sent, 1)
    dx_mine, dx_other, qkv_slice_grads, qkv_total = project_columns_back(
        "self_qkv_back", order, *input_rows, [self_dq, self_dkv], slices, 0, 3
    )
    dx_mine, dx_other, expand_got, *got = hold(
        [dx_mine, dx_other, expand_got, *memory_got, *square_got]
    )
    own = jnp.concatenate(
        [qkv_total[:, :width], qkv_total[:, 2 * width :], kv_total[:, width:]], axis=0
    )
    own = lax.dynamic_update_slice(
        jnp.zeros((3, depth), jnp.float32), own, (jnp.int32(0), place * width)
    )
    vector_grads = jnp.concatenate(
        [
            own[:2],
            first_stat[1:2],
            first_stat[0:1],
            own[2:],
            second_stat[0:1],
            inner_total.reshape(hidden // depth, depth),
            third_stat[0:1],
            first_stat[2:4],
            second_stat[1:3],
            third_stat[1:3],
        ],
        axis=0,
    )
    vector_size = vector_rows * vector_width
    question_size = seqs * question_width
    vector_send = (
        vector_grads.reshape(vector_rows, groups, count, vector_width)
        .transpose(1, 2, 0, 3)
        .reshape(groups, count, vector_size)
    )
    vector_send = jnp.pad(
        vector_send, ((0, 0), (0, 0), (0, extra_rows * width - vector_size))
    ).reshape(groups, count, extra_rows, width)
    slice_sum = HalvingDp(
        jnp.concatenate([qkv_slice_grads, kv_grads, vector_send.astype(low)], axis=2)
    )
    slice_sent = slice_sum.first()
    slice_got = exchange_dp(slice_sent, 1)
    dx_other, *got = hold([dx_other, *got], slice_sent)
    dx_got = exchange(dx_other, 1)
    square_rows = square_sum.middle
    last = seconds((square_sum, *got[2:], 0), (memory_sum, *got[:2], 0))
    prior_rows, expand_got, *contract_last = hold(
        [prior_rows, expand_got, *contract_last], *last
    )
    last = send_last(*last)
    expand_last = exchange_dp(expand_sum.second(expand_got), 2)
    prior_arrived = small_send(prior_rows.reshape(seqs, slots, MEM_P).sum(axis=-1))
    dx_got, expand_last, prior_arrived, slice_got, *last = hold(
        [dx_got, expand_last, prior_arrived, slice_got, *last]
    )
    slice_next = slice_sum.second(slice_got)
    dx_got, *last = hold([dx_got, *last], slice_next)
    slice_last = exchange_dp(slice_next, 2)
    dx_sum = both_cores(dx_mine, dx_got)
    contract_sum = Halving(
        [
            [(one.reshape((-1,) + one.shape[-2:]), k % 2) for one in parts]
            for k, parts in enumerate(
                [(ahead, cores[0], contract_got[0], contract_last[0])] * 2
                + [(across, cores[2], contract_got[1], contract_last[1])] * 2
            )
        ]
    )
    dx_sent = firsts(dx_sum, contract_sum)
    got = send_first(*dx_sent)
    last = hold(last, *dx_sent)
    square_last, memory_last = split_rows(last, square_rows)
    square_far = HalvingDp(square_sum.finish(*square_last).reshape(groups, 3 * part, depth))
    square_got = exchange_dp(square_far.first(), 1)
    square_got, slice_last, *got = hold([square_got, slice_last, *got])
    slice_sum = slice_sum.finish(slice_last)
    prior_grad = jnp.where(usable, small_take(prior_arrived, (seqs, slots)), 0.0)
    score_doc = jnp.where(
        usable, prior_grad - passage_prob * jnp.sum(prior_grad, axis=1, keepdims=True), 0.0
    )
    question_part = jnp.einsum(
        "sk,skc->sc",
        jnp.where(owned_slot, score_doc, 0.0),
        picked.astype(jnp.float32),
        precision=lax.Precision.HIGHEST,
    )

    question_send = (
        question_part.reshape(seqs, count, question_width)
        .transpose(1, 0, 2)
        .reshape(count, question_size)
    )
    question_send = jnp.pad(
        question_send,
        ((0, 0), (vector_size, extra_rows * width - vector_size - question_size)),
    ).reshape(count, extra_rows, width)
    slice_sum = jnp.concatenate(
        [slice_sum[:, : 5 * part], slice_sum[:, 5 * part :] + question_send], axis=1
    )
    slice_send = slice_sum.astype(low)
    arrived = swap(slice_send)
    square_got, *got = hold([square_got, *got], slice_send)
    square_last = exchange_dp(square_far.second(square_got), 2)
    start = dx_sum.middle
    last = send_last(*seconds((dx_sum, *got, 0), (contract_sum, *got, start)))
    dx_last, contract_last = split_rows(last, start)
    input_gradient = first_grad + dx_sum.finish(*dx_last)
    contract_sum = contract_sum.finish(*contract_last)
    memory_last = hold(memory_last, *got)
    memory_gradient = memory_sum.finish(*memory_last).reshape(encoder_memory.shape)
    arrived = arrived.astype(jnp.float32)
    split_grads = (
        arrived[:, : 5 * part]
        .reshape(count, 5, part, width)
        .transpose(1, 2, 0, 3)
        .reshape(5, part, depth)
    )
    extra_sum = jnp.sum(arrived[:, 5 * part :].reshape(count, extra_rows * width), axis=0)
    vector_sum = extra_sum[:vector_size].reshape(vector_rows, vector_width)
    question_gradient = extra_sum[vector_size : vector_size + question_size].reshape(
        seqs, question_width
    )

    expand_sum = (
        expand_sum.finish(expand_last)
        .reshape(hidden // depth, part, depth)
        .transpose(1, 0, 2)
        .reshape(part, hidden)
    )
    square_total = square_far.finish(square_last).reshape(3, part, depth)
    attention_sum = jnp.concatenate(
        [split_grads[:3], square_total[:2], split_grads[3:], square_total[2:]], axis=0
    )

    new_attention = adam_update(
        attention_weight,
        attention_mean,
        attention_square,
        attention_sum,
        rate_attention,
        decay_matrix,
    )
    new_expand = adam_update(
        expand_weight, expand_mean, expand_square, expand_sum, rate_expand, decay_matrix
    )
    new_contract = adam_update(
        contract_weight, contract_mean, contract_square, contract_sum, rate_contract, decay_matrix
    )
    new_vector = adam_update(
        vector_params, vector_mean, vector_square, vector_sum, rate_vector, 0.0
    )
    return (
        layer_output.reshape(decoder_input.shape),
        input_gradient.reshape(decoder_input.shape),
        memory_gradient,
        question_gradient,
        *new_attention,
        *new_expand,
        *new_contract,
        *new_vector,
    )


def body(sizes, *arrays):
    depth = arrays[0].shape[2]
    if sizes == (4, 8) and depth // 8 % 128 == 0:
        return head_body(*arrays)
    return general_body(*arrays)


def solution(mesh):
    return jax.shard_map(
        partial(body, (mesh.shape["dp"], mesh.shape["index"])),
        mesh=mesh,
        in_specs=(
            P("dp", "index", None),
            P("dp", "index", None),
            P("dp", "index"),
            P("index", None),
            P("dp", None),
            P("dp"),
            P("dp", "index", None),
            P(None, ("dp", "index"), None),
            P(("dp", "index"), None),
            P(("dp", "index"), None),
            P(None, ("dp", "index")),
            P(None, ("dp", "index"), None),
            P(None, ("dp", "index"), None),
            P(("dp", "index"), None),
            P(("dp", "index"), None),
            P(("dp", "index"), None),
            P(("dp", "index"), None),
            P(None, ("dp", "index")),
            P(None, ("dp", "index")),
        ),
        out_specs=(
            P("dp", "index", None),
            P("dp", "index", None),
            P("dp", "index", None),
            P("dp", "index"),
            P(None, ("dp", "index"), None),
            P(None, ("dp", "index"), None),
            P(None, ("dp", "index"), None),
            P(("dp", "index"), None),
            P(("dp", "index"), None),
            P(("dp", "index"), None),
            P(("dp", "index"), None),
            P(("dp", "index"), None),
            P(("dp", "index"), None),
            P(None, ("dp", "index")),
            P(None, ("dp", "index")),
            P(None, ("dp", "index")),
        ),
        check_vma=False,
    )
```

```python
from functools import partial

import jax
import jax.numpy as jnp
from jax import lax
from jax.experimental import pallas as pl
from jax.experimental.pallas import tpu as pltpu
from jax.sharding import PartitionSpec as P

HEADS = 16
MEM_P = 192
STEP = 10


negative_fill = -1e30
norm_eps = 1e-05
beta_first = 0.9
beta_second = 0.999
adam_eps = 1e-08
decay_matrix = 0.01
rate_attention = 0.1
rate_expand = 0.02
rate_contract = 0.01
rate_vector = 0.2


def layer_norm(hidden, norm_gain, norm_shift):
    center = hidden - jnp.mean(hidden, axis=-1, keepdims=True)
    spread = jnp.mean(center * center, axis=-1, keepdims=True)
    return center * lax.rsqrt(spread + norm_eps) * norm_gain + norm_shift


def split_heads(matrix):
    return matrix.reshape(matrix.shape[0], matrix.shape[1], HEADS, matrix.shape[2] // HEADS)


def merge_heads(matrix):
    return matrix.reshape(matrix.shape[0], matrix.shape[1], matrix.shape[2] * matrix.shape[3])


def project(left_side, weight):
    return jnp.einsum("srd,de->sre", left_side, weight, preferred_element_type=jnp.float32)


def project_back(gradient, weight):
    return jnp.einsum("sre,de->srd", gradient, weight, preferred_element_type=jnp.float32)


def weight_grad(left_side, gradient):
    return jnp.einsum("srd,sre->de", left_side, gradient, preferred_element_type=jnp.float32)


def row_total(values):
    return jnp.sum(values, axis=(0, 1))


def attend_forward(queries, key_rows, values, score_bias, allowed):
    scores = (
        jnp.einsum(
            "sqhd,skhd->shqk",
            split_heads(queries),
            split_heads(key_rows),
            preferred_element_type=jnp.float32,
        )
        * 0.125
        + score_bias
    )
    scores = jnp.where(allowed, scores, negative_fill)
    maximum = jnp.max(scores, axis=-1)
    exponent = jnp.exp(scores - maximum[..., None])
    partition = jnp.sum(exponent, axis=-1)
    attend_prob = exponent / partition[..., None]
    mixture = jnp.einsum(
        "shqk,skhd->sqhd",
        attend_prob.astype(jnp.bfloat16),
        split_heads(values),
        preferred_element_type=jnp.float32,
    )
    return (merge_heads(mixture).astype(jnp.bfloat16), attend_prob, maximum, partition)


def score_grads(grad_mixed, attend_prob, values):
    grad_prob = jnp.einsum(
        "sqhd,skhd->shqk",
        split_heads(grad_mixed),
        split_heads(values),
        preferred_element_type=jnp.float32,
    )
    row_inner = jnp.sum(attend_prob * grad_prob, axis=-1)
    return ((attend_prob * (grad_prob - row_inner[..., None])).astype(jnp.bfloat16), row_inner)


def to_queries(grad_score, key_rows):
    return (
        merge_heads(
            jnp.einsum(
                "shqk,skhd->sqhd",
                grad_score,
                split_heads(key_rows),
                preferred_element_type=jnp.float32,
            )
        )
        * 0.125
    )


def to_keys(grad_score, attend_prob, queries, grad_mixed):
    grad_key = (
        merge_heads(
            jnp.einsum(
                "shqk,sqhd->skhd",
                grad_score,
                split_heads(queries),
                preferred_element_type=jnp.float32,
            )
        )
        * 0.125
    )
    grad_value = merge_heads(
        jnp.einsum(
            "shqk,sqhd->skhd",
            attend_prob.astype(jnp.bfloat16),
            split_heads(grad_mixed),
            preferred_element_type=jnp.float32,
        )
    )
    return (grad_key, grad_value)


def adam_update(weight, moment_one, moment_two, gradient, step_rate, weight_decay):
    mean_new = beta_first * moment_one + (1.0 - beta_first) * gradient
    square_new = beta_second * moment_two + (1.0 - beta_second) * gradient * gradient
    mean_hat = mean_new / (1.0 - beta_first**STEP)
    square_hat = square_new / (1.0 - beta_second**STEP)
    updated = weight - step_rate * (
        mean_hat / (jnp.sqrt(square_hat) + adam_eps) + weight_decay * weight
    )
    return (updated, mean_new, square_new)


def general_body(
    decoder_input,
    encoder_memory,
    question_vectors,
    passage_vectors,
    passage_ids,
    valid_count,
    output_grad,
    attention_weight,
    expand_weight,
    contract_weight,
    vector_params,
    attention_mean,
    attention_square,
    expand_mean,
    expand_square,
    contract_mean,
    contract_square,
    vector_mean,
    vector_square,
):
    attention_low, expand_low, contract_low, vector_low = (
        lax.all_gather(attention_weight.astype(jnp.bfloat16), ("dp", "index"), axis=1, tiled=True),
        lax.all_gather(expand_weight.astype(jnp.bfloat16), ("dp", "index"), axis=0, tiled=True),
        lax.all_gather(contract_weight.astype(jnp.bfloat16), ("dp", "index"), axis=0, tiled=True),
        lax.all_gather(vector_params.astype(jnp.bfloat16), ("dp", "index"), axis=1, tiled=True),
    )
    vectors = vector_low.astype(jnp.float32)
    seqs_here, rows_here, model_width = decoder_input.shape
    shard_index = lax.axis_index("index")
    length = rows_here * lax.axis_size("index")
    ffn_width = expand_low.shape[1]
    self_query = (project(decoder_input, attention_low[0]) + vectors[0]).astype(jnp.bfloat16)
    self_key = project(decoder_input, attention_low[1]).astype(jnp.bfloat16)
    self_value = (project(decoder_input, attention_low[2]) + vectors[1]).astype(jnp.bfloat16)
    key_all, value_all = (
        lax.all_gather(self_key, "index", axis=1, tiled=True),
        lax.all_gather(self_value, "index", axis=1, tiled=True),
    )
    query_place = shard_index * rows_here + jnp.arange(rows_here)
    causal = (jnp.arange(length)[None, :] <= query_place[:, None])[None, None]
    self_mixed, self_prob, self_peak, self_total = attend_forward(
        self_query, key_all, value_all, 0.0, causal
    )
    first_in = (
        decoder_input.astype(jnp.float32) + project(self_mixed, attention_low[3]) + vectors[2]
    )
    first_out, first_back = jax.vjp(layer_norm, first_in, vectors[11], vectors[12])
    first_low = first_out.astype(jnp.bfloat16)
    cross_query = (project(first_low, attention_low[4]) + vectors[3]).astype(jnp.bfloat16)
    cross_key = project(encoder_memory, attention_low[5]).astype(jnp.bfloat16)
    cross_value = (project(encoder_memory, attention_low[6]) + vectors[4]).astype(jnp.bfloat16)
    memory_keys, memory_values = (
        lax.all_gather(cross_key, "index", axis=1, tiled=True),
        lax.all_gather(cross_value, "index", axis=1, tiled=True),
    )
    question_full = lax.all_gather(question_vectors, "index", axis=1, tiled=True)
    passages_here = passage_vectors.shape[0]
    local_ids = passage_ids - shard_index * passages_here
    owned_slot = (local_ids >= 0) & (local_ids < passages_here)
    picked = passage_vectors[jnp.clip(local_ids, 0, passages_here - 1)]
    local_scores = jnp.einsum(
        "sc,skc->sk", question_full, picked, preferred_element_type=jnp.float32
    )
    slots = passage_ids.shape[1]
    usable = jnp.arange(slots)[None, :] < valid_count[:, None]
    local_peak = jnp.max(jnp.where(owned_slot & usable, local_scores, negative_fill), axis=1)
    maximum = lax.pmax(local_peak, "index")
    local_exp = jnp.where(owned_slot & usable, jnp.exp(local_scores - maximum[:, None]), 0.0)
    exponent, scores = lax.psum((local_exp, jnp.where(owned_slot, local_scores, 0.0)), "index")
    masked = jnp.where(usable, scores, negative_fill)
    partition = jnp.sum(exponent, axis=1)
    passage_prob = exponent / partition[:, None]
    log_prior = masked - maximum[:, None] - jnp.log(partition)[:, None]
    memory_total = memory_keys.shape[1]
    bias_rows = jnp.repeat(log_prior, MEM_P, axis=1)
    key_bias = bias_rows[:, None, None, :]
    key_usable = ((jnp.arange(memory_total) // MEM_P)[None, :] < valid_count[:, None])[
        :, None, None, :
    ]
    cross_mixed, cross_prob, cross_peak, cross_total = attend_forward(
        cross_query, memory_keys, memory_values, key_bias, key_usable
    )
    second_in = first_out + project(cross_mixed, attention_low[7]) + vectors[5]
    second_out, second_back = jax.vjp(layer_norm, second_in, vectors[13], vectors[14])
    second_low = second_out.astype(jnp.bfloat16)
    inner_act = project(second_low, expand_low) + vectors[6:10].reshape(ffn_width)
    activated, gelu_back = jax.vjp(partial(jax.nn.gelu, approximate=False), inner_act)
    activ_low = activated.astype(jnp.bfloat16)
    third_in = second_out + project(activ_low, contract_low) + vectors[10]
    layer_output, third_back = jax.vjp(layer_norm, third_in, vectors[15], vectors[16])
    grad_third, gain_three, shift_three = third_back(output_grad.astype(jnp.float32))
    grad_ffn_low = grad_third.astype(jnp.bfloat16)
    grad_contract = weight_grad(activ_low, grad_ffn_low)
    (grad_inner,) = gelu_back(project_back(grad_ffn_low, contract_low))
    grad_inner_low = grad_inner.astype(jnp.bfloat16)
    grad_expand = weight_grad(second_low, grad_inner_low)
    grad_second = grad_third + project_back(grad_inner_low, expand_low)
    grad_second_in, gain_two, shift_two = second_back(grad_second)
    grad_cross_low = grad_second_in.astype(jnp.bfloat16)
    grad_cmix = project_back(grad_cross_low, attention_low[7]).astype(jnp.bfloat16)
    cross_score, cross_inner = score_grads(grad_cmix, cross_prob, memory_values)
    grad_cq = to_queries(cross_score, memory_keys)
    prior_part = (
        jnp.sum(cross_score, axis=(1, 2), dtype=jnp.float32)
        .reshape(seqs_here, slots, MEM_P)
        .sum(axis=-1)
    )
    prior_grad = jnp.where(usable, lax.psum(prior_part, "index"), 0.0)
    score_doc = jnp.where(
        usable, prior_grad - passage_prob * jnp.sum(prior_grad, axis=1, keepdims=True), 0.0
    )
    question_part = jnp.einsum(
        "sk,skc->sc",
        jnp.where(owned_slot, score_doc, 0.0),
        picked.astype(jnp.float32),
        precision=lax.Precision.HIGHEST,
    )
    question_gradient = lax.psum_scatter(question_part, "index", scatter_dimension=1, tiled=True)
    grad_cq_low = grad_cq.astype(jnp.bfloat16)
    grad_first = grad_second_in + project_back(grad_cq_low, attention_low[4])
    ck_part, cv_part = to_keys(cross_score, cross_prob, cross_query, grad_cmix)
    grad_ck, grad_cv = (
        lax.psum_scatter(
            ck_part.astype(jnp.bfloat16), "index", scatter_dimension=1, tiled=True
        ).astype(jnp.float32),
        lax.psum_scatter(
            cv_part.astype(jnp.bfloat16), "index", scatter_dimension=1, tiled=True
        ).astype(jnp.float32),
    )
    grad_ck_low = grad_ck.astype(jnp.bfloat16)
    grad_cv_low = grad_cv.astype(jnp.bfloat16)
    memory_gradient = project_back(grad_ck_low, attention_low[5]) + project_back(
        grad_cv_low, attention_low[6]
    )
    grad_first_in, gain_one, shift_one = first_back(grad_first)
    grad_self_low = grad_first_in.astype(jnp.bfloat16)
    grad_smix = project_back(grad_self_low, attention_low[3]).astype(jnp.bfloat16)
    self_score, row_inner = score_grads(grad_smix, self_prob, value_all)
    grad_sq = to_queries(self_score, key_all)
    key_part, value_part = to_keys(self_score, self_prob, self_query, grad_smix)
    grad_sk, grad_sv = (
        lax.psum_scatter(
            key_part.astype(jnp.bfloat16), "index", scatter_dimension=1, tiled=True
        ).astype(jnp.float32),
        lax.psum_scatter(
            value_part.astype(jnp.bfloat16), "index", scatter_dimension=1, tiled=True
        ).astype(jnp.float32),
    )
    grad_sq_low = grad_sq.astype(jnp.bfloat16)
    grad_sk_low = grad_sk.astype(jnp.bfloat16)
    grad_sv_low = grad_sv.astype(jnp.bfloat16)
    input_gradient = (
        grad_first_in
        + project_back(grad_sq_low, attention_low[0])
        + project_back(grad_sk_low, attention_low[1])
        + project_back(grad_sv_low, attention_low[2])
    )
    attention_grads = jnp.stack(
        [
            weight_grad(decoder_input, grad_sq_low),
            weight_grad(decoder_input, grad_sk_low),
            weight_grad(decoder_input, grad_sv_low),
            weight_grad(self_mixed, grad_self_low),
            weight_grad(first_low, grad_cq_low),
            weight_grad(encoder_memory, grad_ck_low),
            weight_grad(encoder_memory, grad_cv_low),
            weight_grad(cross_mixed, grad_cross_low),
        ]
    )
    vector_grads = jnp.concatenate(
        [
            jnp.stack(
                [
                    row_total(grad_sq),
                    row_total(grad_sv),
                    row_total(grad_first_in),
                    row_total(grad_cq),
                    row_total(grad_cv),
                    row_total(grad_second_in),
                ]
            ),
            row_total(grad_inner).reshape(ffn_width // model_width, model_width),
            jnp.stack(
                [
                    row_total(grad_third),
                    gain_one,
                    shift_one,
                    gain_two,
                    shift_two,
                    gain_three,
                    shift_three,
                ]
            ),
        ]
    )
    attention_sum, expand_sum, contract_sum, vector_sum = (
        lax.psum_scatter(attention_grads, ("dp", "index"), scatter_dimension=1, tiled=True),
        lax.psum_scatter(grad_expand, ("dp", "index"), scatter_dimension=0, tiled=True),
        lax.psum_scatter(grad_contract, ("dp", "index"), scatter_dimension=0, tiled=True),
        lax.psum_scatter(vector_grads, ("dp", "index"), scatter_dimension=1, tiled=True),
    )
    new_attention = adam_update(
        attention_weight,
        attention_mean,
        attention_square,
        attention_sum,
        rate_attention,
        decay_matrix,
    )
    new_expand = adam_update(
        expand_weight, expand_mean, expand_square, expand_sum, rate_expand, decay_matrix
    )
    new_contract = adam_update(
        contract_weight, contract_mean, contract_square, contract_sum, rate_contract, decay_matrix
    )
    new_vector = adam_update(
        vector_params, vector_mean, vector_square, vector_sum, rate_vector, 0.0
    )
    return (
        layer_output.astype(jnp.bfloat16),
        input_gradient,
        memory_gradient,
        question_gradient,
        new_attention[0],
        new_attention[1],
        new_attention[2],
        new_expand[0],
        new_expand[1],
        new_expand[2],
        new_contract[0],
        new_contract[1],
        new_contract[2],
        new_vector[0],
        new_vector[1],
        new_vector[2],
    )


NT = (((1,), (1,)), ((), ()))
NN = (((1,), (0,)), ((), ()))
TN = (((0,), (0,)), ((), ()))
CHIPS = 4
DP_ORDER = (0, 2, 1, 3)
VMEM_LIMIT = 56 << 20


def dot(left_side, right_side, dims):
    return lax.dot_general(left_side, right_side, dims, preferred_element_type=jnp.float32)


def norm_parts(hidden):
    center = hidden - jnp.mean(hidden, axis=-1, keepdims=True)
    inverse = lax.rsqrt(jnp.mean(center * center, axis=-1, keepdims=True) + norm_eps)
    return center * inverse, inverse


def norm_back(gradient, unit, inverse, gain):
    scaled = gradient * gain
    return inverse * (
        scaled
        - jnp.mean(scaled, axis=-1, keepdims=True)
        - unit * jnp.mean(scaled * unit, axis=-1, keepdims=True)
    )


def column_sum(values):
    return jnp.sum(values, axis=0, keepdims=True)


def join(parts, place=None):
    picked = [parts[j] if place is None else parts[j, place] for j in range(parts.shape[0])]
    return jnp.concatenate(
        [block.reshape(block.shape[0] * block.shape[1], block.shape[2]) for block in picked],
        axis=1,
    )


def spread(out_ref, value):
    count, seqs, rows, width = out_ref.shape
    for j in range(count):
        out_ref[j] = value[:, j * width : (j + 1) * width].reshape(seqs, rows, width)


def times(activation, weight):
    count, groups, rows, width = weight.shape
    depth = count * rows
    total = None
    for d in range(groups):
        part = dot(
            activation[:, d * depth : (d + 1) * depth], weight[:, d].reshape(depth, width), NN
        )
        total = part if total is None else total + part
    return total


def times_back(gradient, weight):
    count, groups, rows, width = weight.shape
    depth = count * rows
    return jnp.concatenate(
        [dot(gradient, weight[:, d].reshape(depth, width), NT) for d in range(groups)], axis=1
    )


def outer(out_ref, left_side, gradient):
    count, groups, rows, width = out_ref.shape
    depth = count * rows
    for d in range(groups):
        out_ref[:, d] = (
            dot(left_side[:, d * depth : (d + 1) * depth], gradient, TN)
            .astype(jnp.bfloat16)
            .reshape(count, rows, width)
        )


def whole(array):
    return pl.BlockSpec(array.shape, lambda *_, rank=len(array.shape): (0,) * rank)


def shape(dims, dtype):
    return jax.ShapeDtypeStruct(tuple(dims), dtype)


def params():
    return pltpu.CompilerParams(vmem_limit_bytes=VMEM_LIMIT)


def cost(flops, moved):
    return pl.CostEstimate(flops=int(flops) // 16, bytes_accessed=int(moved) // 16, transcendentals=0)


def in_head(dims, head_width, head):
    return lax.broadcasted_iota(jnp.int32, dims, 1) // head_width == head


def attend_forward_kernel(causal, head_width, q_ref, k_ref, v_ref, bias_ref, out_ref, stat_ref):
    count, _, tile, width = q_ref.shape
    keys = k_ref.shape[0] * k_ref.shape[2]
    key_rows, values = k_ref[...].reshape(keys, width), v_ref[...].reshape(keys, width)
    step = 4
    rows = step * tile
    for b in range(count // step):
        queries = q_ref[b * step : (b + 1) * step].reshape(rows, width)
        seen = (b + 1) * rows if causal else keys
        mixed = None
        for h in range(width // head_width):
            mask = in_head((rows, width), head_width, h)
            scores = dot(
                jnp.where(mask, queries * 0.125, 0).astype(jnp.bfloat16), key_rows[:seen], NT
            )
            if causal:
                corner = scores[:, seen - rows :]
                corner = jnp.where(
                    lax.broadcasted_iota(jnp.int32, corner.shape, 1)
                    <= lax.broadcasted_iota(jnp.int32, corner.shape, 0),
                    corner,
                    negative_fill,
                )
                if b == 0:
                    scores = corner
                else:
                    scores = jnp.concatenate([scores[:, : seen - rows], corner], axis=1)
            else:
                scores = scores + bias_ref[0]
            peak = jnp.max(scores, axis=1, keepdims=True)
            exponent = jnp.exp(scores - peak)
            total = jnp.sum(exponent, axis=1, keepdims=True)
            part = dot(exponent.astype(jnp.bfloat16), values[:seen], NN) * (1.0 / total)
            mixed = part if mixed is None else jnp.where(mask, part, mixed)
            log_total = jnp.broadcast_to(peak + jnp.log(total), (rows, 128))
            stat_ref[0, h : h + 1, b * rows : (b + 1) * rows] = log_total.T[0:1]
        out_ref[b * step : (b + 1) * step] = mixed.astype(jnp.bfloat16).reshape(
            step, 1, tile, width
        )


def attend_backward_kernel(
    causal,
    head_width,
    q_ref,
    k_ref,
    v_ref,
    grad_ref,
    stat_ref,
    bias_ref,
    _,
    dq_ref,
    dkv_ref,
    prior_ref,
    dk_sum,
    dv_sum,
    prior_sum,
):
    count, _, tile, width = q_ref.shape
    keys = k_ref.shape[0] * k_ref.shape[2]
    key_rows, values = k_ref[...].reshape(keys, width), v_ref[...].reshape(keys, width)
    step = 2
    rows = step * tile
    if not causal:
        bias = jnp.broadcast_to(bias_ref[0], (128, keys)).T[:, :1]
    dk_sum[...] = jnp.zeros_like(dk_sum)
    dv_sum[...] = jnp.zeros_like(dv_sum)
    if not causal:
        prior_sum[...] = jnp.zeros_like(prior_sum)
    for b in range(count // step):
        queries = q_ref[b * step : (b + 1) * step].reshape(rows, width)
        gradient = grad_ref[b * step : (b + 1) * step].reshape(rows, width)
        seen = (b + 1) * rows if causal else keys
        query_grad = None
        for h in range(width // head_width):
            mask = in_head((rows, width), head_width, h)
            one_query = jnp.where(mask, queries * 0.125, 0).astype(jnp.bfloat16)
            one_grad = jnp.where(mask, gradient, 0).astype(jnp.bfloat16)
            scores = dot(key_rows[:seen], one_query, NT)
            if causal:
                corner = scores[seen - rows :]
                corner = jnp.where(
                    lax.broadcasted_iota(jnp.int32, corner.shape, 0)
                    <= lax.broadcasted_iota(jnp.int32, corner.shape, 1),
                    corner,
                    negative_fill,
                )
                if b == 0:
                    scores = corner
                else:
                    scores = jnp.concatenate([scores[: seen - rows], corner], axis=0)
            else:
                scores = scores + bias
            prob = jnp.exp(scores - stat_ref[0, h : h + 1, b * rows : (b + 1) * rows])
            grad_prob = dot(values[:seen], one_grad, NT)
            inner = jnp.sum(prob * grad_prob, axis=0, keepdims=True)
            grad_score = prob * (grad_prob - inner)
            score_low = grad_score.astype(jnp.bfloat16)
            dv_sum[:seen] += dot(prob.astype(jnp.bfloat16), one_grad, NN)
            dk_sum[:seen] += dot(score_low, one_query, NN)
            if not causal:
                partial_sum = grad_score[:, :128]
                for piece in range(128, rows, 128):
                    partial_sum = partial_sum + grad_score[:, piece : piece + 128]
                prior_sum[...] += partial_sum
            part = dot(score_low, key_rows[:seen], TN)
            query_grad = part if query_grad is None else jnp.where(mask, part, query_grad)
        dq_ref[b * step : (b + 1) * step] = (
            (query_grad * 0.125).astype(jnp.bfloat16).reshape(step, 1, tile, width)
        )
    dkv_ref[:, 0] = dk_sum[...].astype(jnp.bfloat16).reshape(k_ref.shape)
    dkv_ref[:, 1] = dv_sum[...].astype(jnp.bfloat16).reshape(k_ref.shape)
    if causal:
        prior_ref[...] = jnp.zeros_like(prior_ref)
    else:
        prior_ref[0] = column_sum(prior_sum[...].T)


def pick(array, place):
    count, _, _, rows, width = array.shape
    return pl.BlockSpec((count, None, 1, rows, width), lambda s: (0, place, s, 0, 0))


def attend(causal, queries, query_at, keys, key_at, value_at, bias):
    count, _, seqs, tile, width = queries.shape
    key_rows = keys.shape[0] * keys.shape[3]
    head_width = width * count // HEADS
    length = count * tile
    heads = width // head_width
    return pl.pallas_call(
        partial(attend_forward_kernel, causal, head_width),
        grid=(seqs,),
        in_specs=[
            pick(queries, query_at),
            pick(keys, key_at),
            pick(keys, value_at),
            pl.BlockSpec(memory_space=pl.ANY)
            if causal
            else pl.BlockSpec((1, 1, key_rows), lambda s: (s, 0, 0)),
        ],
        out_specs=[
            pl.BlockSpec((count, 1, tile, width), lambda s: (0, s, 0, 0)),
            pl.BlockSpec((1, heads, length), lambda s: (s, 0, 0)),
        ],
        out_shape=[
            shape((count, seqs, tile, width), jnp.bfloat16),
            shape((seqs, heads, length), jnp.float32),
        ],
        compiler_params=params(),
        cost_estimate=cost(
            16 * seqs * length * key_rows * width, 4 * seqs * (length + key_rows) * width
        ),
        name="attend_self" if causal else "attend_memory",
    )(queries, keys, keys, bias)


def attend_back(
    causal, queries, query_at, keys, key_at, value_at, gradient, stat, bias, after
):
    count, _, seqs, tile, width = queries.shape
    key_tile = keys.shape[3]
    key_rows = count * key_tile
    head_width = width * count // HEADS
    length = count * tile
    heads = width // head_width
    return pl.pallas_call(
        partial(attend_backward_kernel, causal, head_width),
        grid=(seqs,),
        in_specs=[
            pick(queries, query_at),
            pick(keys, key_at),
            pick(keys, value_at),
            pl.BlockSpec((count, 1, tile, width), lambda s: (0, s, 0, 0)),
            pl.BlockSpec((1, heads, length), lambda s: (s, 0, 0)),
            pl.BlockSpec(memory_space=pl.ANY)
            if causal
            else pl.BlockSpec((1, 1, key_rows), lambda s: (s, 0, 0)),
            pl.BlockSpec(memory_space=pl.ANY),
        ],
        out_specs=[
            pl.BlockSpec((count, 1, tile, width), lambda s: (0, s, 0, 0)),
            pl.BlockSpec((count, 2, 1, key_tile, width), lambda s: (0, 0, s, 0, 0)),
            pl.BlockSpec((1, 1, key_rows), lambda s: (s, 0, 0)),
        ],
        out_shape=[
            shape((count, seqs, tile, width), jnp.bfloat16),
            shape((count, 2, seqs, key_tile, width), jnp.bfloat16),
            shape((seqs, 1, key_rows), jnp.float32),
        ],
        scratch_shapes=[
            pltpu.VMEM((key_rows, width), jnp.float32),
            pltpu.VMEM((key_rows, width), jnp.float32),
            pltpu.VMEM((key_rows, 128), jnp.float32),
        ],
        compiler_params=params(),
        cost_estimate=cost(
            40 * seqs * length * key_rows * width, 8 * seqs * (length + key_rows) * width
        ),
        name="attend_self_back" if causal else "attend_memory_back",
    )(queries, keys, keys, gradient, stat, bias, after)


def take_columns(scratch, slices, first):
    width = slices.shape[3]
    depth = scratch.shape[0]
    rows = depth // (slices.shape[0] * slices.shape[1])
    for m in range(scratch.shape[1] // width):
        start = (first + m) * rows
        scratch[:, m * width : (m + 1) * width] = slices[:, :, start : start + rows].reshape(
            depth, width
        )


def columns_kernel(first, start, seqs, rows, row_ref, slice_ref, bias_ref, out_ref, weight, taken, sem):
    def copy(i):
        return pltpu.make_async_copy(
            row_ref.at[i, :, pl.ds(start, rows)], taken.at[i], sem.at[i]
        )

    count, many = out_ref.shape[:2]
    width = out_ref.shape[4]
    for i in range(count):
        copy(i).start()
    take_columns(weight, slice_ref, first)
    for i in range(count):
        copy(i).wait()
        result = dot(taken[i].reshape(seqs * rows, weight.shape[0]), weight[...], NN) + bias_ref[...]
        for m in range(many):
            out_ref[i, m] = (
                result[:, m * width : (m + 1) * width]
                .astype(jnp.bfloat16)
                .reshape(seqs, rows, width)
            )


def project_columns(name, gathered_rows, start, rows, slices, first, many, bias):
    count, seqs, _, depth = gathered_rows.shape
    width = slices.shape[3]
    out = shape((count, many, seqs, rows, width), jnp.bfloat16)
    return pl.pallas_call(
        partial(columns_kernel, first, start, seqs, rows),
        grid=(1,),
        in_specs=[pl.BlockSpec(memory_space=pl.ANY), whole(slices), whole(bias)],
        out_specs=whole(out),
        out_shape=out,
        scratch_shapes=[
            pltpu.VMEM((depth, many * width), jnp.bfloat16),
            pltpu.VMEM((count, seqs, rows, depth), jnp.bfloat16),
            pltpu.SemaphoreType.DMA((count,)),
        ],
        compiler_params=params(),
        cost_estimate=cost(
            2 * many * count * seqs * rows * depth * width, 2 * count * seqs * rows * depth
        ),
        name=name,
    )(gathered_rows, slices, bias)


def columns_back_kernel(first, start, order, row_ref, *refs):
    grad_refs, (slice_ref, mine_out, other_out, dw_ref, bias_ref) = refs[:-12], refs[-12:-7]
    weight, taken, gradients, moved, total, in_sem, out_sem = refs[-7:]
    count, seqs, rows, depth = taken.shape
    half = count // 2

    def bring(r):
        return pltpu.make_async_copy(
            row_ref.at[order[r], :, pl.ds(start, rows)], taken.at[r], in_sem.at[r]
        )

    def send(r):
        there = (mine_out, other_out)[r // half].at[r % half, 0]
        return pltpu.make_async_copy(moved.at[r], there, out_sem.at[r])

    for r in range(count):
        bring(r).start()
    take_columns(weight, slice_ref, first)
    size = seqs * rows
    for r in range(count):
        i = order[r]
        pieces = []
        for grad_ref in grad_refs:
            width = grad_ref.shape[-1]
            for m in range(grad_ref.shape[1] if len(grad_ref.shape) == 5 else 1):
                piece = grad_ref[i, m] if len(grad_ref.shape) == 5 else grad_ref[i]
                pieces.append(piece.reshape(size, width))
        gradient = jnp.concatenate(pieces, axis=1)
        gradients[r * size : (r + 1) * size] = gradient
        moved[r] = dot(gradient, weight[...], NT).astype(jnp.bfloat16)
        send(r).start()
    whole_gradient = gradients[...]
    bias_ref[...] = column_sum(whole_gradient.astype(jnp.float32))
    for r in range(count):
        bring(r).wait()
    total[...] = dot(whole_gradient, taken[...].reshape(count * size, depth), TN)
    groups, shards, all_rows, _ = dw_ref.shape
    part = depth // (groups * shards)
    for m in range(all_rows // part):
        dw_ref[:, :, m * part : (m + 1) * part] = (
            total[m * width : (m + 1) * width]
            .T.astype(jnp.bfloat16)
            .reshape(groups, shards, part, width)
        )
    for r in range(count):
        send(r).wait()


def project_columns_back(name, order, gathered_rows, start, rows, gradients, slices, first, many):
    count, seqs, _, depth = gathered_rows.shape
    half = count // 2
    groups, shards, _, width = slices.shape
    part = depth // (groups * shards)
    anywhere = pl.BlockSpec(memory_space=pl.ANY)
    halves = shape((half, 1, seqs * rows, depth), jnp.bfloat16)
    dw_shape = shape((groups, shards, many * part, width), jnp.bfloat16)
    bias = shape((1, many * width), jnp.float32)
    return pl.pallas_call(
        partial(columns_back_kernel, first, start),
        grid_spec=pltpu.PrefetchScalarGridSpec(
            num_scalar_prefetch=1,
            grid=(1,),
            in_specs=[anywhere, *[whole(array) for array in gradients], whole(slices)],
            out_specs=[anywhere, anywhere, whole(dw_shape), whole(bias)],
            scratch_shapes=[
                pltpu.VMEM((depth, many * width), jnp.bfloat16),
                pltpu.VMEM((count, seqs, rows, depth), jnp.bfloat16),
                pltpu.VMEM((count * seqs * rows, many * width), jnp.bfloat16),
                pltpu.VMEM((count, seqs * rows, depth), jnp.bfloat16),
                pltpu.VMEM((many * width, depth), jnp.float32),
                pltpu.SemaphoreType.DMA((count,)),
                pltpu.SemaphoreType.DMA((count,)),
            ],
        ),
        out_shape=[halves, halves, dw_shape, bias],
        compiler_params=params(),
        cost_estimate=cost(
            4 * many * count * seqs * rows * depth * width, 4 * count * seqs * rows * depth
        ),
        name=name,
    )(order, gathered_rows, *gradients, slices)


def gathered(weights, width, place):
    count, groups, rows, _ = weights.shape
    return pl.BlockSpec((count, groups, rows, width), lambda *_: (0, 0, 0, place))


def first_kernel(
    mixed_ref, x_ref, out_w, query_w, vector_ref, _, mixed_out, in_out, low_out, query_out
):
    mixed = join(mixed_ref)
    mixed_out[...] = mixed
    first_in = x_ref[...].astype(jnp.float32) + times(mixed, out_w) + vector_ref[2:3]
    in_out[...] = first_in
    unit, _ = norm_parts(first_in)
    low = (unit * vector_ref[11:12] + vector_ref[12:13]).astype(jnp.bfloat16)
    low_out[...] = low
    spread(query_out, (times(low, query_w) + vector_ref[3:4]).astype(jnp.bfloat16))


def first_forward(mixed, x_rows, weights, vectors, after):
    rows, depth = x_rows.shape
    return pl.pallas_call(
        first_kernel,
        grid=(1,),
        in_specs=[
            whole(mixed),
            whole(x_rows),
            gathered(weights, depth, 0),
            gathered(weights, depth, 1),
            whole(vectors),
            pl.BlockSpec(memory_space=pl.ANY),
        ],
        out_specs=[whole(x_rows), whole(x_rows), whole(x_rows), whole(mixed)],
        out_shape=[
            shape((rows, depth), jnp.bfloat16),
            shape((rows, depth), jnp.float32),
            shape((rows, depth), jnp.bfloat16),
            shape(mixed.shape, jnp.bfloat16),
        ],
        compiler_params=params(),
        cost_estimate=cost(4 * rows * depth * depth, 4 * depth * depth),
        name="first_forward",
    )(mixed, x_rows, weights, weights, vectors, after)


def ffn_kernel(
    order,
    places,
    mixed_ref,
    first_ref,
    out_w,
    vector_ref,
    bias_ref,
    grad_ref,
    wide_ref,
    *refs,
):
    contract_refs, refs = refs[:8], refs[8:]
    mixed_out, layer_out, wide_grad = refs[:3]
    contract_grads, refs = refs[3:11], refs[11:]
    dbias_ref, second_grad, cross_low, mixed_grad, stat_out, columns, contracts = refs[:7]
    active, slope, low, third_low, second_in, total, wide_sem, contract_sem = refs[7:]
    blocks, count, groups, rows, block = columns.shape
    part = block // CHIPS
    depth = vector_ref.shape[1]

    def wide_copies(t, array, outward):
        result = []
        for k in range(CHIPS):
            column = pl.multiple_of(order[t % 2 * CHIPS + k] * part, part)
            row = pl.multiple_of(places[t // 2] * rows, rows)
            there = array.at[:, :, pl.ds(row, rows), pl.ds(column, part)]
            here = columns.at[t, :, :, :, pl.ds(k * part, part)]
            ends = (here, there) if outward else (there, here)
            result.append(pltpu.make_async_copy(*ends, wide_sem.at[t, k]))
        return result

    def contract_copies(t, pieces, outward):
        near, far = divmod(DP_ORDER[t // 2], 2)
        first = pieces[t % 2 * 4 + far].at[near]
        last = pieces[t % 2 * 4 + 2 + near].at[far]
        result = []
        for half, there in enumerate((first, last)):
            here = contracts.at[t, pl.ds(half * CHIPS // 2, CHIPS // 2)]
            ends = (here, there) if outward else (there, here)
            result.append(pltpu.make_async_copy(*ends, contract_sem.at[t, half]))
        return result

    for t in range(blocks):
        for copy in wide_copies(t, wide_ref, False):
            copy.start()
        for copy in contract_copies(t, contract_refs, False):
            copy.start()

    mixed = join(mixed_ref)
    mixed_out[...] = mixed
    unit, _ = norm_parts(first_ref[...])
    second_in[...] = (
        unit * vector_ref[11:12] + vector_ref[12:13] + times(mixed, out_w) + vector_ref[5:6]
    )
    unit, _ = norm_parts(second_in[...])
    second = unit * vector_ref[13:14] + vector_ref[14:15]
    low[...] = second.astype(jnp.bfloat16)
    total[...] = second + vector_ref[10:11]

    def shard(t, k):
        return places[t // 2] * count + order[t % 2 * CHIPS + k]

    for t in range(blocks):
        for copy in wide_copies(t, wide_ref, False):
            copy.wait()
        bias = jnp.concatenate([bias_ref[pl.ds(shard(t, k), 1)] for k in range(CHIPS)], axis=1)
        inner = times(low[...], columns.at[t]) + bias
        phi = 0.5 + 0.5 * lax.erf(inner * (0.5**0.5))
        out = (inner * phi).astype(jnp.bfloat16)
        active[t] = out
        slope[t] = phi + inner * jnp.exp(-0.5 * inner * inner) * 0.3989422804014327
        for copy in contract_copies(t, contract_refs, False):
            copy.wait()
        total[...] += dot(out, contracts[t].reshape(block, depth), NN)

    unit, inverse = norm_parts(total[...])
    gain = vector_ref[15:16]
    layer_out[...] = (unit * gain + vector_ref[16:17]).astype(jnp.bfloat16)
    gradient = grad_ref[...].astype(jnp.float32)
    grad_third = norm_back(gradient, unit, inverse, gain)
    stat_out[...] = jnp.zeros_like(stat_out)
    stat_out[0:1] = column_sum(grad_third)
    stat_out[1:2] = column_sum(gradient * unit)
    stat_out[2:3] = column_sum(gradient)
    total[...] = grad_third
    third_low[...] = grad_third.astype(jnp.bfloat16)
    turned = low[...].T

    for t in range(blocks):
        grad_inner = dot(third_low[...], contracts[t].reshape(block, depth), NT) * slope[t]
        inner_low = grad_inner.astype(jnp.bfloat16)
        sums = column_sum(grad_inner)
        for k in range(CHIPS):
            dbias_ref[pl.ds(shard(t, k), 1)] = sums[:, k * part : (k + 1) * part]
        contracts[t] = (
            dot(active[t], third_low[...], TN).astype(jnp.bfloat16).reshape(CHIPS, part, depth)
        )
        for copy in contract_copies(t, contract_grads, True):
            copy.start()
        total[...] += times_back(inner_low, columns.at[t])
        result = dot(turned, inner_low, NN).astype(jnp.bfloat16)
        for d in range(groups):
            columns[t, :, d] = result[d * count * rows : (d + 1) * count * rows].reshape(
                count, rows, block
            )
        for copy in wide_copies(t, wide_grad, True):
            copy.start()

    unit, inverse = norm_parts(second_in[...])
    grad_second = total[...]
    grad_in = norm_back(grad_second, unit, inverse, vector_ref[13:14])
    second_grad[...] = grad_in
    grad_low = grad_in.astype(jnp.bfloat16)
    cross_low[...] = grad_low
    spread(mixed_grad, times_back(grad_low, out_w).astype(jnp.bfloat16))
    stat_out[8:9] = column_sum(grad_in)
    stat_out[9:10] = column_sum(grad_second * unit)
    stat_out[10:11] = column_sum(grad_second)
    for t in range(blocks):
        for copy in contract_copies(t, contract_grads, True) + wide_copies(t, wide_grad, True):
            copy.wait()


def ffn(orders, mixed, first_in, wide, contract, vectors, bias, output_grad):
    rows, depth = first_in.shape
    hidden = bias.size
    block = depth // 2
    count, groups, all_rows, _ = wide.shape
    part = depth // (count * groups)
    blocks = hidden // block
    full = whole(first_in)
    anywhere = pl.BlockSpec(memory_space=pl.ANY)
    heads_out = shape(mixed.shape, jnp.bfloat16)
    stats = shape((16, depth), jnp.float32)
    return pl.pallas_call(
        ffn_kernel,
        grid_spec=pltpu.PrefetchScalarGridSpec(
            num_scalar_prefetch=2,
            grid=(1,),
            in_specs=[
                whole(mixed),
                full,
                pl.BlockSpec((count, groups, part, depth), lambda *_: (0, 0, groups, 0)),
                whole(vectors),
                whole(bias),
                full,
                *[anywhere] * 9,
            ],
            out_specs=[
                full,
                full,
                *[anywhere] * 9,
                whole(bias),
                full,
                full,
                whole(heads_out),
                whole(stats),
            ],
            scratch_shapes=[
                pltpu.VMEM((blocks, count, groups, part, block), jnp.bfloat16),
                pltpu.VMEM((blocks, CHIPS) + contract[0].shape[2:], jnp.bfloat16),
                pltpu.VMEM((blocks, rows, block), jnp.bfloat16),
                pltpu.VMEM((blocks, rows, block), jnp.float32),
                pltpu.VMEM((rows, depth), jnp.bfloat16),
                pltpu.VMEM((rows, depth), jnp.bfloat16),
                pltpu.VMEM((rows, depth), jnp.float32),
                pltpu.VMEM((rows, depth), jnp.float32),
                pltpu.SemaphoreType.DMA((blocks, CHIPS)),
                pltpu.SemaphoreType.DMA((blocks, 2)),
            ],
        ),
        out_shape=[
            shape((rows, depth), jnp.bfloat16),
            shape((rows, depth), jnp.bfloat16),
            shape((count, groups, all_rows - part, depth), jnp.bfloat16),
            *[shape(piece.shape, jnp.bfloat16) for piece in contract],
            shape(bias.shape, jnp.float32),
            shape((rows, depth), jnp.float32),
            shape((rows, depth), jnp.bfloat16),
            heads_out,
            stats,
        ],
        compiler_params=params(),
        cost_estimate=cost(12 * rows * depth * hidden, 16 * depth * hidden),
        name="ffn",
    )(*orders, mixed, first_in, wide, vectors, bias, output_grad, wide, *contract)


def first_back_kernel(
    dq_ref,
    second_grad,
    first_ref,
    out_w,
    query_w,
    vector_ref,
    _,
    query_low,
    grad_in_out,
    self_low,
    mixed_grad,
    stat_out,
):
    query_grad = join(dq_ref)
    query_low[...] = query_grad
    grad_first = second_grad[...] + times_back(query_grad, query_w)
    unit, inverse = norm_parts(first_ref[...])
    grad_in = norm_back(grad_first, unit, inverse, vector_ref[11:12])
    grad_in_out[...] = grad_in
    grad_low = grad_in.astype(jnp.bfloat16)
    self_low[...] = grad_low
    spread(mixed_grad, times_back(grad_low, out_w).astype(jnp.bfloat16))
    stat_out[...] = jnp.zeros_like(stat_out)
    stat_out[0:1] = column_sum(query_grad.astype(jnp.float32))
    stat_out[1:2] = column_sum(grad_in)
    stat_out[2:3] = column_sum(grad_first * unit)
    stat_out[3:4] = column_sum(grad_first)


def first_back(dq, second_grad, first_in, weights, vectors, after):
    rows, depth = first_in.shape
    full = whole(first_in)
    return pl.pallas_call(
        first_back_kernel,
        grid=(1,),
        in_specs=[
            whole(dq),
            full,
            full,
            gathered(weights, depth, 0),
            gathered(weights, depth, 1),
            whole(vectors),
            pl.BlockSpec(memory_space=pl.ANY),
        ],
        out_specs=[full, full, full, whole(dq), pl.BlockSpec((8, depth), lambda *_: (0, 0))],
        out_shape=[
            shape((rows, depth), jnp.bfloat16),
            shape((rows, depth), jnp.float32),
            shape((rows, depth), jnp.bfloat16),
            shape(dq.shape, jnp.bfloat16),
            shape((8, depth), jnp.float32),
        ],
        compiler_params=params(),
        cost_estimate=cost(4 * rows * depth * depth, 4 * depth * depth),
        name="first_back",
    )(dq, second_grad, first_in, weights, weights, vectors, after)


def weight_grads_kernel(
    order,
    mixed,
    self_low,
    first_low,
    query_low,
    cross,
    cross_low,
    mine_out,
    other_out,
    result,
):
    step = pl.program_id(0)
    pairs = ((mixed, self_low), (first_low, query_low), (cross, cross_low))
    half, groups, part, _ = mine_out.shape
    for m, (left_side, gradient) in enumerate(pairs):

        @pl.when(step == m)
        def _(left_side=left_side, gradient=gradient):
            result[...] = dot(left_side[...], gradient[...], TN).astype(jnp.bfloat16)

    for d in range(groups):
        for k in range(half):
            for p, out_ref in enumerate((mine_out, other_out)):
                row = pl.multiple_of((2 * half * d + order[p * half + k]) * part, part)
                out_ref[k, d] = result[pl.ds(row, part)]


def weight_grads(dims, order, mixed, self_low, first_low, query_low, cross, cross_low):
    count, groups, part, depth = dims
    half = pl.BlockSpec((count // 2, groups, part, depth), lambda m, _: (0, 0, m, 0))
    return pl.pallas_call(
        weight_grads_kernel,
        grid_spec=pltpu.PrefetchScalarGridSpec(
            num_scalar_prefetch=1,
            grid=(3,),
            in_specs=[whole(mixed)] * 6,
            out_specs=[half, half],
            scratch_shapes=[pltpu.VMEM((depth, depth), jnp.bfloat16)],
        ),
        out_shape=[shape((count // 2, groups, 3 * part, depth), jnp.bfloat16)] * 2,
        compiler_params=params(),
        cost_estimate=cost(6 * mixed.shape[0] * depth * depth, 6 * depth * depth),
        name="weight_grads",
    )(order, mixed, self_low, first_low, query_low, cross, cross_low)


def send_dp(piece):
    size = lax.axis_size("dp")
    return [
        lax.ppermute(piece, "dp", [(i, (i + shift) % size) for i in range(size)])
        for shift in range(1, size)
    ]


def place_dp(piece, arrived):
    size, me = lax.axis_size("dp"), lax.axis_index("dp")
    result = jnp.zeros((size,) + piece.shape, piece.dtype)
    result = lax.dynamic_update_index_in_dim(result, piece, me, 0)
    for shift, got in enumerate(arrived, 1):
        result = lax.dynamic_update_index_in_dim(result, got, lax.rem(me - shift + size, size), 0)
    return result


class HalvingDp:
    def __init__(self, pieces):
        me = lax.axis_index("dp")
        self.parts = [
            lax.dynamic_index_in_dim(pieces, me ^ flip, 0, keepdims=False) for flip in DP_ORDER
        ]

    def first(self):
        return jnp.stack(self.parts[2:]).astype(jnp.bfloat16)

    def second(self, got):
        self.got = got
        return (
            self.parts[1].astype(jnp.float32) + self.got[1].astype(jnp.float32)
        ).astype(jnp.bfloat16)

    def finish(self, last):
        return sum(one.astype(jnp.float32) for one in (self.parts[0], self.got[0], last))


def relative_order():
    size, me = lax.axis_size("index"), lax.axis_index("index")
    steps = jnp.arange(size // 2, dtype=jnp.int32) * 2
    return jnp.concatenate([me ^ steps, me ^ 1 ^ steps])


def exchange(piece, flip):
    size = lax.axis_size("index")
    return lax.ppermute(piece, "index", [(i, i ^ flip) for i in range(size)])


def exchange_dp(piece, flip):
    size = lax.axis_size("dp")
    return lax.ppermute(piece, "dp", [(i, i ^ flip) for i in range(size)])


def add_kernel(*refs):
    total = sum(ref[...].astype(jnp.float32) for ref in refs[:-1])
    refs[-1][...] = total.astype(jnp.bfloat16)


def add(*terms):
    flat, specs = [], []
    first = terms[0]
    dims = first[0].shape[1:] if isinstance(first, tuple) else first.shape
    rows = 1
    for size in dims[:-1]:
        rows *= size
    block = min(rows, 256)
    for term in terms:
        array, entry = term if isinstance(term, tuple) else (term, 0)
        flat.append(array.reshape(-1, dims[-1]))
        start = entry * rows // block
        specs.append(pl.BlockSpec((block, dims[-1]), lambda i, start=start: (start + i, 0)))
    return pl.pallas_call(
        add_kernel,
        grid=(rows // block,),
        in_specs=specs,
        out_specs=pl.BlockSpec((block, dims[-1]), lambda i: (i, 0)),
        out_shape=shape((rows, dims[-1]), jnp.bfloat16),
        compiler_params=params(),
        cost_estimate=cost(0, 0),
        name="add",
    )(*flat).reshape(dims)


def combine_kernel(plan, *refs):
    ins, outs = list(refs[: -len(plan)]), refs[-len(plan) :]
    for out_ref, entries in zip(outs, plan):
        for e, segments in enumerate(entries):
            start = 0
            for offsets, rows in segments:
                terms, ins = ins[: len(offsets)], ins[len(offsets) :]
                total = sum(
                    ref[0, offset : offset + rows].astype(jnp.float32)
                    for ref, offset in zip(terms, offsets)
                )
                out_ref[e, start : start + rows] = total.astype(jnp.bfloat16)
                start += rows


def combine(*outputs):
    arrays, specs, plan, shapes = [], [], [], []
    for entries in outputs:
        plan.append([])
        for segments in entries:
            plan[-1].append([])
            for terms in segments:
                offsets = []
                for array, e, rows, start in terms:
                    block, place, offset = rows, start // rows, 0
                    if start % rows or array.shape[1] % rows:
                        block, place, offset = array.shape[1], 0, start
                    offsets.append(offset)
                    arrays.append(array)
                    specs.append(
                        pl.BlockSpec(
                            (1, block, array.shape[2]), lambda i, e=e, place=place: (e, place, 0)
                        )
                    )
                plan[-1][-1].append((offsets, terms[0][2]))
        rows = sum(rows for _, rows in plan[-1][0])
        shapes.append(shape((len(entries), rows, arrays[0].shape[2]), jnp.bfloat16))
    return pl.pallas_call(
        partial(combine_kernel, plan),
        grid=(1,),
        in_specs=specs,
        out_specs=[whole(out) for out in shapes],
        out_shape=shapes,
        compiler_params=params(),
        cost_estimate=cost(0, 0),
        name="combine",
    )(*arrays)


class Halving:
    def __init__(self, chips):
        self.chips = chips
        self.middle = chips[0][0][0].shape[1] // 2

    def terms(self, k, half, *more):
        middle = self.middle
        return [(array, e, middle, half * middle) for array, e in self.chips[k]] + [
            (array, e, middle, start) for array, e, start in more
        ]

    def total(self, k, half, *more):
        rows = slice(half * self.middle, (half + 1) * self.middle)
        parts = [array[e, rows] for array, e in self.chips[k]] + [*more]
        return sum(one.astype(jnp.float32) for one in parts)

    def finish(self, top, low):
        return jnp.concatenate(
            [self.total(0, 0, self.got[0][0], top), self.total(0, 1, self.got[1][0], low)], axis=0
        )


def both_cores(mine, other):
    parts = [part.reshape(CHIPS, -1, part.shape[-1]) for part in (mine, other)]
    return Halving([[(part, k) for part in parts] for k in range(CHIPS)])


def firsts(*sums):
    return combine(
        [[one.terms(k, 0) for one in sums] for k in (1, 3)],
        [[one.terms(k, 1) for one in sums] for k in (2, 3)],
    )


def seconds(*sums):
    for one, top, low, start in sums:
        rows = slice(start, start + one.middle)
        one.got = top[:, rows], low[:, rows]
    top, low = combine(
        [[one.terms(2, 0, (top, 1, start)) for one, top, _, start in sums]],
        [[one.terms(1, 1, (low, 1, start)) for one, _, low, start in sums]],
    )
    return top[0], low[0]


def send_first(top, low):
    return [exchange(top, 2), exchange(low, 4)]


def send_last(top, low):
    return [exchange(top, 4), exchange(low, 2)]


def split_rows(arrays, rows):
    return [a[..., :rows, :] for a in arrays], [a[..., rows:, :] for a in arrays]


def small_send(values):
    size = lax.axis_size("index")
    flat = jnp.pad(values.reshape(-1), (0, 1024 - values.size)).reshape(1, 8, 128)
    return swap(jnp.broadcast_to(flat, (size, 8, 128)))


def small_take(arrived, dims):
    size = 1
    for dim in dims:
        size *= dim
    return jnp.sum(arrived, axis=0).reshape(-1)[:size].reshape(dims)


def hold_kernel(*_):
    pass


def hold(values, *others):
    anywhere = pl.BlockSpec(memory_space=pl.ANY)
    return pl.pallas_call(
        hold_kernel,
        in_specs=[anywhere] * (len(values) + len(others)),
        out_specs=[anywhere] * len(values),
        out_shape=[shape(value.shape, value.dtype) for value in values],
        input_output_aliases={i: i for i in range(len(values))},
        name="hold",
    )(*values, *others)


def swap(pieces):
    return lax.all_to_all(pieces, "index", 0, 0, tiled=True)


def head_body(
    decoder_input,
    encoder_memory,
    question_vectors,
    passage_vectors,
    passage_ids,
    valid_count,
    output_grad,
    attention_weight,
    expand_weight,
    contract_weight,
    vector_params,
    attention_mean,
    attention_square,
    expand_mean,
    expand_square,
    contract_mean,
    contract_square,
    vector_mean,
    vector_square,
):
    low = jnp.bfloat16
    count, groups = lax.axis_size("index"), lax.axis_size("dp")
    place = lax.axis_index("index")
    seqs, rows_here, depth = decoder_input.shape
    memory_here = encoder_memory.shape[1]
    width = depth // count
    part = attention_weight.shape[1]
    hidden = expand_weight.shape[1]
    vector_rows, vector_width = vector_params.shape
    question_width = question_vectors.shape[1]
    rows = seqs * rows_here

    attention_low = attention_weight.astype(low)
    extras = jnp.concatenate(
        [vector_params.astype(low).reshape(-1), question_vectors.reshape(-1)]
    )
    extra_rows = -(-extras.shape[0] // (16 * width)) * 16
    extras = jnp.pad(extras, (0, extra_rows * width - extras.shape[0])).reshape(
        1, extra_rows, width
    )
    split = jnp.concatenate([attention_low[:3], attention_low[5:7]], axis=0)
    columns = split.reshape(5, part, count, width).transpose(2, 0, 1, 3)
    package = jnp.concatenate(
        [
            columns.reshape(count, 5 * part, width),
            jnp.broadcast_to(extras, (count, extra_rows, width)),
        ],
        axis=1,
    )
    order = relative_order()
    memory_block = -(-memory_here // rows_here) * rows_here
    rows_all = lax.all_gather(
        jnp.concatenate(
            [
                jnp.pad(encoder_memory, ((0, 0), (0, memory_block - memory_here), (0, 0))),
                decoder_input,
            ],
            axis=1,
        ),
        "index",
        axis=0,
        tiled=False,
    )
    input_rows = (rows_all, memory_block, rows_here)
    memory_rows = (rows_all, 0, memory_here)
    square = attention_low[3:5].transpose(1, 0, 2).reshape(part, 2 * depth)
    received = swap(package)
    square_arrived = hold(send_dp(square), received)
    (received,) = hold([received], *square_arrived)
    received_sent = send_dp(received)
    (contract,) = hold([contract_weight.astype(low)], received)
    contract = [contract] + [exchange(contract, 2 * k) for k in range(1, CHIPS)]
    slices_arrived = hold(received_sent, *contract[1:])
    square_arrived = hold(square_arrived, *slices_arrived)
    square = lax.all_gather(place_dp(square, square_arrived), "index", axis=0, tiled=False)
    slices = place_dp(received, slices_arrived)
    vectors = (
        slices[:, :, 5 * part :]
        .reshape(groups, count, extra_rows * width)[:, :, : vector_rows * vector_width]
        .reshape(groups, count, vector_rows, vector_width)
        .transpose(2, 0, 1, 3)
        .reshape(vector_rows, depth)
        .astype(jnp.float32)
    )
    question_full = (
        received[:, 5 * part :]
        .reshape(count, extra_rows * width)[:, vector_rows * vector_width :][
            :, : seqs * question_width
        ]
        .reshape(count, seqs, question_width)
        .transpose(1, 0, 2)
        .reshape(seqs, count * question_width)
    )
    expand_part = hidden // depth * part
    late = jnp.concatenate(
        [
            expand_weight.astype(low)
            .reshape(part, hidden // depth, depth)
            .transpose(1, 0, 2)
            .reshape(expand_part, depth),
            attention_low[7],
        ],
        axis=0,
    )
    (late,) = hold([late], *slices_arrived)
    late_sent = send_dp(late)

    (passage_ids,) = hold([passage_ids], *slices_arrived)
    passages_here = passage_vectors.shape[0]
    local_ids = passage_ids - place * passages_here
    owned_slot = (local_ids >= 0) & (local_ids < passages_here)
    picked = passage_vectors[jnp.clip(local_ids, 0, passages_here - 1)]
    local_scores = jnp.einsum(
        "sc,skc->sk", question_full, picked, preferred_element_type=jnp.float32
    )
    slots = passage_ids.shape[1]
    usable = jnp.arange(slots)[None, :] < valid_count[:, None]
    scores = small_take(small_send(jnp.where(owned_slot, local_scores, 0.0)), local_scores.shape)
    masked = jnp.where(usable, scores, negative_fill)
    maximum = jnp.max(masked, axis=1)
    exponent = jnp.where(usable, jnp.exp(masked - maximum[:, None]), 0.0)
    partition = jnp.sum(exponent, axis=1)
    passage_prob = exponent / partition[:, None]
    log_prior = jnp.where(
        usable, masked - maximum[:, None] - jnp.log(partition)[:, None], negative_fill
    )
    key_bias = jnp.repeat(log_prior, MEM_P, axis=1)

    vector_here = lax.dynamic_slice_in_dim(vectors[:5], place * width, width, axis=1)
    no_bias = jnp.zeros((1, width), jnp.float32)
    qkv_bias = jnp.concatenate([vector_here[0:1], no_bias, vector_here[1:2]], axis=1)
    kv_bias = jnp.concatenate([no_bias, vector_here[4:5]], axis=1)
    x_rows = decoder_input.reshape(rows, depth)
    qkv = project_columns("self_qkv", *input_rows, slices, 0, 3, qkv_bias)
    self_out, self_stat = attend(True, qkv, 0, qkv, 1, 2, key_bias[:, None, :])
    self_out, *late_arrived = hold([self_out, *late_sent])
    self_got = swap(self_out)
    late = lax.all_gather(place_dp(late, late_arrived), "index", axis=0, tiled=False)
    ahead, across = hold([jnp.stack(contract[:2]), jnp.stack(contract[2:])], *late_arrived)
    self_got, ahead_far, across_far = hold(
        [self_got, exchange_dp(ahead, 2), exchange_dp(across, 1)]
    )
    ahead = jnp.stack([ahead, ahead_far])
    across = jnp.stack([across, across_far])
    contract_sent = [exchange_dp(ahead, 1), exchange_dp(across, 2)]
    self_mixed, first_in, first_low, cross_query = first_forward(
        self_got, x_rows, square, vectors, ahead_far
    )
    (slices,) = hold([slices], first_low)
    memory_kv = project_columns("memory_kv", *memory_rows, slices, 3, 2, kv_bias)
    cross_query = swap(cross_query)[:, None]
    cross_out, cross_stat = attend(
        False, cross_query, 0, memory_kv, 0, 1, key_bias[:, None, :]
    )
    ahead_far, across_far = hold(contract_sent, cross_out)
    contract = [ahead, ahead_far, across, across_far]
    contract += [exchange(piece, 1) for piece in contract]
    places = lax.axis_index("dp") ^ jnp.array(DP_ORDER, jnp.int32)
    (
        cross_mixed,
        layer_output,
        wide_grad,
        *contract_grads,
        inner_total,
        second_grad,
        cross_low,
        cross_mix_grad,
        stats,
    ) = ffn(
        (order, places),
        swap(cross_out),
        first_in,
        late,
        contract,
        vectors,
        vectors[6:10].reshape(groups * count, -1),
        output_grad.reshape(rows, depth),
    )
    third_stat, second_stat = stats[:8], stats[8:]

    expand_part_sum = lax.psum_scatter(wide_grad, "index", scatter_dimension=0, tiled=False)
    ahead, ahead_far, across, across_far = contract_grads[:4]
    cores = [exchange(piece, 1) for piece in contract_grads[4:]]
    cross_mix_got, *contract_sent = hold(
        [swap(cross_mix_grad), add(ahead_far, cores[1]), add(across_far, cores[3])]
    )
    contract_got = [exchange_dp(contract_sent[0], 1), exchange_dp(contract_sent[1], 2)]
    cross_dq, cross_dkv, prior_rows = attend_back(
        False,
        cross_query,
        0,
        memory_kv,
        0,
        1,
        cross_mix_got,
        cross_stat,
        key_bias[:, None, :],
        contract_sent[0],
    )
    memory_mine, memory_other, kv_grads, kv_total = project_columns_back(
        "memory_kv_back", order, *memory_rows, [cross_dkv], slices, 3, 2
    )
    cross_dq, *contract_got = hold([cross_dq, *contract_got], memory_mine)
    contract_next = [
        add((ahead, 1), (cores[0], 1), (contract_got[0], 1)),
        add((across, 1), (cores[2], 1), (contract_got[1], 1)),
    ]
    cross_dq_got, *contract_next = hold([swap(cross_dq), *contract_next])
    contract_last = [exchange_dp(contract_next[0], 2), exchange_dp(contract_next[1], 1)]
    query_low, first_grad, self_low, self_mix_grad, first_stat = first_back(
        cross_dq_got, second_grad, first_in, square, vectors, memory_mine
    )
    memory_sum = both_cores(memory_mine, exchange(memory_other, 1))
    memory_sent = firsts(memory_sum)
    square_mine, square_other = weight_grads(
        (count, groups, part, depth),
        order,
        self_mixed,
        self_low,
        first_low,
        query_low,
        cross_mixed,
        cross_low,
    )
    square_sum = both_cores(square_mine, exchange(square_other, 1))
    square_sent = firsts(square_sum)
    self_mix_got, *contract_last = hold(
        [swap(self_mix_grad), *contract_last], *memory_sent, *square_sent
    )
    memory_got = send_first(*memory_sent)
    square_got = send_first(*square_sent)
    self_dq, self_dkv, _ = attend_back(
        True, qkv, 0, qkv, 1, 2, self_mix_got, self_stat, self_stat, square_mine
    )
    expand_sum = HalvingDp(expand_part_sum)
    self_dq, expand_sent = hold([self_dq, expand_sum.first()])
    dx_mine, dx_other, qkv_slice_grads, qkv_total = project_columns_back(
        "self_qkv_back", order, *input_rows, [self_dq, self_dkv], slices, 0, 3
    )
    dx_mine, dx_other, *got = hold([dx_mine, dx_other, *memory_got, *square_got])
    own = jnp.concatenate(
        [qkv_total[:, :width], qkv_total[:, 2 * width :], kv_total[:, width:]], axis=0
    )
    own = lax.dynamic_update_slice(
        jnp.zeros((3, depth), jnp.float32), own, (jnp.int32(0), place * width)
    )
    vector_grads = jnp.concatenate(
        [
            own[:2],
            first_stat[1:2],
            first_stat[0:1],
            own[2:],
            second_stat[0:1],
            inner_total.reshape(hidden // depth, depth),
            third_stat[0:1],
            first_stat[2:4],
            second_stat[1:3],
            third_stat[1:3],
        ],
        axis=0,
    )
    vector_size = vector_rows * vector_width
    question_size = seqs * question_width
    vector_send = (
        vector_grads.reshape(vector_rows, groups, count, vector_width)
        .transpose(1, 2, 0, 3)
        .reshape(groups, count, vector_size)
    )
    vector_send = jnp.pad(
        vector_send, ((0, 0), (0, 0), (0, extra_rows * width - vector_size))
    ).reshape(groups, count, extra_rows, width)
    slice_sum = HalvingDp(
        jnp.concatenate([qkv_slice_grads, kv_grads, vector_send.astype(low)], axis=2)
    )
    slice_sent = slice_sum.first()
    slice_got = exchange_dp(slice_sent, 1)
    dx_other, *got = hold([dx_other, *got], slice_sent)
    dx_got = exchange(dx_other, 1)
    square_rows = square_sum.middle
    last = seconds((square_sum, *got[2:], 0), (memory_sum, *got[:2], 0))
    prior_rows, expand_sent, *contract_last = hold(
        [prior_rows, expand_sent, *contract_last], *last
    )
    last = send_last(*last)
    expand_got = exchange_dp(expand_sent, 1)
    prior_arrived = small_send(prior_rows.reshape(seqs, slots, MEM_P).sum(axis=-1))
    dx_got, expand_got, prior_arrived, slice_got, *last = hold(
        [dx_got, expand_got, prior_arrived, slice_got, *last]
    )
    slice_next = slice_sum.second(slice_got)
    dx_got, *last = hold([dx_got, *last], slice_next)
    slice_last = exchange_dp(slice_next, 2)
    dx_sum = both_cores(dx_mine, dx_got)
    contract_sum = Halving(
        [
            [(one.reshape((-1,) + one.shape[-2:]), k % 2) for one in parts]
            for k, parts in enumerate(
                [(ahead, cores[0], contract_got[0], contract_last[0])] * 2
                + [(across, cores[2], contract_got[1], contract_last[1])] * 2
            )
        ]
    )
    dx_sent = firsts(dx_sum, contract_sum)
    got = send_first(*dx_sent)
    last = hold(last, *dx_sent)
    square_last, memory_last = split_rows(last, square_rows)
    square_far = HalvingDp(square_sum.finish(*square_last).reshape(groups, 3 * part, depth))
    square_got = exchange_dp(square_far.first(), 1)
    expand_last = exchange_dp(expand_sum.second(expand_got), 2)
    square_got, slice_last, *got = hold([square_got, slice_last, *got])
    slice_sum = slice_sum.finish(slice_last)
    prior_grad = jnp.where(usable, small_take(prior_arrived, (seqs, slots)), 0.0)
    score_doc = jnp.where(
        usable, prior_grad - passage_prob * jnp.sum(prior_grad, axis=1, keepdims=True), 0.0
    )
    question_part = jnp.einsum(
        "sk,skc->sc",
        jnp.where(owned_slot, score_doc, 0.0),
        picked.astype(jnp.float32),
        precision=lax.Precision.HIGHEST,
    )

    question_send = (
        question_part.reshape(seqs, count, question_width)
        .transpose(1, 0, 2)
        .reshape(count, question_size)
    )
    question_send = jnp.pad(
        question_send,
        ((0, 0), (vector_size, extra_rows * width - vector_size - question_size)),
    ).reshape(count, extra_rows, width)
    slice_sum = jnp.concatenate(
        [slice_sum[:, : 5 * part], slice_sum[:, 5 * part :] + question_send], axis=1
    )
    slice_send = slice_sum.astype(low)
    arrived = swap(slice_send)
    square_got, *got = hold([square_got, *got], slice_send)
    square_next = square_far.second(square_got)
    got = hold(got, square_next)
    square_last = exchange_dp(square_next, 2)
    start = dx_sum.middle
    last = send_last(*seconds((dx_sum, *got, 0), (contract_sum, *got, start)))
    dx_last, contract_last = split_rows(last, start)
    input_gradient = first_grad + dx_sum.finish(*dx_last)
    contract_sum = contract_sum.finish(*contract_last)
    memory_last = hold(memory_last, *got)
    memory_gradient = memory_sum.finish(*memory_last).reshape(encoder_memory.shape)
    new_contract = adam_update(
        contract_weight, contract_mean, contract_square, contract_sum, rate_contract, decay_matrix
    )
    (square_last,) = hold([square_last], input_gradient, memory_gradient, *new_contract)
    arrived = arrived.astype(jnp.float32)
    split_grads = (
        arrived[:, : 5 * part]
        .reshape(count, 5, part, width)
        .transpose(1, 2, 0, 3)
        .reshape(5, part, depth)
    )
    extra_sum = jnp.sum(arrived[:, 5 * part :].reshape(count, extra_rows * width), axis=0)
    vector_sum = extra_sum[:vector_size].reshape(vector_rows, vector_width)
    question_gradient = extra_sum[vector_size : vector_size + question_size].reshape(
        seqs, question_width
    )

    expand_sum = (
        expand_sum.finish(expand_last)
        .reshape(hidden // depth, part, depth)
        .transpose(1, 0, 2)
        .reshape(part, hidden)
    )
    square_total = square_far.finish(square_last).reshape(3, part, depth)
    attention_sum = jnp.concatenate(
        [split_grads[:3], square_total[:2], split_grads[3:], square_total[2:]], axis=0
    )

    new_attention = adam_update(
        attention_weight,
        attention_mean,
        attention_square,
        attention_sum,
        rate_attention,
        decay_matrix,
    )
    new_expand = adam_update(
        expand_weight, expand_mean, expand_square, expand_sum, rate_expand, decay_matrix
    )
    new_vector = adam_update(
        vector_params, vector_mean, vector_square, vector_sum, rate_vector, 0.0
    )
    return (
        layer_output.reshape(decoder_input.shape),
        input_gradient.reshape(decoder_input.shape),
        memory_gradient,
        question_gradient,
        *new_attention,
        *new_expand,
        *new_contract,
        *new_vector,
    )


def body(sizes, *arrays):
    depth = arrays[0].shape[2]
    if sizes == (4, 8) and depth // 8 % 128 == 0:
        return head_body(*arrays)
    return general_body(*arrays)


def solution(mesh):
    return jax.shard_map(
        partial(body, (mesh.shape["dp"], mesh.shape["index"])),
        mesh=mesh,
        in_specs=(
            P("dp", "index", None),
            P("dp", "index", None),
            P("dp", "index"),
            P("index", None),
            P("dp", None),
            P("dp"),
            P("dp", "index", None),
            P(None, ("dp", "index"), None),
            P(("dp", "index"), None),
            P(("dp", "index"), None),
            P(None, ("dp", "index")),
            P(None, ("dp", "index"), None),
            P(None, ("dp", "index"), None),
            P(("dp", "index"), None),
            P(("dp", "index"), None),
            P(("dp", "index"), None),
            P(("dp", "index"), None),
            P(None, ("dp", "index")),
            P(None, ("dp", "index")),
        ),
        out_specs=(
            P("dp", "index", None),
            P("dp", "index", None),
            P("dp", "index", None),
            P("dp", "index"),
            P(None, ("dp", "index"), None),
            P(None, ("dp", "index"), None),
            P(None, ("dp", "index"), None),
            P(("dp", "index"), None),
            P(("dp", "index"), None),
            P(("dp", "index"), None),
            P(("dp", "index"), None),
            P(("dp", "index"), None),
            P(("dp", "index"), None),
            P(None, ("dp", "index")),
            P(None, ("dp", "index")),
            P(None, ("dp", "index")),
        ),
        check_vma=False,
    )
```

```python
from functools import partial

import jax
import jax.numpy as jnp
from jax import lax
from jax.experimental import pallas as pl
from jax.experimental.pallas import tpu as pltpu
from jax.sharding import PartitionSpec as P

HEADS = 16
MEM_P = 192
STEP = 10


negative_fill = -1e30
norm_eps = 1e-05
beta_first = 0.9
beta_second = 0.999
adam_eps = 1e-08
decay_matrix = 0.01
rate_attention = 0.1
rate_expand = 0.02
rate_contract = 0.01
rate_vector = 0.2


def layer_norm(hidden, norm_gain, norm_shift):
    center = hidden - jnp.mean(hidden, axis=-1, keepdims=True)
    spread = jnp.mean(center * center, axis=-1, keepdims=True)
    return center * lax.rsqrt(spread + norm_eps) * norm_gain + norm_shift


def split_heads(matrix):
    return matrix.reshape(matrix.shape[0], matrix.shape[1], HEADS, matrix.shape[2] // HEADS)


def merge_heads(matrix):
    return matrix.reshape(matrix.shape[0], matrix.shape[1], matrix.shape[2] * matrix.shape[3])


def project(left_side, weight):
    return jnp.einsum("srd,de->sre", left_side, weight, preferred_element_type=jnp.float32)


def project_back(gradient, weight):
    return jnp.einsum("sre,de->srd", gradient, weight, preferred_element_type=jnp.float32)


def weight_grad(left_side, gradient):
    return jnp.einsum("srd,sre->de", left_side, gradient, preferred_element_type=jnp.float32)


def row_total(values):
    return jnp.sum(values, axis=(0, 1))


def attend_forward(queries, key_rows, values, score_bias, allowed):
    scores = (
        jnp.einsum(
            "sqhd,skhd->shqk",
            split_heads(queries),
            split_heads(key_rows),
            preferred_element_type=jnp.float32,
        )
        * 0.125
        + score_bias
    )
    scores = jnp.where(allowed, scores, negative_fill)
    maximum = jnp.max(scores, axis=-1)
    exponent = jnp.exp(scores - maximum[..., None])
    partition = jnp.sum(exponent, axis=-1)
    attend_prob = exponent / partition[..., None]
    mixture = jnp.einsum(
        "shqk,skhd->sqhd",
        attend_prob.astype(jnp.bfloat16),
        split_heads(values),
        preferred_element_type=jnp.float32,
    )
    return (merge_heads(mixture).astype(jnp.bfloat16), attend_prob, maximum, partition)


def score_grads(grad_mixed, attend_prob, values):
    grad_prob = jnp.einsum(
        "sqhd,skhd->shqk",
        split_heads(grad_mixed),
        split_heads(values),
        preferred_element_type=jnp.float32,
    )
    row_inner = jnp.sum(attend_prob * grad_prob, axis=-1)
    return ((attend_prob * (grad_prob - row_inner[..., None])).astype(jnp.bfloat16), row_inner)


def to_queries(grad_score, key_rows):
    return (
        merge_heads(
            jnp.einsum(
                "shqk,skhd->sqhd",
                grad_score,
                split_heads(key_rows),
                preferred_element_type=jnp.float32,
            )
        )
        * 0.125
    )


def to_keys(grad_score, attend_prob, queries, grad_mixed):
    grad_key = (
        merge_heads(
            jnp.einsum(
                "shqk,sqhd->skhd",
                grad_score,
                split_heads(queries),
                preferred_element_type=jnp.float32,
            )
        )
        * 0.125
    )
    grad_value = merge_heads(
        jnp.einsum(
            "shqk,sqhd->skhd",
            attend_prob.astype(jnp.bfloat16),
            split_heads(grad_mixed),
            preferred_element_type=jnp.float32,
        )
    )
    return (grad_key, grad_value)


def adam_update(weight, moment_one, moment_two, gradient, step_rate, weight_decay):
    mean_new = beta_first * moment_one + (1.0 - beta_first) * gradient
    square_new = beta_second * moment_two + (1.0 - beta_second) * gradient * gradient
    mean_hat = mean_new / (1.0 - beta_first**STEP)
    square_hat = square_new / (1.0 - beta_second**STEP)
    updated = weight - step_rate * (
        mean_hat / (jnp.sqrt(square_hat) + adam_eps) + weight_decay * weight
    )
    return (updated, mean_new, square_new)


def general_body(
    decoder_input,
    encoder_memory,
    question_vectors,
    passage_vectors,
    passage_ids,
    valid_count,
    output_grad,
    attention_weight,
    expand_weight,
    contract_weight,
    vector_params,
    attention_mean,
    attention_square,
    expand_mean,
    expand_square,
    contract_mean,
    contract_square,
    vector_mean,
    vector_square,
):
    attention_low, expand_low, contract_low, vector_low = (
        lax.all_gather(attention_weight.astype(jnp.bfloat16), ("dp", "index"), axis=1, tiled=True),
        lax.all_gather(expand_weight.astype(jnp.bfloat16), ("dp", "index"), axis=0, tiled=True),
        lax.all_gather(contract_weight.astype(jnp.bfloat16), ("dp", "index"), axis=0, tiled=True),
        lax.all_gather(vector_params.astype(jnp.bfloat16), ("dp", "index"), axis=1, tiled=True),
    )
    vectors = vector_low.astype(jnp.float32)
    seqs_here, rows_here, model_width = decoder_input.shape
    shard_index = lax.axis_index("index")
    length = rows_here * lax.axis_size("index")
    ffn_width = expand_low.shape[1]
    self_query = (project(decoder_input, attention_low[0]) + vectors[0]).astype(jnp.bfloat16)
    self_key = project(decoder_input, attention_low[1]).astype(jnp.bfloat16)
    self_value = (project(decoder_input, attention_low[2]) + vectors[1]).astype(jnp.bfloat16)
    key_all, value_all = (
        lax.all_gather(self_key, "index", axis=1, tiled=True),
        lax.all_gather(self_value, "index", axis=1, tiled=True),
    )
    query_place = shard_index * rows_here + jnp.arange(rows_here)
    causal = (jnp.arange(length)[None, :] <= query_place[:, None])[None, None]
    self_mixed, self_prob, self_peak, self_total = attend_forward(
        self_query, key_all, value_all, 0.0, causal
    )
    first_in = (
        decoder_input.astype(jnp.float32) + project(self_mixed, attention_low[3]) + vectors[2]
    )
    first_out, first_back = jax.vjp(layer_norm, first_in, vectors[11], vectors[12])
    first_low = first_out.astype(jnp.bfloat16)
    cross_query = (project(first_low, attention_low[4]) + vectors[3]).astype(jnp.bfloat16)
    cross_key = project(encoder_memory, attention_low[5]).astype(jnp.bfloat16)
    cross_value = (project(encoder_memory, attention_low[6]) + vectors[4]).astype(jnp.bfloat16)
    memory_keys, memory_values = (
        lax.all_gather(cross_key, "index", axis=1, tiled=True),
        lax.all_gather(cross_value, "index", axis=1, tiled=True),
    )
    question_full = lax.all_gather(question_vectors, "index", axis=1, tiled=True)
    passages_here = passage_vectors.shape[0]
    local_ids = passage_ids - shard_index * passages_here
    owned_slot = (local_ids >= 0) & (local_ids < passages_here)
    picked = passage_vectors[jnp.clip(local_ids, 0, passages_here - 1)]
    local_scores = jnp.einsum(
        "sc,skc->sk", question_full, picked, preferred_element_type=jnp.float32
    )
    slots = passage_ids.shape[1]
    usable = jnp.arange(slots)[None, :] < valid_count[:, None]
    local_peak = jnp.max(jnp.where(owned_slot & usable, local_scores, negative_fill), axis=1)
    maximum = lax.pmax(local_peak, "index")
    local_exp = jnp.where(owned_slot & usable, jnp.exp(local_scores - maximum[:, None]), 0.0)
    exponent, scores = lax.psum((local_exp, jnp.where(owned_slot, local_scores, 0.0)), "index")
    masked = jnp.where(usable, scores, negative_fill)
    partition = jnp.sum(exponent, axis=1)
    passage_prob = exponent / partition[:, None]
    log_prior = masked - maximum[:, None] - jnp.log(partition)[:, None]
    memory_total = memory_keys.shape[1]
    bias_rows = jnp.repeat(log_prior, MEM_P, axis=1)
    key_bias = bias_rows[:, None, None, :]
    key_usable = ((jnp.arange(memory_total) // MEM_P)[None, :] < valid_count[:, None])[
        :, None, None, :
    ]
    cross_mixed, cross_prob, cross_peak, cross_total = attend_forward(
        cross_query, memory_keys, memory_values, key_bias, key_usable
    )
    second_in = first_out + project(cross_mixed, attention_low[7]) + vectors[5]
    second_out, second_back = jax.vjp(layer_norm, second_in, vectors[13], vectors[14])
    second_low = second_out.astype(jnp.bfloat16)
    inner_act = project(second_low, expand_low) + vectors[6:10].reshape(ffn_width)
    activated, gelu_back = jax.vjp(partial(jax.nn.gelu, approximate=False), inner_act)
    activ_low = activated.astype(jnp.bfloat16)
    third_in = second_out + project(activ_low, contract_low) + vectors[10]
    layer_output, third_back = jax.vjp(layer_norm, third_in, vectors[15], vectors[16])
    grad_third, gain_three, shift_three = third_back(output_grad.astype(jnp.float32))
    grad_ffn_low = grad_third.astype(jnp.bfloat16)
    grad_contract = weight_grad(activ_low, grad_ffn_low)
    (grad_inner,) = gelu_back(project_back(grad_ffn_low, contract_low))
    grad_inner_low = grad_inner.astype(jnp.bfloat16)
    grad_expand = weight_grad(second_low, grad_inner_low)
    grad_second = grad_third + project_back(grad_inner_low, expand_low)
    grad_second_in, gain_two, shift_two = second_back(grad_second)
    grad_cross_low = grad_second_in.astype(jnp.bfloat16)
    grad_cmix = project_back(grad_cross_low, attention_low[7]).astype(jnp.bfloat16)
    cross_score, cross_inner = score_grads(grad_cmix, cross_prob, memory_values)
    grad_cq = to_queries(cross_score, memory_keys)
    prior_part = (
        jnp.sum(cross_score, axis=(1, 2), dtype=jnp.float32)
        .reshape(seqs_here, slots, MEM_P)
        .sum(axis=-1)
    )
    prior_grad = jnp.where(usable, lax.psum(prior_part, "index"), 0.0)
    score_doc = jnp.where(
        usable, prior_grad - passage_prob * jnp.sum(prior_grad, axis=1, keepdims=True), 0.0
    )
    question_part = jnp.einsum(
        "sk,skc->sc",
        jnp.where(owned_slot, score_doc, 0.0),
        picked.astype(jnp.float32),
        precision=lax.Precision.HIGHEST,
    )
    question_gradient = lax.psum_scatter(question_part, "index", scatter_dimension=1, tiled=True)
    grad_cq_low = grad_cq.astype(jnp.bfloat16)
    grad_first = grad_second_in + project_back(grad_cq_low, attention_low[4])
    ck_part, cv_part = to_keys(cross_score, cross_prob, cross_query, grad_cmix)
    grad_ck, grad_cv = (
        lax.psum_scatter(
            ck_part.astype(jnp.bfloat16), "index", scatter_dimension=1, tiled=True
        ).astype(jnp.float32),
        lax.psum_scatter(
            cv_part.astype(jnp.bfloat16), "index", scatter_dimension=1, tiled=True
        ).astype(jnp.float32),
    )
    grad_ck_low = grad_ck.astype(jnp.bfloat16)
    grad_cv_low = grad_cv.astype(jnp.bfloat16)
    memory_gradient = project_back(grad_ck_low, attention_low[5]) + project_back(
        grad_cv_low, attention_low[6]
    )
    grad_first_in, gain_one, shift_one = first_back(grad_first)
    grad_self_low = grad_first_in.astype(jnp.bfloat16)
    grad_smix = project_back(grad_self_low, attention_low[3]).astype(jnp.bfloat16)
    self_score, row_inner = score_grads(grad_smix, self_prob, value_all)
    grad_sq = to_queries(self_score, key_all)
    key_part, value_part = to_keys(self_score, self_prob, self_query, grad_smix)
    grad_sk, grad_sv = (
        lax.psum_scatter(
            key_part.astype(jnp.bfloat16), "index", scatter_dimension=1, tiled=True
        ).astype(jnp.float32),
        lax.psum_scatter(
            value_part.astype(jnp.bfloat16), "index", scatter_dimension=1, tiled=True
        ).astype(jnp.float32),
    )
    grad_sq_low = grad_sq.astype(jnp.bfloat16)
    grad_sk_low = grad_sk.astype(jnp.bfloat16)
    grad_sv_low = grad_sv.astype(jnp.bfloat16)
    input_gradient = (
        grad_first_in
        + project_back(grad_sq_low, attention_low[0])
        + project_back(grad_sk_low, attention_low[1])
        + project_back(grad_sv_low, attention_low[2])
    )
    attention_grads = jnp.stack(
        [
            weight_grad(decoder_input, grad_sq_low),
            weight_grad(decoder_input, grad_sk_low),
            weight_grad(decoder_input, grad_sv_low),
            weight_grad(self_mixed, grad_self_low),
            weight_grad(first_low, grad_cq_low),
            weight_grad(encoder_memory, grad_ck_low),
            weight_grad(encoder_memory, grad_cv_low),
            weight_grad(cross_mixed, grad_cross_low),
        ]
    )
    vector_grads = jnp.concatenate(
        [
            jnp.stack(
                [
                    row_total(grad_sq),
                    row_total(grad_sv),
                    row_total(grad_first_in),
                    row_total(grad_cq),
                    row_total(grad_cv),
                    row_total(grad_second_in),
                ]
            ),
            row_total(grad_inner).reshape(ffn_width // model_width, model_width),
            jnp.stack(
                [
                    row_total(grad_third),
                    gain_one,
                    shift_one,
                    gain_two,
                    shift_two,
                    gain_three,
                    shift_three,
                ]
            ),
        ]
    )
    attention_sum, expand_sum, contract_sum, vector_sum = (
        lax.psum_scatter(attention_grads, ("dp", "index"), scatter_dimension=1, tiled=True),
        lax.psum_scatter(grad_expand, ("dp", "index"), scatter_dimension=0, tiled=True),
        lax.psum_scatter(grad_contract, ("dp", "index"), scatter_dimension=0, tiled=True),
        lax.psum_scatter(vector_grads, ("dp", "index"), scatter_dimension=1, tiled=True),
    )
    new_attention = adam_update(
        attention_weight,
        attention_mean,
        attention_square,
        attention_sum,
        rate_attention,
        decay_matrix,
    )
    new_expand = adam_update(
        expand_weight, expand_mean, expand_square, expand_sum, rate_expand, decay_matrix
    )
    new_contract = adam_update(
        contract_weight, contract_mean, contract_square, contract_sum, rate_contract, decay_matrix
    )
    new_vector = adam_update(
        vector_params, vector_mean, vector_square, vector_sum, rate_vector, 0.0
    )
    return (
        layer_output.astype(jnp.bfloat16),
        input_gradient,
        memory_gradient,
        question_gradient,
        new_attention[0],
        new_attention[1],
        new_attention[2],
        new_expand[0],
        new_expand[1],
        new_expand[2],
        new_contract[0],
        new_contract[1],
        new_contract[2],
        new_vector[0],
        new_vector[1],
        new_vector[2],
    )


NT = (((1,), (1,)), ((), ()))
NN = (((1,), (0,)), ((), ()))
TN = (((0,), (0,)), ((), ()))
CHIPS = 4
DP_ORDER = (0, 2, 1, 3)
VMEM_LIMIT = 56 << 20


def dot(left_side, right_side, dims):
    return lax.dot_general(left_side, right_side, dims, preferred_element_type=jnp.float32)


def norm_parts(hidden):
    center = hidden - jnp.mean(hidden, axis=-1, keepdims=True)
    inverse = lax.rsqrt(jnp.mean(center * center, axis=-1, keepdims=True) + norm_eps)
    return center * inverse, inverse


def norm_back(gradient, unit, inverse, gain):
    scaled = gradient * gain
    return inverse * (
        scaled
        - jnp.mean(scaled, axis=-1, keepdims=True)
        - unit * jnp.mean(scaled * unit, axis=-1, keepdims=True)
    )


def column_sum(values):
    return jnp.sum(values, axis=0, keepdims=True)


def join(parts, place=None):
    picked = [parts[j] if place is None else parts[j, place] for j in range(parts.shape[0])]
    return jnp.concatenate(
        [block.reshape(block.shape[0] * block.shape[1], block.shape[2]) for block in picked],
        axis=1,
    )


def spread(out_ref, value):
    count, seqs, rows, width = out_ref.shape
    for j in range(count):
        out_ref[j] = value[:, j * width : (j + 1) * width].reshape(seqs, rows, width)


def times(activation, weight):
    count, groups, rows, width = weight.shape
    depth = count * rows
    total = None
    for d in range(groups):
        part = dot(
            activation[:, d * depth : (d + 1) * depth], weight[:, d].reshape(depth, width), NN
        )
        total = part if total is None else total + part
    return total


def times_back(gradient, weight):
    count, groups, rows, width = weight.shape
    depth = count * rows
    return jnp.concatenate(
        [dot(gradient, weight[:, d].reshape(depth, width), NT) for d in range(groups)], axis=1
    )


def outer(out_ref, left_side, gradient):
    count, groups, rows, width = out_ref.shape
    depth = count * rows
    for d in range(groups):
        out_ref[:, d] = (
            dot(left_side[:, d * depth : (d + 1) * depth], gradient, TN)
            .astype(jnp.bfloat16)
            .reshape(count, rows, width)
        )


def whole(array):
    return pl.BlockSpec(array.shape, lambda *_, rank=len(array.shape): (0,) * rank)


def shape(dims, dtype):
    return jax.ShapeDtypeStruct(tuple(dims), dtype)


def params():
    return pltpu.CompilerParams(vmem_limit_bytes=VMEM_LIMIT)


def cost(flops, moved):
    return pl.CostEstimate(flops=int(flops) // 16, bytes_accessed=int(moved) // 16, transcendentals=0)


def in_head(dims, head_width, head):
    return lax.broadcasted_iota(jnp.int32, dims, 1) // head_width == head


def attend_forward_kernel(causal, head_width, q_ref, k_ref, v_ref, bias_ref, out_ref, stat_ref):
    count, _, tile, width = q_ref.shape
    keys = k_ref.shape[0] * k_ref.shape[2]
    key_rows, values = k_ref[...].reshape(keys, width), v_ref[...].reshape(keys, width)
    step = 4
    rows = step * tile
    for b in range(count // step):
        queries = q_ref[b * step : (b + 1) * step].reshape(rows, width)
        seen = (b + 1) * rows if causal else keys
        mixed = None
        for h in range(width // head_width):
            mask = in_head((rows, width), head_width, h)
            scores = dot(
                jnp.where(mask, queries * 0.125, 0).astype(jnp.bfloat16), key_rows[:seen], NT
            )
            if causal:
                corner = scores[:, seen - rows :]
                corner = jnp.where(
                    lax.broadcasted_iota(jnp.int32, corner.shape, 1)
                    <= lax.broadcasted_iota(jnp.int32, corner.shape, 0),
                    corner,
                    negative_fill,
                )
                if b == 0:
                    scores = corner
                else:
                    scores = jnp.concatenate([scores[:, : seen - rows], corner], axis=1)
            else:
                scores = scores + bias_ref[0]
            peak = jnp.max(scores, axis=1, keepdims=True)
            exponent = jnp.exp(scores - peak)
            total = jnp.sum(exponent, axis=1, keepdims=True)
            part = dot(exponent.astype(jnp.bfloat16), values[:seen], NN) * (1.0 / total)
            mixed = part if mixed is None else jnp.where(mask, part, mixed)
            log_total = jnp.broadcast_to(peak + jnp.log(total), (rows, 128))
            stat_ref[0, h : h + 1, b * rows : (b + 1) * rows] = log_total.T[0:1]
        out_ref[b * step : (b + 1) * step] = mixed.astype(jnp.bfloat16).reshape(
            step, 1, tile, width
        )


def attend_backward_kernel(
    causal,
    head_width,
    q_ref,
    k_ref,
    v_ref,
    grad_ref,
    stat_ref,
    bias_ref,
    _,
    dq_ref,
    dkv_ref,
    prior_ref,
    dk_sum,
    dv_sum,
    prior_sum,
):
    count, _, tile, width = q_ref.shape
    keys = k_ref.shape[0] * k_ref.shape[2]
    key_rows, values = k_ref[...].reshape(keys, width), v_ref[...].reshape(keys, width)
    step = 2
    rows = step * tile
    if not causal:
        bias = jnp.broadcast_to(bias_ref[0], (128, keys)).T[:, :1]
    dk_sum[...] = jnp.zeros_like(dk_sum)
    dv_sum[...] = jnp.zeros_like(dv_sum)
    if not causal:
        prior_sum[...] = jnp.zeros_like(prior_sum)
    for b in range(count // step):
        queries = q_ref[b * step : (b + 1) * step].reshape(rows, width)
        gradient = grad_ref[b * step : (b + 1) * step].reshape(rows, width)
        seen = (b + 1) * rows if causal else keys
        query_grad = None
        for h in range(width // head_width):
            mask = in_head((rows, width), head_width, h)
            one_query = jnp.where(mask, queries * 0.125, 0).astype(jnp.bfloat16)
            one_grad = jnp.where(mask, gradient, 0).astype(jnp.bfloat16)
            scores = dot(key_rows[:seen], one_query, NT)
            if causal:
                corner = scores[seen - rows :]
                corner = jnp.where(
                    lax.broadcasted_iota(jnp.int32, corner.shape, 0)
                    <= lax.broadcasted_iota(jnp.int32, corner.shape, 1),
                    corner,
                    negative_fill,
                )
                if b == 0:
                    scores = corner
                else:
                    scores = jnp.concatenate([scores[: seen - rows], corner], axis=0)
            else:
                scores = scores + bias
            prob = jnp.exp(scores - stat_ref[0, h : h + 1, b * rows : (b + 1) * rows])
            grad_prob = dot(values[:seen], one_grad, NT)
            inner = jnp.sum(prob * grad_prob, axis=0, keepdims=True)
            grad_score = prob * (grad_prob - inner)
            score_low = grad_score.astype(jnp.bfloat16)
            dv_sum[:seen] += dot(prob.astype(jnp.bfloat16), one_grad, NN)
            dk_sum[:seen] += dot(score_low, one_query, NN)
            if not causal:
                partial_sum = grad_score[:, :128]
                for piece in range(128, rows, 128):
                    partial_sum = partial_sum + grad_score[:, piece : piece + 128]
                prior_sum[...] += partial_sum
            part = dot(score_low, key_rows[:seen], TN)
            query_grad = part if query_grad is None else jnp.where(mask, part, query_grad)
        dq_ref[b * step : (b + 1) * step] = (
            (query_grad * 0.125).astype(jnp.bfloat16).reshape(step, 1, tile, width)
        )
    dkv_ref[:, 0] = dk_sum[...].astype(jnp.bfloat16).reshape(k_ref.shape)
    dkv_ref[:, 1] = dv_sum[...].astype(jnp.bfloat16).reshape(k_ref.shape)
    if causal:
        prior_ref[...] = jnp.zeros_like(prior_ref)
    else:
        prior_ref[0] = column_sum(prior_sum[...].T)


def pick(array, place):
    count, _, _, rows, width = array.shape
    return pl.BlockSpec((count, None, 1, rows, width), lambda s: (0, place, s, 0, 0))


def attend(causal, queries, query_at, keys, key_at, value_at, bias):
    count, _, seqs, tile, width = queries.shape
    key_rows = keys.shape[0] * keys.shape[3]
    head_width = width * count // HEADS
    length = count * tile
    heads = width // head_width
    return pl.pallas_call(
        partial(attend_forward_kernel, causal, head_width),
        grid=(seqs,),
        in_specs=[
            pick(queries, query_at),
            pick(keys, key_at),
            pick(keys, value_at),
            pl.BlockSpec(memory_space=pl.ANY)
            if causal
            else pl.BlockSpec((1, 1, key_rows), lambda s: (s, 0, 0)),
        ],
        out_specs=[
            pl.BlockSpec((count, 1, tile, width), lambda s: (0, s, 0, 0)),
            pl.BlockSpec((1, heads, length), lambda s: (s, 0, 0)),
        ],
        out_shape=[
            shape((count, seqs, tile, width), jnp.bfloat16),
            shape((seqs, heads, length), jnp.float32),
        ],
        compiler_params=params(),
        cost_estimate=cost(
            16 * seqs * length * key_rows * width, 4 * seqs * (length + key_rows) * width
        ),
        name="attend_self" if causal else "attend_memory",
    )(queries, keys, keys, bias)


def attend_back(
    causal, queries, query_at, keys, key_at, value_at, gradient, stat, bias, after
):
    count, _, seqs, tile, width = queries.shape
    key_tile = keys.shape[3]
    key_rows = count * key_tile
    head_width = width * count // HEADS
    length = count * tile
    heads = width // head_width
    return pl.pallas_call(
        partial(attend_backward_kernel, causal, head_width),
        grid=(seqs,),
        in_specs=[
            pick(queries, query_at),
            pick(keys, key_at),
            pick(keys, value_at),
            pl.BlockSpec((count, 1, tile, width), lambda s: (0, s, 0, 0)),
            pl.BlockSpec((1, heads, length), lambda s: (s, 0, 0)),
            pl.BlockSpec(memory_space=pl.ANY)
            if causal
            else pl.BlockSpec((1, 1, key_rows), lambda s: (s, 0, 0)),
            pl.BlockSpec(memory_space=pl.ANY),
        ],
        out_specs=[
            pl.BlockSpec((count, 1, tile, width), lambda s: (0, s, 0, 0)),
            pl.BlockSpec((count, 2, 1, key_tile, width), lambda s: (0, 0, s, 0, 0)),
            pl.BlockSpec((1, 1, key_rows), lambda s: (s, 0, 0)),
        ],
        out_shape=[
            shape((count, seqs, tile, width), jnp.bfloat16),
            shape((count, 2, seqs, key_tile, width), jnp.bfloat16),
            shape((seqs, 1, key_rows), jnp.float32),
        ],
        scratch_shapes=[
            pltpu.VMEM((key_rows, width), jnp.float32),
            pltpu.VMEM((key_rows, width), jnp.float32),
            pltpu.VMEM((key_rows, 128), jnp.float32),
        ],
        compiler_params=params(),
        cost_estimate=cost(
            40 * seqs * length * key_rows * width, 8 * seqs * (length + key_rows) * width
        ),
        name="attend_self_back" if causal else "attend_memory_back",
    )(queries, keys, keys, gradient, stat, bias, after)


def take_columns(scratch, slices, first):
    width = slices.shape[3]
    depth = scratch.shape[0]
    rows = depth // (slices.shape[0] * slices.shape[1])
    for m in range(scratch.shape[1] // width):
        start = (first + m) * rows
        scratch[:, m * width : (m + 1) * width] = slices[:, :, start : start + rows].reshape(
            depth, width
        )


def columns_kernel(first, start, seqs, rows, row_ref, slice_ref, bias_ref, out_ref, weight, taken, sem):
    def copy(i):
        return pltpu.make_async_copy(
            row_ref.at[i, :, pl.ds(start, rows)], taken.at[i], sem.at[i]
        )

    count, many = out_ref.shape[:2]
    width = out_ref.shape[4]
    for i in range(count):
        copy(i).start()
    take_columns(weight, slice_ref, first)
    for i in range(count):
        copy(i).wait()
        result = dot(taken[i].reshape(seqs * rows, weight.shape[0]), weight[...], NN) + bias_ref[...]
        for m in range(many):
            out_ref[i, m] = (
                result[:, m * width : (m + 1) * width]
                .astype(jnp.bfloat16)
                .reshape(seqs, rows, width)
            )


def project_columns(name, gathered_rows, start, rows, slices, first, many, bias):
    count, seqs, _, depth = gathered_rows.shape
    width = slices.shape[3]
    out = shape((count, many, seqs, rows, width), jnp.bfloat16)
    return pl.pallas_call(
        partial(columns_kernel, first, start, seqs, rows),
        grid=(1,),
        in_specs=[pl.BlockSpec(memory_space=pl.ANY), whole(slices), whole(bias)],
        out_specs=whole(out),
        out_shape=out,
        scratch_shapes=[
            pltpu.VMEM((depth, many * width), jnp.bfloat16),
            pltpu.VMEM((count, seqs, rows, depth), jnp.bfloat16),
            pltpu.SemaphoreType.DMA((count,)),
        ],
        compiler_params=params(),
        cost_estimate=cost(
            2 * many * count * seqs * rows * depth * width, 2 * count * seqs * rows * depth
        ),
        name=name,
    )(gathered_rows, slices, bias)


def columns_back_kernel(first, start, order, row_ref, *refs):
    grad_refs, (slice_ref, mine_out, other_out, dw_ref, bias_ref) = refs[:-12], refs[-12:-7]
    weight, taken, gradients, moved, total, in_sem, out_sem = refs[-7:]
    count, seqs, rows, depth = taken.shape
    half = count // 2

    def bring(r):
        return pltpu.make_async_copy(
            row_ref.at[order[r], :, pl.ds(start, rows)], taken.at[r], in_sem.at[r]
        )

    def send(r):
        there = (mine_out, other_out)[r // half].at[r % half, 0]
        return pltpu.make_async_copy(moved.at[r], there, out_sem.at[r])

    for r in range(count):
        bring(r).start()
    take_columns(weight, slice_ref, first)
    size = seqs * rows
    for r in range(count):
        i = order[r]
        pieces = []
        for grad_ref in grad_refs:
            width = grad_ref.shape[-1]
            for m in range(grad_ref.shape[1] if len(grad_ref.shape) == 5 else 1):
                piece = grad_ref[i, m] if len(grad_ref.shape) == 5 else grad_ref[i]
                pieces.append(piece.reshape(size, width))
        gradient = jnp.concatenate(pieces, axis=1)
        gradients[r * size : (r + 1) * size] = gradient
        moved[r] = dot(gradient, weight[...], NT).astype(jnp.bfloat16)
        send(r).start()
    whole_gradient = gradients[...]
    bias_ref[...] = column_sum(whole_gradient.astype(jnp.float32))
    for r in range(count):
        bring(r).wait()
    total[...] = dot(whole_gradient, taken[...].reshape(count * size, depth), TN)
    groups, shards, all_rows, _ = dw_ref.shape
    part = depth // (groups * shards)
    for m in range(all_rows // part):
        dw_ref[:, :, m * part : (m + 1) * part] = (
            total[m * width : (m + 1) * width]
            .T.astype(jnp.bfloat16)
            .reshape(groups, shards, part, width)
        )
    for r in range(count):
        send(r).wait()


def project_columns_back(name, order, gathered_rows, start, rows, gradients, slices, first, many):
    count, seqs, _, depth = gathered_rows.shape
    half = count // 2
    groups, shards, _, width = slices.shape
    part = depth // (groups * shards)
    anywhere = pl.BlockSpec(memory_space=pl.ANY)
    halves = shape((half, 1, seqs * rows, depth), jnp.bfloat16)
    dw_shape = shape((groups, shards, many * part, width), jnp.bfloat16)
    bias = shape((1, many * width), jnp.float32)
    return pl.pallas_call(
        partial(columns_back_kernel, first, start),
        grid_spec=pltpu.PrefetchScalarGridSpec(
            num_scalar_prefetch=1,
            grid=(1,),
            in_specs=[anywhere, *[whole(array) for array in gradients], whole(slices)],
            out_specs=[anywhere, anywhere, whole(dw_shape), whole(bias)],
            scratch_shapes=[
                pltpu.VMEM((depth, many * width), jnp.bfloat16),
                pltpu.VMEM((count, seqs, rows, depth), jnp.bfloat16),
                pltpu.VMEM((count * seqs * rows, many * width), jnp.bfloat16),
                pltpu.VMEM((count, seqs * rows, depth), jnp.bfloat16),
                pltpu.VMEM((many * width, depth), jnp.float32),
                pltpu.SemaphoreType.DMA((count,)),
                pltpu.SemaphoreType.DMA((count,)),
            ],
        ),
        out_shape=[halves, halves, dw_shape, bias],
        compiler_params=params(),
        cost_estimate=cost(
            4 * many * count * seqs * rows * depth * width, 4 * count * seqs * rows * depth
        ),
        name=name,
    )(order, gathered_rows, *gradients, slices)


def gathered(weights, width, place):
    count, groups, rows, _ = weights.shape
    return pl.BlockSpec((count, groups, rows, width), lambda *_: (0, 0, 0, place))


def first_kernel(
    mixed_ref, x_ref, out_w, query_w, vector_ref, _, mixed_out, in_out, low_out, query_out
):
    mixed = join(mixed_ref)
    mixed_out[...] = mixed
    first_in = x_ref[...].astype(jnp.float32) + times(mixed, out_w) + vector_ref[2:3]
    in_out[...] = first_in
    unit, _ = norm_parts(first_in)
    low = (unit * vector_ref[11:12] + vector_ref[12:13]).astype(jnp.bfloat16)
    low_out[...] = low
    spread(query_out, (times(low, query_w) + vector_ref[3:4]).astype(jnp.bfloat16))


def first_forward(mixed, x_rows, weights, vectors, after):
    rows, depth = x_rows.shape
    return pl.pallas_call(
        first_kernel,
        grid=(1,),
        in_specs=[
            whole(mixed),
            whole(x_rows),
            gathered(weights, depth, 0),
            gathered(weights, depth, 1),
            whole(vectors),
            pl.BlockSpec(memory_space=pl.ANY),
        ],
        out_specs=[whole(x_rows), whole(x_rows), whole(x_rows), whole(mixed)],
        out_shape=[
            shape((rows, depth), jnp.bfloat16),
            shape((rows, depth), jnp.float32),
            shape((rows, depth), jnp.bfloat16),
            shape(mixed.shape, jnp.bfloat16),
        ],
        compiler_params=params(),
        cost_estimate=cost(4 * rows * depth * depth, 4 * depth * depth),
        name="first_forward",
    )(mixed, x_rows, weights, weights, vectors, after)


def ffn_kernel(
    order,
    places,
    mixed_ref,
    first_ref,
    out_w,
    vector_ref,
    bias_ref,
    grad_ref,
    wide_ref,
    *refs,
):
    contract_refs, refs = refs[:8], refs[8:]
    mixed_out, layer_out, wide_grad = refs[:3]
    contract_grads, refs = refs[3:11], refs[11:]
    dbias_ref, second_grad, cross_low, mixed_grad, stat_out, columns, contracts = refs[:7]
    active, slope, low, third_low, second_in, total, wide_sem, contract_sem = refs[7:]
    blocks, count, groups, rows, block = columns.shape
    part = block // CHIPS
    depth = vector_ref.shape[1]

    def wide_copies(t, array, outward):
        result = []
        for k in range(CHIPS):
            column = pl.multiple_of(order[t % 2 * CHIPS + k] * part, part)
            row = pl.multiple_of(places[t // 2] * rows, rows)
            there = array.at[:, :, pl.ds(row, rows), pl.ds(column, part)]
            here = columns.at[t, :, :, :, pl.ds(k * part, part)]
            ends = (here, there) if outward else (there, here)
            result.append(pltpu.make_async_copy(*ends, wide_sem.at[t, k]))
        return result

    def contract_copies(t, pieces, outward):
        near, far = divmod(DP_ORDER[t // 2], 2)
        first = pieces[t % 2 * 4 + far].at[near]
        last = pieces[t % 2 * 4 + 2 + near].at[far]
        result = []
        for half, there in enumerate((first, last)):
            here = contracts.at[t, pl.ds(half * CHIPS // 2, CHIPS // 2)]
            ends = (here, there) if outward else (there, here)
            result.append(pltpu.make_async_copy(*ends, contract_sem.at[t, half]))
        return result

    for t in range(blocks):
        for copy in wide_copies(t, wide_ref, False):
            copy.start()
        for copy in contract_copies(t, contract_refs, False):
            copy.start()

    mixed = join(mixed_ref)
    mixed_out[...] = mixed
    unit, _ = norm_parts(first_ref[...])
    second_in[...] = (
        unit * vector_ref[11:12] + vector_ref[12:13] + times(mixed, out_w) + vector_ref[5:6]
    )
    unit, _ = norm_parts(second_in[...])
    second = unit * vector_ref[13:14] + vector_ref[14:15]
    low[...] = second.astype(jnp.bfloat16)
    total[...] = second + vector_ref[10:11]

    def shard(t, k):
        return places[t // 2] * count + order[t % 2 * CHIPS + k]

    for t in range(blocks):
        for copy in wide_copies(t, wide_ref, False):
            copy.wait()
        bias = jnp.concatenate([bias_ref[pl.ds(shard(t, k), 1)] for k in range(CHIPS)], axis=1)
        inner = times(low[...], columns.at[t]) + bias
        phi = 0.5 + 0.5 * lax.erf(inner * (0.5**0.5))
        out = (inner * phi).astype(jnp.bfloat16)
        active[t] = out
        slope[t] = phi + inner * jnp.exp(-0.5 * inner * inner) * 0.3989422804014327
        for copy in contract_copies(t, contract_refs, False):
            copy.wait()
        total[...] += dot(out, contracts[t].reshape(block, depth), NN)

    unit, inverse = norm_parts(total[...])
    gain = vector_ref[15:16]
    layer_out[...] = (unit * gain + vector_ref[16:17]).astype(jnp.bfloat16)
    gradient = grad_ref[...].astype(jnp.float32)
    grad_third = norm_back(gradient, unit, inverse, gain)
    stat_out[...] = jnp.zeros_like(stat_out)
    stat_out[0:1] = column_sum(grad_third)
    stat_out[1:2] = column_sum(gradient * unit)
    stat_out[2:3] = column_sum(gradient)
    total[...] = grad_third
    third_low[...] = grad_third.astype(jnp.bfloat16)
    turned = low[...].T

    for t in range(blocks):
        grad_inner = dot(third_low[...], contracts[t].reshape(block, depth), NT) * slope[t]
        inner_low = grad_inner.astype(jnp.bfloat16)
        sums = column_sum(grad_inner)
        for k in range(CHIPS):
            dbias_ref[pl.ds(shard(t, k), 1)] = sums[:, k * part : (k + 1) * part]
        contracts[t] = (
            dot(active[t], third_low[...], TN).astype(jnp.bfloat16).reshape(CHIPS, part, depth)
        )
        for copy in contract_copies(t, contract_grads, True):
            copy.start()
        total[...] += times_back(inner_low, columns.at[t])
        result = dot(turned, inner_low, NN).astype(jnp.bfloat16)
        for d in range(groups):
            columns[t, :, d] = result[d * count * rows : (d + 1) * count * rows].reshape(
                count, rows, block
            )
        for copy in wide_copies(t, wide_grad, True):
            copy.start()

    unit, inverse = norm_parts(second_in[...])
    grad_second = total[...]
    grad_in = norm_back(grad_second, unit, inverse, vector_ref[13:14])
    second_grad[...] = grad_in
    grad_low = grad_in.astype(jnp.bfloat16)
    cross_low[...] = grad_low
    spread(mixed_grad, times_back(grad_low, out_w).astype(jnp.bfloat16))
    stat_out[8:9] = column_sum(grad_in)
    stat_out[9:10] = column_sum(grad_second * unit)
    stat_out[10:11] = column_sum(grad_second)
    for t in range(blocks):
        for copy in contract_copies(t, contract_grads, True) + wide_copies(t, wide_grad, True):
            copy.wait()


def ffn(orders, mixed, first_in, wide, contract, vectors, bias, output_grad):
    rows, depth = first_in.shape
    hidden = bias.size
    block = depth // 2
    count, groups, all_rows, _ = wide.shape
    part = depth // (count * groups)
    blocks = hidden // block
    full = whole(first_in)
    anywhere = pl.BlockSpec(memory_space=pl.ANY)
    heads_out = shape(mixed.shape, jnp.bfloat16)
    stats = shape((16, depth), jnp.float32)
    return pl.pallas_call(
        ffn_kernel,
        grid_spec=pltpu.PrefetchScalarGridSpec(
            num_scalar_prefetch=2,
            grid=(1,),
            in_specs=[
                whole(mixed),
                full,
                pl.BlockSpec((count, groups, part, depth), lambda *_: (0, 0, groups, 0)),
                whole(vectors),
                whole(bias),
                full,
                *[anywhere] * 9,
            ],
            out_specs=[
                full,
                full,
                *[anywhere] * 9,
                whole(bias),
                full,
                full,
                whole(heads_out),
                whole(stats),
            ],
            scratch_shapes=[
                pltpu.VMEM((blocks, count, groups, part, block), jnp.bfloat16),
                pltpu.VMEM((blocks, CHIPS) + contract[0].shape[2:], jnp.bfloat16),
                pltpu.VMEM((blocks, rows, block), jnp.bfloat16),
                pltpu.VMEM((blocks, rows, block), jnp.float32),
                pltpu.VMEM((rows, depth), jnp.bfloat16),
                pltpu.VMEM((rows, depth), jnp.bfloat16),
                pltpu.VMEM((rows, depth), jnp.float32),
                pltpu.VMEM((rows, depth), jnp.float32),
                pltpu.SemaphoreType.DMA((blocks, CHIPS)),
                pltpu.SemaphoreType.DMA((blocks, 2)),
            ],
        ),
        out_shape=[
            shape((rows, depth), jnp.bfloat16),
            shape((rows, depth), jnp.bfloat16),
            shape((count, groups, all_rows - part, depth), jnp.bfloat16),
            *[shape(piece.shape, jnp.bfloat16) for piece in contract],
            shape(bias.shape, jnp.float32),
            shape((rows, depth), jnp.float32),
            shape((rows, depth), jnp.bfloat16),
            heads_out,
            stats,
        ],
        compiler_params=params(),
        cost_estimate=cost(12 * rows * depth * hidden, 16 * depth * hidden),
        name="ffn",
    )(*orders, mixed, first_in, wide, vectors, bias, output_grad, wide, *contract)


def first_back_kernel(
    dq_ref,
    second_grad,
    first_ref,
    out_w,
    query_w,
    vector_ref,
    _,
    query_low,
    grad_in_out,
    self_low,
    mixed_grad,
    stat_out,
):
    query_grad = join(dq_ref)
    query_low[...] = query_grad
    grad_first = second_grad[...] + times_back(query_grad, query_w)
    unit, inverse = norm_parts(first_ref[...])
    grad_in = norm_back(grad_first, unit, inverse, vector_ref[11:12])
    grad_in_out[...] = grad_in
    grad_low = grad_in.astype(jnp.bfloat16)
    self_low[...] = grad_low
    spread(mixed_grad, times_back(grad_low, out_w).astype(jnp.bfloat16))
    stat_out[...] = jnp.zeros_like(stat_out)
    stat_out[0:1] = column_sum(query_grad.astype(jnp.float32))
    stat_out[1:2] = column_sum(grad_in)
    stat_out[2:3] = column_sum(grad_first * unit)
    stat_out[3:4] = column_sum(grad_first)


def first_back(dq, second_grad, first_in, weights, vectors, after):
    rows, depth = first_in.shape
    full = whole(first_in)
    return pl.pallas_call(
        first_back_kernel,
        grid=(1,),
        in_specs=[
            whole(dq),
            full,
            full,
            gathered(weights, depth, 0),
            gathered(weights, depth, 1),
            whole(vectors),
            pl.BlockSpec(memory_space=pl.ANY),
        ],
        out_specs=[full, full, full, whole(dq), pl.BlockSpec((8, depth), lambda *_: (0, 0))],
        out_shape=[
            shape((rows, depth), jnp.bfloat16),
            shape((rows, depth), jnp.float32),
            shape((rows, depth), jnp.bfloat16),
            shape(dq.shape, jnp.bfloat16),
            shape((8, depth), jnp.float32),
        ],
        compiler_params=params(),
        cost_estimate=cost(4 * rows * depth * depth, 4 * depth * depth),
        name="first_back",
    )(dq, second_grad, first_in, weights, weights, vectors, after)


def weight_grads_kernel(
    order,
    mixed,
    self_low,
    first_low,
    query_low,
    cross,
    cross_low,
    mine_out,
    other_out,
    result,
):
    step = pl.program_id(0)
    pairs = ((mixed, self_low), (first_low, query_low), (cross, cross_low))
    half, groups, part, _ = mine_out.shape
    for m, (left_side, gradient) in enumerate(pairs):

        @pl.when(step == m)
        def _(left_side=left_side, gradient=gradient):
            result[...] = dot(left_side[...], gradient[...], TN).astype(jnp.bfloat16)

    for d in range(groups):
        for k in range(half):
            for p, out_ref in enumerate((mine_out, other_out)):
                row = pl.multiple_of((2 * half * d + order[p * half + k]) * part, part)
                out_ref[k, d] = result[pl.ds(row, part)]


def weight_grads(dims, order, mixed, self_low, first_low, query_low, cross, cross_low):
    count, groups, part, depth = dims
    half = pl.BlockSpec((count // 2, groups, part, depth), lambda m, _: (0, 0, m, 0))
    return pl.pallas_call(
        weight_grads_kernel,
        grid_spec=pltpu.PrefetchScalarGridSpec(
            num_scalar_prefetch=1,
            grid=(3,),
            in_specs=[whole(mixed)] * 6,
            out_specs=[half, half],
            scratch_shapes=[pltpu.VMEM((depth, depth), jnp.bfloat16)],
        ),
        out_shape=[shape((count // 2, groups, 3 * part, depth), jnp.bfloat16)] * 2,
        compiler_params=params(),
        cost_estimate=cost(6 * mixed.shape[0] * depth * depth, 6 * depth * depth),
        name="weight_grads",
    )(order, mixed, self_low, first_low, query_low, cross, cross_low)


def send_dp(piece):
    size = lax.axis_size("dp")
    return [
        lax.ppermute(piece, "dp", [(i, (i + shift) % size) for i in range(size)])
        for shift in range(1, size)
    ]


def place_dp(piece, arrived):
    size, me = lax.axis_size("dp"), lax.axis_index("dp")
    result = jnp.zeros((size,) + piece.shape, piece.dtype)
    result = lax.dynamic_update_index_in_dim(result, piece, me, 0)
    for shift, got in enumerate(arrived, 1):
        result = lax.dynamic_update_index_in_dim(result, got, lax.rem(me - shift + size, size), 0)
    return result


class HalvingDp:
    def __init__(self, pieces):
        me = lax.axis_index("dp")
        self.parts = [
            lax.dynamic_index_in_dim(pieces, me ^ flip, 0, keepdims=False) for flip in DP_ORDER
        ]

    def first(self):
        return jnp.stack(self.parts[2:]).astype(jnp.bfloat16)

    def second(self, got):
        self.got = got
        return (
            self.parts[1].astype(jnp.float32) + self.got[1].astype(jnp.float32)
        ).astype(jnp.bfloat16)

    def finish(self, last):
        return sum(one.astype(jnp.float32) for one in (self.parts[0], self.got[0], last))


def relative_order():
    size, me = lax.axis_size("index"), lax.axis_index("index")
    steps = jnp.arange(size // 2, dtype=jnp.int32) * 2
    return jnp.concatenate([me ^ steps, me ^ 1 ^ steps])


def exchange(piece, flip):
    size = lax.axis_size("index")
    return lax.ppermute(piece, "index", [(i, i ^ flip) for i in range(size)])


def exchange_dp(piece, flip):
    size = lax.axis_size("dp")
    return lax.ppermute(piece, "dp", [(i, i ^ flip) for i in range(size)])


def add_kernel(*refs):
    total = sum(ref[...].astype(jnp.float32) for ref in refs[:-1])
    refs[-1][...] = total.astype(jnp.bfloat16)


def add(*terms):
    flat, specs = [], []
    first = terms[0]
    dims = first[0].shape[1:] if isinstance(first, tuple) else first.shape
    rows = 1
    for size in dims[:-1]:
        rows *= size
    block = min(rows, 256)
    for term in terms:
        array, entry = term if isinstance(term, tuple) else (term, 0)
        flat.append(array.reshape(-1, dims[-1]))
        start = entry * rows // block
        specs.append(pl.BlockSpec((block, dims[-1]), lambda i, start=start: (start + i, 0)))
    return pl.pallas_call(
        add_kernel,
        grid=(rows // block,),
        in_specs=specs,
        out_specs=pl.BlockSpec((block, dims[-1]), lambda i: (i, 0)),
        out_shape=shape((rows, dims[-1]), jnp.bfloat16),
        compiler_params=params(),
        cost_estimate=cost(0, 0),
        name="add",
    )(*flat).reshape(dims)


def combine_kernel(plan, *refs):
    ins, outs = list(refs[: -len(plan)]), refs[-len(plan) :]
    for out_ref, entries in zip(outs, plan):
        for e, segments in enumerate(entries):
            start = 0
            for offsets, rows in segments:
                terms, ins = ins[: len(offsets)], ins[len(offsets) :]
                total = sum(
                    ref[0, offset : offset + rows].astype(jnp.float32)
                    for ref, offset in zip(terms, offsets)
                )
                out_ref[e, start : start + rows] = total.astype(jnp.bfloat16)
                start += rows


def combine(*outputs):
    arrays, specs, plan, shapes = [], [], [], []
    for entries in outputs:
        plan.append([])
        for segments in entries:
            plan[-1].append([])
            for terms in segments:
                offsets = []
                for array, e, rows, start in terms:
                    block, place, offset = rows, start // rows, 0
                    if start % rows or array.shape[1] % rows:
                        block, place, offset = array.shape[1], 0, start
                    offsets.append(offset)
                    arrays.append(array)
                    specs.append(
                        pl.BlockSpec(
                            (1, block, array.shape[2]), lambda i, e=e, place=place: (e, place, 0)
                        )
                    )
                plan[-1][-1].append((offsets, terms[0][2]))
        rows = sum(rows for _, rows in plan[-1][0])
        shapes.append(shape((len(entries), rows, arrays[0].shape[2]), jnp.bfloat16))
    return pl.pallas_call(
        partial(combine_kernel, plan),
        grid=(1,),
        in_specs=specs,
        out_specs=[whole(out) for out in shapes],
        out_shape=shapes,
        compiler_params=params(),
        cost_estimate=cost(0, 0),
        name="combine",
    )(*arrays)


class Halving:
    def __init__(self, chips):
        self.chips = chips
        self.middle = chips[0][0][0].shape[1] // 2

    def terms(self, k, half, *more):
        middle = self.middle
        return [(array, e, middle, half * middle) for array, e in self.chips[k]] + [
            (array, e, middle, start) for array, e, start in more
        ]

    def total(self, k, half, *more):
        rows = slice(half * self.middle, (half + 1) * self.middle)
        parts = [array[e, rows] for array, e in self.chips[k]] + [*more]
        return sum(one.astype(jnp.float32) for one in parts)

    def finish(self, top, low):
        return jnp.concatenate(
            [self.total(0, 0, self.got[0][0], top), self.total(0, 1, self.got[1][0], low)], axis=0
        )


def both_cores(mine, other):
    parts = [part.reshape(CHIPS, -1, part.shape[-1]) for part in (mine, other)]
    return Halving([[(part, k) for part in parts] for k in range(CHIPS)])


def firsts(*sums):
    return combine(
        [[one.terms(k, 0) for one in sums] for k in (1, 3)],
        [[one.terms(k, 1) for one in sums] for k in (2, 3)],
    )


def seconds(*sums):
    for one, top, low, start in sums:
        rows = slice(start, start + one.middle)
        one.got = top[:, rows], low[:, rows]
    top, low = combine(
        [[one.terms(2, 0, (top, 1, start)) for one, top, _, start in sums]],
        [[one.terms(1, 1, (low, 1, start)) for one, _, low, start in sums]],
    )
    return top[0], low[0]


def send_first(top, low):
    return [exchange(top, 2), exchange(low, 4)]


def send_last(top, low):
    return [exchange(top, 4), exchange(low, 2)]


def split_rows(arrays, rows):
    return [a[..., :rows, :] for a in arrays], [a[..., rows:, :] for a in arrays]


def small_send(values):
    size = lax.axis_size("index")
    flat = jnp.pad(values.reshape(-1), (0, 1024 - values.size)).reshape(1, 8, 128)
    return swap(jnp.broadcast_to(flat, (size, 8, 128)))


def small_take(arrived, dims):
    size = 1
    for dim in dims:
        size *= dim
    return jnp.sum(arrived, axis=0).reshape(-1)[:size].reshape(dims)


def hold_kernel(*_):
    pass


def hold(values, *others):
    anywhere = pl.BlockSpec(memory_space=pl.ANY)
    return pl.pallas_call(
        hold_kernel,
        in_specs=[anywhere] * (len(values) + len(others)),
        out_specs=[anywhere] * len(values),
        out_shape=[shape(value.shape, value.dtype) for value in values],
        input_output_aliases={i: i for i in range(len(values))},
        name="hold",
    )(*values, *others)


def swap(pieces):
    return lax.all_to_all(pieces, "index", 0, 0, tiled=True)


def head_body(
    decoder_input,
    encoder_memory,
    question_vectors,
    passage_vectors,
    passage_ids,
    valid_count,
    output_grad,
    attention_weight,
    expand_weight,
    contract_weight,
    vector_params,
    attention_mean,
    attention_square,
    expand_mean,
    expand_square,
    contract_mean,
    contract_square,
    vector_mean,
    vector_square,
):
    low = jnp.bfloat16
    count, groups = lax.axis_size("index"), lax.axis_size("dp")
    place = lax.axis_index("index")
    seqs, rows_here, depth = decoder_input.shape
    memory_here = encoder_memory.shape[1]
    width = depth // count
    part = attention_weight.shape[1]
    hidden = expand_weight.shape[1]
    vector_rows, vector_width = vector_params.shape
    question_width = question_vectors.shape[1]
    rows = seqs * rows_here

    attention_low = attention_weight.astype(low)
    extras = jnp.concatenate(
        [vector_params.astype(low).reshape(-1), question_vectors.reshape(-1)]
    )
    extra_rows = -(-extras.shape[0] // (16 * width)) * 16
    extras = jnp.pad(extras, (0, extra_rows * width - extras.shape[0])).reshape(
        1, extra_rows, width
    )
    split = jnp.concatenate([attention_low[:3], attention_low[5:7]], axis=0)
    columns = split.reshape(5, part, count, width).transpose(2, 0, 1, 3)
    package = jnp.concatenate(
        [
            columns.reshape(count, 5 * part, width),
            jnp.broadcast_to(extras, (count, extra_rows, width)),
        ],
        axis=1,
    )
    order = relative_order()
    memory_block = -(-memory_here // rows_here) * rows_here
    rows_all = lax.all_gather(
        jnp.concatenate(
            [
                jnp.pad(encoder_memory, ((0, 0), (0, memory_block - memory_here), (0, 0))),
                decoder_input,
            ],
            axis=1,
        ),
        "index",
        axis=0,
        tiled=False,
    )
    input_rows = (rows_all, memory_block, rows_here)
    memory_rows = (rows_all, 0, memory_here)
    square = attention_low[3:5].transpose(1, 0, 2).reshape(part, 2 * depth)
    received = swap(package)
    square_arrived = hold(send_dp(square), received)
    (received,) = hold([received], *square_arrived)
    received_sent = send_dp(received)
    (contract,) = hold([contract_weight.astype(low)], received)
    contract = [contract] + [exchange(contract, 2 * k) for k in range(1, CHIPS)]
    slices_arrived = hold(received_sent, *contract[1:])
    square_arrived = hold(square_arrived, *slices_arrived)
    square = lax.all_gather(place_dp(square, square_arrived), "index", axis=0, tiled=False)
    slices = place_dp(received, slices_arrived)
    vectors = (
        slices[:, :, 5 * part :]
        .reshape(groups, count, extra_rows * width)[:, :, : vector_rows * vector_width]
        .reshape(groups, count, vector_rows, vector_width)
        .transpose(2, 0, 1, 3)
        .reshape(vector_rows, depth)
        .astype(jnp.float32)
    )
    question_full = (
        received[:, 5 * part :]
        .reshape(count, extra_rows * width)[:, vector_rows * vector_width :][
            :, : seqs * question_width
        ]
        .reshape(count, seqs, question_width)
        .transpose(1, 0, 2)
        .reshape(seqs, count * question_width)
    )
    expand_part = hidden // depth * part
    late = jnp.concatenate(
        [
            expand_weight.astype(low)
            .reshape(part, hidden // depth, depth)
            .transpose(1, 0, 2)
            .reshape(expand_part, depth),
            attention_low[7],
        ],
        axis=0,
    )
    (late,) = hold([late], *slices_arrived)
    late_sent = send_dp(late)

    (passage_ids,) = hold([passage_ids], *slices_arrived)
    passages_here = passage_vectors.shape[0]
    local_ids = passage_ids - place * passages_here
    owned_slot = (local_ids >= 0) & (local_ids < passages_here)
    picked = passage_vectors[jnp.clip(local_ids, 0, passages_here - 1)]
    local_scores = jnp.einsum(
        "sc,skc->sk", question_full, picked, preferred_element_type=jnp.float32
    )
    slots = passage_ids.shape[1]
    usable = jnp.arange(slots)[None, :] < valid_count[:, None]
    scores = small_take(small_send(jnp.where(owned_slot, local_scores, 0.0)), local_scores.shape)
    masked = jnp.where(usable, scores, negative_fill)
    maximum = jnp.max(masked, axis=1)
    exponent = jnp.where(usable, jnp.exp(masked - maximum[:, None]), 0.0)
    partition = jnp.sum(exponent, axis=1)
    passage_prob = exponent / partition[:, None]
    log_prior = jnp.where(
        usable, masked - maximum[:, None] - jnp.log(partition)[:, None], negative_fill
    )
    key_bias = jnp.repeat(log_prior, MEM_P, axis=1)

    vector_here = lax.dynamic_slice_in_dim(vectors[:5], place * width, width, axis=1)
    no_bias = jnp.zeros((1, width), jnp.float32)
    qkv_bias = jnp.concatenate([vector_here[0:1], no_bias, vector_here[1:2]], axis=1)
    kv_bias = jnp.concatenate([no_bias, vector_here[4:5]], axis=1)
    x_rows = decoder_input.reshape(rows, depth)
    qkv = project_columns("self_qkv", *input_rows, slices, 0, 3, qkv_bias)
    self_out, self_stat = attend(True, qkv, 0, qkv, 1, 2, key_bias[:, None, :])
    self_out, *late_arrived = hold([self_out, *late_sent])
    self_got = swap(self_out)
    late = lax.all_gather(place_dp(late, late_arrived), "index", axis=0, tiled=False)
    ahead, across = hold([jnp.stack(contract[:2]), jnp.stack(contract[2:])], *late_arrived)
    self_got, ahead_far, across_far = hold(
        [self_got, exchange_dp(ahead, 2), exchange_dp(across, 1)]
    )
    ahead = jnp.stack([ahead, ahead_far])
    across = jnp.stack([across, across_far])
    contract_sent = [exchange_dp(ahead, 1), exchange_dp(across, 2)]
    self_mixed, first_in, first_low, cross_query = first_forward(
        self_got, x_rows, square, vectors, ahead_far
    )
    (slices,) = hold([slices], first_low)
    memory_kv = project_columns("memory_kv", *memory_rows, slices, 3, 2, kv_bias)
    cross_query = swap(cross_query)[:, None]
    cross_out, cross_stat = attend(
        False, cross_query, 0, memory_kv, 0, 1, key_bias[:, None, :]
    )
    ahead_far, across_far = hold(contract_sent, cross_out)
    contract = [ahead, ahead_far, across, across_far]
    contract += [exchange(piece, 1) for piece in contract]
    places = lax.axis_index("dp") ^ jnp.array(DP_ORDER, jnp.int32)
    (
        cross_mixed,
        layer_output,
        wide_grad,
        *contract_grads,
        inner_total,
        second_grad,
        cross_low,
        cross_mix_grad,
        stats,
    ) = ffn(
        (order, places),
        swap(cross_out),
        first_in,
        late,
        contract,
        vectors,
        vectors[6:10].reshape(groups * count, -1),
        output_grad.reshape(rows, depth),
    )
    third_stat, second_stat = stats[:8], stats[8:]

    expand_part_sum = lax.psum_scatter(wide_grad, "index", scatter_dimension=0, tiled=False)
    ahead, ahead_far, across, across_far = contract_grads[:4]
    cores = [exchange(piece, 1) for piece in contract_grads[4:]]
    cross_mix_got, *contract_sent = hold(
        [swap(cross_mix_grad), add(ahead_far, cores[1]), add(across_far, cores[3])]
    )
    contract_got = [exchange_dp(contract_sent[0], 1), exchange_dp(contract_sent[1], 2)]
    cross_dq, cross_dkv, prior_rows = attend_back(
        False,
        cross_query,
        0,
        memory_kv,
        0,
        1,
        cross_mix_got,
        cross_stat,
        key_bias[:, None, :],
        contract_sent[0],
    )
    memory_mine, memory_other, kv_grads, kv_total = project_columns_back(
        "memory_kv_back", order, *memory_rows, [cross_dkv], slices, 3, 2
    )
    cross_dq, *contract_got = hold([cross_dq, *contract_got], memory_mine)
    contract_next = [
        add((ahead, 1), (cores[0], 1), (contract_got[0], 1)),
        add((across, 1), (cores[2], 1), (contract_got[1], 1)),
    ]
    cross_dq_got, *contract_next = hold([swap(cross_dq), *contract_next])
    contract_last = [exchange_dp(contract_next[0], 2), exchange_dp(contract_next[1], 1)]
    query_low, first_grad, self_low, self_mix_grad, first_stat = first_back(
        cross_dq_got, second_grad, first_in, square, vectors, memory_mine
    )
    memory_sum = both_cores(memory_mine, exchange(memory_other, 1))
    memory_sent = firsts(memory_sum)
    square_mine, square_other = weight_grads(
        (count, groups, part, depth),
        order,
        self_mixed,
        self_low,
        first_low,
        query_low,
        cross_mixed,
        cross_low,
    )
    square_sum = both_cores(square_mine, exchange(square_other, 1))
    square_sent = firsts(square_sum)
    expand_sum = HalvingDp(expand_part_sum)
    self_mix_got, expand_sent, *contract_last = hold(
        [swap(self_mix_grad), expand_sum.first(), *contract_last], *memory_sent, *square_sent
    )
    expand_got = exchange_dp(expand_sent, 1)
    memory_got = send_first(*memory_sent)
    square_got = send_first(*square_sent)
    self_dq, self_dkv, _ = attend_back(
        True, qkv, 0, qkv, 1, 2, self_mix_got, self_stat, self_stat, square_mine
    )
    self_dq, expand_got = hold([self_dq, expand_got])
    dx_mine, dx_other, qkv_slice_grads, qkv_total = project_columns_back(
        "self_qkv_back", order, *input_rows, [self_dq, self_dkv], slices, 0, 3
    )
    dx_mine, dx_other, *got = hold([dx_mine, dx_other, *memory_got, *square_got])
    own = jnp.concatenate(
        [qkv_total[:, :width], qkv_total[:, 2 * width :], kv_total[:, width:]], axis=0
    )
    own = lax.dynamic_update_slice(
        jnp.zeros((3, depth), jnp.float32), own, (jnp.int32(0), place * width)
    )
    vector_grads = jnp.concatenate(
        [
            own[:2],
            first_stat[1:2],
            first_stat[0:1],
            own[2:],
            second_stat[0:1],
            inner_total.reshape(hidden // depth, depth),
            third_stat[0:1],
            first_stat[2:4],
            second_stat[1:3],
            third_stat[1:3],
        ],
        axis=0,
    )
    vector_size = vector_rows * vector_width
    question_size = seqs * question_width
    vector_send = (
        vector_grads.reshape(vector_rows, groups, count, vector_width)
        .transpose(1, 2, 0, 3)
        .reshape(groups, count, vector_size)
    )
    vector_send = jnp.pad(
        vector_send, ((0, 0), (0, 0), (0, extra_rows * width - vector_size))
    ).reshape(groups, count, extra_rows, width)
    slice_sum = HalvingDp(
        jnp.concatenate([qkv_slice_grads, kv_grads, vector_send.astype(low)], axis=2)
    )
    slice_sent = slice_sum.first()
    slice_got = exchange_dp(slice_sent, 1)
    dx_other, *got = hold([dx_other, *got], slice_sent)
    dx_got = exchange(dx_other, 1)
    square_rows = square_sum.middle
    last = seconds((square_sum, *got[2:], 0), (memory_sum, *got[:2], 0))
    prior_rows, *contract_last = hold([prior_rows, *contract_last], *last)
    last = send_last(*last)
    prior_arrived = small_send(prior_rows.reshape(seqs, slots, MEM_P).sum(axis=-1))
    dx_got, prior_arrived, slice_got, *last = hold([dx_got, prior_arrived, slice_got, *last])
    slice_next = slice_sum.second(slice_got)
    dx_got, *last = hold([dx_got, *last], slice_next)
    slice_last = exchange_dp(slice_next, 2)
    dx_sum = both_cores(dx_mine, dx_got)
    contract_sum = Halving(
        [
            [(one.reshape((-1,) + one.shape[-2:]), k % 2) for one in parts]
            for k, parts in enumerate(
                [(ahead, cores[0], contract_got[0], contract_last[0])] * 2
                + [(across, cores[2], contract_got[1], contract_last[1])] * 2
            )
        ]
    )
    dx_sent = firsts(dx_sum, contract_sum)
    got = send_first(*dx_sent)
    last = hold(last, *dx_sent)
    square_last, memory_last = split_rows(last, square_rows)
    square_far = HalvingDp(square_sum.finish(*square_last).reshape(groups, 3 * part, depth))
    square_got = exchange_dp(square_far.first(), 1)
    square_got, slice_last, *got = hold([square_got, slice_last, *got])
    slice_sum = slice_sum.finish(slice_last)
    prior_grad = jnp.where(usable, small_take(prior_arrived, (seqs, slots)), 0.0)
    score_doc = jnp.where(
        usable, prior_grad - passage_prob * jnp.sum(prior_grad, axis=1, keepdims=True), 0.0
    )
    question_part = jnp.einsum(
        "sk,skc->sc",
        jnp.where(owned_slot, score_doc, 0.0),
        picked.astype(jnp.float32),
        precision=lax.Precision.HIGHEST,
    )

    question_send = (
        question_part.reshape(seqs, count, question_width)
        .transpose(1, 0, 2)
        .reshape(count, question_size)
    )
    question_send = jnp.pad(
        question_send,
        ((0, 0), (vector_size, extra_rows * width - vector_size - question_size)),
    ).reshape(count, extra_rows, width)
    slice_sum = jnp.concatenate(
        [slice_sum[:, : 5 * part], slice_sum[:, 5 * part :] + question_send], axis=1
    )
    slice_send = slice_sum.astype(low)
    arrived = swap(slice_send)
    square_got, *got = hold([square_got, *got], slice_send)
    square_next = square_far.second(square_got)
    got = hold(got, square_next)
    square_last = exchange_dp(square_next, 2)
    expand_last = exchange_dp(hold([expand_sum.second(expand_got)], *got)[0], 2)
    start = dx_sum.middle
    last = send_last(*seconds((dx_sum, *got, 0), (contract_sum, *got, start)))
    dx_last, contract_last = split_rows(last, start)
    input_gradient = first_grad + dx_sum.finish(*dx_last)
    contract_sum = contract_sum.finish(*contract_last)
    memory_last = hold(memory_last, *got)
    memory_gradient = memory_sum.finish(*memory_last).reshape(encoder_memory.shape)
    new_contract = adam_update(
        contract_weight, contract_mean, contract_square, contract_sum, rate_contract, decay_matrix
    )
    (square_last,) = hold([square_last], input_gradient, memory_gradient, *new_contract)
    arrived = arrived.astype(jnp.float32)
    split_grads = (
        arrived[:, : 5 * part]
        .reshape(count, 5, part, width)
        .transpose(1, 2, 0, 3)
        .reshape(5, part, depth)
    )
    extra_sum = jnp.sum(arrived[:, 5 * part :].reshape(count, extra_rows * width), axis=0)
    vector_sum = extra_sum[:vector_size].reshape(vector_rows, vector_width)
    question_gradient = extra_sum[vector_size : vector_size + question_size].reshape(
        seqs, question_width
    )

    expand_sum = (
        expand_sum.finish(expand_last)
        .reshape(hidden // depth, part, depth)
        .transpose(1, 0, 2)
        .reshape(part, hidden)
    )
    square_total = square_far.finish(square_last).reshape(3, part, depth)
    attention_sum = jnp.concatenate(
        [split_grads[:3], square_total[:2], split_grads[3:], square_total[2:]], axis=0
    )

    new_attention = adam_update(
        attention_weight,
        attention_mean,
        attention_square,
        attention_sum,
        rate_attention,
        decay_matrix,
    )
    new_expand = adam_update(
        expand_weight, expand_mean, expand_square, expand_sum, rate_expand, decay_matrix
    )
    new_vector = adam_update(
        vector_params, vector_mean, vector_square, vector_sum, rate_vector, 0.0
    )
    return (
        layer_output.reshape(decoder_input.shape),
        input_gradient.reshape(decoder_input.shape),
        memory_gradient,
        question_gradient,
        *new_attention,
        *new_expand,
        *new_contract,
        *new_vector,
    )


def body(sizes, *arrays):
    depth = arrays[0].shape[2]
    if sizes == (4, 8) and depth // 8 % 128 == 0:
        return head_body(*arrays)
    return general_body(*arrays)


def solution(mesh):
    return jax.shard_map(
        partial(body, (mesh.shape["dp"], mesh.shape["index"])),
        mesh=mesh,
        in_specs=(
            P("dp", "index", None),
            P("dp", "index", None),
            P("dp", "index"),
            P("index", None),
            P("dp", None),
            P("dp"),
            P("dp", "index", None),
            P(None, ("dp", "index"), None),
            P(("dp", "index"), None),
            P(("dp", "index"), None),
            P(None, ("dp", "index")),
            P(None, ("dp", "index"), None),
            P(None, ("dp", "index"), None),
            P(("dp", "index"), None),
            P(("dp", "index"), None),
            P(("dp", "index"), None),
            P(("dp", "index"), None),
            P(None, ("dp", "index")),
            P(None, ("dp", "index")),
        ),
        out_specs=(
            P("dp", "index", None),
            P("dp", "index", None),
            P("dp", "index", None),
            P("dp", "index"),
            P(None, ("dp", "index"), None),
            P(None, ("dp", "index"), None),
            P(None, ("dp", "index"), None),
            P(("dp", "index"), None),
            P(("dp", "index"), None),
            P(("dp", "index"), None),
            P(("dp", "index"), None),
            P(("dp", "index"), None),
            P(("dp", "index"), None),
            P(None, ("dp", "index")),
            P(None, ("dp", "index")),
            P(None, ("dp", "index")),
        ),
        check_vma=False,
    )
```

```python
from functools import partial

import jax
import jax.numpy as jnp
from jax import lax
from jax.experimental import pallas as pl
from jax.experimental.pallas import tpu as pltpu
from jax.sharding import PartitionSpec as P

HEADS = 16
MEM_P = 192
STEP = 10


negative_fill = -1e30
norm_eps = 1e-05
beta_first = 0.9
beta_second = 0.999
adam_eps = 1e-08
decay_matrix = 0.01
rate_attention = 0.1
rate_expand = 0.02
rate_contract = 0.01
rate_vector = 0.2


def layer_norm(hidden, norm_gain, norm_shift):
    center = hidden - jnp.mean(hidden, axis=-1, keepdims=True)
    spread = jnp.mean(center * center, axis=-1, keepdims=True)
    return center * lax.rsqrt(spread + norm_eps) * norm_gain + norm_shift


def split_heads(matrix):
    return matrix.reshape(matrix.shape[0], matrix.shape[1], HEADS, matrix.shape[2] // HEADS)


def merge_heads(matrix):
    return matrix.reshape(matrix.shape[0], matrix.shape[1], matrix.shape[2] * matrix.shape[3])


def project(left_side, weight):
    return jnp.einsum("srd,de->sre", left_side, weight, preferred_element_type=jnp.float32)


def project_back(gradient, weight):
    return jnp.einsum("sre,de->srd", gradient, weight, preferred_element_type=jnp.float32)


def weight_grad(left_side, gradient):
    return jnp.einsum("srd,sre->de", left_side, gradient, preferred_element_type=jnp.float32)


def row_total(values):
    return jnp.sum(values, axis=(0, 1))


def attend_forward(queries, key_rows, values, score_bias, allowed):
    scores = (
        jnp.einsum(
            "sqhd,skhd->shqk",
            split_heads(queries),
            split_heads(key_rows),
            preferred_element_type=jnp.float32,
        )
        * 0.125
        + score_bias
    )
    scores = jnp.where(allowed, scores, negative_fill)
    maximum = jnp.max(scores, axis=-1)
    exponent = jnp.exp(scores - maximum[..., None])
    partition = jnp.sum(exponent, axis=-1)
    attend_prob = exponent / partition[..., None]
    mixture = jnp.einsum(
        "shqk,skhd->sqhd",
        attend_prob.astype(jnp.bfloat16),
        split_heads(values),
        preferred_element_type=jnp.float32,
    )
    return (merge_heads(mixture).astype(jnp.bfloat16), attend_prob, maximum, partition)


def score_grads(grad_mixed, attend_prob, values):
    grad_prob = jnp.einsum(
        "sqhd,skhd->shqk",
        split_heads(grad_mixed),
        split_heads(values),
        preferred_element_type=jnp.float32,
    )
    row_inner = jnp.sum(attend_prob * grad_prob, axis=-1)
    return ((attend_prob * (grad_prob - row_inner[..., None])).astype(jnp.bfloat16), row_inner)


def to_queries(grad_score, key_rows):
    return (
        merge_heads(
            jnp.einsum(
                "shqk,skhd->sqhd",
                grad_score,
                split_heads(key_rows),
                preferred_element_type=jnp.float32,
            )
        )
        * 0.125
    )


def to_keys(grad_score, attend_prob, queries, grad_mixed):
    grad_key = (
        merge_heads(
            jnp.einsum(
                "shqk,sqhd->skhd",
                grad_score,
                split_heads(queries),
                preferred_element_type=jnp.float32,
            )
        )
        * 0.125
    )
    grad_value = merge_heads(
        jnp.einsum(
            "shqk,sqhd->skhd",
            attend_prob.astype(jnp.bfloat16),
            split_heads(grad_mixed),
            preferred_element_type=jnp.float32,
        )
    )
    return (grad_key, grad_value)


def adam_update(weight, moment_one, moment_two, gradient, step_rate, weight_decay):
    mean_new = beta_first * moment_one + (1.0 - beta_first) * gradient
    square_new = beta_second * moment_two + (1.0 - beta_second) * gradient * gradient
    mean_hat = mean_new / (1.0 - beta_first**STEP)
    square_hat = square_new / (1.0 - beta_second**STEP)
    updated = weight - step_rate * (
        mean_hat / (jnp.sqrt(square_hat) + adam_eps) + weight_decay * weight
    )
    return (updated, mean_new, square_new)


def general_body(
    decoder_input,
    encoder_memory,
    question_vectors,
    passage_vectors,
    passage_ids,
    valid_count,
    output_grad,
    attention_weight,
    expand_weight,
    contract_weight,
    vector_params,
    attention_mean,
    attention_square,
    expand_mean,
    expand_square,
    contract_mean,
    contract_square,
    vector_mean,
    vector_square,
):
    attention_low, expand_low, contract_low, vector_low = (
        lax.all_gather(attention_weight.astype(jnp.bfloat16), ("dp", "index"), axis=1, tiled=True),
        lax.all_gather(expand_weight.astype(jnp.bfloat16), ("dp", "index"), axis=0, tiled=True),
        lax.all_gather(contract_weight.astype(jnp.bfloat16), ("dp", "index"), axis=0, tiled=True),
        lax.all_gather(vector_params.astype(jnp.bfloat16), ("dp", "index"), axis=1, tiled=True),
    )
    vectors = vector_low.astype(jnp.float32)
    seqs_here, rows_here, model_width = decoder_input.shape
    shard_index = lax.axis_index("index")
    length = rows_here * lax.axis_size("index")
    ffn_width = expand_low.shape[1]
    self_query = (project(decoder_input, attention_low[0]) + vectors[0]).astype(jnp.bfloat16)
    self_key = project(decoder_input, attention_low[1]).astype(jnp.bfloat16)
    self_value = (project(decoder_input, attention_low[2]) + vectors[1]).astype(jnp.bfloat16)
    key_all, value_all = (
        lax.all_gather(self_key, "index", axis=1, tiled=True),
        lax.all_gather(self_value, "index", axis=1, tiled=True),
    )
    query_place = shard_index * rows_here + jnp.arange(rows_here)
    causal = (jnp.arange(length)[None, :] <= query_place[:, None])[None, None]
    self_mixed, self_prob, self_peak, self_total = attend_forward(
        self_query, key_all, value_all, 0.0, causal
    )
    first_in = (
        decoder_input.astype(jnp.float32) + project(self_mixed, attention_low[3]) + vectors[2]
    )
    first_out, first_back = jax.vjp(layer_norm, first_in, vectors[11], vectors[12])
    first_low = first_out.astype(jnp.bfloat16)
    cross_query = (project(first_low, attention_low[4]) + vectors[3]).astype(jnp.bfloat16)
    cross_key = project(encoder_memory, attention_low[5]).astype(jnp.bfloat16)
    cross_value = (project(encoder_memory, attention_low[6]) + vectors[4]).astype(jnp.bfloat16)
    memory_keys, memory_values = (
        lax.all_gather(cross_key, "index", axis=1, tiled=True),
        lax.all_gather(cross_value, "index", axis=1, tiled=True),
    )
    question_full = lax.all_gather(question_vectors, "index", axis=1, tiled=True)
    passages_here = passage_vectors.shape[0]
    local_ids = passage_ids - shard_index * passages_here
    owned_slot = (local_ids >= 0) & (local_ids < passages_here)
    picked = passage_vectors[jnp.clip(local_ids, 0, passages_here - 1)]
    local_scores = jnp.einsum(
        "sc,skc->sk", question_full, picked, preferred_element_type=jnp.float32
    )
    slots = passage_ids.shape[1]
    usable = jnp.arange(slots)[None, :] < valid_count[:, None]
    local_peak = jnp.max(jnp.where(owned_slot & usable, local_scores, negative_fill), axis=1)
    maximum = lax.pmax(local_peak, "index")
    local_exp = jnp.where(owned_slot & usable, jnp.exp(local_scores - maximum[:, None]), 0.0)
    exponent, scores = lax.psum((local_exp, jnp.where(owned_slot, local_scores, 0.0)), "index")
    masked = jnp.where(usable, scores, negative_fill)
    partition = jnp.sum(exponent, axis=1)
    passage_prob = exponent / partition[:, None]
    log_prior = masked - maximum[:, None] - jnp.log(partition)[:, None]
    memory_total = memory_keys.shape[1]
    bias_rows = jnp.repeat(log_prior, MEM_P, axis=1)
    key_bias = bias_rows[:, None, None, :]
    key_usable = ((jnp.arange(memory_total) // MEM_P)[None, :] < valid_count[:, None])[
        :, None, None, :
    ]
    cross_mixed, cross_prob, cross_peak, cross_total = attend_forward(
        cross_query, memory_keys, memory_values, key_bias, key_usable
    )
    second_in = first_out + project(cross_mixed, attention_low[7]) + vectors[5]
    second_out, second_back = jax.vjp(layer_norm, second_in, vectors[13], vectors[14])
    second_low = second_out.astype(jnp.bfloat16)
    inner_act = project(second_low, expand_low) + vectors[6:10].reshape(ffn_width)
    activated, gelu_back = jax.vjp(partial(jax.nn.gelu, approximate=False), inner_act)
    activ_low = activated.astype(jnp.bfloat16)
    third_in = second_out + project(activ_low, contract_low) + vectors[10]
    layer_output, third_back = jax.vjp(layer_norm, third_in, vectors[15], vectors[16])
    grad_third, gain_three, shift_three = third_back(output_grad.astype(jnp.float32))
    grad_ffn_low = grad_third.astype(jnp.bfloat16)
    grad_contract = weight_grad(activ_low, grad_ffn_low)
    (grad_inner,) = gelu_back(project_back(grad_ffn_low, contract_low))
    grad_inner_low = grad_inner.astype(jnp.bfloat16)
    grad_expand = weight_grad(second_low, grad_inner_low)
    grad_second = grad_third + project_back(grad_inner_low, expand_low)
    grad_second_in, gain_two, shift_two = second_back(grad_second)
    grad_cross_low = grad_second_in.astype(jnp.bfloat16)
    grad_cmix = project_back(grad_cross_low, attention_low[7]).astype(jnp.bfloat16)
    cross_score, cross_inner = score_grads(grad_cmix, cross_prob, memory_values)
    grad_cq = to_queries(cross_score, memory_keys)
    prior_part = (
        jnp.sum(cross_score, axis=(1, 2), dtype=jnp.float32)
        .reshape(seqs_here, slots, MEM_P)
        .sum(axis=-1)
    )
    prior_grad = jnp.where(usable, lax.psum(prior_part, "index"), 0.0)
    score_doc = jnp.where(
        usable, prior_grad - passage_prob * jnp.sum(prior_grad, axis=1, keepdims=True), 0.0
    )
    question_part = jnp.einsum(
        "sk,skc->sc",
        jnp.where(owned_slot, score_doc, 0.0),
        picked.astype(jnp.float32),
        precision=lax.Precision.HIGHEST,
    )
    question_gradient = lax.psum_scatter(question_part, "index", scatter_dimension=1, tiled=True)
    grad_cq_low = grad_cq.astype(jnp.bfloat16)
    grad_first = grad_second_in + project_back(grad_cq_low, attention_low[4])
    ck_part, cv_part = to_keys(cross_score, cross_prob, cross_query, grad_cmix)
    grad_ck, grad_cv = (
        lax.psum_scatter(
            ck_part.astype(jnp.bfloat16), "index", scatter_dimension=1, tiled=True
        ).astype(jnp.float32),
        lax.psum_scatter(
            cv_part.astype(jnp.bfloat16), "index", scatter_dimension=1, tiled=True
        ).astype(jnp.float32),
    )
    grad_ck_low = grad_ck.astype(jnp.bfloat16)
    grad_cv_low = grad_cv.astype(jnp.bfloat16)
    memory_gradient = project_back(grad_ck_low, attention_low[5]) + project_back(
        grad_cv_low, attention_low[6]
    )
    grad_first_in, gain_one, shift_one = first_back(grad_first)
    grad_self_low = grad_first_in.astype(jnp.bfloat16)
    grad_smix = project_back(grad_self_low, attention_low[3]).astype(jnp.bfloat16)
    self_score, row_inner = score_grads(grad_smix, self_prob, value_all)
    grad_sq = to_queries(self_score, key_all)
    key_part, value_part = to_keys(self_score, self_prob, self_query, grad_smix)
    grad_sk, grad_sv = (
        lax.psum_scatter(
            key_part.astype(jnp.bfloat16), "index", scatter_dimension=1, tiled=True
        ).astype(jnp.float32),
        lax.psum_scatter(
            value_part.astype(jnp.bfloat16), "index", scatter_dimension=1, tiled=True
        ).astype(jnp.float32),
    )
    grad_sq_low = grad_sq.astype(jnp.bfloat16)
    grad_sk_low = grad_sk.astype(jnp.bfloat16)
    grad_sv_low = grad_sv.astype(jnp.bfloat16)
    input_gradient = (
        grad_first_in
        + project_back(grad_sq_low, attention_low[0])
        + project_back(grad_sk_low, attention_low[1])
        + project_back(grad_sv_low, attention_low[2])
    )
    attention_grads = jnp.stack(
        [
            weight_grad(decoder_input, grad_sq_low),
            weight_grad(decoder_input, grad_sk_low),
            weight_grad(decoder_input, grad_sv_low),
            weight_grad(self_mixed, grad_self_low),
            weight_grad(first_low, grad_cq_low),
            weight_grad(encoder_memory, grad_ck_low),
            weight_grad(encoder_memory, grad_cv_low),
            weight_grad(cross_mixed, grad_cross_low),
        ]
    )
    vector_grads = jnp.concatenate(
        [
            jnp.stack(
                [
                    row_total(grad_sq),
                    row_total(grad_sv),
                    row_total(grad_first_in),
                    row_total(grad_cq),
                    row_total(grad_cv),
                    row_total(grad_second_in),
                ]
            ),
            row_total(grad_inner).reshape(ffn_width // model_width, model_width),
            jnp.stack(
                [
                    row_total(grad_third),
                    gain_one,
                    shift_one,
                    gain_two,
                    shift_two,
                    gain_three,
                    shift_three,
                ]
            ),
        ]
    )
    attention_sum, expand_sum, contract_sum, vector_sum = (
        lax.psum_scatter(attention_grads, ("dp", "index"), scatter_dimension=1, tiled=True),
        lax.psum_scatter(grad_expand, ("dp", "index"), scatter_dimension=0, tiled=True),
        lax.psum_scatter(grad_contract, ("dp", "index"), scatter_dimension=0, tiled=True),
        lax.psum_scatter(vector_grads, ("dp", "index"), scatter_dimension=1, tiled=True),
    )
    new_attention = adam_update(
        attention_weight,
        attention_mean,
        attention_square,
        attention_sum,
        rate_attention,
        decay_matrix,
    )
    new_expand = adam_update(
        expand_weight, expand_mean, expand_square, expand_sum, rate_expand, decay_matrix
    )
    new_contract = adam_update(
        contract_weight, contract_mean, contract_square, contract_sum, rate_contract, decay_matrix
    )
    new_vector = adam_update(
        vector_params, vector_mean, vector_square, vector_sum, rate_vector, 0.0
    )
    return (
        layer_output.astype(jnp.bfloat16),
        input_gradient,
        memory_gradient,
        question_gradient,
        new_attention[0],
        new_attention[1],
        new_attention[2],
        new_expand[0],
        new_expand[1],
        new_expand[2],
        new_contract[0],
        new_contract[1],
        new_contract[2],
        new_vector[0],
        new_vector[1],
        new_vector[2],
    )


NT = (((1,), (1,)), ((), ()))
NN = (((1,), (0,)), ((), ()))
TN = (((0,), (0,)), ((), ()))
CHIPS = 4
DP_ORDER = (0, 2, 1, 3)
VMEM_LIMIT = 56 << 20


def dot(left_side, right_side, dims):
    return lax.dot_general(left_side, right_side, dims, preferred_element_type=jnp.float32)


def norm_parts(hidden):
    center = hidden - jnp.mean(hidden, axis=-1, keepdims=True)
    inverse = lax.rsqrt(jnp.mean(center * center, axis=-1, keepdims=True) + norm_eps)
    return center * inverse, inverse


def norm_back(gradient, unit, inverse, gain):
    scaled = gradient * gain
    return inverse * (
        scaled
        - jnp.mean(scaled, axis=-1, keepdims=True)
        - unit * jnp.mean(scaled * unit, axis=-1, keepdims=True)
    )


def column_sum(values):
    return jnp.sum(values, axis=0, keepdims=True)


def join(parts, place=None):
    picked = [parts[j] if place is None else parts[j, place] for j in range(parts.shape[0])]
    return jnp.concatenate(
        [block.reshape(block.shape[0] * block.shape[1], block.shape[2]) for block in picked],
        axis=1,
    )


def spread(out_ref, value):
    count, seqs, rows, width = out_ref.shape
    for j in range(count):
        out_ref[j] = value[:, j * width : (j + 1) * width].reshape(seqs, rows, width)


def times(activation, weight):
    count, groups, rows, width = weight.shape
    depth = count * rows
    total = None
    for d in range(groups):
        part = dot(
            activation[:, d * depth : (d + 1) * depth], weight[:, d].reshape(depth, width), NN
        )
        total = part if total is None else total + part
    return total


def times_back(gradient, weight):
    count, groups, rows, width = weight.shape
    depth = count * rows
    return jnp.concatenate(
        [dot(gradient, weight[:, d].reshape(depth, width), NT) for d in range(groups)], axis=1
    )


def outer(out_ref, left_side, gradient):
    count, groups, rows, width = out_ref.shape
    depth = count * rows
    for d in range(groups):
        out_ref[:, d] = (
            dot(left_side[:, d * depth : (d + 1) * depth], gradient, TN)
            .astype(jnp.bfloat16)
            .reshape(count, rows, width)
        )


def whole(array):
    return pl.BlockSpec(array.shape, lambda *_, rank=len(array.shape): (0,) * rank)


def shape(dims, dtype):
    return jax.ShapeDtypeStruct(tuple(dims), dtype)


def params():
    return pltpu.CompilerParams(vmem_limit_bytes=VMEM_LIMIT)


def cost(flops, moved):
    return pl.CostEstimate(flops=int(flops) // 16, bytes_accessed=int(moved) // 16, transcendentals=0)


def in_head(dims, head_width, head):
    return lax.broadcasted_iota(jnp.int32, dims, 1) // head_width == head


def attend_forward_kernel(causal, head_width, q_ref, k_ref, v_ref, bias_ref, out_ref, stat_ref):
    count, _, tile, width = q_ref.shape
    keys = k_ref.shape[0] * k_ref.shape[2]
    key_rows, values = k_ref[...].reshape(keys, width), v_ref[...].reshape(keys, width)
    step = 4
    rows = step * tile
    for b in range(count // step):
        queries = q_ref[b * step : (b + 1) * step].reshape(rows, width)
        seen = (b + 1) * rows if causal else keys
        mixed = None
        for h in range(width // head_width):
            mask = in_head((rows, width), head_width, h)
            scores = dot(
                jnp.where(mask, queries * 0.125, 0).astype(jnp.bfloat16), key_rows[:seen], NT
            )
            if causal:
                corner = scores[:, seen - rows :]
                corner = jnp.where(
                    lax.broadcasted_iota(jnp.int32, corner.shape, 1)
                    <= lax.broadcasted_iota(jnp.int32, corner.shape, 0),
                    corner,
                    negative_fill,
                )
                if b == 0:
                    scores = corner
                else:
                    scores = jnp.concatenate([scores[:, : seen - rows], corner], axis=1)
            else:
                scores = scores + bias_ref[0]
            peak = jnp.max(scores, axis=1, keepdims=True)
            exponent = jnp.exp(scores - peak)
            total = jnp.sum(exponent, axis=1, keepdims=True)
            part = dot(exponent.astype(jnp.bfloat16), values[:seen], NN) * (1.0 / total)
            mixed = part if mixed is None else jnp.where(mask, part, mixed)
            log_total = jnp.broadcast_to(peak + jnp.log(total), (rows, 128))
            stat_ref[0, h : h + 1, b * rows : (b + 1) * rows] = log_total.T[0:1]
        out_ref[b * step : (b + 1) * step] = mixed.astype(jnp.bfloat16).reshape(
            step, 1, tile, width
        )


def attend_backward_kernel(
    causal,
    head_width,
    q_ref,
    k_ref,
    v_ref,
    grad_ref,
    stat_ref,
    bias_ref,
    _,
    dq_ref,
    dkv_ref,
    prior_ref,
    dk_sum,
    dv_sum,
    prior_sum,
):
    count, _, tile, width = q_ref.shape
    keys = k_ref.shape[0] * k_ref.shape[2]
    key_rows, values = k_ref[...].reshape(keys, width), v_ref[...].reshape(keys, width)
    step = 2
    rows = step * tile
    if not causal:
        bias = jnp.broadcast_to(bias_ref[0], (128, keys)).T[:, :1]
    dk_sum[...] = jnp.zeros_like(dk_sum)
    dv_sum[...] = jnp.zeros_like(dv_sum)
    if not causal:
        prior_sum[...] = jnp.zeros_like(prior_sum)
    for b in range(count // step):
        queries = q_ref[b * step : (b + 1) * step].reshape(rows, width)
        gradient = grad_ref[b * step : (b + 1) * step].reshape(rows, width)
        seen = (b + 1) * rows if causal else keys
        query_grad = None
        for h in range(width // head_width):
            mask = in_head((rows, width), head_width, h)
            one_query = jnp.where(mask, queries * 0.125, 0).astype(jnp.bfloat16)
            one_grad = jnp.where(mask, gradient, 0).astype(jnp.bfloat16)
            scores = dot(key_rows[:seen], one_query, NT)
            if causal:
                corner = scores[seen - rows :]
                corner = jnp.where(
                    lax.broadcasted_iota(jnp.int32, corner.shape, 0)
                    <= lax.broadcasted_iota(jnp.int32, corner.shape, 1),
                    corner,
                    negative_fill,
                )
                if b == 0:
                    scores = corner
                else:
                    scores = jnp.concatenate([scores[: seen - rows], corner], axis=0)
            else:
                scores = scores + bias
            prob = jnp.exp(scores - stat_ref[0, h : h + 1, b * rows : (b + 1) * rows])
            grad_prob = dot(values[:seen], one_grad, NT)
            inner = jnp.sum(prob * grad_prob, axis=0, keepdims=True)
            grad_score = prob * (grad_prob - inner)
            score_low = grad_score.astype(jnp.bfloat16)
            dv_sum[:seen] += dot(prob.astype(jnp.bfloat16), one_grad, NN)
            dk_sum[:seen] += dot(score_low, one_query, NN)
            if not causal:
                partial_sum = grad_score[:, :128]
                for piece in range(128, rows, 128):
                    partial_sum = partial_sum + grad_score[:, piece : piece + 128]
                prior_sum[...] += partial_sum
            part = dot(score_low, key_rows[:seen], TN)
            query_grad = part if query_grad is None else jnp.where(mask, part, query_grad)
        dq_ref[b * step : (b + 1) * step] = (
            (query_grad * 0.125).astype(jnp.bfloat16).reshape(step, 1, tile, width)
        )
    dkv_ref[:, 0] = dk_sum[...].astype(jnp.bfloat16).reshape(k_ref.shape)
    dkv_ref[:, 1] = dv_sum[...].astype(jnp.bfloat16).reshape(k_ref.shape)
    if causal:
        prior_ref[...] = jnp.zeros_like(prior_ref)
    else:
        prior_ref[0] = column_sum(prior_sum[...].T)


def pick(array, place):
    count, _, _, rows, width = array.shape
    return pl.BlockSpec((count, None, 1, rows, width), lambda s: (0, place, s, 0, 0))


def attend(causal, queries, query_at, keys, key_at, value_at, bias):
    count, _, seqs, tile, width = queries.shape
    key_rows = keys.shape[0] * keys.shape[3]
    head_width = width * count // HEADS
    length = count * tile
    heads = width // head_width
    return pl.pallas_call(
        partial(attend_forward_kernel, causal, head_width),
        grid=(seqs,),
        in_specs=[
            pick(queries, query_at),
            pick(keys, key_at),
            pick(keys, value_at),
            pl.BlockSpec(memory_space=pl.ANY)
            if causal
            else pl.BlockSpec((1, 1, key_rows), lambda s: (s, 0, 0)),
        ],
        out_specs=[
            pl.BlockSpec((count, 1, tile, width), lambda s: (0, s, 0, 0)),
            pl.BlockSpec((1, heads, length), lambda s: (s, 0, 0)),
        ],
        out_shape=[
            shape((count, seqs, tile, width), jnp.bfloat16),
            shape((seqs, heads, length), jnp.float32),
        ],
        compiler_params=params(),
        cost_estimate=cost(
            16 * seqs * length * key_rows * width, 4 * seqs * (length + key_rows) * width
        ),
        name="attend_self" if causal else "attend_memory",
    )(queries, keys, keys, bias)


def attend_back(
    causal, queries, query_at, keys, key_at, value_at, gradient, stat, bias, after
):
    count, _, seqs, tile, width = queries.shape
    key_tile = keys.shape[3]
    key_rows = count * key_tile
    head_width = width * count // HEADS
    length = count * tile
    heads = width // head_width
    return pl.pallas_call(
        partial(attend_backward_kernel, causal, head_width),
        grid=(seqs,),
        in_specs=[
            pick(queries, query_at),
            pick(keys, key_at),
            pick(keys, value_at),
            pl.BlockSpec((count, 1, tile, width), lambda s: (0, s, 0, 0)),
            pl.BlockSpec((1, heads, length), lambda s: (s, 0, 0)),
            pl.BlockSpec(memory_space=pl.ANY)
            if causal
            else pl.BlockSpec((1, 1, key_rows), lambda s: (s, 0, 0)),
            pl.BlockSpec(memory_space=pl.ANY),
        ],
        out_specs=[
            pl.BlockSpec((count, 1, tile, width), lambda s: (0, s, 0, 0)),
            pl.BlockSpec((count, 2, 1, key_tile, width), lambda s: (0, 0, s, 0, 0)),
            pl.BlockSpec((1, 1, key_rows), lambda s: (s, 0, 0)),
        ],
        out_shape=[
            shape((count, seqs, tile, width), jnp.bfloat16),
            shape((count, 2, seqs, key_tile, width), jnp.bfloat16),
            shape((seqs, 1, key_rows), jnp.float32),
        ],
        scratch_shapes=[
            pltpu.VMEM((key_rows, width), jnp.float32),
            pltpu.VMEM((key_rows, width), jnp.float32),
            pltpu.VMEM((key_rows, 128), jnp.float32),
        ],
        compiler_params=params(),
        cost_estimate=cost(
            40 * seqs * length * key_rows * width, 8 * seqs * (length + key_rows) * width
        ),
        name="attend_self_back" if causal else "attend_memory_back",
    )(queries, keys, keys, gradient, stat, bias, after)


def take_columns(scratch, slices, first):
    width = slices.shape[3]
    depth = scratch.shape[0]
    rows = depth // (slices.shape[0] * slices.shape[1])
    for m in range(scratch.shape[1] // width):
        start = (first + m) * rows
        scratch[:, m * width : (m + 1) * width] = slices[:, :, start : start + rows].reshape(
            depth, width
        )


def columns_kernel(first, start, seqs, rows, row_ref, slice_ref, bias_ref, out_ref, weight, taken, sem):
    def copy(i):
        return pltpu.make_async_copy(
            row_ref.at[i, :, pl.ds(start, rows)], taken.at[i], sem.at[i]
        )

    count, many = out_ref.shape[:2]
    width = out_ref.shape[4]
    for i in range(count):
        copy(i).start()
    take_columns(weight, slice_ref, first)
    for i in range(count):
        copy(i).wait()
        result = dot(taken[i].reshape(seqs * rows, weight.shape[0]), weight[...], NN) + bias_ref[...]
        for m in range(many):
            out_ref[i, m] = (
                result[:, m * width : (m + 1) * width]
                .astype(jnp.bfloat16)
                .reshape(seqs, rows, width)
            )


def project_columns(name, gathered_rows, start, rows, slices, first, many, bias):
    count, seqs, _, depth = gathered_rows.shape
    width = slices.shape[3]
    out = shape((count, many, seqs, rows, width), jnp.bfloat16)
    return pl.pallas_call(
        partial(columns_kernel, first, start, seqs, rows),
        grid=(1,),
        in_specs=[pl.BlockSpec(memory_space=pl.ANY), whole(slices), whole(bias)],
        out_specs=whole(out),
        out_shape=out,
        scratch_shapes=[
            pltpu.VMEM((depth, many * width), jnp.bfloat16),
            pltpu.VMEM((count, seqs, rows, depth), jnp.bfloat16),
            pltpu.SemaphoreType.DMA((count,)),
        ],
        compiler_params=params(),
        cost_estimate=cost(
            2 * many * count * seqs * rows * depth * width, 2 * count * seqs * rows * depth
        ),
        name=name,
    )(gathered_rows, slices, bias)


def columns_back_kernel(first, start, order, row_ref, *refs):
    grad_refs, (slice_ref, mine_out, other_out, dw_ref, bias_ref) = refs[:-12], refs[-12:-7]
    weight, taken, gradients, moved, total, in_sem, out_sem = refs[-7:]
    count, seqs, rows, depth = taken.shape
    half = count // 2

    def bring(r):
        return pltpu.make_async_copy(
            row_ref.at[order[r], :, pl.ds(start, rows)], taken.at[r], in_sem.at[r]
        )

    def send(r):
        there = (mine_out, other_out)[r // half].at[r % half, 0]
        return pltpu.make_async_copy(moved.at[r], there, out_sem.at[r])

    for r in range(count):
        bring(r).start()
    take_columns(weight, slice_ref, first)
    size = seqs * rows
    for r in range(count):
        i = order[r]
        pieces = []
        for grad_ref in grad_refs:
            width = grad_ref.shape[-1]
            for m in range(grad_ref.shape[1] if len(grad_ref.shape) == 5 else 1):
                piece = grad_ref[i, m] if len(grad_ref.shape) == 5 else grad_ref[i]
                pieces.append(piece.reshape(size, width))
        gradient = jnp.concatenate(pieces, axis=1)
        gradients[r * size : (r + 1) * size] = gradient
        moved[r] = dot(gradient, weight[...], NT).astype(jnp.bfloat16)
        send(r).start()
    whole_gradient = gradients[...]
    bias_ref[...] = column_sum(whole_gradient.astype(jnp.float32))
    for r in range(count):
        bring(r).wait()
    total[...] = dot(whole_gradient, taken[...].reshape(count * size, depth), TN)
    groups, shards, all_rows, _ = dw_ref.shape
    part = depth // (groups * shards)
    for m in range(all_rows // part):
        dw_ref[:, :, m * part : (m + 1) * part] = (
            total[m * width : (m + 1) * width]
            .T.astype(jnp.bfloat16)
            .reshape(groups, shards, part, width)
        )
    for r in range(count):
        send(r).wait()


def project_columns_back(name, order, gathered_rows, start, rows, gradients, slices, first, many):
    count, seqs, _, depth = gathered_rows.shape
    half = count // 2
    groups, shards, _, width = slices.shape
    part = depth // (groups * shards)
    anywhere = pl.BlockSpec(memory_space=pl.ANY)
    halves = shape((half, 1, seqs * rows, depth), jnp.bfloat16)
    dw_shape = shape((groups, shards, many * part, width), jnp.bfloat16)
    bias = shape((1, many * width), jnp.float32)
    return pl.pallas_call(
        partial(columns_back_kernel, first, start),
        grid_spec=pltpu.PrefetchScalarGridSpec(
            num_scalar_prefetch=1,
            grid=(1,),
            in_specs=[anywhere, *[whole(array) for array in gradients], whole(slices)],
            out_specs=[anywhere, anywhere, whole(dw_shape), whole(bias)],
            scratch_shapes=[
                pltpu.VMEM((depth, many * width), jnp.bfloat16),
                pltpu.VMEM((count, seqs, rows, depth), jnp.bfloat16),
                pltpu.VMEM((count * seqs * rows, many * width), jnp.bfloat16),
                pltpu.VMEM((count, seqs * rows, depth), jnp.bfloat16),
                pltpu.VMEM((many * width, depth), jnp.float32),
                pltpu.SemaphoreType.DMA((count,)),
                pltpu.SemaphoreType.DMA((count,)),
            ],
        ),
        out_shape=[halves, halves, dw_shape, bias],
        compiler_params=params(),
        cost_estimate=cost(
            4 * many * count * seqs * rows * depth * width, 4 * count * seqs * rows * depth
        ),
        name=name,
    )(order, gathered_rows, *gradients, slices)


def gathered(weights, width, place):
    count, groups, rows, _ = weights.shape
    return pl.BlockSpec((count, groups, rows, width), lambda *_: (0, 0, 0, place))


def first_kernel(
    mixed_ref, x_ref, out_w, query_w, vector_ref, _, mixed_out, in_out, low_out, query_out
):
    mixed = join(mixed_ref)
    mixed_out[...] = mixed
    first_in = x_ref[...].astype(jnp.float32) + times(mixed, out_w) + vector_ref[2:3]
    in_out[...] = first_in
    unit, _ = norm_parts(first_in)
    low = (unit * vector_ref[11:12] + vector_ref[12:13]).astype(jnp.bfloat16)
    low_out[...] = low
    spread(query_out, (times(low, query_w) + vector_ref[3:4]).astype(jnp.bfloat16))


def first_forward(mixed, x_rows, weights, vectors, after):
    rows, depth = x_rows.shape
    return pl.pallas_call(
        first_kernel,
        grid=(1,),
        in_specs=[
            whole(mixed),
            whole(x_rows),
            gathered(weights, depth, 0),
            gathered(weights, depth, 1),
            whole(vectors),
            pl.BlockSpec(memory_space=pl.ANY),
        ],
        out_specs=[whole(x_rows), whole(x_rows), whole(x_rows), whole(mixed)],
        out_shape=[
            shape((rows, depth), jnp.bfloat16),
            shape((rows, depth), jnp.float32),
            shape((rows, depth), jnp.bfloat16),
            shape(mixed.shape, jnp.bfloat16),
        ],
        compiler_params=params(),
        cost_estimate=cost(4 * rows * depth * depth, 4 * depth * depth),
        name="first_forward",
    )(mixed, x_rows, weights, weights, vectors, after)


def ffn_kernel(
    order,
    places,
    mixed_ref,
    first_ref,
    out_w,
    vector_ref,
    bias_ref,
    grad_ref,
    wide_ref,
    *refs,
):
    contract_refs, refs = refs[:8], refs[8:]
    mixed_out, layer_out, wide_grad = refs[:3]
    contract_grads, refs = refs[3:11], refs[11:]
    dbias_ref, second_grad, cross_low, mixed_grad, stat_out, columns, contracts = refs[:7]
    active, slope, low, third_low, second_in, total, wide_sem, contract_sem = refs[7:]
    blocks, count, groups, rows, block = columns.shape
    part = block // CHIPS
    depth = vector_ref.shape[1]

    def wide_copies(t, array, outward):
        result = []
        for k in range(CHIPS):
            column = pl.multiple_of(order[t % 2 * CHIPS + k] * part, part)
            row = pl.multiple_of(places[t // 2] * rows, rows)
            there = array.at[:, :, pl.ds(row, rows), pl.ds(column, part)]
            here = columns.at[t, :, :, :, pl.ds(k * part, part)]
            ends = (here, there) if outward else (there, here)
            result.append(pltpu.make_async_copy(*ends, wide_sem.at[t, k]))
        return result

    def contract_copies(t, pieces, outward):
        near, far = divmod(DP_ORDER[t // 2], 2)
        first = pieces[t % 2 * 4 + far].at[near]
        last = pieces[t % 2 * 4 + 2 + near].at[far]
        result = []
        for half, there in enumerate((first, last)):
            here = contracts.at[t, pl.ds(half * CHIPS // 2, CHIPS // 2)]
            ends = (here, there) if outward else (there, here)
            result.append(pltpu.make_async_copy(*ends, contract_sem.at[t, half]))
        return result

    for t in range(blocks):
        for copy in wide_copies(t, wide_ref, False):
            copy.start()
        for copy in contract_copies(t, contract_refs, False):
            copy.start()

    mixed = join(mixed_ref)
    mixed_out[...] = mixed
    unit, _ = norm_parts(first_ref[...])
    second_in[...] = (
        unit * vector_ref[11:12] + vector_ref[12:13] + times(mixed, out_w) + vector_ref[5:6]
    )
    unit, _ = norm_parts(second_in[...])
    second = unit * vector_ref[13:14] + vector_ref[14:15]
    low[...] = second.astype(jnp.bfloat16)
    total[...] = second + vector_ref[10:11]

    def shard(t, k):
        return places[t // 2] * count + order[t % 2 * CHIPS + k]

    for t in range(blocks):
        for copy in wide_copies(t, wide_ref, False):
            copy.wait()
        bias = jnp.concatenate([bias_ref[pl.ds(shard(t, k), 1)] for k in range(CHIPS)], axis=1)
        inner = times(low[...], columns.at[t]) + bias
        phi = 0.5 + 0.5 * lax.erf(inner * (0.5**0.5))
        out = (inner * phi).astype(jnp.bfloat16)
        active[t] = out
        slope[t] = phi + inner * jnp.exp(-0.5 * inner * inner) * 0.3989422804014327
        for copy in contract_copies(t, contract_refs, False):
            copy.wait()
        total[...] += dot(out, contracts[t].reshape(block, depth), NN)

    unit, inverse = norm_parts(total[...])
    gain = vector_ref[15:16]
    layer_out[...] = (unit * gain + vector_ref[16:17]).astype(jnp.bfloat16)
    gradient = grad_ref[...].astype(jnp.float32)
    grad_third = norm_back(gradient, unit, inverse, gain)
    stat_out[...] = jnp.zeros_like(stat_out)
    stat_out[0:1] = column_sum(grad_third)
    stat_out[1:2] = column_sum(gradient * unit)
    stat_out[2:3] = column_sum(gradient)
    total[...] = grad_third
    third_low[...] = grad_third.astype(jnp.bfloat16)
    turned = low[...].T

    for t in range(blocks):
        grad_inner = dot(third_low[...], contracts[t].reshape(block, depth), NT) * slope[t]
        inner_low = grad_inner.astype(jnp.bfloat16)
        sums = column_sum(grad_inner)
        for k in range(CHIPS):
            dbias_ref[pl.ds(shard(t, k), 1)] = sums[:, k * part : (k + 1) * part]
        contracts[t] = (
            dot(active[t], third_low[...], TN).astype(jnp.bfloat16).reshape(CHIPS, part, depth)
        )
        for copy in contract_copies(t, contract_grads, True):
            copy.start()
        total[...] += times_back(inner_low, columns.at[t])
        result = dot(turned, inner_low, NN).astype(jnp.bfloat16)
        for d in range(groups):
            columns[t, :, d] = result[d * count * rows : (d + 1) * count * rows].reshape(
                count, rows, block
            )
        for copy in wide_copies(t, wide_grad, True):
            copy.start()

    unit, inverse = norm_parts(second_in[...])
    grad_second = total[...]
    grad_in = norm_back(grad_second, unit, inverse, vector_ref[13:14])
    second_grad[...] = grad_in
    grad_low = grad_in.astype(jnp.bfloat16)
    cross_low[...] = grad_low
    spread(mixed_grad, times_back(grad_low, out_w).astype(jnp.bfloat16))
    stat_out[8:9] = column_sum(grad_in)
    stat_out[9:10] = column_sum(grad_second * unit)
    stat_out[10:11] = column_sum(grad_second)
    for t in range(blocks):
        for copy in contract_copies(t, contract_grads, True) + wide_copies(t, wide_grad, True):
            copy.wait()


def ffn(orders, mixed, first_in, wide, contract, vectors, bias, output_grad):
    rows, depth = first_in.shape
    hidden = bias.size
    block = depth // 2
    count, groups, all_rows, _ = wide.shape
    part = depth // (count * groups)
    blocks = hidden // block
    full = whole(first_in)
    anywhere = pl.BlockSpec(memory_space=pl.ANY)
    heads_out = shape(mixed.shape, jnp.bfloat16)
    stats = shape((16, depth), jnp.float32)
    return pl.pallas_call(
        ffn_kernel,
        grid_spec=pltpu.PrefetchScalarGridSpec(
            num_scalar_prefetch=2,
            grid=(1,),
            in_specs=[
                whole(mixed),
                full,
                pl.BlockSpec((count, groups, part, depth), lambda *_: (0, 0, groups, 0)),
                whole(vectors),
                whole(bias),
                full,
                *[anywhere] * 9,
            ],
            out_specs=[
                full,
                full,
                *[anywhere] * 9,
                whole(bias),
                full,
                full,
                whole(heads_out),
                whole(stats),
            ],
            scratch_shapes=[
                pltpu.VMEM((blocks, count, groups, part, block), jnp.bfloat16),
                pltpu.VMEM((blocks, CHIPS) + contract[0].shape[2:], jnp.bfloat16),
                pltpu.VMEM((blocks, rows, block), jnp.bfloat16),
                pltpu.VMEM((blocks, rows, block), jnp.float32),
                pltpu.VMEM((rows, depth), jnp.bfloat16),
                pltpu.VMEM((rows, depth), jnp.bfloat16),
                pltpu.VMEM((rows, depth), jnp.float32),
                pltpu.VMEM((rows, depth), jnp.float32),
                pltpu.SemaphoreType.DMA((blocks, CHIPS)),
                pltpu.SemaphoreType.DMA((blocks, 2)),
            ],
        ),
        out_shape=[
            shape((rows, depth), jnp.bfloat16),
            shape((rows, depth), jnp.bfloat16),
            shape((count, groups, all_rows - part, depth), jnp.bfloat16),
            *[shape(piece.shape, jnp.bfloat16) for piece in contract],
            shape(bias.shape, jnp.float32),
            shape((rows, depth), jnp.float32),
            shape((rows, depth), jnp.bfloat16),
            heads_out,
            stats,
        ],
        compiler_params=params(),
        cost_estimate=cost(12 * rows * depth * hidden, 16 * depth * hidden),
        name="ffn",
    )(*orders, mixed, first_in, wide, vectors, bias, output_grad, wide, *contract)


def first_back_kernel(
    dq_ref,
    second_grad,
    first_ref,
    out_w,
    query_w,
    vector_ref,
    _,
    query_low,
    grad_in_out,
    self_low,
    mixed_grad,
    stat_out,
):
    query_grad = join(dq_ref)
    query_low[...] = query_grad
    grad_first = second_grad[...] + times_back(query_grad, query_w)
    unit, inverse = norm_parts(first_ref[...])
    grad_in = norm_back(grad_first, unit, inverse, vector_ref[11:12])
    grad_in_out[...] = grad_in
    grad_low = grad_in.astype(jnp.bfloat16)
    self_low[...] = grad_low
    spread(mixed_grad, times_back(grad_low, out_w).astype(jnp.bfloat16))
    stat_out[...] = jnp.zeros_like(stat_out)
    stat_out[0:1] = column_sum(query_grad.astype(jnp.float32))
    stat_out[1:2] = column_sum(grad_in)
    stat_out[2:3] = column_sum(grad_first * unit)
    stat_out[3:4] = column_sum(grad_first)


def first_back(dq, second_grad, first_in, weights, vectors, after):
    rows, depth = first_in.shape
    full = whole(first_in)
    return pl.pallas_call(
        first_back_kernel,
        grid=(1,),
        in_specs=[
            whole(dq),
            full,
            full,
            gathered(weights, depth, 0),
            gathered(weights, depth, 1),
            whole(vectors),
            pl.BlockSpec(memory_space=pl.ANY),
        ],
        out_specs=[full, full, full, whole(dq), pl.BlockSpec((8, depth), lambda *_: (0, 0))],
        out_shape=[
            shape((rows, depth), jnp.bfloat16),
            shape((rows, depth), jnp.float32),
            shape((rows, depth), jnp.bfloat16),
            shape(dq.shape, jnp.bfloat16),
            shape((8, depth), jnp.float32),
        ],
        compiler_params=params(),
        cost_estimate=cost(4 * rows * depth * depth, 4 * depth * depth),
        name="first_back",
    )(dq, second_grad, first_in, weights, weights, vectors, after)


def weight_grads_kernel(
    order,
    mixed,
    self_low,
    first_low,
    query_low,
    cross,
    cross_low,
    mine_out,
    other_out,
    result,
):
    step = pl.program_id(0)
    pairs = ((mixed, self_low), (first_low, query_low), (cross, cross_low))
    half, groups, part, _ = mine_out.shape
    for m, (left_side, gradient) in enumerate(pairs):

        @pl.when(step == m)
        def _(left_side=left_side, gradient=gradient):
            result[...] = dot(left_side[...], gradient[...], TN).astype(jnp.bfloat16)

    for d in range(groups):
        for k in range(half):
            for p, out_ref in enumerate((mine_out, other_out)):
                row = pl.multiple_of((2 * half * d + order[p * half + k]) * part, part)
                out_ref[k, d] = result[pl.ds(row, part)]


def weight_grads(dims, order, mixed, self_low, first_low, query_low, cross, cross_low):
    count, groups, part, depth = dims
    half = pl.BlockSpec((count // 2, groups, part, depth), lambda m, _: (0, 0, m, 0))
    return pl.pallas_call(
        weight_grads_kernel,
        grid_spec=pltpu.PrefetchScalarGridSpec(
            num_scalar_prefetch=1,
            grid=(3,),
            in_specs=[whole(mixed)] * 6,
            out_specs=[half, half],
            scratch_shapes=[pltpu.VMEM((depth, depth), jnp.bfloat16)],
        ),
        out_shape=[shape((count // 2, groups, 3 * part, depth), jnp.bfloat16)] * 2,
        compiler_params=params(),
        cost_estimate=cost(6 * mixed.shape[0] * depth * depth, 6 * depth * depth),
        name="weight_grads",
    )(order, mixed, self_low, first_low, query_low, cross, cross_low)


def send_dp(piece):
    size = lax.axis_size("dp")
    return [
        lax.ppermute(piece, "dp", [(i, (i + shift) % size) for i in range(size)])
        for shift in range(1, size)
    ]


def place_dp(piece, arrived):
    size, me = lax.axis_size("dp"), lax.axis_index("dp")
    result = jnp.zeros((size,) + piece.shape, piece.dtype)
    result = lax.dynamic_update_index_in_dim(result, piece, me, 0)
    for shift, got in enumerate(arrived, 1):
        result = lax.dynamic_update_index_in_dim(result, got, lax.rem(me - shift + size, size), 0)
    return result


class HalvingDp:
    def __init__(self, pieces):
        me = lax.axis_index("dp")
        self.parts = [
            lax.dynamic_index_in_dim(pieces, me ^ flip, 0, keepdims=False) for flip in DP_ORDER
        ]

    def first(self):
        return jnp.stack(self.parts[2:]).astype(jnp.bfloat16)

    def second(self, got):
        self.got = got
        return (
            self.parts[1].astype(jnp.float32) + self.got[1].astype(jnp.float32)
        ).astype(jnp.bfloat16)

    def finish(self, last):
        return sum(one.astype(jnp.float32) for one in (self.parts[0], self.got[0], last))


def relative_order():
    size, me = lax.axis_size("index"), lax.axis_index("index")
    steps = jnp.arange(size // 2, dtype=jnp.int32) * 2
    return jnp.concatenate([me ^ steps, me ^ 1 ^ steps])


def exchange(piece, flip):
    size = lax.axis_size("index")
    return lax.ppermute(piece, "index", [(i, i ^ flip) for i in range(size)])


def exchange_dp(piece, flip):
    size = lax.axis_size("dp")
    return lax.ppermute(piece, "dp", [(i, i ^ flip) for i in range(size)])


def add_kernel(*refs):
    total = sum(ref[...].astype(jnp.float32) for ref in refs[:-1])
    refs[-1][...] = total.astype(jnp.bfloat16)


def add(*terms):
    flat, specs = [], []
    first = terms[0]
    dims = first[0].shape[1:] if isinstance(first, tuple) else first.shape
    rows = 1
    for size in dims[:-1]:
        rows *= size
    block = min(rows, 256)
    for term in terms:
        array, entry = term if isinstance(term, tuple) else (term, 0)
        flat.append(array.reshape(-1, dims[-1]))
        start = entry * rows // block
        specs.append(pl.BlockSpec((block, dims[-1]), lambda i, start=start: (start + i, 0)))
    return pl.pallas_call(
        add_kernel,
        grid=(rows // block,),
        in_specs=specs,
        out_specs=pl.BlockSpec((block, dims[-1]), lambda i: (i, 0)),
        out_shape=shape((rows, dims[-1]), jnp.bfloat16),
        compiler_params=params(),
        cost_estimate=cost(0, 0),
        name="add",
    )(*flat).reshape(dims)


def combine_kernel(plan, *refs):
    ins, outs = list(refs[: -len(plan)]), refs[-len(plan) :]
    for out_ref, entries in zip(outs, plan):
        for e, segments in enumerate(entries):
            start = 0
            for offsets, rows in segments:
                terms, ins = ins[: len(offsets)], ins[len(offsets) :]
                total = sum(
                    ref[0, offset : offset + rows].astype(jnp.float32)
                    for ref, offset in zip(terms, offsets)
                )
                out_ref[e, start : start + rows] = total.astype(jnp.bfloat16)
                start += rows


def combine(*outputs):
    arrays, specs, plan, shapes = [], [], [], []
    for entries in outputs:
        plan.append([])
        for segments in entries:
            plan[-1].append([])
            for terms in segments:
                offsets = []
                for array, e, rows, start in terms:
                    block, place, offset = rows, start // rows, 0
                    if start % rows or array.shape[1] % rows:
                        block, place, offset = array.shape[1], 0, start
                    offsets.append(offset)
                    arrays.append(array)
                    specs.append(
                        pl.BlockSpec(
                            (1, block, array.shape[2]), lambda i, e=e, place=place: (e, place, 0)
                        )
                    )
                plan[-1][-1].append((offsets, terms[0][2]))
        rows = sum(rows for _, rows in plan[-1][0])
        shapes.append(shape((len(entries), rows, arrays[0].shape[2]), jnp.bfloat16))
    return pl.pallas_call(
        partial(combine_kernel, plan),
        grid=(1,),
        in_specs=specs,
        out_specs=[whole(out) for out in shapes],
        out_shape=shapes,
        compiler_params=params(),
        cost_estimate=cost(0, 0),
        name="combine",
    )(*arrays)


class Halving:
    def __init__(self, chips):
        self.chips = chips
        self.middle = chips[0][0][0].shape[1] // 2

    def terms(self, k, half, *more):
        middle = self.middle
        return [(array, e, middle, half * middle) for array, e in self.chips[k]] + [
            (array, e, middle, start) for array, e, start in more
        ]

    def total(self, k, half, *more):
        rows = slice(half * self.middle, (half + 1) * self.middle)
        parts = [array[e, rows] for array, e in self.chips[k]] + [*more]
        return sum(one.astype(jnp.float32) for one in parts)

    def finish(self, top, low):
        return jnp.concatenate(
            [self.total(0, 0, self.got[0][0], top), self.total(0, 1, self.got[1][0], low)], axis=0
        )


def both_cores(mine, other):
    parts = [part.reshape(CHIPS, -1, part.shape[-1]) for part in (mine, other)]
    return Halving([[(part, k) for part in parts] for k in range(CHIPS)])


def firsts(*sums):
    return combine(
        [[one.terms(k, 0) for one in sums] for k in (1, 3)],
        [[one.terms(k, 1) for one in sums] for k in (2, 3)],
    )


def seconds(*sums):
    for one, top, low, start in sums:
        rows = slice(start, start + one.middle)
        one.got = top[:, rows], low[:, rows]
    top, low = combine(
        [[one.terms(2, 0, (top, 1, start)) for one, top, _, start in sums]],
        [[one.terms(1, 1, (low, 1, start)) for one, _, low, start in sums]],
    )
    return top[0], low[0]


def send_first(top, low):
    return [exchange(top, 2), exchange(low, 4)]


def send_last(top, low):
    return [exchange(top, 4), exchange(low, 2)]


def split_rows(arrays, rows):
    return [a[..., :rows, :] for a in arrays], [a[..., rows:, :] for a in arrays]


def small_send(values):
    size = lax.axis_size("index")
    flat = jnp.pad(values.reshape(-1), (0, 1024 - values.size)).reshape(1, 8, 128)
    return swap(jnp.broadcast_to(flat, (size, 8, 128)))


def small_take(arrived, dims):
    size = 1
    for dim in dims:
        size *= dim
    return jnp.sum(arrived, axis=0).reshape(-1)[:size].reshape(dims)


def hold_kernel(*_):
    pass


def hold(values, *others):
    anywhere = pl.BlockSpec(memory_space=pl.ANY)
    return pl.pallas_call(
        hold_kernel,
        in_specs=[anywhere] * (len(values) + len(others)),
        out_specs=[anywhere] * len(values),
        out_shape=[shape(value.shape, value.dtype) for value in values],
        input_output_aliases={i: i for i in range(len(values))},
        name="hold",
    )(*values, *others)


def swap(pieces):
    return lax.all_to_all(pieces, "index", 0, 0, tiled=True)


def head_body(
    decoder_input,
    encoder_memory,
    question_vectors,
    passage_vectors,
    passage_ids,
    valid_count,
    output_grad,
    attention_weight,
    expand_weight,
    contract_weight,
    vector_params,
    attention_mean,
    attention_square,
    expand_mean,
    expand_square,
    contract_mean,
    contract_square,
    vector_mean,
    vector_square,
):
    low = jnp.bfloat16
    count, groups = lax.axis_size("index"), lax.axis_size("dp")
    place = lax.axis_index("index")
    seqs, rows_here, depth = decoder_input.shape
    memory_here = encoder_memory.shape[1]
    width = depth // count
    part = attention_weight.shape[1]
    hidden = expand_weight.shape[1]
    vector_rows, vector_width = vector_params.shape
    question_width = question_vectors.shape[1]
    rows = seqs * rows_here

    attention_low = attention_weight.astype(low)
    extras = jnp.concatenate(
        [vector_params.astype(low).reshape(-1), question_vectors.reshape(-1)]
    )
    extra_rows = -(-extras.shape[0] // (16 * width)) * 16
    extras = jnp.pad(extras, (0, extra_rows * width - extras.shape[0])).reshape(
        1, extra_rows, width
    )
    split = jnp.concatenate([attention_low[:3], attention_low[5:7]], axis=0)
    columns = split.reshape(5, part, count, width).transpose(2, 0, 1, 3)
    package = jnp.concatenate(
        [
            columns.reshape(count, 5 * part, width),
            jnp.broadcast_to(extras, (count, extra_rows, width)),
        ],
        axis=1,
    )
    order = relative_order()
    memory_block = -(-memory_here // rows_here) * rows_here
    rows_all = lax.all_gather(
        jnp.concatenate(
            [
                jnp.pad(encoder_memory, ((0, 0), (0, memory_block - memory_here), (0, 0))),
                decoder_input,
            ],
            axis=1,
        ),
        "index",
        axis=0,
        tiled=False,
    )
    input_rows = (rows_all, memory_block, rows_here)
    memory_rows = (rows_all, 0, memory_here)
    square = attention_low[3:5].transpose(1, 0, 2).reshape(part, 2 * depth)
    received = swap(package)
    square_arrived = hold(send_dp(square), received)
    (received,) = hold([received], *square_arrived)
    received_sent = send_dp(received)
    (contract,) = hold([contract_weight.astype(low)], received)
    contract = [contract] + [exchange(contract, 2 * k) for k in range(1, CHIPS)]
    slices_arrived = hold(received_sent, *contract[1:])
    square_arrived = hold(square_arrived, *slices_arrived)
    square = lax.all_gather(place_dp(square, square_arrived), "index", axis=0, tiled=False)
    slices = place_dp(received, slices_arrived)
    vectors = (
        slices[:, :, 5 * part :]
        .reshape(groups, count, extra_rows * width)[:, :, : vector_rows * vector_width]
        .reshape(groups, count, vector_rows, vector_width)
        .transpose(2, 0, 1, 3)
        .reshape(vector_rows, depth)
        .astype(jnp.float32)
    )
    question_full = (
        received[:, 5 * part :]
        .reshape(count, extra_rows * width)[:, vector_rows * vector_width :][
            :, : seqs * question_width
        ]
        .reshape(count, seqs, question_width)
        .transpose(1, 0, 2)
        .reshape(seqs, count * question_width)
    )
    expand_part = hidden // depth * part
    late = jnp.concatenate(
        [
            expand_weight.astype(low)
            .reshape(part, hidden // depth, depth)
            .transpose(1, 0, 2)
            .reshape(expand_part, depth),
            attention_low[7],
        ],
        axis=0,
    )
    (late,) = hold([late], *slices_arrived)
    late_sent = send_dp(late)

    (passage_ids,) = hold([passage_ids], *slices_arrived)
    passages_here = passage_vectors.shape[0]
    local_ids = passage_ids - place * passages_here
    owned_slot = (local_ids >= 0) & (local_ids < passages_here)
    picked = passage_vectors[jnp.clip(local_ids, 0, passages_here - 1)]
    local_scores = jnp.einsum(
        "sc,skc->sk", question_full, picked, preferred_element_type=jnp.float32
    )
    slots = passage_ids.shape[1]
    usable = jnp.arange(slots)[None, :] < valid_count[:, None]
    scores = small_take(small_send(jnp.where(owned_slot, local_scores, 0.0)), local_scores.shape)
    masked = jnp.where(usable, scores, negative_fill)
    maximum = jnp.max(masked, axis=1)
    exponent = jnp.where(usable, jnp.exp(masked - maximum[:, None]), 0.0)
    partition = jnp.sum(exponent, axis=1)
    passage_prob = exponent / partition[:, None]
    log_prior = jnp.where(
        usable, masked - maximum[:, None] - jnp.log(partition)[:, None], negative_fill
    )
    key_bias = jnp.repeat(log_prior, MEM_P, axis=1)

    vector_here = lax.dynamic_slice_in_dim(vectors[:5], place * width, width, axis=1)
    no_bias = jnp.zeros((1, width), jnp.float32)
    qkv_bias = jnp.concatenate([vector_here[0:1], no_bias, vector_here[1:2]], axis=1)
    kv_bias = jnp.concatenate([no_bias, vector_here[4:5]], axis=1)
    x_rows = decoder_input.reshape(rows, depth)
    qkv = project_columns("self_qkv", *input_rows, slices, 0, 3, qkv_bias)
    self_out, self_stat = attend(True, qkv, 0, qkv, 1, 2, key_bias[:, None, :])
    self_out, *late_arrived = hold([self_out, *late_sent])
    self_got = swap(self_out)
    late = lax.all_gather(place_dp(late, late_arrived), "index", axis=0, tiled=False)
    ahead, across = hold([jnp.stack(contract[:2]), jnp.stack(contract[2:])], *late_arrived)
    self_got, ahead_far, across_far = hold(
        [self_got, exchange_dp(ahead, 2), exchange_dp(across, 1)]
    )
    ahead = jnp.stack([ahead, ahead_far])
    across = jnp.stack([across, across_far])
    contract_sent = [exchange_dp(ahead, 1), exchange_dp(across, 2)]
    self_mixed, first_in, first_low, cross_query = first_forward(
        self_got, x_rows, square, vectors, ahead_far
    )
    (slices,) = hold([slices], first_low)
    memory_kv = project_columns("memory_kv", *memory_rows, slices, 3, 2, kv_bias)
    cross_query = swap(cross_query)[:, None]
    cross_out, cross_stat = attend(
        False, cross_query, 0, memory_kv, 0, 1, key_bias[:, None, :]
    )
    ahead_far, across_far = hold(contract_sent, cross_out)
    contract = [ahead, ahead_far, across, across_far]
    contract += [exchange(piece, 1) for piece in contract]
    places = lax.axis_index("dp") ^ jnp.array(DP_ORDER, jnp.int32)
    (
        cross_mixed,
        layer_output,
        wide_grad,
        *contract_grads,
        inner_total,
        second_grad,
        cross_low,
        cross_mix_grad,
        stats,
    ) = ffn(
        (order, places),
        swap(cross_out),
        first_in,
        late,
        contract,
        vectors,
        vectors[6:10].reshape(groups * count, -1),
        output_grad.reshape(rows, depth),
    )
    third_stat, second_stat = stats[:8], stats[8:]

    expand_part_sum = lax.psum_scatter(wide_grad, "index", scatter_dimension=0, tiled=False)
    ahead, ahead_far, across, across_far = contract_grads[:4]
    cores = [exchange(piece, 1) for piece in contract_grads[4:]]
    cross_mix_got, *contract_sent = hold(
        [swap(cross_mix_grad), add(ahead_far, cores[1]), add(across_far, cores[3])]
    )
    contract_got = [exchange_dp(contract_sent[0], 1), exchange_dp(contract_sent[1], 2)]
    cross_dq, cross_dkv, prior_rows = attend_back(
        False,
        cross_query,
        0,
        memory_kv,
        0,
        1,
        cross_mix_got,
        cross_stat,
        key_bias[:, None, :],
        contract_sent[0],
    )
    memory_mine, memory_other, kv_grads, kv_total = project_columns_back(
        "memory_kv_back", order, *memory_rows, [cross_dkv], slices, 3, 2
    )
    cross_dq, *contract_got = hold([cross_dq, *contract_got], memory_mine)
    contract_next = [
        add((ahead, 1), (cores[0], 1), (contract_got[0], 1)),
        add((across, 1), (cores[2], 1), (contract_got[1], 1)),
    ]
    cross_dq_got, *contract_next = hold([swap(cross_dq), *contract_next])
    contract_last = [exchange_dp(contract_next[0], 2), exchange_dp(contract_next[1], 1)]
    query_low, first_grad, self_low, self_mix_grad, first_stat = first_back(
        cross_dq_got, second_grad, first_in, square, vectors, memory_mine
    )
    memory_sum = both_cores(memory_mine, exchange(memory_other, 1))
    memory_sent = firsts(memory_sum)
    square_mine, square_other = weight_grads(
        (count, groups, part, depth),
        order,
        self_mixed,
        self_low,
        first_low,
        query_low,
        cross_mixed,
        cross_low,
    )
    square_sum = both_cores(square_mine, exchange(square_other, 1))
    square_sent = firsts(square_sum)
    self_mix_got, *contract_last = hold(
        [swap(self_mix_grad), *contract_last], *memory_sent, *square_sent
    )
    memory_got = send_first(*memory_sent)
    square_got = send_first(*square_sent)
    self_dq, self_dkv, _ = attend_back(
        True, qkv, 0, qkv, 1, 2, self_mix_got, self_stat, self_stat, square_mine
    )
    expand_sum = HalvingDp(expand_part_sum)
    self_dq, expand_sent = hold([self_dq, expand_sum.first()])
    dx_mine, dx_other, qkv_slice_grads, qkv_total = project_columns_back(
        "self_qkv_back", order, *input_rows, [self_dq, self_dkv], slices, 0, 3
    )
    dx_mine, dx_other, *got = hold([dx_mine, dx_other, *memory_got, *square_got])
    own = jnp.concatenate(
        [qkv_total[:, :width], qkv_total[:, 2 * width :], kv_total[:, width:]], axis=0
    )
    own = lax.dynamic_update_slice(
        jnp.zeros((3, depth), jnp.float32), own, (jnp.int32(0), place * width)
    )
    vector_grads = jnp.concatenate(
        [
            own[:2],
            first_stat[1:2],
            first_stat[0:1],
            own[2:],
            second_stat[0:1],
            inner_total.reshape(hidden // depth, depth),
            third_stat[0:1],
            first_stat[2:4],
            second_stat[1:3],
            third_stat[1:3],
        ],
        axis=0,
    )
    vector_size = vector_rows * vector_width
    question_size = seqs * question_width
    vector_send = (
        vector_grads.reshape(vector_rows, groups, count, vector_width)
        .transpose(1, 2, 0, 3)
        .reshape(groups, count, vector_size)
    )
    vector_send = jnp.pad(
        vector_send, ((0, 0), (0, 0), (0, extra_rows * width - vector_size))
    ).reshape(groups, count, extra_rows, width)
    slice_sum = HalvingDp(
        jnp.concatenate([qkv_slice_grads, kv_grads, vector_send.astype(low)], axis=2)
    )
    slice_sent = slice_sum.first()
    slice_got = exchange_dp(slice_sent, 1)
    dx_other, *got = hold([dx_other, *got], slice_sent)
    dx_got = exchange(dx_other, 1)
    square_rows = square_sum.middle
    last = seconds((square_sum, *got[2:], 0), (memory_sum, *got[:2], 0))
    prior_rows, expand_sent, *contract_last = hold(
        [prior_rows, expand_sent, *contract_last], *last
    )
    last = send_last(*last)
    expand_got = exchange_dp(expand_sent, 1)
    prior_arrived = small_send(prior_rows.reshape(seqs, slots, MEM_P).sum(axis=-1))
    dx_got, prior_arrived, slice_got, *last = hold([dx_got, prior_arrived, slice_got, *last])
    slice_next = slice_sum.second(slice_got)
    dx_got, *last = hold([dx_got, *last], slice_next)
    slice_last = exchange_dp(slice_next, 2)
    dx_sum = both_cores(dx_mine, dx_got)
    contract_sum = Halving(
        [
            [(one.reshape((-1,) + one.shape[-2:]), k % 2) for one in parts]
            for k, parts in enumerate(
                [(ahead, cores[0], contract_got[0], contract_last[0])] * 2
                + [(across, cores[2], contract_got[1], contract_last[1])] * 2
            )
        ]
    )
    dx_sent = firsts(dx_sum, contract_sum)
    got = send_first(*dx_sent)
    last = hold(last, *dx_sent)
    square_last, memory_last = split_rows(last, square_rows)
    square_far = HalvingDp(square_sum.finish(*square_last).reshape(groups, 3 * part, depth))
    square_got = exchange_dp(square_far.first(), 1)
    slice_sum = slice_sum.finish(slice_last)
    prior_grad = jnp.where(usable, small_take(prior_arrived, (seqs, slots)), 0.0)
    score_doc = jnp.where(
        usable, prior_grad - passage_prob * jnp.sum(prior_grad, axis=1, keepdims=True), 0.0
    )
    question_part = jnp.einsum(
        "sk,skc->sc",
        jnp.where(owned_slot, score_doc, 0.0),
        picked.astype(jnp.float32),
        precision=lax.Precision.HIGHEST,
    )

    question_send = (
        question_part.reshape(seqs, count, question_width)
        .transpose(1, 0, 2)
        .reshape(count, question_size)
    )
    question_send = jnp.pad(
        question_send,
        ((0, 0), (vector_size, extra_rows * width - vector_size - question_size)),
    ).reshape(count, extra_rows, width)
    slice_sum = jnp.concatenate(
        [slice_sum[:, : 5 * part], slice_sum[:, 5 * part :] + question_send], axis=1
    )
    slice_send = slice_sum.astype(low)
    arrived = swap(slice_send)
    got = hold(got, slice_send)
    start = dx_sum.middle
    last = seconds((dx_sum, *got, 0), (contract_sum, *got, start))
    square_got, expand_got = hold([square_got, expand_got], *last)
    last = send_last(*last)
    square_last = exchange_dp(square_far.second(square_got), 2)
    expand_last = exchange_dp(expand_sum.second(expand_got), 2)
    dx_last, contract_last = split_rows(last, start)
    input_gradient = first_grad + dx_sum.finish(*dx_last)
    contract_sum = contract_sum.finish(*contract_last)
    memory_last = hold(memory_last, *got)
    memory_gradient = memory_sum.finish(*memory_last).reshape(encoder_memory.shape)
    new_contract = adam_update(
        contract_weight, contract_mean, contract_square, contract_sum, rate_contract, decay_matrix
    )
    (square_last,) = hold([square_last], input_gradient, memory_gradient, *new_contract)
    arrived = arrived.astype(jnp.float32)
    split_grads = (
        arrived[:, : 5 * part]
        .reshape(count, 5, part, width)
        .transpose(1, 2, 0, 3)
        .reshape(5, part, depth)
    )
    extra_sum = jnp.sum(arrived[:, 5 * part :].reshape(count, extra_rows * width), axis=0)
    vector_sum = extra_sum[:vector_size].reshape(vector_rows, vector_width)
    question_gradient = extra_sum[vector_size : vector_size + question_size].reshape(
        seqs, question_width
    )

    expand_sum = (
        expand_sum.finish(expand_last)
        .reshape(hidden // depth, part, depth)
        .transpose(1, 0, 2)
        .reshape(part, hidden)
    )
    square_total = square_far.finish(square_last).reshape(3, part, depth)
    attention_sum = jnp.concatenate(
        [split_grads[:3], square_total[:2], split_grads[3:], square_total[2:]], axis=0
    )

    new_attention = adam_update(
        attention_weight,
        attention_mean,
        attention_square,
        attention_sum,
        rate_attention,
        decay_matrix,
    )
    new_expand = adam_update(
        expand_weight, expand_mean, expand_square, expand_sum, rate_expand, decay_matrix
    )
    new_vector = adam_update(
        vector_params, vector_mean, vector_square, vector_sum, rate_vector, 0.0
    )
    return (
        layer_output.reshape(decoder_input.shape),
        input_gradient.reshape(decoder_input.shape),
        memory_gradient,
        question_gradient,
        *new_attention,
        *new_expand,
        *new_contract,
        *new_vector,
    )


def body(sizes, *arrays):
    depth = arrays[0].shape[2]
    if sizes == (4, 8) and depth // 8 % 128 == 0:
        return head_body(*arrays)
    return general_body(*arrays)


def solution(mesh):
    return jax.shard_map(
        partial(body, (mesh.shape["dp"], mesh.shape["index"])),
        mesh=mesh,
        in_specs=(
            P("dp", "index", None),
            P("dp", "index", None),
            P("dp", "index"),
            P("index", None),
            P("dp", None),
            P("dp"),
            P("dp", "index", None),
            P(None, ("dp", "index"), None),
            P(("dp", "index"), None),
            P(("dp", "index"), None),
            P(None, ("dp", "index")),
            P(None, ("dp", "index"), None),
            P(None, ("dp", "index"), None),
            P(("dp", "index"), None),
            P(("dp", "index"), None),
            P(("dp", "index"), None),
            P(("dp", "index"), None),
            P(None, ("dp", "index")),
            P(None, ("dp", "index")),
        ),
        out_specs=(
            P("dp", "index", None),
            P("dp", "index", None),
            P("dp", "index", None),
            P("dp", "index"),
            P(None, ("dp", "index"), None),
            P(None, ("dp", "index"), None),
            P(None, ("dp", "index"), None),
            P(("dp", "index"), None),
            P(("dp", "index"), None),
            P(("dp", "index"), None),
            P(("dp", "index"), None),
            P(("dp", "index"), None),
            P(("dp", "index"), None),
            P(None, ("dp", "index")),
            P(None, ("dp", "index")),
            P(None, ("dp", "index")),
        ),
        check_vma=False,
    )
```

```python
from functools import partial

import jax
import jax.numpy as jnp
from jax import lax
from jax.experimental import pallas as pl
from jax.experimental.pallas import tpu as pltpu
from jax.sharding import PartitionSpec as P

HEADS = 16
MEM_P = 192
STEP = 10


negative_fill = -1e30
norm_eps = 1e-05
beta_first = 0.9
beta_second = 0.999
adam_eps = 1e-08
decay_matrix = 0.01
rate_attention = 0.1
rate_expand = 0.02
rate_contract = 0.01
rate_vector = 0.2


def layer_norm(hidden, norm_gain, norm_shift):
    center = hidden - jnp.mean(hidden, axis=-1, keepdims=True)
    spread = jnp.mean(center * center, axis=-1, keepdims=True)
    return center * lax.rsqrt(spread + norm_eps) * norm_gain + norm_shift


def split_heads(matrix):
    return matrix.reshape(matrix.shape[0], matrix.shape[1], HEADS, matrix.shape[2] // HEADS)


def merge_heads(matrix):
    return matrix.reshape(matrix.shape[0], matrix.shape[1], matrix.shape[2] * matrix.shape[3])


def project(left_side, weight):
    return jnp.einsum("srd,de->sre", left_side, weight, preferred_element_type=jnp.float32)


def project_back(gradient, weight):
    return jnp.einsum("sre,de->srd", gradient, weight, preferred_element_type=jnp.float32)


def weight_grad(left_side, gradient):
    return jnp.einsum("srd,sre->de", left_side, gradient, preferred_element_type=jnp.float32)


def row_total(values):
    return jnp.sum(values, axis=(0, 1))


def attend_forward(queries, key_rows, values, score_bias, allowed):
    scores = (
        jnp.einsum(
            "sqhd,skhd->shqk",
            split_heads(queries),
            split_heads(key_rows),
            preferred_element_type=jnp.float32,
        )
        * 0.125
        + score_bias
    )
    scores = jnp.where(allowed, scores, negative_fill)
    maximum = jnp.max(scores, axis=-1)
    exponent = jnp.exp(scores - maximum[..., None])
    partition = jnp.sum(exponent, axis=-1)
    attend_prob = exponent / partition[..., None]
    mixture = jnp.einsum(
        "shqk,skhd->sqhd",
        attend_prob.astype(jnp.bfloat16),
        split_heads(values),
        preferred_element_type=jnp.float32,
    )
    return (merge_heads(mixture).astype(jnp.bfloat16), attend_prob, maximum, partition)


def score_grads(grad_mixed, attend_prob, values):
    grad_prob = jnp.einsum(
        "sqhd,skhd->shqk",
        split_heads(grad_mixed),
        split_heads(values),
        preferred_element_type=jnp.float32,
    )
    row_inner = jnp.sum(attend_prob * grad_prob, axis=-1)
    return ((attend_prob * (grad_prob - row_inner[..., None])).astype(jnp.bfloat16), row_inner)


def to_queries(grad_score, key_rows):
    return (
        merge_heads(
            jnp.einsum(
                "shqk,skhd->sqhd",
                grad_score,
                split_heads(key_rows),
                preferred_element_type=jnp.float32,
            )
        )
        * 0.125
    )


def to_keys(grad_score, attend_prob, queries, grad_mixed):
    grad_key = (
        merge_heads(
            jnp.einsum(
                "shqk,sqhd->skhd",
                grad_score,
                split_heads(queries),
                preferred_element_type=jnp.float32,
            )
        )
        * 0.125
    )
    grad_value = merge_heads(
        jnp.einsum(
            "shqk,sqhd->skhd",
            attend_prob.astype(jnp.bfloat16),
            split_heads(grad_mixed),
            preferred_element_type=jnp.float32,
        )
    )
    return (grad_key, grad_value)


def adam_update(weight, moment_one, moment_two, gradient, step_rate, weight_decay):
    mean_new = beta_first * moment_one + (1.0 - beta_first) * gradient
    square_new = beta_second * moment_two + (1.0 - beta_second) * gradient * gradient
    mean_hat = mean_new / (1.0 - beta_first**STEP)
    square_hat = square_new / (1.0 - beta_second**STEP)
    updated = weight - step_rate * (
        mean_hat / (jnp.sqrt(square_hat) + adam_eps) + weight_decay * weight
    )
    return (updated, mean_new, square_new)


def general_body(
    decoder_input,
    encoder_memory,
    question_vectors,
    passage_vectors,
    passage_ids,
    valid_count,
    output_grad,
    attention_weight,
    expand_weight,
    contract_weight,
    vector_params,
    attention_mean,
    attention_square,
    expand_mean,
    expand_square,
    contract_mean,
    contract_square,
    vector_mean,
    vector_square,
):
    attention_low, expand_low, contract_low, vector_low = (
        lax.all_gather(attention_weight.astype(jnp.bfloat16), ("dp", "index"), axis=1, tiled=True),
        lax.all_gather(expand_weight.astype(jnp.bfloat16), ("dp", "index"), axis=0, tiled=True),
        lax.all_gather(contract_weight.astype(jnp.bfloat16), ("dp", "index"), axis=0, tiled=True),
        lax.all_gather(vector_params.astype(jnp.bfloat16), ("dp", "index"), axis=1, tiled=True),
    )
    vectors = vector_low.astype(jnp.float32)
    seqs_here, rows_here, model_width = decoder_input.shape
    shard_index = lax.axis_index("index")
    length = rows_here * lax.axis_size("index")
    ffn_width = expand_low.shape[1]
    self_query = (project(decoder_input, attention_low[0]) + vectors[0]).astype(jnp.bfloat16)
    self_key = project(decoder_input, attention_low[1]).astype(jnp.bfloat16)
    self_value = (project(decoder_input, attention_low[2]) + vectors[1]).astype(jnp.bfloat16)
    key_all, value_all = (
        lax.all_gather(self_key, "index", axis=1, tiled=True),
        lax.all_gather(self_value, "index", axis=1, tiled=True),
    )
    query_place = shard_index * rows_here + jnp.arange(rows_here)
    causal = (jnp.arange(length)[None, :] <= query_place[:, None])[None, None]
    self_mixed, self_prob, self_peak, self_total = attend_forward(
        self_query, key_all, value_all, 0.0, causal
    )
    first_in = (
        decoder_input.astype(jnp.float32) + project(self_mixed, attention_low[3]) + vectors[2]
    )
    first_out, first_back = jax.vjp(layer_norm, first_in, vectors[11], vectors[12])
    first_low = first_out.astype(jnp.bfloat16)
    cross_query = (project(first_low, attention_low[4]) + vectors[3]).astype(jnp.bfloat16)
    cross_key = project(encoder_memory, attention_low[5]).astype(jnp.bfloat16)
    cross_value = (project(encoder_memory, attention_low[6]) + vectors[4]).astype(jnp.bfloat16)
    memory_keys, memory_values = (
        lax.all_gather(cross_key, "index", axis=1, tiled=True),
        lax.all_gather(cross_value, "index", axis=1, tiled=True),
    )
    question_full = lax.all_gather(question_vectors, "index", axis=1, tiled=True)
    passages_here = passage_vectors.shape[0]
    local_ids = passage_ids - shard_index * passages_here
    owned_slot = (local_ids >= 0) & (local_ids < passages_here)
    picked = passage_vectors[jnp.clip(local_ids, 0, passages_here - 1)]
    local_scores = jnp.einsum(
        "sc,skc->sk", question_full, picked, preferred_element_type=jnp.float32
    )
    slots = passage_ids.shape[1]
    usable = jnp.arange(slots)[None, :] < valid_count[:, None]
    local_peak = jnp.max(jnp.where(owned_slot & usable, local_scores, negative_fill), axis=1)
    maximum = lax.pmax(local_peak, "index")
    local_exp = jnp.where(owned_slot & usable, jnp.exp(local_scores - maximum[:, None]), 0.0)
    exponent, scores = lax.psum((local_exp, jnp.where(owned_slot, local_scores, 0.0)), "index")
    masked = jnp.where(usable, scores, negative_fill)
    partition = jnp.sum(exponent, axis=1)
    passage_prob = exponent / partition[:, None]
    log_prior = masked - maximum[:, None] - jnp.log(partition)[:, None]
    memory_total = memory_keys.shape[1]
    bias_rows = jnp.repeat(log_prior, MEM_P, axis=1)
    key_bias = bias_rows[:, None, None, :]
    key_usable = ((jnp.arange(memory_total) // MEM_P)[None, :] < valid_count[:, None])[
        :, None, None, :
    ]
    cross_mixed, cross_prob, cross_peak, cross_total = attend_forward(
        cross_query, memory_keys, memory_values, key_bias, key_usable
    )
    second_in = first_out + project(cross_mixed, attention_low[7]) + vectors[5]
    second_out, second_back = jax.vjp(layer_norm, second_in, vectors[13], vectors[14])
    second_low = second_out.astype(jnp.bfloat16)
    inner_act = project(second_low, expand_low) + vectors[6:10].reshape(ffn_width)
    activated, gelu_back = jax.vjp(partial(jax.nn.gelu, approximate=False), inner_act)
    activ_low = activated.astype(jnp.bfloat16)
    third_in = second_out + project(activ_low, contract_low) + vectors[10]
    layer_output, third_back = jax.vjp(layer_norm, third_in, vectors[15], vectors[16])
    grad_third, gain_three, shift_three = third_back(output_grad.astype(jnp.float32))
    grad_ffn_low = grad_third.astype(jnp.bfloat16)
    grad_contract = weight_grad(activ_low, grad_ffn_low)
    (grad_inner,) = gelu_back(project_back(grad_ffn_low, contract_low))
    grad_inner_low = grad_inner.astype(jnp.bfloat16)
    grad_expand = weight_grad(second_low, grad_inner_low)
    grad_second = grad_third + project_back(grad_inner_low, expand_low)
    grad_second_in, gain_two, shift_two = second_back(grad_second)
    grad_cross_low = grad_second_in.astype(jnp.bfloat16)
    grad_cmix = project_back(grad_cross_low, attention_low[7]).astype(jnp.bfloat16)
    cross_score, cross_inner = score_grads(grad_cmix, cross_prob, memory_values)
    grad_cq = to_queries(cross_score, memory_keys)
    prior_part = (
        jnp.sum(cross_score, axis=(1, 2), dtype=jnp.float32)
        .reshape(seqs_here, slots, MEM_P)
        .sum(axis=-1)
    )
    prior_grad = jnp.where(usable, lax.psum(prior_part, "index"), 0.0)
    score_doc = jnp.where(
        usable, prior_grad - passage_prob * jnp.sum(prior_grad, axis=1, keepdims=True), 0.0
    )
    question_part = jnp.einsum(
        "sk,skc->sc",
        jnp.where(owned_slot, score_doc, 0.0),
        picked.astype(jnp.float32),
        precision=lax.Precision.HIGHEST,
    )
    question_gradient = lax.psum_scatter(question_part, "index", scatter_dimension=1, tiled=True)
    grad_cq_low = grad_cq.astype(jnp.bfloat16)
    grad_first = grad_second_in + project_back(grad_cq_low, attention_low[4])
    ck_part, cv_part = to_keys(cross_score, cross_prob, cross_query, grad_cmix)
    grad_ck, grad_cv = (
        lax.psum_scatter(
            ck_part.astype(jnp.bfloat16), "index", scatter_dimension=1, tiled=True
        ).astype(jnp.float32),
        lax.psum_scatter(
            cv_part.astype(jnp.bfloat16), "index", scatter_dimension=1, tiled=True
        ).astype(jnp.float32),
    )
    grad_ck_low = grad_ck.astype(jnp.bfloat16)
    grad_cv_low = grad_cv.astype(jnp.bfloat16)
    memory_gradient = project_back(grad_ck_low, attention_low[5]) + project_back(
        grad_cv_low, attention_low[6]
    )
    grad_first_in, gain_one, shift_one = first_back(grad_first)
    grad_self_low = grad_first_in.astype(jnp.bfloat16)
    grad_smix = project_back(grad_self_low, attention_low[3]).astype(jnp.bfloat16)
    self_score, row_inner = score_grads(grad_smix, self_prob, value_all)
    grad_sq = to_queries(self_score, key_all)
    key_part, value_part = to_keys(self_score, self_prob, self_query, grad_smix)
    grad_sk, grad_sv = (
        lax.psum_scatter(
            key_part.astype(jnp.bfloat16), "index", scatter_dimension=1, tiled=True
        ).astype(jnp.float32),
        lax.psum_scatter(
            value_part.astype(jnp.bfloat16), "index", scatter_dimension=1, tiled=True
        ).astype(jnp.float32),
    )
    grad_sq_low = grad_sq.astype(jnp.bfloat16)
    grad_sk_low = grad_sk.astype(jnp.bfloat16)
    grad_sv_low = grad_sv.astype(jnp.bfloat16)
    input_gradient = (
        grad_first_in
        + project_back(grad_sq_low, attention_low[0])
        + project_back(grad_sk_low, attention_low[1])
        + project_back(grad_sv_low, attention_low[2])
    )
    attention_grads = jnp.stack(
        [
            weight_grad(decoder_input, grad_sq_low),
            weight_grad(decoder_input, grad_sk_low),
            weight_grad(decoder_input, grad_sv_low),
            weight_grad(self_mixed, grad_self_low),
            weight_grad(first_low, grad_cq_low),
            weight_grad(encoder_memory, grad_ck_low),
            weight_grad(encoder_memory, grad_cv_low),
            weight_grad(cross_mixed, grad_cross_low),
        ]
    )
    vector_grads = jnp.concatenate(
        [
            jnp.stack(
                [
                    row_total(grad_sq),
                    row_total(grad_sv),
                    row_total(grad_first_in),
                    row_total(grad_cq),
                    row_total(grad_cv),
                    row_total(grad_second_in),
                ]
            ),
            row_total(grad_inner).reshape(ffn_width // model_width, model_width),
            jnp.stack(
                [
                    row_total(grad_third),
                    gain_one,
                    shift_one,
                    gain_two,
                    shift_two,
                    gain_three,
                    shift_three,
                ]
            ),
        ]
    )
    attention_sum, expand_sum, contract_sum, vector_sum = (
        lax.psum_scatter(attention_grads, ("dp", "index"), scatter_dimension=1, tiled=True),
        lax.psum_scatter(grad_expand, ("dp", "index"), scatter_dimension=0, tiled=True),
        lax.psum_scatter(grad_contract, ("dp", "index"), scatter_dimension=0, tiled=True),
        lax.psum_scatter(vector_grads, ("dp", "index"), scatter_dimension=1, tiled=True),
    )
    new_attention = adam_update(
        attention_weight,
        attention_mean,
        attention_square,
        attention_sum,
        rate_attention,
        decay_matrix,
    )
    new_expand = adam_update(
        expand_weight, expand_mean, expand_square, expand_sum, rate_expand, decay_matrix
    )
    new_contract = adam_update(
        contract_weight, contract_mean, contract_square, contract_sum, rate_contract, decay_matrix
    )
    new_vector = adam_update(
        vector_params, vector_mean, vector_square, vector_sum, rate_vector, 0.0
    )
    return (
        layer_output.astype(jnp.bfloat16),
        input_gradient,
        memory_gradient,
        question_gradient,
        new_attention[0],
        new_attention[1],
        new_attention[2],
        new_expand[0],
        new_expand[1],
        new_expand[2],
        new_contract[0],
        new_contract[1],
        new_contract[2],
        new_vector[0],
        new_vector[1],
        new_vector[2],
    )


NT = (((1,), (1,)), ((), ()))
NN = (((1,), (0,)), ((), ()))
TN = (((0,), (0,)), ((), ()))
CHIPS = 4
DP_ORDER = (0, 2, 1, 3)
VMEM_LIMIT = 56 << 20


def dot(left_side, right_side, dims):
    return lax.dot_general(left_side, right_side, dims, preferred_element_type=jnp.float32)


def norm_parts(hidden):
    center = hidden - jnp.mean(hidden, axis=-1, keepdims=True)
    inverse = lax.rsqrt(jnp.mean(center * center, axis=-1, keepdims=True) + norm_eps)
    return center * inverse, inverse


def norm_back(gradient, unit, inverse, gain):
    scaled = gradient * gain
    return inverse * (
        scaled
        - jnp.mean(scaled, axis=-1, keepdims=True)
        - unit * jnp.mean(scaled * unit, axis=-1, keepdims=True)
    )


def column_sum(values):
    return jnp.sum(values, axis=0, keepdims=True)


def join(parts, place=None):
    picked = [parts[j] if place is None else parts[j, place] for j in range(parts.shape[0])]
    return jnp.concatenate(
        [block.reshape(block.shape[0] * block.shape[1], block.shape[2]) for block in picked],
        axis=1,
    )


def spread(out_ref, value):
    count, seqs, rows, width = out_ref.shape
    for j in range(count):
        out_ref[j] = value[:, j * width : (j + 1) * width].reshape(seqs, rows, width)


def times(activation, weight):
    count, groups, rows, width = weight.shape
    depth = count * rows
    total = None
    for d in range(groups):
        part = dot(
            activation[:, d * depth : (d + 1) * depth], weight[:, d].reshape(depth, width), NN
        )
        total = part if total is None else total + part
    return total


def times_back(gradient, weight):
    count, groups, rows, width = weight.shape
    depth = count * rows
    return jnp.concatenate(
        [dot(gradient, weight[:, d].reshape(depth, width), NT) for d in range(groups)], axis=1
    )


def outer(out_ref, left_side, gradient):
    count, groups, rows, width = out_ref.shape
    depth = count * rows
    for d in range(groups):
        out_ref[:, d] = (
            dot(left_side[:, d * depth : (d + 1) * depth], gradient, TN)
            .astype(jnp.bfloat16)
            .reshape(count, rows, width)
        )


def whole(array):
    return pl.BlockSpec(array.shape, lambda *_, rank=len(array.shape): (0,) * rank)


def shape(dims, dtype):
    return jax.ShapeDtypeStruct(tuple(dims), dtype)


def params():
    return pltpu.CompilerParams(vmem_limit_bytes=VMEM_LIMIT)


def cost(flops, moved):
    return pl.CostEstimate(flops=int(flops) // 16, bytes_accessed=int(moved) // 16, transcendentals=0)


def in_head(dims, head_width, head):
    return lax.broadcasted_iota(jnp.int32, dims, 1) // head_width == head


def attend_forward_kernel(causal, head_width, q_ref, k_ref, v_ref, bias_ref, out_ref, stat_ref):
    count, _, tile, width = q_ref.shape
    keys = k_ref.shape[0] * k_ref.shape[2]
    key_rows, values = k_ref[...].reshape(keys, width), v_ref[...].reshape(keys, width)
    step = 4
    rows = step * tile
    for b in range(count // step):
        queries = q_ref[b * step : (b + 1) * step].reshape(rows, width)
        seen = (b + 1) * rows if causal else keys
        mixed = None
        for h in range(width // head_width):
            mask = in_head((rows, width), head_width, h)
            scores = dot(
                jnp.where(mask, queries * 0.125, 0).astype(jnp.bfloat16), key_rows[:seen], NT
            )
            if causal:
                corner = scores[:, seen - rows :]
                corner = jnp.where(
                    lax.broadcasted_iota(jnp.int32, corner.shape, 1)
                    <= lax.broadcasted_iota(jnp.int32, corner.shape, 0),
                    corner,
                    negative_fill,
                )
                if b == 0:
                    scores = corner
                else:
                    scores = jnp.concatenate([scores[:, : seen - rows], corner], axis=1)
            else:
                scores = scores + bias_ref[0]
            peak = jnp.max(scores, axis=1, keepdims=True)
            exponent = jnp.exp(scores - peak)
            total = jnp.sum(exponent, axis=1, keepdims=True)
            part = dot(exponent.astype(jnp.bfloat16), values[:seen], NN) * (1.0 / total)
            mixed = part if mixed is None else jnp.where(mask, part, mixed)
            log_total = jnp.broadcast_to(peak + jnp.log(total), (rows, 128))
            stat_ref[0, h : h + 1, b * rows : (b + 1) * rows] = log_total.T[0:1]
        out_ref[b * step : (b + 1) * step] = mixed.astype(jnp.bfloat16).reshape(
            step, 1, tile, width
        )


def attend_backward_kernel(
    causal,
    head_width,
    q_ref,
    k_ref,
    v_ref,
    grad_ref,
    stat_ref,
    bias_ref,
    _,
    dq_ref,
    dkv_ref,
    prior_ref,
    dk_sum,
    dv_sum,
    prior_sum,
):
    count, _, tile, width = q_ref.shape
    keys = k_ref.shape[0] * k_ref.shape[2]
    key_rows, values = k_ref[...].reshape(keys, width), v_ref[...].reshape(keys, width)
    step = 2
    rows = step * tile
    if not causal:
        bias = jnp.broadcast_to(bias_ref[0], (128, keys)).T[:, :1]
    dk_sum[...] = jnp.zeros_like(dk_sum)
    dv_sum[...] = jnp.zeros_like(dv_sum)
    if not causal:
        prior_sum[...] = jnp.zeros_like(prior_sum)
    for b in range(count // step):
        queries = q_ref[b * step : (b + 1) * step].reshape(rows, width)
        gradient = grad_ref[b * step : (b + 1) * step].reshape(rows, width)
        seen = (b + 1) * rows if causal else keys
        query_grad = None
        for h in range(width // head_width):
            mask = in_head((rows, width), head_width, h)
            one_query = jnp.where(mask, queries * 0.125, 0).astype(jnp.bfloat16)
            one_grad = jnp.where(mask, gradient, 0).astype(jnp.bfloat16)
            scores = dot(key_rows[:seen], one_query, NT)
            if causal:
                corner = scores[seen - rows :]
                corner = jnp.where(
                    lax.broadcasted_iota(jnp.int32, corner.shape, 0)
                    <= lax.broadcasted_iota(jnp.int32, corner.shape, 1),
                    corner,
                    negative_fill,
                )
                if b == 0:
                    scores = corner
                else:
                    scores = jnp.concatenate([scores[: seen - rows], corner], axis=0)
            else:
                scores = scores + bias
            prob = jnp.exp(scores - stat_ref[0, h : h + 1, b * rows : (b + 1) * rows])
            grad_prob = dot(values[:seen], one_grad, NT)
            inner = jnp.sum(prob * grad_prob, axis=0, keepdims=True)
            grad_score = prob * (grad_prob - inner)
            score_low = grad_score.astype(jnp.bfloat16)
            dv_sum[:seen] += dot(prob.astype(jnp.bfloat16), one_grad, NN)
            dk_sum[:seen] += dot(score_low, one_query, NN)
            if not causal:
                partial_sum = grad_score[:, :128]
                for piece in range(128, rows, 128):
                    partial_sum = partial_sum + grad_score[:, piece : piece + 128]
                prior_sum[...] += partial_sum
            part = dot(score_low, key_rows[:seen], TN)
            query_grad = part if query_grad is None else jnp.where(mask, part, query_grad)
        dq_ref[b * step : (b + 1) * step] = (
            (query_grad * 0.125).astype(jnp.bfloat16).reshape(step, 1, tile, width)
        )
    dkv_ref[:, 0] = dk_sum[...].astype(jnp.bfloat16).reshape(k_ref.shape)
    dkv_ref[:, 1] = dv_sum[...].astype(jnp.bfloat16).reshape(k_ref.shape)
    if causal:
        prior_ref[...] = jnp.zeros_like(prior_ref)
    else:
        prior_ref[0] = column_sum(prior_sum[...].T)


def pick(array, place):
    count, _, _, rows, width = array.shape
    return pl.BlockSpec((count, None, 1, rows, width), lambda s: (0, place, s, 0, 0))


def attend(causal, queries, query_at, keys, key_at, value_at, bias):
    count, _, seqs, tile, width = queries.shape
    key_rows = keys.shape[0] * keys.shape[3]
    head_width = width * count // HEADS
    length = count * tile
    heads = width // head_width
    return pl.pallas_call(
        partial(attend_forward_kernel, causal, head_width),
        grid=(seqs,),
        in_specs=[
            pick(queries, query_at),
            pick(keys, key_at),
            pick(keys, value_at),
            pl.BlockSpec(memory_space=pl.ANY)
            if causal
            else pl.BlockSpec((1, 1, key_rows), lambda s: (s, 0, 0)),
        ],
        out_specs=[
            pl.BlockSpec((count, 1, tile, width), lambda s: (0, s, 0, 0)),
            pl.BlockSpec((1, heads, length), lambda s: (s, 0, 0)),
        ],
        out_shape=[
            shape((count, seqs, tile, width), jnp.bfloat16),
            shape((seqs, heads, length), jnp.float32),
        ],
        compiler_params=params(),
        cost_estimate=cost(
            16 * seqs * length * key_rows * width, 4 * seqs * (length + key_rows) * width
        ),
        name="attend_self" if causal else "attend_memory",
    )(queries, keys, keys, bias)


def attend_back(
    causal, queries, query_at, keys, key_at, value_at, gradient, stat, bias, after
):
    count, _, seqs, tile, width = queries.shape
    key_tile = keys.shape[3]
    key_rows = count * key_tile
    head_width = width * count // HEADS
    length = count * tile
    heads = width // head_width
    return pl.pallas_call(
        partial(attend_backward_kernel, causal, head_width),
        grid=(seqs,),
        in_specs=[
            pick(queries, query_at),
            pick(keys, key_at),
            pick(keys, value_at),
            pl.BlockSpec((count, 1, tile, width), lambda s: (0, s, 0, 0)),
            pl.BlockSpec((1, heads, length), lambda s: (s, 0, 0)),
            pl.BlockSpec(memory_space=pl.ANY)
            if causal
            else pl.BlockSpec((1, 1, key_rows), lambda s: (s, 0, 0)),
            pl.BlockSpec(memory_space=pl.ANY),
        ],
        out_specs=[
            pl.BlockSpec((count, 1, tile, width), lambda s: (0, s, 0, 0)),
            pl.BlockSpec((count, 2, 1, key_tile, width), lambda s: (0, 0, s, 0, 0)),
            pl.BlockSpec((1, 1, key_rows), lambda s: (s, 0, 0)),
        ],
        out_shape=[
            shape((count, seqs, tile, width), jnp.bfloat16),
            shape((count, 2, seqs, key_tile, width), jnp.bfloat16),
            shape((seqs, 1, key_rows), jnp.float32),
        ],
        scratch_shapes=[
            pltpu.VMEM((key_rows, width), jnp.float32),
            pltpu.VMEM((key_rows, width), jnp.float32),
            pltpu.VMEM((key_rows, 128), jnp.float32),
        ],
        compiler_params=params(),
        cost_estimate=cost(
            40 * seqs * length * key_rows * width, 8 * seqs * (length + key_rows) * width
        ),
        name="attend_self_back" if causal else "attend_memory_back",
    )(queries, keys, keys, gradient, stat, bias, after)


def take_columns(scratch, slices, first):
    width = slices.shape[3]
    depth = scratch.shape[0]
    rows = depth // (slices.shape[0] * slices.shape[1])
    for m in range(scratch.shape[1] // width):
        start = (first + m) * rows
        scratch[:, m * width : (m + 1) * width] = slices[:, :, start : start + rows].reshape(
            depth, width
        )


def columns_kernel(first, start, seqs, rows, row_ref, slice_ref, bias_ref, out_ref, weight, taken, sem):
    def copy(i):
        return pltpu.make_async_copy(
            row_ref.at[i, :, pl.ds(start, rows)], taken.at[i], sem.at[i]
        )

    count, many = out_ref.shape[:2]
    width = out_ref.shape[4]
    for i in range(count):
        copy(i).start()
    take_columns(weight, slice_ref, first)
    for i in range(count):
        copy(i).wait()
        result = dot(taken[i].reshape(seqs * rows, weight.shape[0]), weight[...], NN) + bias_ref[...]
        for m in range(many):
            out_ref[i, m] = (
                result[:, m * width : (m + 1) * width]
                .astype(jnp.bfloat16)
                .reshape(seqs, rows, width)
            )


def project_columns(name, gathered_rows, start, rows, slices, first, many, bias):
    count, seqs, _, depth = gathered_rows.shape
    width = slices.shape[3]
    out = shape((count, many, seqs, rows, width), jnp.bfloat16)
    return pl.pallas_call(
        partial(columns_kernel, first, start, seqs, rows),
        grid=(1,),
        in_specs=[pl.BlockSpec(memory_space=pl.ANY), whole(slices), whole(bias)],
        out_specs=whole(out),
        out_shape=out,
        scratch_shapes=[
            pltpu.VMEM((depth, many * width), jnp.bfloat16),
            pltpu.VMEM((count, seqs, rows, depth), jnp.bfloat16),
            pltpu.SemaphoreType.DMA((count,)),
        ],
        compiler_params=params(),
        cost_estimate=cost(
            2 * many * count * seqs * rows * depth * width, 2 * count * seqs * rows * depth
        ),
        name=name,
    )(gathered_rows, slices, bias)


def columns_back_kernel(first, start, order, row_ref, *refs):
    grad_refs, (slice_ref, mine_out, other_out, dw_ref, bias_ref) = refs[:-12], refs[-12:-7]
    weight, taken, gradients, moved, total, in_sem, out_sem = refs[-7:]
    count, seqs, rows, depth = taken.shape
    half = count // 2

    def bring(r):
        return pltpu.make_async_copy(
            row_ref.at[order[r], :, pl.ds(start, rows)], taken.at[r], in_sem.at[r]
        )

    def send(r):
        there = (mine_out, other_out)[r // half].at[r % half, 0]
        return pltpu.make_async_copy(moved.at[r], there, out_sem.at[r])

    for r in range(count):
        bring(r).start()
    take_columns(weight, slice_ref, first)
    size = seqs * rows
    for r in range(count):
        i = order[r]
        pieces = []
        for grad_ref in grad_refs:
            width = grad_ref.shape[-1]
            for m in range(grad_ref.shape[1] if len(grad_ref.shape) == 5 else 1):
                piece = grad_ref[i, m] if len(grad_ref.shape) == 5 else grad_ref[i]
                pieces.append(piece.reshape(size, width))
        gradient = jnp.concatenate(pieces, axis=1)
        gradients[r * size : (r + 1) * size] = gradient
        moved[r] = dot(gradient, weight[...], NT).astype(jnp.bfloat16)
        send(r).start()
    whole_gradient = gradients[...]
    bias_ref[...] = column_sum(whole_gradient.astype(jnp.float32))
    for r in range(count):
        bring(r).wait()
    total[...] = dot(whole_gradient, taken[...].reshape(count * size, depth), TN)
    groups, shards, all_rows, _ = dw_ref.shape
    part = depth // (groups * shards)
    for m in range(all_rows // part):
        dw_ref[:, :, m * part : (m + 1) * part] = (
            total[m * width : (m + 1) * width]
            .T.astype(jnp.bfloat16)
            .reshape(groups, shards, part, width)
        )
    for r in range(count):
        send(r).wait()


def project_columns_back(name, order, gathered_rows, start, rows, gradients, slices, first, many):
    count, seqs, _, depth = gathered_rows.shape
    half = count // 2
    groups, shards, _, width = slices.shape
    part = depth // (groups * shards)
    anywhere = pl.BlockSpec(memory_space=pl.ANY)
    halves = shape((half, 1, seqs * rows, depth), jnp.bfloat16)
    dw_shape = shape((groups, shards, many * part, width), jnp.bfloat16)
    bias = shape((1, many * width), jnp.float32)
    return pl.pallas_call(
        partial(columns_back_kernel, first, start),
        grid_spec=pltpu.PrefetchScalarGridSpec(
            num_scalar_prefetch=1,
            grid=(1,),
            in_specs=[anywhere, *[whole(array) for array in gradients], whole(slices)],
            out_specs=[anywhere, anywhere, whole(dw_shape), whole(bias)],
            scratch_shapes=[
                pltpu.VMEM((depth, many * width), jnp.bfloat16),
                pltpu.VMEM((count, seqs, rows, depth), jnp.bfloat16),
                pltpu.VMEM((count * seqs * rows, many * width), jnp.bfloat16),
                pltpu.VMEM((count, seqs * rows, depth), jnp.bfloat16),
                pltpu.VMEM((many * width, depth), jnp.float32),
                pltpu.SemaphoreType.DMA((count,)),
                pltpu.SemaphoreType.DMA((count,)),
            ],
        ),
        out_shape=[halves, halves, dw_shape, bias],
        compiler_params=params(),
        cost_estimate=cost(
            4 * many * count * seqs * rows * depth * width, 4 * count * seqs * rows * depth
        ),
        name=name,
    )(order, gathered_rows, *gradients, slices)


def gathered(weights, width, place):
    count, groups, rows, _ = weights.shape
    return pl.BlockSpec((count, groups, rows, width), lambda *_: (0, 0, 0, place))


def first_kernel(
    mixed_ref, x_ref, out_w, query_w, vector_ref, _, mixed_out, in_out, low_out, query_out
):
    mixed = join(mixed_ref)
    mixed_out[...] = mixed
    first_in = x_ref[...].astype(jnp.float32) + times(mixed, out_w) + vector_ref[2:3]
    in_out[...] = first_in
    unit, _ = norm_parts(first_in)
    low = (unit * vector_ref[11:12] + vector_ref[12:13]).astype(jnp.bfloat16)
    low_out[...] = low
    spread(query_out, (times(low, query_w) + vector_ref[3:4]).astype(jnp.bfloat16))


def first_forward(mixed, x_rows, weights, vectors, after):
    rows, depth = x_rows.shape
    return pl.pallas_call(
        first_kernel,
        grid=(1,),
        in_specs=[
            whole(mixed),
            whole(x_rows),
            gathered(weights, depth, 0),
            gathered(weights, depth, 1),
            whole(vectors),
            pl.BlockSpec(memory_space=pl.ANY),
        ],
        out_specs=[whole(x_rows), whole(x_rows), whole(x_rows), whole(mixed)],
        out_shape=[
            shape((rows, depth), jnp.bfloat16),
            shape((rows, depth), jnp.float32),
            shape((rows, depth), jnp.bfloat16),
            shape(mixed.shape, jnp.bfloat16),
        ],
        compiler_params=params(),
        cost_estimate=cost(4 * rows * depth * depth, 4 * depth * depth),
        name="first_forward",
    )(mixed, x_rows, weights, weights, vectors, after)


def ffn_kernel(
    order,
    places,
    mixed_ref,
    first_ref,
    out_w,
    vector_ref,
    bias_ref,
    grad_ref,
    wide_ref,
    *refs,
):
    contract_refs, refs = refs[:8], refs[8:]
    mixed_out, layer_out, wide_grad = refs[:3]
    contract_grads, refs = refs[3:11], refs[11:]
    dbias_ref, second_grad, cross_low, mixed_grad, stat_out, columns, contracts = refs[:7]
    active, slope, low, third_low, second_in, total, wide_sem, contract_sem = refs[7:]
    blocks, count, groups, rows, block = columns.shape
    part = block // CHIPS
    depth = vector_ref.shape[1]

    def wide_copies(t, array, outward):
        result = []
        for k in range(CHIPS):
            column = pl.multiple_of(order[t % 2 * CHIPS + k] * part, part)
            row = pl.multiple_of(places[t // 2] * rows, rows)
            there = array.at[:, :, pl.ds(row, rows), pl.ds(column, part)]
            here = columns.at[t, :, :, :, pl.ds(k * part, part)]
            ends = (here, there) if outward else (there, here)
            result.append(pltpu.make_async_copy(*ends, wide_sem.at[t, k]))
        return result

    def contract_copies(t, pieces, outward):
        near, far = divmod(DP_ORDER[t // 2], 2)
        first = pieces[t % 2 * 4 + far].at[near]
        last = pieces[t % 2 * 4 + 2 + near].at[far]
        result = []
        for half, there in enumerate((first, last)):
            here = contracts.at[t, pl.ds(half * CHIPS // 2, CHIPS // 2)]
            ends = (here, there) if outward else (there, here)
            result.append(pltpu.make_async_copy(*ends, contract_sem.at[t, half]))
        return result

    for t in range(blocks):
        for copy in wide_copies(t, wide_ref, False):
            copy.start()
        for copy in contract_copies(t, contract_refs, False):
            copy.start()

    mixed = join(mixed_ref)
    mixed_out[...] = mixed
    unit, _ = norm_parts(first_ref[...])
    second_in[...] = (
        unit * vector_ref[11:12] + vector_ref[12:13] + times(mixed, out_w) + vector_ref[5:6]
    )
    unit, _ = norm_parts(second_in[...])
    second = unit * vector_ref[13:14] + vector_ref[14:15]
    low[...] = second.astype(jnp.bfloat16)
    total[...] = second + vector_ref[10:11]

    def shard(t, k):
        return places[t // 2] * count + order[t % 2 * CHIPS + k]

    for t in range(blocks):
        for copy in wide_copies(t, wide_ref, False):
            copy.wait()
        bias = jnp.concatenate([bias_ref[pl.ds(shard(t, k), 1)] for k in range(CHIPS)], axis=1)
        inner = times(low[...], columns.at[t]) + bias
        phi = 0.5 + 0.5 * lax.erf(inner * (0.5**0.5))
        out = (inner * phi).astype(jnp.bfloat16)
        active[t] = out
        slope[t] = phi + inner * jnp.exp(-0.5 * inner * inner) * 0.3989422804014327
        for copy in contract_copies(t, contract_refs, False):
            copy.wait()
        total[...] += dot(out, contracts[t].reshape(block, depth), NN)

    unit, inverse = norm_parts(total[...])
    gain = vector_ref[15:16]
    layer_out[...] = (unit * gain + vector_ref[16:17]).astype(jnp.bfloat16)
    gradient = grad_ref[...].astype(jnp.float32)
    grad_third = norm_back(gradient, unit, inverse, gain)
    stat_out[...] = jnp.zeros_like(stat_out)
    stat_out[0:1] = column_sum(grad_third)
    stat_out[1:2] = column_sum(gradient * unit)
    stat_out[2:3] = column_sum(gradient)
    total[...] = grad_third
    third_low[...] = grad_third.astype(jnp.bfloat16)
    turned = low[...].T

    for t in range(blocks):
        grad_inner = dot(third_low[...], contracts[t].reshape(block, depth), NT) * slope[t]
        inner_low = grad_inner.astype(jnp.bfloat16)
        sums = column_sum(grad_inner)
        for k in range(CHIPS):
            dbias_ref[pl.ds(shard(t, k), 1)] = sums[:, k * part : (k + 1) * part]
        contracts[t] = (
            dot(active[t], third_low[...], TN).astype(jnp.bfloat16).reshape(CHIPS, part, depth)
        )
        for copy in contract_copies(t, contract_grads, True):
            copy.start()
        total[...] += times_back(inner_low, columns.at[t])
        result = dot(turned, inner_low, NN).astype(jnp.bfloat16)
        for d in range(groups):
            columns[t, :, d] = result[d * count * rows : (d + 1) * count * rows].reshape(
                count, rows, block
            )
        for copy in wide_copies(t, wide_grad, True):
            copy.start()

    unit, inverse = norm_parts(second_in[...])
    grad_second = total[...]
    grad_in = norm_back(grad_second, unit, inverse, vector_ref[13:14])
    second_grad[...] = grad_in
    grad_low = grad_in.astype(jnp.bfloat16)
    cross_low[...] = grad_low
    spread(mixed_grad, times_back(grad_low, out_w).astype(jnp.bfloat16))
    stat_out[8:9] = column_sum(grad_in)
    stat_out[9:10] = column_sum(grad_second * unit)
    stat_out[10:11] = column_sum(grad_second)
    for t in range(blocks):
        for copy in contract_copies(t, contract_grads, True) + wide_copies(t, wide_grad, True):
            copy.wait()


def ffn(orders, mixed, first_in, wide, contract, vectors, bias, output_grad):
    rows, depth = first_in.shape
    hidden = bias.size
    block = depth // 2
    count, groups, all_rows, _ = wide.shape
    part = depth // (count * groups)
    blocks = hidden // block
    full = whole(first_in)
    anywhere = pl.BlockSpec(memory_space=pl.ANY)
    heads_out = shape(mixed.shape, jnp.bfloat16)
    stats = shape((16, depth), jnp.float32)
    return pl.pallas_call(
        ffn_kernel,
        grid_spec=pltpu.PrefetchScalarGridSpec(
            num_scalar_prefetch=2,
            grid=(1,),
            in_specs=[
                whole(mixed),
                full,
                pl.BlockSpec((count, groups, part, depth), lambda *_: (0, 0, groups, 0)),
                whole(vectors),
                whole(bias),
                full,
                *[anywhere] * 9,
            ],
            out_specs=[
                full,
                full,
                *[anywhere] * 9,
                whole(bias),
                full,
                full,
                whole(heads_out),
                whole(stats),
            ],
            scratch_shapes=[
                pltpu.VMEM((blocks, count, groups, part, block), jnp.bfloat16),
                pltpu.VMEM((blocks, CHIPS) + contract[0].shape[2:], jnp.bfloat16),
                pltpu.VMEM((blocks, rows, block), jnp.bfloat16),
                pltpu.VMEM((blocks, rows, block), jnp.float32),
                pltpu.VMEM((rows, depth), jnp.bfloat16),
                pltpu.VMEM((rows, depth), jnp.bfloat16),
                pltpu.VMEM((rows, depth), jnp.float32),
                pltpu.VMEM((rows, depth), jnp.float32),
                pltpu.SemaphoreType.DMA((blocks, CHIPS)),
                pltpu.SemaphoreType.DMA((blocks, 2)),
            ],
        ),
        out_shape=[
            shape((rows, depth), jnp.bfloat16),
            shape((rows, depth), jnp.bfloat16),
            shape((count, groups, all_rows - part, depth), jnp.bfloat16),
            *[shape(piece.shape, jnp.bfloat16) for piece in contract],
            shape(bias.shape, jnp.float32),
            shape((rows, depth), jnp.float32),
            shape((rows, depth), jnp.bfloat16),
            heads_out,
            stats,
        ],
        compiler_params=params(),
        cost_estimate=cost(12 * rows * depth * hidden, 16 * depth * hidden),
        name="ffn",
    )(*orders, mixed, first_in, wide, vectors, bias, output_grad, wide, *contract)


def first_back_kernel(
    dq_ref,
    second_grad,
    first_ref,
    out_w,
    query_w,
    vector_ref,
    _,
    query_low,
    grad_in_out,
    self_low,
    mixed_grad,
    stat_out,
):
    query_grad = join(dq_ref)
    query_low[...] = query_grad
    grad_first = second_grad[...] + times_back(query_grad, query_w)
    unit, inverse = norm_parts(first_ref[...])
    grad_in = norm_back(grad_first, unit, inverse, vector_ref[11:12])
    grad_in_out[...] = grad_in
    grad_low = grad_in.astype(jnp.bfloat16)
    self_low[...] = grad_low
    spread(mixed_grad, times_back(grad_low, out_w).astype(jnp.bfloat16))
    stat_out[...] = jnp.zeros_like(stat_out)
    stat_out[0:1] = column_sum(query_grad.astype(jnp.float32))
    stat_out[1:2] = column_sum(grad_in)
    stat_out[2:3] = column_sum(grad_first * unit)
    stat_out[3:4] = column_sum(grad_first)


def first_back(dq, second_grad, first_in, weights, vectors, after):
    rows, depth = first_in.shape
    full = whole(first_in)
    return pl.pallas_call(
        first_back_kernel,
        grid=(1,),
        in_specs=[
            whole(dq),
            full,
            full,
            gathered(weights, depth, 0),
            gathered(weights, depth, 1),
            whole(vectors),
            pl.BlockSpec(memory_space=pl.ANY),
        ],
        out_specs=[full, full, full, whole(dq), pl.BlockSpec((8, depth), lambda *_: (0, 0))],
        out_shape=[
            shape((rows, depth), jnp.bfloat16),
            shape((rows, depth), jnp.float32),
            shape((rows, depth), jnp.bfloat16),
            shape(dq.shape, jnp.bfloat16),
            shape((8, depth), jnp.float32),
        ],
        compiler_params=params(),
        cost_estimate=cost(4 * rows * depth * depth, 4 * depth * depth),
        name="first_back",
    )(dq, second_grad, first_in, weights, weights, vectors, after)


def weight_grads_kernel(
    order,
    mixed,
    self_low,
    first_low,
    query_low,
    cross,
    cross_low,
    mine_out,
    other_out,
    result,
):
    step = pl.program_id(0)
    pairs = ((mixed, self_low), (first_low, query_low), (cross, cross_low))
    half, groups, part, _ = mine_out.shape
    for m, (left_side, gradient) in enumerate(pairs):

        @pl.when(step == m)
        def _(left_side=left_side, gradient=gradient):
            result[...] = dot(left_side[...], gradient[...], TN).astype(jnp.bfloat16)

    for d in range(groups):
        for k in range(half):
            for p, out_ref in enumerate((mine_out, other_out)):
                row = pl.multiple_of((2 * half * d + order[p * half + k]) * part, part)
                out_ref[k, d] = result[pl.ds(row, part)]


def weight_grads(dims, order, mixed, self_low, first_low, query_low, cross, cross_low):
    count, groups, part, depth = dims
    half = pl.BlockSpec((count // 2, groups, part, depth), lambda m, _: (0, 0, m, 0))
    return pl.pallas_call(
        weight_grads_kernel,
        grid_spec=pltpu.PrefetchScalarGridSpec(
            num_scalar_prefetch=1,
            grid=(3,),
            in_specs=[whole(mixed)] * 6,
            out_specs=[half, half],
            scratch_shapes=[pltpu.VMEM((depth, depth), jnp.bfloat16)],
        ),
        out_shape=[shape((count // 2, groups, 3 * part, depth), jnp.bfloat16)] * 2,
        compiler_params=params(),
        cost_estimate=cost(6 * mixed.shape[0] * depth * depth, 6 * depth * depth),
        name="weight_grads",
    )(order, mixed, self_low, first_low, query_low, cross, cross_low)


def send_dp(piece):
    size = lax.axis_size("dp")
    return [
        lax.ppermute(piece, "dp", [(i, (i + shift) % size) for i in range(size)])
        for shift in range(1, size)
    ]


def place_dp(piece, arrived):
    size, me = lax.axis_size("dp"), lax.axis_index("dp")
    result = jnp.zeros((size,) + piece.shape, piece.dtype)
    result = lax.dynamic_update_index_in_dim(result, piece, me, 0)
    for shift, got in enumerate(arrived, 1):
        result = lax.dynamic_update_index_in_dim(result, got, lax.rem(me - shift + size, size), 0)
    return result


class HalvingDp:
    def __init__(self, pieces):
        me = lax.axis_index("dp")
        self.parts = [
            lax.dynamic_index_in_dim(pieces, me ^ flip, 0, keepdims=False) for flip in DP_ORDER
        ]

    def first(self):
        return jnp.stack(self.parts[2:]).astype(jnp.bfloat16)

    def second(self, got):
        self.got = got
        return (
            self.parts[1].astype(jnp.float32) + self.got[1].astype(jnp.float32)
        ).astype(jnp.bfloat16)

    def finish(self, last):
        return sum(one.astype(jnp.float32) for one in (self.parts[0], self.got[0], last))


def relative_order():
    size, me = lax.axis_size("index"), lax.axis_index("index")
    steps = jnp.arange(size // 2, dtype=jnp.int32) * 2
    return jnp.concatenate([me ^ steps, me ^ 1 ^ steps])


def exchange(piece, flip):
    size = lax.axis_size("index")
    return lax.ppermute(piece, "index", [(i, i ^ flip) for i in range(size)])


def exchange_dp(piece, flip):
    size = lax.axis_size("dp")
    return lax.ppermute(piece, "dp", [(i, i ^ flip) for i in range(size)])


def add_kernel(*refs):
    total = sum(ref[...].astype(jnp.float32) for ref in refs[:-1])
    refs[-1][...] = total.astype(jnp.bfloat16)


def add(*terms):
    flat, specs = [], []
    first = terms[0]
    dims = first[0].shape[1:] if isinstance(first, tuple) else first.shape
    rows = 1
    for size in dims[:-1]:
        rows *= size
    block = min(rows, 256)
    for term in terms:
        array, entry = term if isinstance(term, tuple) else (term, 0)
        flat.append(array.reshape(-1, dims[-1]))
        start = entry * rows // block
        specs.append(pl.BlockSpec((block, dims[-1]), lambda i, start=start: (start + i, 0)))
    return pl.pallas_call(
        add_kernel,
        grid=(rows // block,),
        in_specs=specs,
        out_specs=pl.BlockSpec((block, dims[-1]), lambda i: (i, 0)),
        out_shape=shape((rows, dims[-1]), jnp.bfloat16),
        compiler_params=params(),
        cost_estimate=cost(0, 0),
        name="add",
    )(*flat).reshape(dims)


def combine_kernel(plan, *refs):
    ins, outs = list(refs[: -len(plan)]), refs[-len(plan) :]
    for out_ref, entries in zip(outs, plan):
        for e, segments in enumerate(entries):
            start = 0
            for offsets, rows in segments:
                terms, ins = ins[: len(offsets)], ins[len(offsets) :]
                total = sum(
                    ref[0, offset : offset + rows].astype(jnp.float32)
                    for ref, offset in zip(terms, offsets)
                )
                out_ref[e, start : start + rows] = total.astype(jnp.bfloat16)
                start += rows


def combine(*outputs):
    arrays, specs, plan, shapes = [], [], [], []
    for entries in outputs:
        plan.append([])
        for segments in entries:
            plan[-1].append([])
            for terms in segments:
                offsets = []
                for array, e, rows, start in terms:
                    block, place, offset = rows, start // rows, 0
                    if start % rows or array.shape[1] % rows:
                        block, place, offset = array.shape[1], 0, start
                    offsets.append(offset)
                    arrays.append(array)
                    specs.append(
                        pl.BlockSpec(
                            (1, block, array.shape[2]), lambda i, e=e, place=place: (e, place, 0)
                        )
                    )
                plan[-1][-1].append((offsets, terms[0][2]))
        rows = sum(rows for _, rows in plan[-1][0])
        shapes.append(shape((len(entries), rows, arrays[0].shape[2]), jnp.bfloat16))
    return pl.pallas_call(
        partial(combine_kernel, plan),
        grid=(1,),
        in_specs=specs,
        out_specs=[whole(out) for out in shapes],
        out_shape=shapes,
        compiler_params=params(),
        cost_estimate=cost(0, 0),
        name="combine",
    )(*arrays)


class Halving:
    def __init__(self, chips):
        self.chips = chips
        self.middle = chips[0][0][0].shape[1] // 2

    def terms(self, k, half, *more):
        middle = self.middle
        return [(array, e, middle, half * middle) for array, e in self.chips[k]] + [
            (array, e, middle, start) for array, e, start in more
        ]

    def total(self, k, half, *more):
        rows = slice(half * self.middle, (half + 1) * self.middle)
        parts = [array[e, rows] for array, e in self.chips[k]] + [*more]
        return sum(one.astype(jnp.float32) for one in parts)

    def finish(self, top, low):
        return jnp.concatenate(
            [self.total(0, 0, self.got[0][0], top), self.total(0, 1, self.got[1][0], low)], axis=0
        )


def both_cores(mine, other):
    parts = [part.reshape(CHIPS, -1, part.shape[-1]) for part in (mine, other)]
    return Halving([[(part, k) for part in parts] for k in range(CHIPS)])


def firsts(*sums):
    return combine(
        [[one.terms(k, 0) for one in sums] for k in (1, 3)],
        [[one.terms(k, 1) for one in sums] for k in (2, 3)],
    )


def seconds(*sums):
    for one, top, low, start in sums:
        rows = slice(start, start + one.middle)
        one.got = top[:, rows], low[:, rows]
    top, low = combine(
        [[one.terms(2, 0, (top, 1, start)) for one, top, _, start in sums]],
        [[one.terms(1, 1, (low, 1, start)) for one, _, low, start in sums]],
    )
    return top[0], low[0]


def send_first(top, low):
    return [exchange(top, 2), exchange(low, 4)]


def send_last(top, low):
    return [exchange(top, 4), exchange(low, 2)]


def split_rows(arrays, rows):
    return [a[..., :rows, :] for a in arrays], [a[..., rows:, :] for a in arrays]


def small_send(values):
    size = lax.axis_size("index")
    flat = jnp.pad(values.reshape(-1), (0, 1024 - values.size)).reshape(1, 8, 128)
    return swap(jnp.broadcast_to(flat, (size, 8, 128)))


def small_take(arrived, dims):
    size = 1
    for dim in dims:
        size *= dim
    return jnp.sum(arrived, axis=0).reshape(-1)[:size].reshape(dims)


def hold_kernel(*_):
    pass


def hold(values, *others):
    anywhere = pl.BlockSpec(memory_space=pl.ANY)
    return pl.pallas_call(
        hold_kernel,
        in_specs=[anywhere] * (len(values) + len(others)),
        out_specs=[anywhere] * len(values),
        out_shape=[shape(value.shape, value.dtype) for value in values],
        input_output_aliases={i: i for i in range(len(values))},
        name="hold",
    )(*values, *others)


def swap(pieces):
    return lax.all_to_all(pieces, "index", 0, 0, tiled=True)


def head_body(
    decoder_input,
    encoder_memory,
    question_vectors,
    passage_vectors,
    passage_ids,
    valid_count,
    output_grad,
    attention_weight,
    expand_weight,
    contract_weight,
    vector_params,
    attention_mean,
    attention_square,
    expand_mean,
    expand_square,
    contract_mean,
    contract_square,
    vector_mean,
    vector_square,
):
    low = jnp.bfloat16
    count, groups = lax.axis_size("index"), lax.axis_size("dp")
    place = lax.axis_index("index")
    seqs, rows_here, depth = decoder_input.shape
    memory_here = encoder_memory.shape[1]
    width = depth // count
    part = attention_weight.shape[1]
    hidden = expand_weight.shape[1]
    vector_rows, vector_width = vector_params.shape
    question_width = question_vectors.shape[1]
    rows = seqs * rows_here

    attention_low = attention_weight.astype(low)
    extras = jnp.concatenate(
        [vector_params.astype(low).reshape(-1), question_vectors.reshape(-1)]
    )
    extra_rows = -(-extras.shape[0] // (16 * width)) * 16
    extras = jnp.pad(extras, (0, extra_rows * width - extras.shape[0])).reshape(
        1, extra_rows, width
    )
    split = jnp.concatenate([attention_low[:3], attention_low[5:7]], axis=0)
    columns = split.reshape(5, part, count, width).transpose(2, 0, 1, 3)
    package = jnp.concatenate(
        [
            columns.reshape(count, 5 * part, width),
            jnp.broadcast_to(extras, (count, extra_rows, width)),
        ],
        axis=1,
    )
    order = relative_order()
    memory_block = -(-memory_here // rows_here) * rows_here
    rows_all = lax.all_gather(
        jnp.concatenate(
            [
                jnp.pad(encoder_memory, ((0, 0), (0, memory_block - memory_here), (0, 0))),
                decoder_input,
            ],
            axis=1,
        ),
        "index",
        axis=0,
        tiled=False,
    )
    input_rows = (rows_all, memory_block, rows_here)
    memory_rows = (rows_all, 0, memory_here)
    square = attention_low[3:5].transpose(1, 0, 2).reshape(part, 2 * depth)
    received = swap(package)
    square_arrived = hold(send_dp(square), received)
    (received,) = hold([received], *square_arrived)
    received_sent = send_dp(received)
    (contract,) = hold([contract_weight.astype(low)], received)
    contract = [contract] + [exchange(contract, 2 * k) for k in range(1, CHIPS)]
    slices_arrived = hold(received_sent, *contract[1:])
    square_arrived = hold(square_arrived, *slices_arrived)
    square = lax.all_gather(place_dp(square, square_arrived), "index", axis=0, tiled=False)
    slices = place_dp(received, slices_arrived)
    vectors = (
        slices[:, :, 5 * part :]
        .reshape(groups, count, extra_rows * width)[:, :, : vector_rows * vector_width]
        .reshape(groups, count, vector_rows, vector_width)
        .transpose(2, 0, 1, 3)
        .reshape(vector_rows, depth)
        .astype(jnp.float32)
    )
    question_full = (
        received[:, 5 * part :]
        .reshape(count, extra_rows * width)[:, vector_rows * vector_width :][
            :, : seqs * question_width
        ]
        .reshape(count, seqs, question_width)
        .transpose(1, 0, 2)
        .reshape(seqs, count * question_width)
    )
    expand_part = hidden // depth * part
    late = jnp.concatenate(
        [
            expand_weight.astype(low)
            .reshape(part, hidden // depth, depth)
            .transpose(1, 0, 2)
            .reshape(expand_part, depth),
            attention_low[7],
        ],
        axis=0,
    )
    (late,) = hold([late], *slices_arrived)
    late_sent = send_dp(late)

    (passage_ids,) = hold([passage_ids], *slices_arrived)
    passages_here = passage_vectors.shape[0]
    local_ids = passage_ids - place * passages_here
    owned_slot = (local_ids >= 0) & (local_ids < passages_here)
    picked = passage_vectors[jnp.clip(local_ids, 0, passages_here - 1)]
    local_scores = jnp.einsum(
        "sc,skc->sk", question_full, picked, preferred_element_type=jnp.float32
    )
    slots = passage_ids.shape[1]
    usable = jnp.arange(slots)[None, :] < valid_count[:, None]
    scores = small_take(small_send(jnp.where(owned_slot, local_scores, 0.0)), local_scores.shape)
    masked = jnp.where(usable, scores, negative_fill)
    maximum = jnp.max(masked, axis=1)
    exponent = jnp.where(usable, jnp.exp(masked - maximum[:, None]), 0.0)
    partition = jnp.sum(exponent, axis=1)
    passage_prob = exponent / partition[:, None]
    log_prior = jnp.where(
        usable, masked - maximum[:, None] - jnp.log(partition)[:, None], negative_fill
    )
    key_bias = jnp.repeat(log_prior, MEM_P, axis=1)

    vector_here = lax.dynamic_slice_in_dim(vectors[:5], place * width, width, axis=1)
    no_bias = jnp.zeros((1, width), jnp.float32)
    qkv_bias = jnp.concatenate([vector_here[0:1], no_bias, vector_here[1:2]], axis=1)
    kv_bias = jnp.concatenate([no_bias, vector_here[4:5]], axis=1)
    x_rows = decoder_input.reshape(rows, depth)
    qkv = project_columns("self_qkv", *input_rows, slices, 0, 3, qkv_bias)
    self_out, self_stat = attend(True, qkv, 0, qkv, 1, 2, key_bias[:, None, :])
    self_out, *late_arrived = hold([self_out, *late_sent])
    self_got = swap(self_out)
    late = lax.all_gather(place_dp(late, late_arrived), "index", axis=0, tiled=False)
    ahead, across = hold([jnp.stack(contract[:2]), jnp.stack(contract[2:])], *late_arrived)
    self_got, ahead_far, across_far = hold(
        [self_got, exchange_dp(ahead, 2), exchange_dp(across, 1)]
    )
    ahead = jnp.stack([ahead, ahead_far])
    across = jnp.stack([across, across_far])
    contract_sent = [exchange_dp(ahead, 1), exchange_dp(across, 2)]
    self_mixed, first_in, first_low, cross_query = first_forward(
        self_got, x_rows, square, vectors, ahead_far
    )
    (slices,) = hold([slices], first_low)
    memory_kv = project_columns("memory_kv", *memory_rows, slices, 3, 2, kv_bias)
    cross_query = swap(cross_query)[:, None]
    cross_out, cross_stat = attend(
        False, cross_query, 0, memory_kv, 0, 1, key_bias[:, None, :]
    )
    ahead_far, across_far = hold(contract_sent, cross_out)
    contract = [ahead, ahead_far, across, across_far]
    contract += [exchange(piece, 1) for piece in contract]
    places = lax.axis_index("dp") ^ jnp.array(DP_ORDER, jnp.int32)
    (
        cross_mixed,
        layer_output,
        wide_grad,
        *contract_grads,
        inner_total,
        second_grad,
        cross_low,
        cross_mix_grad,
        stats,
    ) = ffn(
        (order, places),
        swap(cross_out),
        first_in,
        late,
        contract,
        vectors,
        vectors[6:10].reshape(groups * count, -1),
        output_grad.reshape(rows, depth),
    )
    third_stat, second_stat = stats[:8], stats[8:]

    expand_part_sum = lax.psum_scatter(wide_grad, "index", scatter_dimension=0, tiled=False)
    ahead, ahead_far, across, across_far = contract_grads[:4]
    cores = [exchange(piece, 1) for piece in contract_grads[4:]]
    cross_mix_got, *contract_sent = hold(
        [swap(cross_mix_grad), add(ahead_far, cores[1]), add(across_far, cores[3])]
    )
    contract_got = [exchange_dp(contract_sent[0], 1), exchange_dp(contract_sent[1], 2)]
    cross_dq, cross_dkv, prior_rows = attend_back(
        False,
        cross_query,
        0,
        memory_kv,
        0,
        1,
        cross_mix_got,
        cross_stat,
        key_bias[:, None, :],
        contract_sent[0],
    )
    memory_mine, memory_other, kv_grads, kv_total = project_columns_back(
        "memory_kv_back", order, *memory_rows, [cross_dkv], slices, 3, 2
    )
    cross_dq, *contract_got = hold([cross_dq, *contract_got], memory_mine)
    contract_next = [
        add((ahead, 1), (cores[0], 1), (contract_got[0], 1)),
        add((across, 1), (cores[2], 1), (contract_got[1], 1)),
    ]
    cross_dq_got, *contract_next = hold([swap(cross_dq), *contract_next])
    contract_last = [exchange_dp(contract_next[0], 2), exchange_dp(contract_next[1], 1)]
    query_low, first_grad, self_low, self_mix_grad, first_stat = first_back(
        cross_dq_got, second_grad, first_in, square, vectors, memory_mine
    )
    memory_sum = both_cores(memory_mine, exchange(memory_other, 1))
    memory_sent = firsts(memory_sum)
    square_mine, square_other = weight_grads(
        (count, groups, part, depth),
        order,
        self_mixed,
        self_low,
        first_low,
        query_low,
        cross_mixed,
        cross_low,
    )
    square_sum = both_cores(square_mine, exchange(square_other, 1))
    square_sent = firsts(square_sum)
    self_mix_got, *contract_last = hold(
        [swap(self_mix_grad), *contract_last], *memory_sent, *square_sent
    )
    memory_got = send_first(*memory_sent)
    square_got = send_first(*square_sent)
    self_dq, self_dkv, _ = attend_back(
        True, qkv, 0, qkv, 1, 2, self_mix_got, self_stat, self_stat, square_mine
    )
    expand_sum = HalvingDp(expand_part_sum)
    self_dq, expand_sent = hold([self_dq, expand_sum.first()])
    dx_mine, dx_other, qkv_slice_grads, qkv_total = project_columns_back(
        "self_qkv_back", order, *input_rows, [self_dq, self_dkv], slices, 0, 3
    )
    dx_mine, dx_other, *got = hold([dx_mine, dx_other, *memory_got, *square_got])
    own = jnp.concatenate(
        [qkv_total[:, :width], qkv_total[:, 2 * width :], kv_total[:, width:]], axis=0
    )
    own = lax.dynamic_update_slice(
        jnp.zeros((3, depth), jnp.float32), own, (jnp.int32(0), place * width)
    )
    vector_grads = jnp.concatenate(
        [
            own[:2],
            first_stat[1:2],
            first_stat[0:1],
            own[2:],
            second_stat[0:1],
            inner_total.reshape(hidden // depth, depth),
            third_stat[0:1],
            first_stat[2:4],
            second_stat[1:3],
            third_stat[1:3],
        ],
        axis=0,
    )
    vector_size = vector_rows * vector_width
    question_size = seqs * question_width
    vector_send = (
        vector_grads.reshape(vector_rows, groups, count, vector_width)
        .transpose(1, 2, 0, 3)
        .reshape(groups, count, vector_size)
    )
    vector_send = jnp.pad(
        vector_send, ((0, 0), (0, 0), (0, extra_rows * width - vector_size))
    ).reshape(groups, count, extra_rows, width)
    slice_sum = HalvingDp(
        jnp.concatenate([qkv_slice_grads, kv_grads, vector_send.astype(low)], axis=2)
    )
    slice_sent = slice_sum.first()
    slice_got = exchange_dp(slice_sent, 1)
    dx_other, *got = hold([dx_other, *got], slice_sent)
    dx_got = exchange(dx_other, 1)
    square_rows = square_sum.middle
    last = seconds((square_sum, *got[2:], 0), (memory_sum, *got[:2], 0))
    prior_rows, expand_sent, *contract_last = hold(
        [prior_rows, expand_sent, *contract_last], *last
    )
    last = send_last(*last)
    expand_got = exchange_dp(expand_sent, 1)
    prior_arrived = small_send(prior_rows.reshape(seqs, slots, MEM_P).sum(axis=-1))
    dx_got, prior_arrived, slice_got, *last = hold([dx_got, prior_arrived, slice_got, *last])
    slice_next = slice_sum.second(slice_got)
    dx_got, *last = hold([dx_got, *last], slice_next)
    slice_last = exchange_dp(slice_next, 2)
    dx_sum = both_cores(dx_mine, dx_got)
    contract_sum = Halving(
        [
            [(one.reshape((-1,) + one.shape[-2:]), k % 2) for one in parts]
            for k, parts in enumerate(
                [(ahead, cores[0], contract_got[0], contract_last[0])] * 2
                + [(across, cores[2], contract_got[1], contract_last[1])] * 2
            )
        ]
    )
    dx_sent = firsts(dx_sum, contract_sum)
    got = send_first(*dx_sent)
    last = hold(last, *dx_sent)
    square_last, memory_last = split_rows(last, square_rows)
    square_far = HalvingDp(square_sum.finish(*square_last).reshape(groups, 3 * part, depth))
    square_got = exchange_dp(square_far.first(), 1)
    slice_sum = slice_sum.finish(slice_last)
    prior_grad = jnp.where(usable, small_take(prior_arrived, (seqs, slots)), 0.0)
    score_doc = jnp.where(
        usable, prior_grad - passage_prob * jnp.sum(prior_grad, axis=1, keepdims=True), 0.0
    )
    question_part = jnp.einsum(
        "sk,skc->sc",
        jnp.where(owned_slot, score_doc, 0.0),
        picked.astype(jnp.float32),
        precision=lax.Precision.HIGHEST,
    )

    question_send = (
        question_part.reshape(seqs, count, question_width)
        .transpose(1, 0, 2)
        .reshape(count, question_size)
    )
    question_send = jnp.pad(
        question_send,
        ((0, 0), (vector_size, extra_rows * width - vector_size - question_size)),
    ).reshape(count, extra_rows, width)
    slice_sum = jnp.concatenate(
        [slice_sum[:, : 5 * part], slice_sum[:, 5 * part :] + question_send], axis=1
    )
    slice_send = slice_sum.astype(low)
    arrived = swap(slice_send)
    square_got, expand_got = hold([square_got, expand_got], slice_send)
    square_next, expand_next = square_far.second(square_got), expand_sum.second(expand_got)
    got = hold(got, square_next, expand_next)
    square_last, expand_last = exchange_dp(square_next, 2), exchange_dp(expand_next, 2)
    start = dx_sum.middle
    last = seconds((dx_sum, *got, 0), (contract_sum, *got, start))
    square_last, expand_last = hold([square_last, expand_last], *last)
    last = send_last(*last)
    dx_last, contract_last = split_rows(last, start)
    input_gradient = first_grad + dx_sum.finish(*dx_last)
    contract_sum = contract_sum.finish(*contract_last)
    memory_last = hold(memory_last, *got)
    memory_gradient = memory_sum.finish(*memory_last).reshape(encoder_memory.shape)
    new_contract = adam_update(
        contract_weight, contract_mean, contract_square, contract_sum, rate_contract, decay_matrix
    )
    arrived = arrived.astype(jnp.float32)
    split_grads = (
        arrived[:, : 5 * part]
        .reshape(count, 5, part, width)
        .transpose(1, 2, 0, 3)
        .reshape(5, part, depth)
    )
    extra_sum = jnp.sum(arrived[:, 5 * part :].reshape(count, extra_rows * width), axis=0)
    vector_sum = extra_sum[:vector_size].reshape(vector_rows, vector_width)
    question_gradient = extra_sum[vector_size : vector_size + question_size].reshape(
        seqs, question_width
    )

    expand_sum = (
        expand_sum.finish(expand_last)
        .reshape(hidden // depth, part, depth)
        .transpose(1, 0, 2)
        .reshape(part, hidden)
    )
    square_total = square_far.finish(square_last).reshape(3, part, depth)
    attention_sum = jnp.concatenate(
        [split_grads[:3], square_total[:2], split_grads[3:], square_total[2:]], axis=0
    )

    new_attention = adam_update(
        attention_weight,
        attention_mean,
        attention_square,
        attention_sum,
        rate_attention,
        decay_matrix,
    )
    new_expand = adam_update(
        expand_weight, expand_mean, expand_square, expand_sum, rate_expand, decay_matrix
    )
    new_vector = adam_update(
        vector_params, vector_mean, vector_square, vector_sum, rate_vector, 0.0
    )
    return (
        layer_output.reshape(decoder_input.shape),
        input_gradient.reshape(decoder_input.shape),
        memory_gradient,
        question_gradient,
        *new_attention,
        *new_expand,
        *new_contract,
        *new_vector,
    )


def body(sizes, *arrays):
    depth = arrays[0].shape[2]
    if sizes == (4, 8) and depth // 8 % 128 == 0:
        return head_body(*arrays)
    return general_body(*arrays)


def solution(mesh):
    return jax.shard_map(
        partial(body, (mesh.shape["dp"], mesh.shape["index"])),
        mesh=mesh,
        in_specs=(
            P("dp", "index", None),
            P("dp", "index", None),
            P("dp", "index"),
            P("index", None),
            P("dp", None),
            P("dp"),
            P("dp", "index", None),
            P(None, ("dp", "index"), None),
            P(("dp", "index"), None),
            P(("dp", "index"), None),
            P(None, ("dp", "index")),
            P(None, ("dp", "index"), None),
            P(None, ("dp", "index"), None),
            P(("dp", "index"), None),
            P(("dp", "index"), None),
            P(("dp", "index"), None),
            P(("dp", "index"), None),
            P(None, ("dp", "index")),
            P(None, ("dp", "index")),
        ),
        out_specs=(
            P("dp", "index", None),
            P("dp", "index", None),
            P("dp", "index", None),
            P("dp", "index"),
            P(None, ("dp", "index"), None),
            P(None, ("dp", "index"), None),
            P(None, ("dp", "index"), None),
            P(("dp", "index"), None),
            P(("dp", "index"), None),
            P(("dp", "index"), None),
            P(("dp", "index"), None),
            P(("dp", "index"), None),
            P(("dp", "index"), None),
            P(None, ("dp", "index")),
            P(None, ("dp", "index")),
            P(None, ("dp", "index")),
        ),
        check_vma=False,
    )
```

```python
from functools import partial

import jax
import jax.numpy as jnp
from jax import lax
from jax.experimental import pallas as pl
from jax.experimental.pallas import tpu as pltpu
from jax.sharding import PartitionSpec as P

HEADS = 16
MEM_P = 192
STEP = 10


negative_fill = -1e30
norm_eps = 1e-05
beta_first = 0.9
beta_second = 0.999
adam_eps = 1e-08
decay_matrix = 0.01
rate_attention = 0.1
rate_expand = 0.02
rate_contract = 0.01
rate_vector = 0.2


def layer_norm(hidden, norm_gain, norm_shift):
    center = hidden - jnp.mean(hidden, axis=-1, keepdims=True)
    spread = jnp.mean(center * center, axis=-1, keepdims=True)
    return center * lax.rsqrt(spread + norm_eps) * norm_gain + norm_shift


def split_heads(matrix):
    return matrix.reshape(matrix.shape[0], matrix.shape[1], HEADS, matrix.shape[2] // HEADS)


def merge_heads(matrix):
    return matrix.reshape(matrix.shape[0], matrix.shape[1], matrix.shape[2] * matrix.shape[3])


def project(left_side, weight):
    return jnp.einsum("srd,de->sre", left_side, weight, preferred_element_type=jnp.float32)


def project_back(gradient, weight):
    return jnp.einsum("sre,de->srd", gradient, weight, preferred_element_type=jnp.float32)


def weight_grad(left_side, gradient):
    return jnp.einsum("srd,sre->de", left_side, gradient, preferred_element_type=jnp.float32)


def row_total(values):
    return jnp.sum(values, axis=(0, 1))


def attend_forward(queries, key_rows, values, score_bias, allowed):
    scores = (
        jnp.einsum(
            "sqhd,skhd->shqk",
            split_heads(queries),
            split_heads(key_rows),
            preferred_element_type=jnp.float32,
        )
        * 0.125
        + score_bias
    )
    scores = jnp.where(allowed, scores, negative_fill)
    maximum = jnp.max(scores, axis=-1)
    exponent = jnp.exp(scores - maximum[..., None])
    partition = jnp.sum(exponent, axis=-1)
    attend_prob = exponent / partition[..., None]
    mixture = jnp.einsum(
        "shqk,skhd->sqhd",
        attend_prob.astype(jnp.bfloat16),
        split_heads(values),
        preferred_element_type=jnp.float32,
    )
    return (merge_heads(mixture).astype(jnp.bfloat16), attend_prob, maximum, partition)


def score_grads(grad_mixed, attend_prob, values):
    grad_prob = jnp.einsum(
        "sqhd,skhd->shqk",
        split_heads(grad_mixed),
        split_heads(values),
        preferred_element_type=jnp.float32,
    )
    row_inner = jnp.sum(attend_prob * grad_prob, axis=-1)
    return ((attend_prob * (grad_prob - row_inner[..., None])).astype(jnp.bfloat16), row_inner)


def to_queries(grad_score, key_rows):
    return (
        merge_heads(
            jnp.einsum(
                "shqk,skhd->sqhd",
                grad_score,
                split_heads(key_rows),
                preferred_element_type=jnp.float32,
            )
        )
        * 0.125
    )


def to_keys(grad_score, attend_prob, queries, grad_mixed):
    grad_key = (
        merge_heads(
            jnp.einsum(
                "shqk,sqhd->skhd",
                grad_score,
                split_heads(queries),
                preferred_element_type=jnp.float32,
            )
        )
        * 0.125
    )
    grad_value = merge_heads(
        jnp.einsum(
            "shqk,sqhd->skhd",
            attend_prob.astype(jnp.bfloat16),
            split_heads(grad_mixed),
            preferred_element_type=jnp.float32,
        )
    )
    return (grad_key, grad_value)


def adam_update(weight, moment_one, moment_two, gradient, step_rate, weight_decay):
    mean_new = beta_first * moment_one + (1.0 - beta_first) * gradient
    square_new = beta_second * moment_two + (1.0 - beta_second) * gradient * gradient
    mean_hat = mean_new / (1.0 - beta_first**STEP)
    square_hat = square_new / (1.0 - beta_second**STEP)
    updated = weight - step_rate * (
        mean_hat / (jnp.sqrt(square_hat) + adam_eps) + weight_decay * weight
    )
    return (updated, mean_new, square_new)


def general_body(
    decoder_input,
    encoder_memory,
    question_vectors,
    passage_vectors,
    passage_ids,
    valid_count,
    output_grad,
    attention_weight,
    expand_weight,
    contract_weight,
    vector_params,
    attention_mean,
    attention_square,
    expand_mean,
    expand_square,
    contract_mean,
    contract_square,
    vector_mean,
    vector_square,
):
    attention_low, expand_low, contract_low, vector_low = (
        lax.all_gather(attention_weight.astype(jnp.bfloat16), ("dp", "index"), axis=1, tiled=True),
        lax.all_gather(expand_weight.astype(jnp.bfloat16), ("dp", "index"), axis=0, tiled=True),
        lax.all_gather(contract_weight.astype(jnp.bfloat16), ("dp", "index"), axis=0, tiled=True),
        lax.all_gather(vector_params.astype(jnp.bfloat16), ("dp", "index"), axis=1, tiled=True),
    )
    vectors = vector_low.astype(jnp.float32)
    seqs_here, rows_here, model_width = decoder_input.shape
    shard_index = lax.axis_index("index")
    length = rows_here * lax.axis_size("index")
    ffn_width = expand_low.shape[1]
    self_query = (project(decoder_input, attention_low[0]) + vectors[0]).astype(jnp.bfloat16)
    self_key = project(decoder_input, attention_low[1]).astype(jnp.bfloat16)
    self_value = (project(decoder_input, attention_low[2]) + vectors[1]).astype(jnp.bfloat16)
    key_all, value_all = (
        lax.all_gather(self_key, "index", axis=1, tiled=True),
        lax.all_gather(self_value, "index", axis=1, tiled=True),
    )
    query_place = shard_index * rows_here + jnp.arange(rows_here)
    causal = (jnp.arange(length)[None, :] <= query_place[:, None])[None, None]
    self_mixed, self_prob, self_peak, self_total = attend_forward(
        self_query, key_all, value_all, 0.0, causal
    )
    first_in = (
        decoder_input.astype(jnp.float32) + project(self_mixed, attention_low[3]) + vectors[2]
    )
    first_out, first_back = jax.vjp(layer_norm, first_in, vectors[11], vectors[12])
    first_low = first_out.astype(jnp.bfloat16)
    cross_query = (project(first_low, attention_low[4]) + vectors[3]).astype(jnp.bfloat16)
    cross_key = project(encoder_memory, attention_low[5]).astype(jnp.bfloat16)
    cross_value = (project(encoder_memory, attention_low[6]) + vectors[4]).astype(jnp.bfloat16)
    memory_keys, memory_values = (
        lax.all_gather(cross_key, "index", axis=1, tiled=True),
        lax.all_gather(cross_value, "index", axis=1, tiled=True),
    )
    question_full = lax.all_gather(question_vectors, "index", axis=1, tiled=True)
    passages_here = passage_vectors.shape[0]
    local_ids = passage_ids - shard_index * passages_here
    owned_slot = (local_ids >= 0) & (local_ids < passages_here)
    picked = passage_vectors[jnp.clip(local_ids, 0, passages_here - 1)]
    local_scores = jnp.einsum(
        "sc,skc->sk", question_full, picked, preferred_element_type=jnp.float32
    )
    slots = passage_ids.shape[1]
    usable = jnp.arange(slots)[None, :] < valid_count[:, None]
    local_peak = jnp.max(jnp.where(owned_slot & usable, local_scores, negative_fill), axis=1)
    maximum = lax.pmax(local_peak, "index")
    local_exp = jnp.where(owned_slot & usable, jnp.exp(local_scores - maximum[:, None]), 0.0)
    exponent, scores = lax.psum((local_exp, jnp.where(owned_slot, local_scores, 0.0)), "index")
    masked = jnp.where(usable, scores, negative_fill)
    partition = jnp.sum(exponent, axis=1)
    passage_prob = exponent / partition[:, None]
    log_prior = masked - maximum[:, None] - jnp.log(partition)[:, None]
    memory_total = memory_keys.shape[1]
    bias_rows = jnp.repeat(log_prior, MEM_P, axis=1)
    key_bias = bias_rows[:, None, None, :]
    key_usable = ((jnp.arange(memory_total) // MEM_P)[None, :] < valid_count[:, None])[
        :, None, None, :
    ]
    cross_mixed, cross_prob, cross_peak, cross_total = attend_forward(
        cross_query, memory_keys, memory_values, key_bias, key_usable
    )
    second_in = first_out + project(cross_mixed, attention_low[7]) + vectors[5]
    second_out, second_back = jax.vjp(layer_norm, second_in, vectors[13], vectors[14])
    second_low = second_out.astype(jnp.bfloat16)
    inner_act = project(second_low, expand_low) + vectors[6:10].reshape(ffn_width)
    activated, gelu_back = jax.vjp(partial(jax.nn.gelu, approximate=False), inner_act)
    activ_low = activated.astype(jnp.bfloat16)
    third_in = second_out + project(activ_low, contract_low) + vectors[10]
    layer_output, third_back = jax.vjp(layer_norm, third_in, vectors[15], vectors[16])
    grad_third, gain_three, shift_three = third_back(output_grad.astype(jnp.float32))
    grad_ffn_low = grad_third.astype(jnp.bfloat16)
    grad_contract = weight_grad(activ_low, grad_ffn_low)
    (grad_inner,) = gelu_back(project_back(grad_ffn_low, contract_low))
    grad_inner_low = grad_inner.astype(jnp.bfloat16)
    grad_expand = weight_grad(second_low, grad_inner_low)
    grad_second = grad_third + project_back(grad_inner_low, expand_low)
    grad_second_in, gain_two, shift_two = second_back(grad_second)
    grad_cross_low = grad_second_in.astype(jnp.bfloat16)
    grad_cmix = project_back(grad_cross_low, attention_low[7]).astype(jnp.bfloat16)
    cross_score, cross_inner = score_grads(grad_cmix, cross_prob, memory_values)
    grad_cq = to_queries(cross_score, memory_keys)
    prior_part = (
        jnp.sum(cross_score, axis=(1, 2), dtype=jnp.float32)
        .reshape(seqs_here, slots, MEM_P)
        .sum(axis=-1)
    )
    prior_grad = jnp.where(usable, lax.psum(prior_part, "index"), 0.0)
    score_doc = jnp.where(
        usable, prior_grad - passage_prob * jnp.sum(prior_grad, axis=1, keepdims=True), 0.0
    )
    question_part = jnp.einsum(
        "sk,skc->sc",
        jnp.where(owned_slot, score_doc, 0.0),
        picked.astype(jnp.float32),
        precision=lax.Precision.HIGHEST,
    )
    question_gradient = lax.psum_scatter(question_part, "index", scatter_dimension=1, tiled=True)
    grad_cq_low = grad_cq.astype(jnp.bfloat16)
    grad_first = grad_second_in + project_back(grad_cq_low, attention_low[4])
    ck_part, cv_part = to_keys(cross_score, cross_prob, cross_query, grad_cmix)
    grad_ck, grad_cv = (
        lax.psum_scatter(
            ck_part.astype(jnp.bfloat16), "index", scatter_dimension=1, tiled=True
        ).astype(jnp.float32),
        lax.psum_scatter(
            cv_part.astype(jnp.bfloat16), "index", scatter_dimension=1, tiled=True
        ).astype(jnp.float32),
    )
    grad_ck_low = grad_ck.astype(jnp.bfloat16)
    grad_cv_low = grad_cv.astype(jnp.bfloat16)
    memory_gradient = project_back(grad_ck_low, attention_low[5]) + project_back(
        grad_cv_low, attention_low[6]
    )
    grad_first_in, gain_one, shift_one = first_back(grad_first)
    grad_self_low = grad_first_in.astype(jnp.bfloat16)
    grad_smix = project_back(grad_self_low, attention_low[3]).astype(jnp.bfloat16)
    self_score, row_inner = score_grads(grad_smix, self_prob, value_all)
    grad_sq = to_queries(self_score, key_all)
    key_part, value_part = to_keys(self_score, self_prob, self_query, grad_smix)
    grad_sk, grad_sv = (
        lax.psum_scatter(
            key_part.astype(jnp.bfloat16), "index", scatter_dimension=1, tiled=True
        ).astype(jnp.float32),
        lax.psum_scatter(
            value_part.astype(jnp.bfloat16), "index", scatter_dimension=1, tiled=True
        ).astype(jnp.float32),
    )
    grad_sq_low = grad_sq.astype(jnp.bfloat16)
    grad_sk_low = grad_sk.astype(jnp.bfloat16)
    grad_sv_low = grad_sv.astype(jnp.bfloat16)
    input_gradient = (
        grad_first_in
        + project_back(grad_sq_low, attention_low[0])
        + project_back(grad_sk_low, attention_low[1])
        + project_back(grad_sv_low, attention_low[2])
    )
    attention_grads = jnp.stack(
        [
            weight_grad(decoder_input, grad_sq_low),
            weight_grad(decoder_input, grad_sk_low),
            weight_grad(decoder_input, grad_sv_low),
            weight_grad(self_mixed, grad_self_low),
            weight_grad(first_low, grad_cq_low),
            weight_grad(encoder_memory, grad_ck_low),
            weight_grad(encoder_memory, grad_cv_low),
            weight_grad(cross_mixed, grad_cross_low),
        ]
    )
    vector_grads = jnp.concatenate(
        [
            jnp.stack(
                [
                    row_total(grad_sq),
                    row_total(grad_sv),
                    row_total(grad_first_in),
                    row_total(grad_cq),
                    row_total(grad_cv),
                    row_total(grad_second_in),
                ]
            ),
            row_total(grad_inner).reshape(ffn_width // model_width, model_width),
            jnp.stack(
                [
                    row_total(grad_third),
                    gain_one,
                    shift_one,
                    gain_two,
                    shift_two,
                    gain_three,
                    shift_three,
                ]
            ),
        ]
    )
    attention_sum, expand_sum, contract_sum, vector_sum = (
        lax.psum_scatter(attention_grads, ("dp", "index"), scatter_dimension=1, tiled=True),
        lax.psum_scatter(grad_expand, ("dp", "index"), scatter_dimension=0, tiled=True),
        lax.psum_scatter(grad_contract, ("dp", "index"), scatter_dimension=0, tiled=True),
        lax.psum_scatter(vector_grads, ("dp", "index"), scatter_dimension=1, tiled=True),
    )
    new_attention = adam_update(
        attention_weight,
        attention_mean,
        attention_square,
        attention_sum,
        rate_attention,
        decay_matrix,
    )
    new_expand = adam_update(
        expand_weight, expand_mean, expand_square, expand_sum, rate_expand, decay_matrix
    )
    new_contract = adam_update(
        contract_weight, contract_mean, contract_square, contract_sum, rate_contract, decay_matrix
    )
    new_vector = adam_update(
        vector_params, vector_mean, vector_square, vector_sum, rate_vector, 0.0
    )
    return (
        layer_output.astype(jnp.bfloat16),
        input_gradient,
        memory_gradient,
        question_gradient,
        new_attention[0],
        new_attention[1],
        new_attention[2],
        new_expand[0],
        new_expand[1],
        new_expand[2],
        new_contract[0],
        new_contract[1],
        new_contract[2],
        new_vector[0],
        new_vector[1],
        new_vector[2],
    )


NT = (((1,), (1,)), ((), ()))
NN = (((1,), (0,)), ((), ()))
TN = (((0,), (0,)), ((), ()))
CHIPS = 4
DP_ORDER = (0, 2, 1, 3)
VMEM_LIMIT = 56 << 20


def dot(left_side, right_side, dims):
    return lax.dot_general(left_side, right_side, dims, preferred_element_type=jnp.float32)


def norm_parts(hidden):
    center = hidden - jnp.mean(hidden, axis=-1, keepdims=True)
    inverse = lax.rsqrt(jnp.mean(center * center, axis=-1, keepdims=True) + norm_eps)
    return center * inverse, inverse


def norm_back(gradient, unit, inverse, gain):
    scaled = gradient * gain
    return inverse * (
        scaled
        - jnp.mean(scaled, axis=-1, keepdims=True)
        - unit * jnp.mean(scaled * unit, axis=-1, keepdims=True)
    )


def column_sum(values):
    return jnp.sum(values, axis=0, keepdims=True)


def join(parts, place=None):
    picked = [parts[j] if place is None else parts[j, place] for j in range(parts.shape[0])]
    return jnp.concatenate(
        [block.reshape(block.shape[0] * block.shape[1], block.shape[2]) for block in picked],
        axis=1,
    )


def spread(out_ref, value):
    count, seqs, rows, width = out_ref.shape
    for j in range(count):
        out_ref[j] = value[:, j * width : (j + 1) * width].reshape(seqs, rows, width)


def times(activation, weight):
    count, groups, rows, width = weight.shape
    depth = count * rows
    total = None
    for d in range(groups):
        part = dot(
            activation[:, d * depth : (d + 1) * depth], weight[:, d].reshape(depth, width), NN
        )
        total = part if total is None else total + part
    return total


def times_back(gradient, weight):
    count, groups, rows, width = weight.shape
    depth = count * rows
    return jnp.concatenate(
        [dot(gradient, weight[:, d].reshape(depth, width), NT) for d in range(groups)], axis=1
    )


def outer(out_ref, left_side, gradient):
    count, groups, rows, width = out_ref.shape
    depth = count * rows
    for d in range(groups):
        out_ref[:, d] = (
            dot(left_side[:, d * depth : (d + 1) * depth], gradient, TN)
            .astype(jnp.bfloat16)
            .reshape(count, rows, width)
        )


def whole(array):
    return pl.BlockSpec(array.shape, lambda *_, rank=len(array.shape): (0,) * rank)


def shape(dims, dtype):
    return jax.ShapeDtypeStruct(tuple(dims), dtype)


def params():
    return pltpu.CompilerParams(vmem_limit_bytes=VMEM_LIMIT)


def cost(flops, moved):
    return pl.CostEstimate(flops=int(flops) // 16, bytes_accessed=int(moved) // 16, transcendentals=0)


def in_head(dims, head_width, head):
    return lax.broadcasted_iota(jnp.int32, dims, 1) // head_width == head


def attend_forward_kernel(causal, head_width, q_ref, k_ref, v_ref, bias_ref, out_ref, stat_ref):
    count, _, tile, width = q_ref.shape
    keys = k_ref.shape[0] * k_ref.shape[2]
    key_rows, values = k_ref[...].reshape(keys, width), v_ref[...].reshape(keys, width)
    step = 4
    rows = step * tile
    for b in range(count // step):
        queries = q_ref[b * step : (b + 1) * step].reshape(rows, width)
        seen = (b + 1) * rows if causal else keys
        mixed = None
        for h in range(width // head_width):
            mask = in_head((rows, width), head_width, h)
            scores = dot(
                jnp.where(mask, queries * 0.125, 0).astype(jnp.bfloat16), key_rows[:seen], NT
            )
            if causal:
                corner = scores[:, seen - rows :]
                corner = jnp.where(
                    lax.broadcasted_iota(jnp.int32, corner.shape, 1)
                    <= lax.broadcasted_iota(jnp.int32, corner.shape, 0),
                    corner,
                    negative_fill,
                )
                if b == 0:
                    scores = corner
                else:
                    scores = jnp.concatenate([scores[:, : seen - rows], corner], axis=1)
            else:
                scores = scores + bias_ref[0]
            peak = jnp.max(scores, axis=1, keepdims=True)
            exponent = jnp.exp(scores - peak)
            total = jnp.sum(exponent, axis=1, keepdims=True)
            part = dot(exponent.astype(jnp.bfloat16), values[:seen], NN) * (1.0 / total)
            mixed = part if mixed is None else jnp.where(mask, part, mixed)
            log_total = jnp.broadcast_to(peak + jnp.log(total), (rows, 128))
            stat_ref[0, h : h + 1, b * rows : (b + 1) * rows] = log_total.T[0:1]
        out_ref[b * step : (b + 1) * step] = mixed.astype(jnp.bfloat16).reshape(
            step, 1, tile, width
        )


def attend_backward_kernel(
    causal,
    head_width,
    q_ref,
    k_ref,
    v_ref,
    grad_ref,
    stat_ref,
    bias_ref,
    _,
    dq_ref,
    dkv_ref,
    prior_ref,
    dk_sum,
    dv_sum,
    prior_sum,
):
    count, _, tile, width = q_ref.shape
    keys = k_ref.shape[0] * k_ref.shape[2]
    key_rows, values = k_ref[...].reshape(keys, width), v_ref[...].reshape(keys, width)
    step = 2
    rows = step * tile
    if not causal:
        bias = jnp.broadcast_to(bias_ref[0], (128, keys)).T[:, :1]
    dk_sum[...] = jnp.zeros_like(dk_sum)
    dv_sum[...] = jnp.zeros_like(dv_sum)
    if not causal:
        prior_sum[...] = jnp.zeros_like(prior_sum)
    for b in range(count // step):
        queries = q_ref[b * step : (b + 1) * step].reshape(rows, width)
        gradient = grad_ref[b * step : (b + 1) * step].reshape(rows, width)
        seen = (b + 1) * rows if causal else keys
        query_grad = None
        for h in range(width // head_width):
            mask = in_head((rows, width), head_width, h)
            one_query = jnp.where(mask, queries * 0.125, 0).astype(jnp.bfloat16)
            one_grad = jnp.where(mask, gradient, 0).astype(jnp.bfloat16)
            scores = dot(key_rows[:seen], one_query, NT)
            if causal:
                corner = scores[seen - rows :]
                corner = jnp.where(
                    lax.broadcasted_iota(jnp.int32, corner.shape, 0)
                    <= lax.broadcasted_iota(jnp.int32, corner.shape, 1),
                    corner,
                    negative_fill,
                )
                if b == 0:
                    scores = corner
                else:
                    scores = jnp.concatenate([scores[: seen - rows], corner], axis=0)
            else:
                scores = scores + bias
            prob = jnp.exp(scores - stat_ref[0, h : h + 1, b * rows : (b + 1) * rows])
            grad_prob = dot(values[:seen], one_grad, NT)
            inner = jnp.sum(prob * grad_prob, axis=0, keepdims=True)
            grad_score = prob * (grad_prob - inner)
            score_low = grad_score.astype(jnp.bfloat16)
            dv_sum[:seen] += dot(prob.astype(jnp.bfloat16), one_grad, NN)
            dk_sum[:seen] += dot(score_low, one_query, NN)
            if not causal:
                partial_sum = grad_score[:, :128]
                for piece in range(128, rows, 128):
                    partial_sum = partial_sum + grad_score[:, piece : piece + 128]
                prior_sum[...] += partial_sum
            part = dot(score_low, key_rows[:seen], TN)
            query_grad = part if query_grad is None else jnp.where(mask, part, query_grad)
        dq_ref[b * step : (b + 1) * step] = (
            (query_grad * 0.125).astype(jnp.bfloat16).reshape(step, 1, tile, width)
        )
    dkv_ref[:, 0] = dk_sum[...].astype(jnp.bfloat16).reshape(k_ref.shape)
    dkv_ref[:, 1] = dv_sum[...].astype(jnp.bfloat16).reshape(k_ref.shape)
    if causal:
        prior_ref[...] = jnp.zeros_like(prior_ref)
    else:
        prior_ref[0] = column_sum(prior_sum[...].T)


def pick(array, place):
    count, _, _, rows, width = array.shape
    return pl.BlockSpec((count, None, 1, rows, width), lambda s: (0, place, s, 0, 0))


def attend(causal, queries, query_at, keys, key_at, value_at, bias):
    count, _, seqs, tile, width = queries.shape
    key_rows = keys.shape[0] * keys.shape[3]
    head_width = width * count // HEADS
    length = count * tile
    heads = width // head_width
    return pl.pallas_call(
        partial(attend_forward_kernel, causal, head_width),
        grid=(seqs,),
        in_specs=[
            pick(queries, query_at),
            pick(keys, key_at),
            pick(keys, value_at),
            pl.BlockSpec(memory_space=pl.ANY)
            if causal
            else pl.BlockSpec((1, 1, key_rows), lambda s: (s, 0, 0)),
        ],
        out_specs=[
            pl.BlockSpec((count, 1, tile, width), lambda s: (0, s, 0, 0)),
            pl.BlockSpec((1, heads, length), lambda s: (s, 0, 0)),
        ],
        out_shape=[
            shape((count, seqs, tile, width), jnp.bfloat16),
            shape((seqs, heads, length), jnp.float32),
        ],
        compiler_params=params(),
        cost_estimate=cost(
            16 * seqs * length * key_rows * width, 4 * seqs * (length + key_rows) * width
        ),
        name="attend_self" if causal else "attend_memory",
    )(queries, keys, keys, bias)


def attend_back(
    causal, queries, query_at, keys, key_at, value_at, gradient, stat, bias, after
):
    count, _, seqs, tile, width = queries.shape
    key_tile = keys.shape[3]
    key_rows = count * key_tile
    head_width = width * count // HEADS
    length = count * tile
    heads = width // head_width
    return pl.pallas_call(
        partial(attend_backward_kernel, causal, head_width),
        grid=(seqs,),
        in_specs=[
            pick(queries, query_at),
            pick(keys, key_at),
            pick(keys, value_at),
            pl.BlockSpec((count, 1, tile, width), lambda s: (0, s, 0, 0)),
            pl.BlockSpec((1, heads, length), lambda s: (s, 0, 0)),
            pl.BlockSpec(memory_space=pl.ANY)
            if causal
            else pl.BlockSpec((1, 1, key_rows), lambda s: (s, 0, 0)),
            pl.BlockSpec(memory_space=pl.ANY),
        ],
        out_specs=[
            pl.BlockSpec((count, 1, tile, width), lambda s: (0, s, 0, 0)),
            pl.BlockSpec((count, 2, 1, key_tile, width), lambda s: (0, 0, s, 0, 0)),
            pl.BlockSpec((1, 1, key_rows), lambda s: (s, 0, 0)),
        ],
        out_shape=[
            shape((count, seqs, tile, width), jnp.bfloat16),
            shape((count, 2, seqs, key_tile, width), jnp.bfloat16),
            shape((seqs, 1, key_rows), jnp.float32),
        ],
        scratch_shapes=[
            pltpu.VMEM((key_rows, width), jnp.float32),
            pltpu.VMEM((key_rows, width), jnp.float32),
            pltpu.VMEM((key_rows, 128), jnp.float32),
        ],
        compiler_params=params(),
        cost_estimate=cost(
            40 * seqs * length * key_rows * width, 8 * seqs * (length + key_rows) * width
        ),
        name="attend_self_back" if causal else "attend_memory_back",
    )(queries, keys, keys, gradient, stat, bias, after)


def take_columns(scratch, slices, first):
    width = slices.shape[3]
    depth = scratch.shape[0]
    rows = depth // (slices.shape[0] * slices.shape[1])
    for m in range(scratch.shape[1] // width):
        start = (first + m) * rows
        scratch[:, m * width : (m + 1) * width] = slices[:, :, start : start + rows].reshape(
            depth, width
        )


def columns_kernel(first, start, seqs, rows, row_ref, slice_ref, bias_ref, out_ref, weight, taken, sem):
    def copy(i):
        return pltpu.make_async_copy(
            row_ref.at[i, :, pl.ds(start, rows)], taken.at[i], sem.at[i]
        )

    count, many = out_ref.shape[:2]
    width = out_ref.shape[4]
    for i in range(count):
        copy(i).start()
    take_columns(weight, slice_ref, first)
    for i in range(count):
        copy(i).wait()
        result = dot(taken[i].reshape(seqs * rows, weight.shape[0]), weight[...], NN) + bias_ref[...]
        for m in range(many):
            out_ref[i, m] = (
                result[:, m * width : (m + 1) * width]
                .astype(jnp.bfloat16)
                .reshape(seqs, rows, width)
            )


def project_columns(name, gathered_rows, start, rows, slices, first, many, bias):
    count, seqs, _, depth = gathered_rows.shape
    width = slices.shape[3]
    out = shape((count, many, seqs, rows, width), jnp.bfloat16)
    return pl.pallas_call(
        partial(columns_kernel, first, start, seqs, rows),
        grid=(1,),
        in_specs=[pl.BlockSpec(memory_space=pl.ANY), whole(slices), whole(bias)],
        out_specs=whole(out),
        out_shape=out,
        scratch_shapes=[
            pltpu.VMEM((depth, many * width), jnp.bfloat16),
            pltpu.VMEM((count, seqs, rows, depth), jnp.bfloat16),
            pltpu.SemaphoreType.DMA((count,)),
        ],
        compiler_params=params(),
        cost_estimate=cost(
            2 * many * count * seqs * rows * depth * width, 2 * count * seqs * rows * depth
        ),
        name=name,
    )(gathered_rows, slices, bias)


def columns_back_kernel(first, start, order, row_ref, *refs):
    grad_refs, (slice_ref, mine_out, other_out, dw_ref, bias_ref) = refs[:-12], refs[-12:-7]
    weight, taken, gradients, moved, total, in_sem, out_sem = refs[-7:]
    count, seqs, rows, depth = taken.shape
    half = count // 2

    def bring(r):
        return pltpu.make_async_copy(
            row_ref.at[order[r], :, pl.ds(start, rows)], taken.at[r], in_sem.at[r]
        )

    def send(r):
        there = (mine_out, other_out)[r // half].at[r % half, 0]
        return pltpu.make_async_copy(moved.at[r], there, out_sem.at[r])

    for r in range(count):
        bring(r).start()
    take_columns(weight, slice_ref, first)
    size = seqs * rows
    for r in range(count):
        i = order[r]
        pieces = []
        for grad_ref in grad_refs:
            width = grad_ref.shape[-1]
            for m in range(grad_ref.shape[1] if len(grad_ref.shape) == 5 else 1):
                piece = grad_ref[i, m] if len(grad_ref.shape) == 5 else grad_ref[i]
                pieces.append(piece.reshape(size, width))
        gradient = jnp.concatenate(pieces, axis=1)
        gradients[r * size : (r + 1) * size] = gradient
        moved[r] = dot(gradient, weight[...], NT).astype(jnp.bfloat16)
        send(r).start()
    whole_gradient = gradients[...]
    bias_ref[...] = column_sum(whole_gradient.astype(jnp.float32))
    for r in range(count):
        bring(r).wait()
    total[...] = dot(whole_gradient, taken[...].reshape(count * size, depth), TN)
    groups, shards, all_rows, _ = dw_ref.shape
    part = depth // (groups * shards)
    for m in range(all_rows // part):
        dw_ref[:, :, m * part : (m + 1) * part] = (
            total[m * width : (m + 1) * width]
            .T.astype(jnp.bfloat16)
            .reshape(groups, shards, part, width)
        )
    for r in range(count):
        send(r).wait()


def project_columns_back(name, order, gathered_rows, start, rows, gradients, slices, first, many):
    count, seqs, _, depth = gathered_rows.shape
    half = count // 2
    groups, shards, _, width = slices.shape
    part = depth // (groups * shards)
    anywhere = pl.BlockSpec(memory_space=pl.ANY)
    halves = shape((half, 1, seqs * rows, depth), jnp.bfloat16)
    dw_shape = shape((groups, shards, many * part, width), jnp.bfloat16)
    bias = shape((1, many * width), jnp.float32)
    return pl.pallas_call(
        partial(columns_back_kernel, first, start),
        grid_spec=pltpu.PrefetchScalarGridSpec(
            num_scalar_prefetch=1,
            grid=(1,),
            in_specs=[anywhere, *[whole(array) for array in gradients], whole(slices)],
            out_specs=[anywhere, anywhere, whole(dw_shape), whole(bias)],
            scratch_shapes=[
                pltpu.VMEM((depth, many * width), jnp.bfloat16),
                pltpu.VMEM((count, seqs, rows, depth), jnp.bfloat16),
                pltpu.VMEM((count * seqs * rows, many * width), jnp.bfloat16),
                pltpu.VMEM((count, seqs * rows, depth), jnp.bfloat16),
                pltpu.VMEM((many * width, depth), jnp.float32),
                pltpu.SemaphoreType.DMA((count,)),
                pltpu.SemaphoreType.DMA((count,)),
            ],
        ),
        out_shape=[halves, halves, dw_shape, bias],
        compiler_params=params(),
        cost_estimate=cost(
            4 * many * count * seqs * rows * depth * width, 4 * count * seqs * rows * depth
        ),
        name=name,
    )(order, gathered_rows, *gradients, slices)


def gathered(weights, width, place):
    count, groups, rows, _ = weights.shape
    return pl.BlockSpec((count, groups, rows, width), lambda *_: (0, 0, 0, place))


def first_kernel(
    mixed_ref, x_ref, out_w, query_w, vector_ref, _, mixed_out, in_out, low_out, query_out
):
    mixed = join(mixed_ref)
    mixed_out[...] = mixed
    first_in = x_ref[...].astype(jnp.float32) + times(mixed, out_w) + vector_ref[2:3]
    in_out[...] = first_in
    unit, _ = norm_parts(first_in)
    low = (unit * vector_ref[11:12] + vector_ref[12:13]).astype(jnp.bfloat16)
    low_out[...] = low
    spread(query_out, (times(low, query_w) + vector_ref[3:4]).astype(jnp.bfloat16))


def first_forward(mixed, x_rows, weights, vectors, after):
    rows, depth = x_rows.shape
    return pl.pallas_call(
        first_kernel,
        grid=(1,),
        in_specs=[
            whole(mixed),
            whole(x_rows),
            gathered(weights, depth, 0),
            gathered(weights, depth, 1),
            whole(vectors),
            pl.BlockSpec(memory_space=pl.ANY),
        ],
        out_specs=[whole(x_rows), whole(x_rows), whole(x_rows), whole(mixed)],
        out_shape=[
            shape((rows, depth), jnp.bfloat16),
            shape((rows, depth), jnp.float32),
            shape((rows, depth), jnp.bfloat16),
            shape(mixed.shape, jnp.bfloat16),
        ],
        compiler_params=params(),
        cost_estimate=cost(4 * rows * depth * depth, 4 * depth * depth),
        name="first_forward",
    )(mixed, x_rows, weights, weights, vectors, after)


def ffn_kernel(
    order,
    places,
    mixed_ref,
    first_ref,
    out_w,
    vector_ref,
    bias_ref,
    grad_ref,
    wide_ref,
    *refs,
):
    contract_refs, refs = refs[:8], refs[8:]
    mixed_out, layer_out, wide_grad = refs[:3]
    contract_grads, refs = refs[3:11], refs[11:]
    dbias_ref, second_grad, cross_low, mixed_grad, stat_out, columns, contracts = refs[:7]
    active, slope, low, third_low, second_in, total, wide_sem, contract_sem = refs[7:]
    blocks, count, groups, rows, block = columns.shape
    part = block // CHIPS
    depth = vector_ref.shape[1]

    def wide_copies(t, array, outward):
        result = []
        for k in range(CHIPS):
            column = pl.multiple_of(order[t % 2 * CHIPS + k] * part, part)
            row = pl.multiple_of(places[t // 2] * rows, rows)
            there = array.at[:, :, pl.ds(row, rows), pl.ds(column, part)]
            here = columns.at[t, :, :, :, pl.ds(k * part, part)]
            ends = (here, there) if outward else (there, here)
            result.append(pltpu.make_async_copy(*ends, wide_sem.at[t, k]))
        return result

    def contract_copies(t, pieces, outward):
        near, far = divmod(DP_ORDER[t // 2], 2)
        first = pieces[t % 2 * 4 + far].at[near]
        last = pieces[t % 2 * 4 + 2 + near].at[far]
        result = []
        for half, there in enumerate((first, last)):
            here = contracts.at[t, pl.ds(half * CHIPS // 2, CHIPS // 2)]
            ends = (here, there) if outward else (there, here)
            result.append(pltpu.make_async_copy(*ends, contract_sem.at[t, half]))
        return result

    for t in range(blocks):
        for copy in wide_copies(t, wide_ref, False):
            copy.start()
        for copy in contract_copies(t, contract_refs, False):
            copy.start()

    mixed = join(mixed_ref)
    mixed_out[...] = mixed
    unit, _ = norm_parts(first_ref[...])
    second_in[...] = (
        unit * vector_ref[11:12] + vector_ref[12:13] + times(mixed, out_w) + vector_ref[5:6]
    )
    unit, _ = norm_parts(second_in[...])
    second = unit * vector_ref[13:14] + vector_ref[14:15]
    low[...] = second.astype(jnp.bfloat16)
    total[...] = second + vector_ref[10:11]

    def shard(t, k):
        return places[t // 2] * count + order[t % 2 * CHIPS + k]

    for t in range(blocks):
        for copy in wide_copies(t, wide_ref, False):
            copy.wait()
        bias = jnp.concatenate([bias_ref[pl.ds(shard(t, k), 1)] for k in range(CHIPS)], axis=1)
        inner = times(low[...], columns.at[t]) + bias
        phi = 0.5 + 0.5 * lax.erf(inner * (0.5**0.5))
        out = (inner * phi).astype(jnp.bfloat16)
        active[t] = out
        slope[t] = phi + inner * jnp.exp(-0.5 * inner * inner) * 0.3989422804014327
        for copy in contract_copies(t, contract_refs, False):
            copy.wait()
        total[...] += dot(out, contracts[t].reshape(block, depth), NN)

    unit, inverse = norm_parts(total[...])
    gain = vector_ref[15:16]
    layer_out[...] = (unit * gain + vector_ref[16:17]).astype(jnp.bfloat16)
    gradient = grad_ref[...].astype(jnp.float32)
    grad_third = norm_back(gradient, unit, inverse, gain)
    stat_out[...] = jnp.zeros_like(stat_out)
    stat_out[0:1] = column_sum(grad_third)
    stat_out[1:2] = column_sum(gradient * unit)
    stat_out[2:3] = column_sum(gradient)
    total[...] = grad_third
    third_low[...] = grad_third.astype(jnp.bfloat16)
    turned = low[...].T

    for t in range(blocks):
        grad_inner = dot(third_low[...], contracts[t].reshape(block, depth), NT) * slope[t]
        inner_low = grad_inner.astype(jnp.bfloat16)
        sums = column_sum(grad_inner)
        for k in range(CHIPS):
            dbias_ref[pl.ds(shard(t, k), 1)] = sums[:, k * part : (k + 1) * part]
        contracts[t] = (
            dot(active[t], third_low[...], TN).astype(jnp.bfloat16).reshape(CHIPS, part, depth)
        )
        for copy in contract_copies(t, contract_grads, True):
            copy.start()
        total[...] += times_back(inner_low, columns.at[t])
        result = dot(turned, inner_low, NN).astype(jnp.bfloat16)
        for d in range(groups):
            columns[t, :, d] = result[d * count * rows : (d + 1) * count * rows].reshape(
                count, rows, block
            )
        for copy in wide_copies(t, wide_grad, True):
            copy.start()

    unit, inverse = norm_parts(second_in[...])
    grad_second = total[...]
    grad_in = norm_back(grad_second, unit, inverse, vector_ref[13:14])
    second_grad[...] = grad_in
    grad_low = grad_in.astype(jnp.bfloat16)
    cross_low[...] = grad_low
    spread(mixed_grad, times_back(grad_low, out_w).astype(jnp.bfloat16))
    stat_out[8:9] = column_sum(grad_in)
    stat_out[9:10] = column_sum(grad_second * unit)
    stat_out[10:11] = column_sum(grad_second)
    for t in range(blocks):
        for copy in contract_copies(t, contract_grads, True) + wide_copies(t, wide_grad, True):
            copy.wait()


def ffn(orders, mixed, first_in, wide, contract, vectors, bias, output_grad):
    rows, depth = first_in.shape
    hidden = bias.size
    block = depth // 2
    count, groups, all_rows, _ = wide.shape
    part = depth // (count * groups)
    blocks = hidden // block
    full = whole(first_in)
    anywhere = pl.BlockSpec(memory_space=pl.ANY)
    heads_out = shape(mixed.shape, jnp.bfloat16)
    stats = shape((16, depth), jnp.float32)
    return pl.pallas_call(
        ffn_kernel,
        grid_spec=pltpu.PrefetchScalarGridSpec(
            num_scalar_prefetch=2,
            grid=(1,),
            in_specs=[
                whole(mixed),
                full,
                pl.BlockSpec((count, groups, part, depth), lambda *_: (0, 0, groups, 0)),
                whole(vectors),
                whole(bias),
                full,
                *[anywhere] * 9,
            ],
            out_specs=[
                full,
                full,
                *[anywhere] * 9,
                whole(bias),
                full,
                full,
                whole(heads_out),
                whole(stats),
            ],
            scratch_shapes=[
                pltpu.VMEM((blocks, count, groups, part, block), jnp.bfloat16),
                pltpu.VMEM((blocks, CHIPS) + contract[0].shape[2:], jnp.bfloat16),
                pltpu.VMEM((blocks, rows, block), jnp.bfloat16),
                pltpu.VMEM((blocks, rows, block), jnp.float32),
                pltpu.VMEM((rows, depth), jnp.bfloat16),
                pltpu.VMEM((rows, depth), jnp.bfloat16),
                pltpu.VMEM((rows, depth), jnp.float32),
                pltpu.VMEM((rows, depth), jnp.float32),
                pltpu.SemaphoreType.DMA((blocks, CHIPS)),
                pltpu.SemaphoreType.DMA((blocks, 2)),
            ],
        ),
        out_shape=[
            shape((rows, depth), jnp.bfloat16),
            shape((rows, depth), jnp.bfloat16),
            shape((count, groups, all_rows - part, depth), jnp.bfloat16),
            *[shape(piece.shape, jnp.bfloat16) for piece in contract],
            shape(bias.shape, jnp.float32),
            shape((rows, depth), jnp.float32),
            shape((rows, depth), jnp.bfloat16),
            heads_out,
            stats,
        ],
        compiler_params=params(),
        cost_estimate=cost(12 * rows * depth * hidden, 16 * depth * hidden),
        name="ffn",
    )(*orders, mixed, first_in, wide, vectors, bias, output_grad, wide, *contract)


def first_back_kernel(
    dq_ref,
    second_grad,
    first_ref,
    out_w,
    query_w,
    vector_ref,
    _,
    query_low,
    grad_in_out,
    self_low,
    mixed_grad,
    stat_out,
):
    query_grad = join(dq_ref)
    query_low[...] = query_grad
    grad_first = second_grad[...] + times_back(query_grad, query_w)
    unit, inverse = norm_parts(first_ref[...])
    grad_in = norm_back(grad_first, unit, inverse, vector_ref[11:12])
    grad_in_out[...] = grad_in
    grad_low = grad_in.astype(jnp.bfloat16)
    self_low[...] = grad_low
    spread(mixed_grad, times_back(grad_low, out_w).astype(jnp.bfloat16))
    stat_out[...] = jnp.zeros_like(stat_out)
    stat_out[0:1] = column_sum(query_grad.astype(jnp.float32))
    stat_out[1:2] = column_sum(grad_in)
    stat_out[2:3] = column_sum(grad_first * unit)
    stat_out[3:4] = column_sum(grad_first)


def first_back(dq, second_grad, first_in, weights, vectors, after):
    rows, depth = first_in.shape
    full = whole(first_in)
    return pl.pallas_call(
        first_back_kernel,
        grid=(1,),
        in_specs=[
            whole(dq),
            full,
            full,
            gathered(weights, depth, 0),
            gathered(weights, depth, 1),
            whole(vectors),
            pl.BlockSpec(memory_space=pl.ANY),
        ],
        out_specs=[full, full, full, whole(dq), pl.BlockSpec((8, depth), lambda *_: (0, 0))],
        out_shape=[
            shape((rows, depth), jnp.bfloat16),
            shape((rows, depth), jnp.float32),
            shape((rows, depth), jnp.bfloat16),
            shape(dq.shape, jnp.bfloat16),
            shape((8, depth), jnp.float32),
        ],
        compiler_params=params(),
        cost_estimate=cost(4 * rows * depth * depth, 4 * depth * depth),
        name="first_back",
    )(dq, second_grad, first_in, weights, weights, vectors, after)


def weight_grads_kernel(
    order,
    mixed,
    self_low,
    first_low,
    query_low,
    cross,
    cross_low,
    mine_out,
    other_out,
    result,
):
    step = pl.program_id(0)
    pairs = ((mixed, self_low), (first_low, query_low), (cross, cross_low))
    half, groups, part, _ = mine_out.shape
    for m, (left_side, gradient) in enumerate(pairs):

        @pl.when(step == m)
        def _(left_side=left_side, gradient=gradient):
            result[...] = dot(left_side[...], gradient[...], TN).astype(jnp.bfloat16)

    for d in range(groups):
        for k in range(half):
            for p, out_ref in enumerate((mine_out, other_out)):
                row = pl.multiple_of((2 * half * d + order[p * half + k]) * part, part)
                out_ref[k, d] = result[pl.ds(row, part)]


def weight_grads(dims, order, mixed, self_low, first_low, query_low, cross, cross_low):
    count, groups, part, depth = dims
    half = pl.BlockSpec((count // 2, groups, part, depth), lambda m, _: (0, 0, m, 0))
    return pl.pallas_call(
        weight_grads_kernel,
        grid_spec=pltpu.PrefetchScalarGridSpec(
            num_scalar_prefetch=1,
            grid=(3,),
            in_specs=[whole(mixed)] * 6,
            out_specs=[half, half],
            scratch_shapes=[pltpu.VMEM((depth, depth), jnp.bfloat16)],
        ),
        out_shape=[shape((count // 2, groups, 3 * part, depth), jnp.bfloat16)] * 2,
        compiler_params=params(),
        cost_estimate=cost(6 * mixed.shape[0] * depth * depth, 6 * depth * depth),
        name="weight_grads",
    )(order, mixed, self_low, first_low, query_low, cross, cross_low)


def send_dp(piece):
    size = lax.axis_size("dp")
    return [
        lax.ppermute(piece, "dp", [(i, (i + shift) % size) for i in range(size)])
        for shift in range(1, size)
    ]


def place_dp(piece, arrived):
    size, me = lax.axis_size("dp"), lax.axis_index("dp")
    result = jnp.zeros((size,) + piece.shape, piece.dtype)
    result = lax.dynamic_update_index_in_dim(result, piece, me, 0)
    for shift, got in enumerate(arrived, 1):
        result = lax.dynamic_update_index_in_dim(result, got, lax.rem(me - shift + size, size), 0)
    return result


class HalvingDp:
    def __init__(self, pieces):
        me = lax.axis_index("dp")
        self.parts = [
            lax.dynamic_index_in_dim(pieces, me ^ flip, 0, keepdims=False) for flip in DP_ORDER
        ]

    def first(self):
        return jnp.stack(self.parts[2:]).astype(jnp.bfloat16)

    def second(self, got):
        self.got = got
        return (
            self.parts[1].astype(jnp.float32) + self.got[1].astype(jnp.float32)
        ).astype(jnp.bfloat16)

    def finish(self, last):
        return sum(one.astype(jnp.float32) for one in (self.parts[0], self.got[0], last))


def relative_order():
    size, me = lax.axis_size("index"), lax.axis_index("index")
    steps = jnp.arange(size // 2, dtype=jnp.int32) * 2
    return jnp.concatenate([me ^ steps, me ^ 1 ^ steps])


def exchange(piece, flip):
    size = lax.axis_size("index")
    return lax.ppermute(piece, "index", [(i, i ^ flip) for i in range(size)])


def exchange_dp(piece, flip):
    size = lax.axis_size("dp")
    return lax.ppermute(piece, "dp", [(i, i ^ flip) for i in range(size)])


def add_kernel(*refs):
    total = sum(ref[...].astype(jnp.float32) for ref in refs[:-1])
    refs[-1][...] = total.astype(jnp.bfloat16)


def add(*terms):
    flat, specs = [], []
    first = terms[0]
    dims = first[0].shape[1:] if isinstance(first, tuple) else first.shape
    rows = 1
    for size in dims[:-1]:
        rows *= size
    block = min(rows, 256)
    for term in terms:
        array, entry = term if isinstance(term, tuple) else (term, 0)
        flat.append(array.reshape(-1, dims[-1]))
        start = entry * rows // block
        specs.append(pl.BlockSpec((block, dims[-1]), lambda i, start=start: (start + i, 0)))
    return pl.pallas_call(
        add_kernel,
        grid=(rows // block,),
        in_specs=specs,
        out_specs=pl.BlockSpec((block, dims[-1]), lambda i: (i, 0)),
        out_shape=shape((rows, dims[-1]), jnp.bfloat16),
        compiler_params=params(),
        cost_estimate=cost(0, 0),
        name="add",
    )(*flat).reshape(dims)


def combine_kernel(plan, *refs):
    ins, outs = list(refs[: -len(plan)]), refs[-len(plan) :]
    for out_ref, entries in zip(outs, plan):
        for e, segments in enumerate(entries):
            start = 0
            for offsets, rows in segments:
                terms, ins = ins[: len(offsets)], ins[len(offsets) :]
                total = sum(
                    ref[0, offset : offset + rows].astype(jnp.float32)
                    for ref, offset in zip(terms, offsets)
                )
                out_ref[e, start : start + rows] = total.astype(jnp.bfloat16)
                start += rows


def combine(*outputs):
    arrays, specs, plan, shapes = [], [], [], []
    for entries in outputs:
        plan.append([])
        for segments in entries:
            plan[-1].append([])
            for terms in segments:
                offsets = []
                for array, e, rows, start in terms:
                    block, place, offset = rows, start // rows, 0
                    if start % rows or array.shape[1] % rows:
                        block, place, offset = array.shape[1], 0, start
                    offsets.append(offset)
                    arrays.append(array)
                    specs.append(
                        pl.BlockSpec(
                            (1, block, array.shape[2]), lambda i, e=e, place=place: (e, place, 0)
                        )
                    )
                plan[-1][-1].append((offsets, terms[0][2]))
        rows = sum(rows for _, rows in plan[-1][0])
        shapes.append(shape((len(entries), rows, arrays[0].shape[2]), jnp.bfloat16))
    return pl.pallas_call(
        partial(combine_kernel, plan),
        grid=(1,),
        in_specs=specs,
        out_specs=[whole(out) for out in shapes],
        out_shape=shapes,
        compiler_params=params(),
        cost_estimate=cost(0, 0),
        name="combine",
    )(*arrays)


class Halving:
    def __init__(self, chips):
        self.chips = chips
        self.middle = chips[0][0][0].shape[1] // 2

    def terms(self, k, half, *more):
        middle = self.middle
        return [(array, e, middle, half * middle) for array, e in self.chips[k]] + [
            (array, e, middle, start) for array, e, start in more
        ]

    def total(self, k, half, *more):
        rows = slice(half * self.middle, (half + 1) * self.middle)
        parts = [array[e, rows] for array, e in self.chips[k]] + [*more]
        return sum(one.astype(jnp.float32) for one in parts)

    def finish(self, top, low):
        return jnp.concatenate(
            [self.total(0, 0, self.got[0][0], top), self.total(0, 1, self.got[1][0], low)], axis=0
        )


def both_cores(mine, other):
    parts = [part.reshape(CHIPS, -1, part.shape[-1]) for part in (mine, other)]
    return Halving([[(part, k) for part in parts] for k in range(CHIPS)])


def firsts(*sums):
    return combine(
        [[one.terms(k, 0) for one in sums] for k in (1, 3)],
        [[one.terms(k, 1) for one in sums] for k in (2, 3)],
    )


def seconds(*sums):
    for one, top, low, start in sums:
        rows = slice(start, start + one.middle)
        one.got = top[:, rows], low[:, rows]
    top, low = combine(
        [[one.terms(2, 0, (top, 1, start)) for one, top, _, start in sums]],
        [[one.terms(1, 1, (low, 1, start)) for one, _, low, start in sums]],
    )
    return top[0], low[0]


def send_first(top, low):
    return [exchange(top, 2), exchange(low, 4)]


def send_last(top, low):
    return [exchange(top, 4), exchange(low, 2)]


def split_rows(arrays, rows):
    return [a[..., :rows, :] for a in arrays], [a[..., rows:, :] for a in arrays]


def small_send(values):
    size = lax.axis_size("index")
    flat = jnp.pad(values.reshape(-1), (0, 1024 - values.size)).reshape(1, 8, 128)
    return swap(jnp.broadcast_to(flat, (size, 8, 128)))


def small_take(arrived, dims):
    size = 1
    for dim in dims:
        size *= dim
    return jnp.sum(arrived, axis=0).reshape(-1)[:size].reshape(dims)


def hold_kernel(*_):
    pass


def hold(values, *others):
    anywhere = pl.BlockSpec(memory_space=pl.ANY)
    return pl.pallas_call(
        hold_kernel,
        in_specs=[anywhere] * (len(values) + len(others)),
        out_specs=[anywhere] * len(values),
        out_shape=[shape(value.shape, value.dtype) for value in values],
        input_output_aliases={i: i for i in range(len(values))},
        name="hold",
    )(*values, *others)


def swap(pieces):
    return lax.all_to_all(pieces, "index", 0, 0, tiled=True)


def head_body(
    decoder_input,
    encoder_memory,
    question_vectors,
    passage_vectors,
    passage_ids,
    valid_count,
    output_grad,
    attention_weight,
    expand_weight,
    contract_weight,
    vector_params,
    attention_mean,
    attention_square,
    expand_mean,
    expand_square,
    contract_mean,
    contract_square,
    vector_mean,
    vector_square,
):
    low = jnp.bfloat16
    count, groups = lax.axis_size("index"), lax.axis_size("dp")
    place = lax.axis_index("index")
    seqs, rows_here, depth = decoder_input.shape
    memory_here = encoder_memory.shape[1]
    width = depth // count
    part = attention_weight.shape[1]
    hidden = expand_weight.shape[1]
    vector_rows, vector_width = vector_params.shape
    question_width = question_vectors.shape[1]
    rows = seqs * rows_here

    attention_low = attention_weight.astype(low)
    extras = jnp.concatenate(
        [vector_params.astype(low).reshape(-1), question_vectors.reshape(-1)]
    )
    extra_rows = -(-extras.shape[0] // (16 * width)) * 16
    extras = jnp.pad(extras, (0, extra_rows * width - extras.shape[0])).reshape(
        1, extra_rows, width
    )
    split = jnp.concatenate([attention_low[:3], attention_low[5:7]], axis=0)
    columns = split.reshape(5, part, count, width).transpose(2, 0, 1, 3)
    package = jnp.concatenate(
        [
            columns.reshape(count, 5 * part, width),
            jnp.broadcast_to(extras, (count, extra_rows, width)),
        ],
        axis=1,
    )
    order = relative_order()
    memory_block = -(-memory_here // 16) * 16
    rows_all = lax.all_gather(
        jnp.concatenate(
            [
                jnp.pad(encoder_memory, ((0, 0), (0, memory_block - memory_here), (0, 0))),
                decoder_input,
            ],
            axis=1,
        ),
        "index",
        axis=0,
        tiled=False,
    )
    input_rows = (rows_all, memory_block, rows_here)
    memory_rows = (rows_all, 0, memory_here)
    square = attention_low[3:5].transpose(1, 0, 2).reshape(part, 2 * depth)
    received = swap(package)
    square_arrived = hold(send_dp(square), received)
    (received,) = hold([received], *square_arrived)
    received_sent = send_dp(received)
    (contract,) = hold([contract_weight.astype(low)], received)
    contract = [contract] + [exchange(contract, 2 * k) for k in range(1, CHIPS)]
    slices_arrived = hold(received_sent, *contract[1:])
    square_arrived = hold(square_arrived, *slices_arrived)
    square = lax.all_gather(place_dp(square, square_arrived), "index", axis=0, tiled=False)
    slices = place_dp(received, slices_arrived)
    vectors = (
        slices[:, :, 5 * part :]
        .reshape(groups, count, extra_rows * width)[:, :, : vector_rows * vector_width]
        .reshape(groups, count, vector_rows, vector_width)
        .transpose(2, 0, 1, 3)
        .reshape(vector_rows, depth)
        .astype(jnp.float32)
    )
    question_full = (
        received[:, 5 * part :]
        .reshape(count, extra_rows * width)[:, vector_rows * vector_width :][
            :, : seqs * question_width
        ]
        .reshape(count, seqs, question_width)
        .transpose(1, 0, 2)
        .reshape(seqs, count * question_width)
    )
    expand_part = hidden // depth * part
    late = jnp.concatenate(
        [
            expand_weight.astype(low)
            .reshape(part, hidden // depth, depth)
            .transpose(1, 0, 2)
            .reshape(expand_part, depth),
            attention_low[7],
        ],
        axis=0,
    )
    (late,) = hold([late], *slices_arrived)
    late_sent = send_dp(late)

    (passage_ids,) = hold([passage_ids], *slices_arrived)
    passages_here = passage_vectors.shape[0]
    local_ids = passage_ids - place * passages_here
    owned_slot = (local_ids >= 0) & (local_ids < passages_here)
    picked = passage_vectors[jnp.clip(local_ids, 0, passages_here - 1)]
    local_scores = jnp.einsum(
        "sc,skc->sk", question_full, picked, preferred_element_type=jnp.float32
    )
    slots = passage_ids.shape[1]
    usable = jnp.arange(slots)[None, :] < valid_count[:, None]
    scores = small_take(small_send(jnp.where(owned_slot, local_scores, 0.0)), local_scores.shape)
    masked = jnp.where(usable, scores, negative_fill)
    maximum = jnp.max(masked, axis=1)
    exponent = jnp.where(usable, jnp.exp(masked - maximum[:, None]), 0.0)
    partition = jnp.sum(exponent, axis=1)
    passage_prob = exponent / partition[:, None]
    log_prior = jnp.where(
        usable, masked - maximum[:, None] - jnp.log(partition)[:, None], negative_fill
    )
    key_bias = jnp.repeat(log_prior, MEM_P, axis=1)

    vector_here = lax.dynamic_slice_in_dim(vectors[:5], place * width, width, axis=1)
    no_bias = jnp.zeros((1, width), jnp.float32)
    qkv_bias = jnp.concatenate([vector_here[0:1], no_bias, vector_here[1:2]], axis=1)
    kv_bias = jnp.concatenate([no_bias, vector_here[4:5]], axis=1)
    x_rows = decoder_input.reshape(rows, depth)
    qkv = project_columns("self_qkv", *input_rows, slices, 0, 3, qkv_bias)
    self_out, self_stat = attend(True, qkv, 0, qkv, 1, 2, key_bias[:, None, :])
    self_out, *late_arrived = hold([self_out, *late_sent])
    self_got = swap(self_out)
    late = lax.all_gather(place_dp(late, late_arrived), "index", axis=0, tiled=False)
    ahead, across = hold([jnp.stack(contract[:2]), jnp.stack(contract[2:])], *late_arrived)
    self_got, ahead_far, across_far = hold(
        [self_got, exchange_dp(ahead, 2), exchange_dp(across, 1)]
    )
    ahead = jnp.stack([ahead, ahead_far])
    across = jnp.stack([across, across_far])
    contract_sent = [exchange_dp(ahead, 1), exchange_dp(across, 2)]
    self_mixed, first_in, first_low, cross_query = first_forward(
        self_got, x_rows, square, vectors, ahead_far
    )
    (slices,) = hold([slices], first_low)
    memory_kv = project_columns("memory_kv", *memory_rows, slices, 3, 2, kv_bias)
    cross_query = swap(cross_query)[:, None]
    cross_out, cross_stat = attend(
        False, cross_query, 0, memory_kv, 0, 1, key_bias[:, None, :]
    )
    ahead_far, across_far = hold(contract_sent, cross_out)
    contract = [ahead, ahead_far, across, across_far]
    contract += [exchange(piece, 1) for piece in contract]
    places = lax.axis_index("dp") ^ jnp.array(DP_ORDER, jnp.int32)
    (
        cross_mixed,
        layer_output,
        wide_grad,
        *contract_grads,
        inner_total,
        second_grad,
        cross_low,
        cross_mix_grad,
        stats,
    ) = ffn(
        (order, places),
        swap(cross_out),
        first_in,
        late,
        contract,
        vectors,
        vectors[6:10].reshape(groups * count, -1),
        output_grad.reshape(rows, depth),
    )
    third_stat, second_stat = stats[:8], stats[8:]

    expand_part_sum = lax.psum_scatter(wide_grad, "index", scatter_dimension=0, tiled=False)
    ahead, ahead_far, across, across_far = contract_grads[:4]
    cores = [exchange(piece, 1) for piece in contract_grads[4:]]
    cross_mix_got, *contract_sent = hold(
        [swap(cross_mix_grad), add(ahead_far, cores[1]), add(across_far, cores[3])]
    )
    contract_got = [exchange_dp(contract_sent[0], 1), exchange_dp(contract_sent[1], 2)]
    cross_dq, cross_dkv, prior_rows = attend_back(
        False,
        cross_query,
        0,
        memory_kv,
        0,
        1,
        cross_mix_got,
        cross_stat,
        key_bias[:, None, :],
        contract_sent[0],
    )
    memory_mine, memory_other, kv_grads, kv_total = project_columns_back(
        "memory_kv_back", order, *memory_rows, [cross_dkv], slices, 3, 2
    )
    cross_dq, *contract_got = hold([cross_dq, *contract_got], memory_mine)
    contract_next = [
        add((ahead, 1), (cores[0], 1), (contract_got[0], 1)),
        add((across, 1), (cores[2], 1), (contract_got[1], 1)),
    ]
    cross_dq_got, *contract_next = hold([swap(cross_dq), *contract_next])
    contract_last = [exchange_dp(contract_next[0], 2), exchange_dp(contract_next[1], 1)]
    query_low, first_grad, self_low, self_mix_grad, first_stat = first_back(
        cross_dq_got, second_grad, first_in, square, vectors, memory_mine
    )
    memory_sum = both_cores(memory_mine, exchange(memory_other, 1))
    memory_sent = firsts(memory_sum)
    square_mine, square_other = weight_grads(
        (count, groups, part, depth),
        order,
        self_mixed,
        self_low,
        first_low,
        query_low,
        cross_mixed,
        cross_low,
    )
    square_sum = both_cores(square_mine, exchange(square_other, 1))
    square_sent = firsts(square_sum)
    self_mix_got, *contract_last = hold(
        [swap(self_mix_grad), *contract_last], *memory_sent, *square_sent
    )
    memory_got = send_first(*memory_sent)
    square_got = send_first(*square_sent)
    self_dq, self_dkv, _ = attend_back(
        True, qkv, 0, qkv, 1, 2, self_mix_got, self_stat, self_stat, square_mine
    )
    expand_sum = HalvingDp(expand_part_sum)
    self_dq, expand_sent = hold([self_dq, expand_sum.first()])
    dx_mine, dx_other, qkv_slice_grads, qkv_total = project_columns_back(
        "self_qkv_back", order, *input_rows, [self_dq, self_dkv], slices, 0, 3
    )
    dx_mine, dx_other, *got = hold([dx_mine, dx_other, *memory_got, *square_got])
    own = jnp.concatenate(
        [qkv_total[:, :width], qkv_total[:, 2 * width :], kv_total[:, width:]], axis=0
    )
    own = lax.dynamic_update_slice(
        jnp.zeros((3, depth), jnp.float32), own, (jnp.int32(0), place * width)
    )
    vector_grads = jnp.concatenate(
        [
            own[:2],
            first_stat[1:2],
            first_stat[0:1],
            own[2:],
            second_stat[0:1],
            inner_total.reshape(hidden // depth, depth),
            third_stat[0:1],
            first_stat[2:4],
            second_stat[1:3],
            third_stat[1:3],
        ],
        axis=0,
    )
    vector_size = vector_rows * vector_width
    question_size = seqs * question_width
    vector_send = (
        vector_grads.reshape(vector_rows, groups, count, vector_width)
        .transpose(1, 2, 0, 3)
        .reshape(groups, count, vector_size)
    )
    vector_send = jnp.pad(
        vector_send, ((0, 0), (0, 0), (0, extra_rows * width - vector_size))
    ).reshape(groups, count, extra_rows, width)
    slice_sum = HalvingDp(
        jnp.concatenate([qkv_slice_grads, kv_grads, vector_send.astype(low)], axis=2)
    )
    slice_sent = slice_sum.first()
    slice_got = exchange_dp(slice_sent, 1)
    dx_other, *got = hold([dx_other, *got], slice_sent)
    dx_got = exchange(dx_other, 1)
    square_rows = square_sum.middle
    last = seconds((square_sum, *got[2:], 0), (memory_sum, *got[:2], 0))
    prior_rows, expand_sent, *contract_last = hold(
        [prior_rows, expand_sent, *contract_last], *last
    )
    last = send_last(*last)
    expand_got = exchange_dp(expand_sent, 1)
    prior_arrived = small_send(prior_rows.reshape(seqs, slots, MEM_P).sum(axis=-1))
    dx_got, prior_arrived, slice_got, *last = hold([dx_got, prior_arrived, slice_got, *last])
    slice_next = slice_sum.second(slice_got)
    dx_got, *last = hold([dx_got, *last], slice_next)
    slice_last = exchange_dp(slice_next, 2)
    dx_sum = both_cores(dx_mine, dx_got)
    contract_sum = Halving(
        [
            [(one.reshape((-1,) + one.shape[-2:]), k % 2) for one in parts]
            for k, parts in enumerate(
                [(ahead, cores[0], contract_got[0], contract_last[0])] * 2
                + [(across, cores[2], contract_got[1], contract_last[1])] * 2
            )
        ]
    )
    dx_sent = firsts(dx_sum, contract_sum)
    got = send_first(*dx_sent)
    last = hold(last, *dx_sent)
    square_last, memory_last = split_rows(last, square_rows)
    square_far = HalvingDp(square_sum.finish(*square_last).reshape(groups, 3 * part, depth))
    square_got = exchange_dp(square_far.first(), 1)
    slice_sum = slice_sum.finish(slice_last)
    prior_grad = jnp.where(usable, small_take(prior_arrived, (seqs, slots)), 0.0)
    score_doc = jnp.where(
        usable, prior_grad - passage_prob * jnp.sum(prior_grad, axis=1, keepdims=True), 0.0
    )
    question_part = jnp.einsum(
        "sk,skc->sc",
        jnp.where(owned_slot, score_doc, 0.0),
        picked.astype(jnp.float32),
        precision=lax.Precision.HIGHEST,
    )

    question_send = (
        question_part.reshape(seqs, count, question_width)
        .transpose(1, 0, 2)
        .reshape(count, question_size)
    )
    question_send = jnp.pad(
        question_send,
        ((0, 0), (vector_size, extra_rows * width - vector_size - question_size)),
    ).reshape(count, extra_rows, width)
    slice_sum = jnp.concatenate(
        [slice_sum[:, : 5 * part], slice_sum[:, 5 * part :] + question_send], axis=1
    )
    slice_send = slice_sum.astype(low)
    arrived = swap(slice_send)
    square_got, expand_got = hold([square_got, expand_got], slice_send)
    square_next, expand_next = square_far.second(square_got), expand_sum.second(expand_got)
    got = hold(got, square_next, expand_next)
    square_last, expand_last = exchange_dp(square_next, 2), exchange_dp(expand_next, 2)
    start = dx_sum.middle
    last = seconds((dx_sum, *got, 0), (contract_sum, *got, start))
    square_last, expand_last = hold([square_last, expand_last], *last)
    last = send_last(*last)
    dx_last, contract_last = split_rows(last, start)
    input_gradient = first_grad + dx_sum.finish(*dx_last)
    contract_sum = contract_sum.finish(*contract_last)
    memory_last = hold(memory_last, *got)
    memory_gradient = memory_sum.finish(*memory_last).reshape(encoder_memory.shape)
    new_contract = adam_update(
        contract_weight, contract_mean, contract_square, contract_sum, rate_contract, decay_matrix
    )
    arrived = arrived.astype(jnp.float32)
    split_grads = (
        arrived[:, : 5 * part]
        .reshape(count, 5, part, width)
        .transpose(1, 2, 0, 3)
        .reshape(5, part, depth)
    )
    extra_sum = jnp.sum(arrived[:, 5 * part :].reshape(count, extra_rows * width), axis=0)
    vector_sum = extra_sum[:vector_size].reshape(vector_rows, vector_width)
    question_gradient = extra_sum[vector_size : vector_size + question_size].reshape(
        seqs, question_width
    )

    expand_sum = (
        expand_sum.finish(expand_last)
        .reshape(hidden // depth, part, depth)
        .transpose(1, 0, 2)
        .reshape(part, hidden)
    )
    square_total = square_far.finish(square_last).reshape(3, part, depth)
    attention_sum = jnp.concatenate(
        [split_grads[:3], square_total[:2], split_grads[3:], square_total[2:]], axis=0
    )

    new_attention = adam_update(
        attention_weight,
        attention_mean,
        attention_square,
        attention_sum,
        rate_attention,
        decay_matrix,
    )
    new_expand = adam_update(
        expand_weight, expand_mean, expand_square, expand_sum, rate_expand, decay_matrix
    )
    new_vector = adam_update(
        vector_params, vector_mean, vector_square, vector_sum, rate_vector, 0.0
    )
    return (
        layer_output.reshape(decoder_input.shape),
        input_gradient.reshape(decoder_input.shape),
        memory_gradient,
        question_gradient,
        *new_attention,
        *new_expand,
        *new_contract,
        *new_vector,
    )


def body(sizes, *arrays):
    depth = arrays[0].shape[2]
    if sizes == (4, 8) and depth // 8 % 128 == 0:
        return head_body(*arrays)
    return general_body(*arrays)


def solution(mesh):
    return jax.shard_map(
        partial(body, (mesh.shape["dp"], mesh.shape["index"])),
        mesh=mesh,
        in_specs=(
            P("dp", "index", None),
            P("dp", "index", None),
            P("dp", "index"),
            P("index", None),
            P("dp", None),
            P("dp"),
            P("dp", "index", None),
            P(None, ("dp", "index"), None),
            P(("dp", "index"), None),
            P(("dp", "index"), None),
            P(None, ("dp", "index")),
            P(None, ("dp", "index"), None),
            P(None, ("dp", "index"), None),
            P(("dp", "index"), None),
            P(("dp", "index"), None),
            P(("dp", "index"), None),
            P(("dp", "index"), None),
            P(None, ("dp", "index")),
            P(None, ("dp", "index")),
        ),
        out_specs=(
            P("dp", "index", None),
            P("dp", "index", None),
            P("dp", "index", None),
            P("dp", "index"),
            P(None, ("dp", "index"), None),
            P(None, ("dp", "index"), None),
            P(None, ("dp", "index"), None),
            P(("dp", "index"), None),
            P(("dp", "index"), None),
            P(("dp", "index"), None),
            P(("dp", "index"), None),
            P(("dp", "index"), None),
            P(("dp", "index"), None),
            P(None, ("dp", "index")),
            P(None, ("dp", "index")),
            P(None, ("dp", "index")),
        ),
        check_vma=False,
    )
```
